32 devices in a mesh: groups: 2 (over y), seq: 4 (over z), tp: 2 (over x), section: 2 (over core).
Axes of the slice: x: 2, y: 2, z: 4, core: 2. Of those that a mesh axis runs over, the one named last changes fastest.
Arguments:
- tokens: bfloat16 [2048, 16384], P(('groups', 'tp', 'section'), 'seq'), parts along dimension 0, may hold values from -6 to 6
- kv_weight: bfloat16 [16384, 1024], P('seq'), may hold values from -0.046875 to 0.046875
- owners: int32 [8, 256, 1], P(('groups', 'tp', 'section'), 'seq'), parts along dimension 0, may hold values from 0 to 3; in each aligned block of 64 rows (0 to 63, 64 to 127, ..., all dimensions but the last counted through in order) at most 32 rows name the same one
- requests: int32 [8, 256], P(('groups', 'tp', 'section'), 'seq'), parts along dimension 0, may hold values from 0 to 7
- signs: int32 [8, 128], replicated, may hold values from 0 to 1
- queries: bfloat16 [8, 2, 8, 4096], P(('groups', 'seq'), 'section'), parts along dimension 0, may hold values from -96 to 96
- kv_cache: bfloat16 [8, 2, 8, 256, 1024], P(('groups', 'seq'), 'section', None, 'tp'), parts along dimension 0, may hold values from -96 to 96
- lengths: int32 [8, 2, 8], P(('groups', 'seq'), 'section'), parts along dimension 0, may hold values from 1 to 256, 1280 in all within a row
Outputs:
- attended: bfloat16 [8, 2, 8, 4096], P(('groups', 'seq'), 'section'), parts along dimension 0
The draws below stay inside these ranges and needn't reach their ends.
There are 2 independent parts, one for each index of `groups`. The reference program is written for one: setup_inputs(seed, part) draws one part's arguments, and reference() takes and returns one part's arrays. A program takes and returns all parts, laid end to end along the dimension named above; an argument that names none is the same for every part. Nothing has to cross between parts.
Inputs may be any that keep to these rules, and one draw needn't show every extreme that they name: `owners`: in the rows of one device (64 aligned rows) no owner is named more than 32 times. The lengths of one owner's requests sum to 1280.
All inputs are finite; a program needn't handle non-finite values.
Results may differ from the reference program's by a relative error of at most 0.025.
Values may be sent and summed in bfloat16 or wider, within the bound.
No kernel may reach another device: no remote copies, remote signals or barrier semaphores. Data moves between devices by JAX's collectives and lax.ppermute only.
A program may use at most 64 MiB of HBM per device.

```python
import math
import jax
import jax.numpy as jnp
import numpy as np
from jax import lax

D = 16384
HD = 128
KVH = 4
PRE_DEV = 64
REQ = 8
NQH = 32
CACHE = 256
TOKENS = 1024
CAP = 32
N_SEQ = 4
N_TP = 2
N_SECTION = 2


def draw_queries(key, part):
    key = jax.random.fold_in(key, 11)
    base_key = jax.random.fold_in(key, 0)
    base = jnp.clip(jax.random.normal(base_key, (N_SEQ, N_SECTION, REQ, NQH * HD), jnp.float32), -6.0, 6.0)
    values = base
    return values.astype(jnp.bfloat16)


def draw_kv_cache(key, part):
    key = jax.random.fold_in(key, 23)
    base_key = jax.random.fold_in(key, 0)
    shape = (N_SEQ, N_SECTION, REQ, CACHE, 2 * KVH * HD)
    base = jnp.clip(jax.random.normal(base_key, shape, jnp.float32), -6.0, 6.0)
    values = base
    return values.astype(jnp.bfloat16)


def with_ends(entries, key, low, high):
    longest = entries.shape.index(max(entries.shape))
    spots = []
    for shift in (0, 1):
        where = [jax.random.randint(jax.random.fold_in(key, axis), (), 0, length) for axis, length in enumerate(entries.shape)]
        where[longest] = (where[longest] + shift) % entries.shape[longest]
        spots.append(tuple(where))
    return entries.at[spots[0]].set(low).at[spots[1]].set(high)


def raised(entries, key, source, target, blocks, factor):
    def block_of(axis_at):
        return (jnp.arange(entries.shape[axis_at]) // (entries.shape[axis_at] // blocks)).reshape((-1,) + (1,) * (entries.ndim - 1 - axis_at))

    near = jax.random.permutation(key, blocks)[block_of(target)]
    far = (block_of(target) + blocks // 2) % blocks
    return jnp.where((block_of(source) == near) | (block_of(source) == far), factor * entries, entries)


def block_levels(own_key, shape, cuts, smallest, top_value):
    level = 1.0
    for position, shards_of in cuts:
        heights = jax.random.uniform(jax.random.fold_in(jax.random.fold_in(own_key, 6), position), (shards_of,), jnp.float32, smallest / len(cuts), top_value / len(cuts))
        level = level * jnp.repeat(jnp.exp(heights), shape[position] // shards_of).reshape((-1,) + (1,) * (len(shape) - 1 - position))
    return level


def split_up(count, total, most, slope):
    loads = [(1 << 20) // math.isqrt(grade ** slope) + 1 for grade in range(2, count + 1)]
    surplus, given = total - most - (count - 1), [1] * (count - 1)
    while surplus > 0:
        movable = [i for i in range(count - 1) if given[i] < most]
        whole, remaining = sum([loads[i] for i in movable]), surplus
        for i in movable:
            addition = min(most - given[i], max(1, remaining * loads[i] // whole), surplus)
            given[i] = given[i] + addition
            surplus = surplus - addition
    return np.array([most] + given)


def ragged_sizes(own_key, number_of, total, reach, skew):
    if number_of == 2:
        one = jax.random.randint(own_key, (), max(1, total - reach), min(reach, total - 1) + 1)
        return jnp.stack([one, total - one])
    sizes = jnp.asarray(split_up(number_of, total, reach, skew), jnp.int32)
    couples = (number_of - 1) // 2
    donor, receiver = sizes[1:1 + 2 * couples:2], sizes[2:2 + 2 * couples:2]
    margin = jnp.minimum(donor - 1, reach - receiver)
    passed = jax.random.randint(jax.random.fold_in(own_key, 1), (couples,), 0, 1 << 20) % (margin + 1)
    sizes = sizes.at[1:1 + 2 * couples:2].set(donor - passed).at[2:2 + 2 * couples:2].set(receiver + passed)
    return sizes[jax.random.permutation(jax.random.fold_in(own_key, 2), number_of)]


def shared_out(stream_key, own, number, rows, count, top, limit, slope):
    sequence = jax.random.permutation(stream_key, count)
    packed, ordinary = shares(count, rows * top, limit, slope, True), shares(count, rows * top, limit, slope, False)
    places = jnp.arange(count)

    def named(tallies, offset_by):
        used = int((tallies > 0).sum())
        fixed = max(1, used // 4)
        moved = fixed + (places - fixed + offset_by * (used - fixed)) % max(1, count - fixed)
        return jnp.zeros((count,), jnp.int32).at[sequence[jnp.where(places < fixed, places, moved)]].set(jnp.asarray(tallies, jnp.int32))

    tallies = jnp.where(number % 4 == 0, named(packed, number // 4), named(ordinary, number - number // 4 - 1))
    mixed = jax.random.permutation(jax.random.fold_in(own, 3), count)
    donor, taker = mixed[0:count // 2 * 2:2], mixed[1:count // 2 * 2:2]
    slack = jnp.minimum(tallies[donor] - 1, limit - tallies[taker]) // 2
    slack = jnp.where((donor == sequence[0]) | (taker == sequence[0]) | (tallies[taker] == 0), 0, jnp.maximum(slack, 0))
    moved = jax.random.randint(jax.random.fold_in(own, 4), (count // 2,), 0, 1 << 20) % (slack + 1)
    tallies = tallies.at[donor].add(-moved).at[taker].add(moved)
    labels = jnp.searchsorted(jnp.cumsum(tallies), jnp.arange(rows * top), side="right").astype(jnp.int32)
    listing = labels.reshape(top, rows).T
    listing = listing[jax.random.permutation(jax.random.fold_in(own, 1), rows)]
    offset_by = jax.random.randint(jax.random.fold_in(own, 2), (rows, 1), 0, top)
    return jnp.take_along_axis(listing, (jnp.arange(top)[None, :] + offset_by) % top, axis=1)


def shares(count, total, reach, skew, full):
    loads = [(1 << 20) // math.isqrt(rank ** skew) + 1 for rank in range(1, count + 1)]
    largest = reach if full else min(reach, max(-(-total // count), total * loads[0] // sum(loads)))
    least = 1 if total - largest >= count - 1 else 0
    given, surplus = [largest] + [least] * (count - 1), total - largest - least * (count - 1)
    while surplus > 0:
        free = [i for i in range(1, count) if given[i] < largest] or [i for i in range(1, count) if given[i] < reach]
        pool, left = sum([loads[i] for i in free]), surplus
        for i in free:
            addition = min(reach - given[i], max(1, left * loads[i] // pool), surplus)
            given[i] = given[i] + addition
            surplus = surplus - addition
    return np.array(given)


def normal_values(stream_key, shape, scale, limit, cuts=(), kind=jnp.bfloat16):
    drawn = scale * jax.random.normal(stream_key, shape, jnp.float32)
    if cuts:
        drawn = drawn * block_levels(stream_key, shape, cuts, -0.22, 0.18)
    return jnp.clip(drawn, -limit, limit).astype(kind)


def bell_draw_with(key, extent, scale, most, cuts, heavy, kind=jnp.bfloat16):
    drawn = scale * jax.random.normal(key, extent, jnp.float32)
    if cuts:
        drawn = drawn * block_levels(key, extent, cuts, -0.22, 0.18)
    return jnp.clip(raised(drawn, jax.random.fold_in(key, 3), *heavy), -most, most).astype(kind)


def setup_inputs(seed: int = 0, part: int = 0) -> dict:
    key_list = jax.random.split(jax.random.key(seed), 9)
    own_keys = jax.random.split(jax.random.fold_in(key_list[8], part), 9)
    tokens = bell_draw_with(own_keys[0], (TOKENS, D), 1.0, 6.0, ((0, 4), (1, 4)), (1, 0, 4, 2.0))
    kv_weight = normal_values(key_list[1], (D, 2 * KVH * HD), D ** -0.5, 0.046875, ((0, 4),))
    owners_keys = jax.random.split(jax.random.fold_in(own_keys[2], 1), (N_TP * N_SECTION) * (N_SEQ * PRE_DEV) // PRE_DEV)
    owners_turns = jax.random.permutation(jax.random.fold_in(own_keys[2], 3), (N_TP * N_SECTION) * (N_SEQ * PRE_DEV) // PRE_DEV)
    owners = jax.vmap(lambda own, number: shared_out(jax.random.fold_in(own_keys[2], 2), own, number, PRE_DEV, N_SEQ, 1, CAP, 2))(owners_keys, owners_turns).reshape((N_TP * N_SECTION, N_SEQ * PRE_DEV, 1))
    requests = with_ends(jax.random.randint(own_keys[3], (N_TP * N_SECTION, N_SEQ * PRE_DEV), 0, REQ), jax.random.fold_in(own_keys[3], 1), 0, REQ - 1).astype(jnp.int32)
    signs = with_ends(jax.random.randint(key_list[4], (2 * KVH, HD), 0, 2), jax.random.fold_in(key_list[4], 1), 0, 1).astype(jnp.int32)
    queries = draw_queries(jax.random.fold_in(jax.random.fold_in(key_list[8], part), 71), part)
    kv_cache = draw_kv_cache(jax.random.fold_in(jax.random.fold_in(key_list[8], part), 71), part)
    lengths = jax.vmap(lambda own: ragged_sizes(own, REQ, 5 * REQ * CACHE // 8, CACHE, 2))(jax.random.split(own_keys[7], N_SEQ * N_SECTION)).reshape((N_SEQ, N_SECTION, REQ)).astype(jnp.int32)
    return {"tokens": tokens, "kv_weight": kv_weight, "owners": owners, "requests": requests, "signs": signs, "queries": queries, "kv_cache": kv_cache, "lengths": lengths}


def hadamard(order):
    rows = lax.broadcasted_iota(jnp.int32, (order, order), 0)
    cols = lax.broadcasted_iota(jnp.int32, (order, order), 1)
    parity = jnp.zeros((order, order), jnp.int32)
    for bit_number in range(order.bit_length() - 1):
        parity = parity + rows // 2 ** bit_number % 2 * (cols // 2 ** bit_number % 2)
    return (1 - 2 * (parity % 2)).astype(jnp.float32)

def rotate(blocks, sign_rows, matrix):
    product = jnp.einsum('...h,hk->...k', blocks * sign_rows, matrix, precision=lax.Precision.HIGHEST)
    return product / math.sqrt(matrix.shape[0])

def encode(rotated):
    largest = lax.optimization_barrier(jnp.max(jnp.abs(rotated), axis=-1)) + 1e-06
    scales = largest.astype(jnp.bfloat16)
    encoded = (rotated / scales.astype(jnp.float32)[..., None]).astype(jnp.bfloat16)
    return (encoded, scales)

def decode(encoded, scales):
    return (encoded.astype(jnp.float32) * scales.astype(jnp.float32)[..., None]).astype(jnp.bfloat16)

def reference(tokens, kv_weight, owners, requests, signs, queries, kv_cache, lengths):
    matrix = hadamard(HD)
    sign_rows = (2 * signs - 1).astype(jnp.float32)
    features = D // N_SEQ
    width = 2 * KVH * HD

    def add_block(index, total):
        start = index * features
        part_rows = lax.dynamic_slice_in_dim(tokens, start, features, 1)
        part_weight = lax.dynamic_slice_in_dim(kv_weight, start, features, 0)
        partial_sum = jnp.dot(part_rows, part_weight, preferred_element_type=jnp.float32).astype(jnp.bfloat16)
        partial_sum = lax.optimization_barrier(partial_sum)
        return total + partial_sum.astype(jnp.float32)
    summed = lax.fori_loop(0, N_SEQ, add_block, jnp.zeros((TOKENS, width), jnp.float32))
    rotated = rotate(summed.reshape(TOKENS, 2 * KVH, HD), sign_rows, matrix)
    encoded, scales = encode(rotated)
    new_kv = decode(encoded, scales)
    block_rows = N_SEQ * PRE_DEV
    new_kv = new_kv.reshape(N_TP, N_SECTION, block_rows, 2 * KVH, HD)
    owner_grid = owners.reshape(N_TP, N_SECTION, block_rows)
    request_grid = requests.reshape(N_TP, N_SECTION, block_rows)
    group = NQH // KVH
    query = queries.astype(jnp.float32).reshape(N_SEQ, N_SECTION, REQ, KVH, group, HD)
    query_rot = rotate(query, sign_rows[:KVH][:, None, :], matrix).astype(jnp.bfloat16)
    cache = kv_cache.reshape(N_SEQ, N_SECTION, REQ, CACHE, 2 * KVH, HD)
    score_scale = 1.0 / math.sqrt(HD)
    lowest = -1e+30
    highest = lax.Precision.HIGHEST

    def attend(flat):
        seq_rank = flat // N_SECTION
        section_rank = flat % N_SECTION
        query_here = query_rot[seq_rank, section_rank].astype(jnp.float32)
        cache_here = cache[seq_rank, section_rank].astype(jnp.float32)
        rows_new = jnp.take(new_kv, section_rank, axis=1).reshape(N_TP * block_rows, 2 * KVH, HD).astype(jnp.float32)
        owner_new = jnp.take(owner_grid, section_rank, axis=1).reshape(N_TP * block_rows)
        request_new = jnp.take(request_grid, section_rank, axis=1).reshape(N_TP * block_rows)
        score_cache = jnp.einsum('rkgd,rckd->rkgc', query_here, cache_here[:, :, :KVH], precision=highest) * score_scale
        score_new = jnp.einsum('rkgd,nkd->rkgn', query_here, rows_new[:, :KVH], precision=highest) * score_scale
        live = lax.iota(jnp.int32, CACHE)[None, :] < lengths[seq_rank, section_rank][:, None]
        mask_cache = live[:, None, None, :]
        match = (owner_new == seq_rank)[None, :] & (request_new[None, :] == lax.iota(jnp.int32, REQ)[:, None])
        mask_new = match[:, None, None, :]
        top = jnp.maximum(lax.optimization_barrier(jnp.max(jnp.where(mask_cache, score_cache, lowest), axis=-1)), lax.optimization_barrier(jnp.max(jnp.where(mask_new, score_new, lowest), axis=-1)))
        probs_cache = jnp.where(mask_cache, jnp.exp(score_cache - top[..., None]), 0.0)
        probs_new = jnp.where(mask_new, jnp.exp(score_new - top[..., None]), 0.0)
        total = lax.optimization_barrier(jnp.sum(probs_cache, axis=-1)) + lax.optimization_barrier(jnp.sum(probs_new, axis=-1))
        mixed = jnp.einsum('rkgc,rckd->rkgd', probs_cache, cache_here[:, :, KVH:], precision=highest)
        mixed = mixed + jnp.einsum('rkgn,nkd->rkgd', probs_new, rows_new[:, KVH:], precision=highest)
        mixed = mixed / total[..., None]
        output = rotate(mixed, 1.0, matrix) * sign_rows[KVH:][None, :, None, :]
        return output.reshape(REQ, NQH * HD).astype(jnp.bfloat16)
    result = lax.map(attend, jnp.arange(N_SEQ * N_SECTION, dtype=jnp.int32))
    return result.reshape(N_SEQ, N_SECTION, REQ, NQH * HD)
```

```python
import functools
import math

import jax
import jax.numpy as jnp
from jax import lax
from jax.experimental import pallas as pl
from jax.experimental.pallas import tpu as pltpu
from jax.sharding import PartitionSpec as P

LOWEST = -1e30
VMEM_LIMIT = 48 * 1024 * 1024
NT = (((1,), (1,)), ((), ()))


def params():
    return pltpu.CompilerParams(vmem_limit_bytes=VMEM_LIMIT)


def hadamard_tile(order):
    rows = lax.broadcasted_iota(jnp.int32, (order, order), 0)
    cols = lax.broadcasted_iota(jnp.int32, (order, order), 1)
    common = rows & cols
    parity = jnp.zeros((order, order), jnp.int32)
    for bit_number in range(order.bit_length() - 1):
        parity = parity ^ (common >> bit_number)
    return (1 - 2 * (parity & 1)).astype(jnp.float32).astype(jnp.bfloat16)


def project_kernel(tokens_ref, weight_ref, out_ref, acc_ref):
    step = pl.program_id(0)
    part = jnp.dot(tokens_ref[...], weight_ref[...], preferred_element_type=jnp.float32)

    @pl.when(step == 0)
    def _():
        acc_ref[...] = part

    @pl.when(step > 0)
    def _():
        acc_ref[...] += part

    @pl.when(step == pl.num_programs(0) - 1)
    def _():
        out_ref[...] = acc_ref[...].astype(out_ref.dtype)


def project(tokens, weight):
    rows, features = tokens.shape
    width = weight.shape[1]
    block = min(512, features)
    return pl.pallas_call(
        project_kernel,
        grid=(features // block,),
        in_specs=[
            pl.BlockSpec((rows, block), lambda i: (0, i)),
            pl.BlockSpec((block, width), lambda i: (i, 0)),
        ],
        out_specs=pl.BlockSpec((rows, width), lambda i: (0, 0)),
        out_shape=jax.ShapeDtypeStruct((rows, width), jnp.bfloat16),
        scratch_shapes=[pltpu.VMEM((rows, width), jnp.float32)],
        compiler_params=params(),
        cost_estimate=pl.CostEstimate(
            flops=2 * rows * features * width,
            bytes_accessed=2 * (rows * features + features * width),
            transcendentals=0,
        ),
        name="project",
    )(tokens, weight)


def cache_kernel(heads, lengths_ref, query_ref, keys_ref, values_ref, signs_ref, mixed_ref, stats_ref):
    requests, span, size = keys_ref.shape
    group = query_ref.shape[1] // size
    head = pl.program_id(0)
    matrix = hadamard_tile(size)
    norm = 1.0 / math.sqrt(size)
    key_sign = (2 * signs_ref[pl.ds(head, 1), :] - 1).astype(jnp.float32)
    value_sign = (2 * signs_ref[pl.ds(heads + head, 1), :] - 1).astype(jnp.float32)
    query = query_ref[...].astype(jnp.float32)
    query = jnp.concatenate([query[:, g * size : (g + 1) * size] for g in range(group)], axis=0)
    query = (query * key_sign).astype(jnp.bfloat16)
    rotated = (jnp.dot(query, matrix, preferred_element_type=jnp.float32) * norm).astype(jnp.bfloat16)
    keys = keys_ref[...].reshape(requests * span, size)
    scores = lax.dot_general(rotated, keys, NT, preferred_element_type=jnp.float32) * norm
    shape = scores.shape
    row_request = lax.broadcasted_iota(jnp.int32, shape, 0) % requests
    lane = lax.broadcasted_iota(jnp.int32, shape, 1)
    position = lax.axis_index("tp") * span + lane % span
    limit = jnp.concatenate(
        [jnp.full((1, span), lengths_ref[0, 0, r], jnp.int32) for r in range(requests)], axis=1
    )
    live = (row_request == lane // span) & (position < limit)
    top = jnp.max(jnp.where(live, scores, LOWEST), axis=1, keepdims=True)
    probs = jnp.where(live, jnp.exp(scores - top), 0.0)
    total = jnp.sum(probs, axis=1, keepdims=True)
    values = values_ref[...].reshape(requests * span, size)
    mixed = jnp.dot(probs.astype(jnp.bfloat16), values, preferred_element_type=jnp.float32)
    high = mixed.astype(jnp.bfloat16)
    low = (mixed - high.astype(jnp.float32)).astype(jnp.bfloat16)
    plain = jnp.dot(high, matrix, preferred_element_type=jnp.float32)
    plain = plain + jnp.dot(low, matrix, preferred_element_type=jnp.float32)
    plain = plain * (value_sign * norm)

    @pl.when(head == 0)
    def _():
        stats_ref[...] = jnp.zeros_like(stats_ref)

    columns = lax.broadcasted_iota(jnp.int32, (requests, stats_ref.shape[1]), 1)
    for g in range(group):
        rows = slice(g * requests, (g + 1) * requests)
        mixed_ref[:, g * size : (g + 1) * size] = plain[rows]
        here = columns == head * group + g
        stats_ref[:requests, :] = jnp.where(here, top[rows], stats_ref[:requests, :])
        stats_ref[requests:, :] = jnp.where(here, total[rows], stats_ref[requests:, :])


def cache_part(lengths, query, cache, signs):
    requests, span, width = cache.shape
    blocks, size = signs.shape
    heads = blocks // 2
    columns = query.shape[1] // heads
    return pl.pallas_call(
        functools.partial(cache_kernel, heads),
        grid=(heads,),
        in_specs=[
            pl.BlockSpec(memory_space=pltpu.SMEM),
            pl.BlockSpec((requests, columns), lambda k: (0, k)),
            pl.BlockSpec((requests, span, size), lambda k: (0, 0, k)),
            pl.BlockSpec((requests, span, size), lambda k: (0, 0, heads + k)),
            pl.BlockSpec((blocks, size), lambda k: (0, 0)),
        ],
        out_specs=[
            pl.BlockSpec((requests, columns), lambda k: (0, k)),
            pl.BlockSpec((2 * requests, 128), lambda k: (0, 0)),
        ],
        out_shape=[
            jax.ShapeDtypeStruct(query.shape, jnp.float32),
            jax.ShapeDtypeStruct((2 * requests, 128), jnp.float32),
        ],
        compiler_params=params(),
        cost_estimate=pl.CostEstimate(
            flops=4 * requests * query.shape[1] * requests * span,
            bytes_accessed=2 * requests * span * width,
            transcendentals=requests * span * requests * columns // size * heads,
        ),
        name="cache_part",
    )(lengths, query, cache, cache, signs)


def code_row(message_refs, start, requests):
    code = sum(ref[0:1, start:].astype(jnp.float32) for ref in message_refs).astype(jnp.int32)
    me = lax.axis_index("seq")
    return ((code // requests) ^ me) * requests + code % requests


def score_kernel(heads, partial_ref, *refs):
    message_refs, (scores_ref, code_ref) = refs[:-2], refs[-2:]
    requests = message_refs[0].shape[0]
    size = partial_ref.shape[1] // heads
    tokens = partial_ref.shape[0]
    start = message_refs[0].shape[1] - tokens
    group = start // (heads * size)
    code = code_row(message_refs, start, requests)
    code_ref[...] = jnp.broadcast_to(code, code_ref.shape)
    span = len(message_refs) * requests
    here = lax.broadcasted_iota(jnp.int32, (span, tokens), 0) == code
    queries = [ref[:, :start].astype(jnp.float32) for ref in message_refs]
    for k in range(heads):
        rows = []
        for g in range(group):
            at = (k * group + g) * size
            rows += [query[:, at : at + size] for query in queries]
        query = jnp.concatenate(rows, axis=0).astype(jnp.bfloat16)
        keys = partial_ref[:, k * size : (k + 1) * size]
        scores = lax.dot_general(query, keys, NT, preferred_element_type=jnp.float32)
        lines = [
            jnp.sum(jnp.where(here, scores[g * span : (g + 1) * span], 0.0), axis=0, keepdims=True)
            for g in range(group)
        ]
        scores_ref[k * group : (k + 1) * group, :] = jnp.concatenate(lines, axis=0) * (
            1.0 / math.sqrt(size)
        )


def partial_scores(heads, width, partials, messages):
    tokens = partials.shape[0]
    size = width // heads
    query_heads = (messages[0].shape[1] - tokens) // size
    return pl.pallas_call(
        functools.partial(score_kernel, heads),
        grid=(1,),
        in_specs=[pl.BlockSpec((tokens, width), lambda i: (0, 0))]
        + [pl.BlockSpec(m.shape, lambda i: (0, 0)) for m in messages],
        out_specs=[
            pl.BlockSpec((query_heads, tokens), lambda i: (0, 0)),
            pl.BlockSpec((8, tokens), lambda i: (0, 0)),
        ],
        out_shape=[
            jax.ShapeDtypeStruct((query_heads, tokens), jnp.float32),
            jax.ShapeDtypeStruct((8, tokens), jnp.int32),
        ],
        compiler_params=params(),
        name="partial_scores",
    )(partials, *messages)


def mix_kernel(heads, count, code_ref, values_ref, cache_stats_ref, *refs):
    score_refs = refs[:count]
    mixed_refs = refs[count : 2 * count]
    new_stats_ref, stats_ref = refs[2 * count :]
    tokens = values_ref.shape[0]
    size = values_ref.shape[1] // heads
    requests = stats_ref.shape[0] // 2
    group = score_refs[0].shape[0] // heads
    span = count * requests
    here = lax.broadcasted_iota(jnp.int32, (span, tokens), 0) == code_ref[0:1, :]
    parts = [ref[...] for ref in score_refs]
    while len(parts) > 1:
        parts = [parts[i] + parts[i + 1] for i in range(0, len(parts), 2)]
    scores = parts[0]
    columns = lax.broadcasted_iota(jnp.int32, (requests, stats_ref.shape[1]), 1)
    tops = jnp.full(columns.shape, 0.0, jnp.float32)
    totals = jnp.zeros(columns.shape, jnp.float32)
    mixed = []
    for k in range(heads):
        weights = []
        for g in range(group):
            row = k * group + g
            line = jnp.broadcast_to(scores[row : row + 1, :], (span, tokens))
            top = jnp.max(jnp.where(here, line, LOWEST), axis=1, keepdims=True)
            probs = jnp.where(here, jnp.exp(line - top), 0.0)
            total = jnp.sum(probs, axis=1, keepdims=True)
            weights.append(probs)
            tops = jnp.where(columns == row, top[:requests], tops)
            totals = jnp.where(columns == row, total[:requests], totals)
        weights = jnp.concatenate(weights, axis=0).astype(jnp.bfloat16)
        values = values_ref[:, k * size : (k + 1) * size]
        mixed.append(jnp.dot(weights, values, preferred_element_type=jnp.float32))
    half = heads // 2
    for k in range(half):
        for g in range(group):
            at = (k * group + g) * size
            for d in range(count):
                rows = slice(g * span + d * requests, g * span + (d + 1) * requests)
                pair = jnp.concatenate([mixed[k][rows], mixed[k + half][rows]], axis=0)
                mixed_refs[d][:, at : at + size] = pair.astype(jnp.bfloat16)
    new_stats_ref[:requests, :] = tops
    new_stats_ref[requests:, :] = totals
    cache_tops = cache_stats_ref[:requests, :]
    both = jnp.maximum(cache_tops, tops)
    stats_ref[:requests, :] = both
    stats_ref[requests:, :] = cache_stats_ref[requests:, :] * jnp.exp(cache_tops - both) + totals * jnp.exp(
        tops - both
    )


def mix(heads, width, code, partials, cache_stats, scores):
    count = len(scores)
    tokens = partials.shape[0]
    requests = cache_stats.shape[0] // 2
    columns = scores[0].shape[0] * (width // heads) // 2
    whole = lambda shape: pl.BlockSpec(shape, lambda i: (0, 0))
    return pl.pallas_call(
        functools.partial(mix_kernel, heads, count),
        grid=(1,),
        in_specs=[
            whole(code.shape),
            pl.BlockSpec((tokens, width), lambda i: (0, 1)),
            whole(cache_stats.shape),
        ]
        + [whole(s.shape) for s in scores],
        out_specs=[whole((2 * requests, columns))] * count + [whole(cache_stats.shape)] * 2,
        out_shape=[jax.ShapeDtypeStruct((2 * requests, columns), jnp.bfloat16)] * count
        + [jax.ShapeDtypeStruct(cache_stats.shape, jnp.float32)] * 2,
        compiler_params=params(),
        name="mix",
    )(code, partials, cache_stats, *scores)


def merge_kernel(count, size, cache_ref, cache_stats_ref, new_stats_ref, stats_ref, other_ref, *refs):
    mixed_refs, out_ref = refs[:count], refs[count]
    requests = cache_ref.shape[0]
    half = out_ref.shape[1] // 2
    top = stats_ref[:requests, :]
    other_top = other_ref[:requests, :]
    both = jnp.maximum(top, other_top)
    total = stats_ref[requests:, :] * jnp.exp(top - both) + other_ref[requests:, :] * jnp.exp(
        other_top - both
    )
    inverse = 1.0 / total
    cache_factor = jnp.exp(cache_stats_ref[:requests, :] - both) * inverse
    new_factor = jnp.exp(new_stats_ref[:requests, :] - both) * inverse
    for at in range(0, half, size):
        new = sum(ref[:, at : at + size].astype(jnp.float32) for ref in mixed_refs)
        pair = []
        for side in range(2):
            head = (side * half + at) // size
            column = slice(side * half + at, side * half + at + size)
            pair.append(
                cache_ref[:, column] * cache_factor[:, head : head + 1]
                + new[side * requests : (side + 1) * requests] * new_factor[:, head : head + 1]
            )
        out_ref[:, at : at + size] = pair[0].astype(out_ref.dtype)
        out_ref[:, half + at : half + at + size] = pair[1].astype(out_ref.dtype)


def merge(size, cache_mixed, cache_stats, new_stats, stats, other, mixed):
    whole = lambda shape: pl.BlockSpec(shape, lambda i: (0, 0))
    inputs = [cache_mixed, cache_stats, new_stats, stats, other] + list(mixed)
    return pl.pallas_call(
        functools.partial(merge_kernel, len(mixed), size),
        grid=(1,),
        in_specs=[whole(x.shape) for x in inputs],
        out_specs=whole(cache_mixed.shape),
        out_shape=jax.ShapeDtypeStruct(cache_mixed.shape, jnp.bfloat16),
        compiler_params=params(),
        name="merge",
    )(*inputs)


def from_partner(x, axis, distance):
    count = lax.axis_size(axis)
    return lax.ppermute(x, axis, [(i, i ^ distance) for i in range(count)])


def on_device(tokens, kv_weight, owners, requests, signs, queries, kv_cache, lengths):
    seq_count = lax.axis_size("seq")
    blocks, size = signs.shape
    heads = blocks // 2
    width = heads * size
    query = queries[0, 0]
    request_count, columns = query.shape
    per_device = owners.shape[1]
    token_count = tokens.shape[0]
    code = owners[0, :, 0] * request_count + requests[0]
    spread = jnp.where(
        lax.iota(jnp.int32, token_count) // per_device == lax.axis_index("seq"),
        jnp.tile(code, seq_count),
        0,
    ).astype(jnp.bfloat16)
    message = jnp.concatenate(
        [query, jnp.broadcast_to(spread[None], (request_count, token_count))], axis=1
    )
    messages = [message] + [from_partner(message, "seq", d) for d in range(1, seq_count)]
    partials = project(tokens, kv_weight)
    cache_mixed, cache_stats = cache_part(lengths, query, kv_cache[0, 0], signs)
    scores, relative = partial_scores(heads, width, partials, messages)
    scores = [scores] + [from_partner(scores, "seq", d) for d in range(1, seq_count)]
    results = mix(heads, width, relative, partials, cache_stats, scores)
    mixed, (new_stats, stats) = results[:seq_count], results[seq_count:]
    other = from_partner(stats, "tp", 1)
    mixed = [mixed[0]] + [from_partner(mixed[d], "seq", d) for d in range(1, seq_count)]
    own = merge(size, cache_mixed, cache_stats, new_stats, stats, other, mixed)
    far = from_partner(own, "tp", 1)
    output = (own.astype(jnp.float32) + far.astype(jnp.float32)).astype(jnp.bfloat16)
    return output.reshape(1, 1, request_count, columns)


def hadamard(order):
    rows = lax.broadcasted_iota(jnp.int32, (order, order), 0)
    cols = lax.broadcasted_iota(jnp.int32, (order, order), 1)
    parity = jnp.zeros((order, order), jnp.int32)
    for bit_number in range(order.bit_length() - 1):
        parity = parity + rows // 2**bit_number % 2 * (cols // 2**bit_number % 2)
    return (1 - 2 * (parity % 2)).astype(jnp.float32)


def rotate(blocks, sign_rows, matrix):
    product = jnp.einsum(
        "...h,hk->...k", blocks * sign_rows, matrix, precision=lax.Precision.HIGHEST
    )
    return product / math.sqrt(matrix.shape[0])


def encode(rotated):
    largest = jnp.max(jnp.abs(rotated), axis=-1) + 1e-06
    scales = largest.astype(jnp.bfloat16)
    encoded = (rotated / scales.astype(jnp.float32)[..., None]).astype(jnp.bfloat16)
    return (encoded, scales)


def decode(encoded, scales):
    return (encoded.astype(jnp.float32) * scales.astype(jnp.float32)[..., None]).astype(
        jnp.bfloat16
    )


def slot_numbers(targets, count, room):
    onehot = (targets[:, None] == lax.iota(jnp.int32, count)[None, :]).astype(jnp.int32)
    within = jnp.sum((jnp.cumsum(onehot, axis=0) - 1) * onehot, axis=1)
    return targets * room + within


def on_device_long(tokens, kv_weight, owners, requests, signs, queries, kv_cache, lengths):
    seq_count = lax.axis_size("seq")
    per_device = owners.shape[1]
    slots = max(2, (2 * per_device + seq_count - 1) // seq_count)
    head_blocks = signs.shape[0]
    kv_heads = head_blocks // 2
    head_size = signs.shape[1]
    matrix = hadamard(head_size)
    sign_rows = (2 * signs - 1).astype(jnp.float32)
    summed = lax.psum_scatter(
        jnp.dot(tokens, kv_weight, preferred_element_type=jnp.float32).astype(jnp.bfloat16),
        "seq",
        scatter_dimension=0,
        tiled=True,
    ).astype(jnp.float32)
    encoded, scales = encode(
        rotate(summed.reshape(per_device, head_blocks, head_size), sign_rows, matrix)
    )
    slot_index = slot_numbers(owners[0, :, 0], seq_count, slots)
    slot_total = seq_count * slots
    send_values = (
        jnp.zeros((slot_total, head_blocks, head_size), jnp.bfloat16).at[slot_index].set(encoded)
    )
    send_scales = jnp.zeros((slot_total, head_blocks), jnp.bfloat16).at[slot_index].set(scales)
    send_codes = jnp.zeros((slot_total,), jnp.int32).at[slot_index].set(requests[0] + 1)
    got_values, got_scales, arrived_codes = (
        lax.all_to_all(send_values, "seq", split_axis=0, concat_axis=0, tiled=True),
        lax.all_to_all(send_scales, "seq", split_axis=0, concat_axis=0, tiled=True),
        lax.all_to_all(send_codes, "seq", split_axis=0, concat_axis=0, tiled=True),
    )
    arrived = decode(got_values, got_scales)
    query = queries[0, 0]
    request_count = query.shape[0]
    group = query.shape[1] // (kv_heads * head_size)
    query_blocks = query.astype(jnp.float32).reshape(request_count, kv_heads, group, head_size)
    query_rot = rotate(query_blocks, sign_rows[:kv_heads][:, None, :], matrix).astype(jnp.bfloat16)
    local_cache = kv_cache[0, 0]
    cache_span = local_cache.shape[1]
    local_cache = local_cache.reshape(request_count, cache_span, head_blocks, head_size)
    score_scale = 1.0 / math.sqrt(head_size)
    lowest = -1e30
    highest = lax.Precision.HIGHEST
    score_cache = (
        jnp.einsum(
            "rkgd,rckd->rkgc",
            query_rot,
            local_cache[:, :, :kv_heads],
            preferred_element_type=jnp.float32,
        )
        * score_scale
    )
    score_new = (
        jnp.einsum(
            "rkgd,nkd->rkgn", query_rot, arrived[:, :kv_heads], preferred_element_type=jnp.float32
        )
        * score_scale
    )
    positions = lax.axis_index("tp") * cache_span + lax.iota(jnp.int32, cache_span)
    mask_cache = (positions[None, :] < lengths[0, 0][:, None])[:, None, None, :]
    match = arrived_codes[None, :] == (lax.iota(jnp.int32, request_count) + 1)[:, None]
    mask_new = match[:, None, None, :]
    top = jnp.maximum(
        jnp.max(jnp.where(mask_cache, score_cache, lowest), axis=-1),
        jnp.max(jnp.where(mask_new, score_new, lowest), axis=-1),
    )
    probs_cache = jnp.where(mask_cache, jnp.exp(score_cache - top[..., None]), 0.0)
    probs_new = jnp.where(mask_new, jnp.exp(score_new - top[..., None]), 0.0)
    total = jnp.sum(probs_cache, axis=-1) + jnp.sum(probs_new, axis=-1)
    mixed = jnp.einsum(
        "rkgc,rckd->rkgd",
        probs_cache,
        local_cache[:, :, kv_heads:].astype(jnp.float32),
        precision=highest,
    )
    mixed = mixed + jnp.einsum(
        "rkgn,nkd->rkgd", probs_new, arrived[:, kv_heads:].astype(jnp.float32), precision=highest
    )
    shared_top = lax.pmax(top, "tp")
    factor = jnp.exp(top - shared_top)
    total, mixed = (
        lax.psum((total * factor).astype(jnp.bfloat16), "tp").astype(jnp.float32),
        lax.psum((mixed * factor[..., None]).astype(jnp.bfloat16), "tp").astype(jnp.float32),
    )
    mixed = mixed / total[..., None]
    output = rotate(mixed, 1.0, matrix) * sign_rows[kv_heads:][None, :, None, :]
    return output.reshape(1, 1, request_count, group * kv_heads * head_size).astype(jnp.bfloat16)


def solution(mesh):
    placed = (
        P(("groups", "tp", "section"), "seq"),
        P("seq", None),
        P(("groups", "tp", "section"), "seq", None),
        P(("groups", "tp", "section"), "seq"),
        P(),
        P(("groups", "seq"), "section", None, None),
        P(("groups", "seq"), "section", None, "tp", None),
        P(("groups", "seq"), "section", None),
    )
    short = mesh.shape["seq"] == 4 and mesh.shape["tp"] == 2
    return jax.shard_map(
        on_device if short else on_device_long,
        mesh=mesh,
        in_specs=placed,
        out_specs=P(("groups", "seq"), "section", None, None),
        check_vma=False,
    )
```

```python
import functools
import math

import jax
import jax.numpy as jnp
from jax import lax
from jax.experimental import pallas as pl
from jax.experimental.pallas import tpu as pltpu
from jax.sharding import PartitionSpec as P

LOWEST = -1e30
MIB = 1024 * 1024
NT = (((1,), (1,)), ((), ()))


def params(mib=32):
    return pltpu.CompilerParams(vmem_limit_bytes=mib * MIB)


def in_hbm(x):
    return pltpu.with_memory_space_constraint(x, pltpu.HBM)


def hadamard_tile(order):
    rows = lax.broadcasted_iota(jnp.int32, (order, order), 0)
    cols = lax.broadcasted_iota(jnp.int32, (order, order), 1)
    common = rows & cols
    parity = jnp.zeros((order, order), jnp.int32)
    for bit_number in range(order.bit_length() - 1):
        parity = parity ^ (common >> bit_number)
    return (1 - 2 * (parity & 1)).astype(jnp.float32).astype(jnp.bfloat16)


def project_kernel(tokens_ref, weight_ref, out_ref, tokens_buf, weight_buf, acc_ref, sems):
    steps, block, width = weight_buf.shape
    copies = []
    for step in range(steps):
        span = slice(step * block, (step + 1) * block)
        pair = (
            pltpu.make_async_copy(tokens_ref.at[:, span], tokens_buf.at[step], sems.at[0, step]),
            pltpu.make_async_copy(weight_ref.at[span, :], weight_buf.at[step], sems.at[1, step]),
        )
        for copy in pair:
            copy.start()
        copies.append(pair)
    for step in range(steps):
        for copy in copies[step]:
            copy.wait()
        part = jnp.dot(tokens_buf[step], weight_buf[step], preferred_element_type=jnp.float32)
        if step == 0:
            acc_ref[...] = part
        elif step < steps - 1:
            acc_ref[...] += part
        else:
            out_ref[...] = (acc_ref[...] + part).astype(out_ref.dtype)


def project(tokens, weight):
    rows, features = tokens.shape
    width = weight.shape[1]
    block = min(512, features // 2)
    steps = features // block
    return pl.pallas_call(
        project_kernel,
        in_specs=[pl.BlockSpec(memory_space=pl.ANY)] * 2,
        out_specs=pl.BlockSpec(memory_space=pltpu.VMEM),
        out_shape=jax.ShapeDtypeStruct((rows, width), jnp.bfloat16),
        scratch_shapes=[
            pltpu.VMEM((steps, rows, block), jnp.bfloat16),
            pltpu.VMEM((steps, block, width), jnp.bfloat16),
            pltpu.VMEM((rows, width), jnp.float32),
            pltpu.SemaphoreType.DMA((2, steps)),
        ],
        compiler_params=params(48),
        cost_estimate=pl.CostEstimate(
            flops=2 * rows * features * width,
            bytes_accessed=2 * (rows * features + features * width),
            transcendentals=0,
        ),
        name="project",
    )(in_hbm(tokens), in_hbm(weight))


def message_kernel(query_ref, owners_ref, requests_ref, out_ref, query_buf, owners_buf, requests_buf, sems):
    requests, columns = query_ref.shape
    per_device = owners_ref.shape[1]
    tokens = out_ref.shape[1] - columns
    copies = [
        pltpu.make_async_copy(source, target, sems.at[i])
        for i, (source, target) in enumerate(
            ((query_ref, query_buf), (owners_ref, owners_buf), (requests_ref, requests_buf))
        )
    ]
    for copy in copies:
        copy.start()
    for copy in copies:
        copy.wait()
    out_ref[:, :columns] = query_buf[...]
    code = (owners_buf[...] * requests + requests_buf[...]).astype(jnp.float32)
    spread = jnp.concatenate([code] * (tokens // per_device), axis=1)
    spread = jnp.broadcast_to(spread, (requests, tokens))
    start = lax.axis_index("seq") * per_device
    lane = lax.broadcasted_iota(jnp.int32, spread.shape, 1)
    mine = (lane >= start) & (lane < start + per_device)
    out_ref[:, columns:] = jnp.where(mine, spread, 0.0).astype(out_ref.dtype)


def make_message(query, owners, requests, tokens):
    count, columns = query.shape
    return pl.pallas_call(
        message_kernel,
        in_specs=[pl.BlockSpec(memory_space=pl.ANY)] * 3,
        out_specs=pl.BlockSpec(memory_space=pltpu.VMEM),
        out_shape=jax.ShapeDtypeStruct((count, columns + tokens), query.dtype),
        scratch_shapes=[
            pltpu.VMEM(query.shape, query.dtype),
            pltpu.VMEM(owners.shape, owners.dtype),
            pltpu.VMEM(requests.shape, requests.dtype),
            pltpu.SemaphoreType.DMA((3,)),
        ],
        compiler_params=params(48),
        name="make_message",
    )(in_hbm(query), in_hbm(owners), in_hbm(requests))


def cache_kernel(
    lengths_ref, query_ref, cache_ref, signs_ref, tops_ref, totals_ref, mixed_ref, stats_ref, factor_ref, order_ref
):
    requests, span, _ = cache_ref.shape
    blocks, size = signs_ref.shape
    heads = blocks // 2
    count = query_ref.shape[1] // size
    group = count // heads
    norm = 1.0 / math.sqrt(size)
    matrix = hadamard_tile(size)
    signs = (2 * signs_ref[...] - 1).astype(jnp.float32)
    query = query_ref[...].astype(jnp.float32)
    query = jnp.concatenate(
        [query[:, h * size : (h + 1) * size] * signs[h // group : h // group + 1] for h in range(count)], axis=0
    )
    rotated = jnp.dot(query.astype(jnp.bfloat16), matrix, preferred_element_type=jnp.float32) * norm
    order_ref[0] = rotated
    position = lax.axis_index("tp") * span + lax.broadcasted_iota(jnp.int32, (group, span), 1)
    mixed = []
    for r in range(requests):
        rows = order_ref[0, pl.ds(r, count, stride=requests), :]
        live = position < lengths_ref[0, 0, r]
        for k in range(heads):
            keys = cache_ref[r, :, k * size : (k + 1) * size]
            values = cache_ref[r, :, (heads + k) * size : (heads + k + 1) * size]
            here = rows[k * group : (k + 1) * group].astype(jnp.bfloat16)
            scores = lax.dot_general(here, keys, NT, preferred_element_type=jnp.float32) * norm
            top = jnp.max(jnp.where(live, scores, LOWEST), axis=1, keepdims=True)
            probs = jnp.where(live, jnp.exp(scores - top), 0.0)
            total = jnp.sum(probs, axis=1, keepdims=True)
            mixed.append(jnp.dot(probs.astype(jnp.bfloat16), values, preferred_element_type=jnp.float32))
            at = slice(r * count + k * group, r * count + (k + 1) * group)
            order_ref[1, at, :] = jnp.broadcast_to(top, (group, size))
            order_ref[2, at, :] = jnp.broadcast_to(total, (group, size))
    mixed = jnp.concatenate(mixed, axis=0)
    high = mixed.astype(jnp.bfloat16)
    low = (mixed - high.astype(jnp.float32)).astype(jnp.bfloat16)
    plain = jnp.dot(high, matrix, preferred_element_type=jnp.float32)
    order_ref[3] = plain + jnp.dot(low, matrix, preferred_element_type=jnp.float32)
    lane = lax.broadcasted_iota(jnp.int32, stats_ref.shape, 1)
    stats = jnp.zeros(stats_ref.shape, jnp.float32)
    for h in range(count):
        pick = pl.ds(h, requests, stride=count)
        k = heads + h // group
        top = order_ref[1, pick, :]
        column = slice(h * size, (h + 1) * size)
        new_top = tops_ref[:, column]
        both = jnp.maximum(top, new_top)
        cache_factor = jnp.exp(top - both)
        new_factor = jnp.exp(new_top - both)
        total = order_ref[2, pick, :] * cache_factor + totals_ref[:, column] * new_factor
        factor_ref[:, column] = new_factor
        mixed_ref[:, column] = order_ref[3, pick, :] * (cache_factor * (signs[k : k + 1] * norm))
        for start, value in ((0, both), (3 * count, total)):
            for part in range(3):
                piece = value.astype(jnp.bfloat16).astype(jnp.float32)
                value = value - piece
                stats = jnp.where(lane == start + part * count + h, jnp.tile(piece, (1, 2)), stats)
    stats_ref[...] = stats.astype(jnp.bfloat16)


def cache_part(lengths, query, cache, signs, tops, totals):
    requests, span, width = cache.shape
    size = signs.shape[1]
    columns = query.shape[1]
    vmem = pl.BlockSpec(memory_space=pltpu.VMEM)
    return pl.pallas_call(
        cache_kernel,
        in_specs=[pl.BlockSpec(memory_space=pltpu.SMEM)] + [vmem] * 5,
        out_shape=[
            jax.ShapeDtypeStruct(query.shape, jnp.float32),
            jax.ShapeDtypeStruct((requests, 2 * size), jnp.bfloat16),
            jax.ShapeDtypeStruct(query.shape, jnp.float32),
        ],
        scratch_shapes=[pltpu.VMEM((4, requests * columns // size, size), jnp.float32)],
        compiler_params=params(),
        cost_estimate=pl.CostEstimate(
            flops=4 * span * requests * columns,
            bytes_accessed=2 * requests * span * width,
            transcendentals=span * requests * columns // size,
        ),
        name="cache_part",
    )(lengths, query, cache, signs, tops, totals)


def code_row(message_refs, start, requests):
    code = sum(ref[0:1, start:].astype(jnp.float32) for ref in message_refs).astype(jnp.int32)
    me = lax.axis_index("seq")
    return ((code // requests) ^ me) * requests + code % requests


def score_kernel(heads, partial_ref, *refs):
    message_refs, (scores_ref, code_ref) = refs[:-2], refs[-2:]
    requests = message_refs[0].shape[0]
    size = partial_ref.shape[1] // heads
    tokens = partial_ref.shape[0]
    start = message_refs[0].shape[1] - tokens
    group = start // (heads * size)
    code = code_row(message_refs, start, requests)
    code_ref[...] = jnp.broadcast_to(code, code_ref.shape)
    span = len(message_refs) * requests
    here = lax.broadcasted_iota(jnp.int32, (span, tokens), 0) == code
    queries = [ref[:, :start].astype(jnp.float32) for ref in message_refs]
    for k in range(heads):
        rows = []
        for g in range(group):
            at = (k * group + g) * size
            rows += [query[:, at : at + size] for query in queries]
        query = jnp.concatenate(rows, axis=0).astype(jnp.bfloat16)
        keys = partial_ref[:, k * size : (k + 1) * size]
        scores = lax.dot_general(query, keys, NT, preferred_element_type=jnp.float32)
        lines = [
            jnp.sum(jnp.where(here, scores[g * span : (g + 1) * span], 0.0), axis=0, keepdims=True)
            for g in range(group)
        ]
        scores_ref[k * group : (k + 1) * group, :] = jnp.concatenate(lines, axis=0) * (
            1.0 / math.sqrt(size)
        )


def partial_scores(heads, width, partials, messages):
    tokens = partials.shape[0]
    size = width // heads
    query_heads = (messages[0].shape[1] - tokens) // size
    return pl.pallas_call(
        functools.partial(score_kernel, heads),
        grid=(1,),
        in_specs=[pl.BlockSpec((tokens, width), lambda i: (0, 0))]
        + [pl.BlockSpec(m.shape, lambda i: (0, 0)) for m in messages],
        out_specs=[
            pl.BlockSpec((query_heads, tokens), lambda i: (0, 0)),
            pl.BlockSpec((8, tokens), lambda i: (0, 0)),
        ],
        out_shape=[
            jax.ShapeDtypeStruct((query_heads, tokens), jnp.float32),
            jax.ShapeDtypeStruct((8, tokens), jnp.int32),
        ],
        compiler_params=params(),
        name="partial_scores",
    )(partials, *messages)


def mix_kernel(heads, count, code_ref, values_ref, *refs):
    score_refs = refs[:count]
    mixed_refs = refs[count : 2 * count]
    tops_ref, totals_ref = refs[2 * count :]
    tokens = values_ref.shape[0]
    size = values_ref.shape[1] // heads
    requests = tops_ref.shape[0]
    group = score_refs[0].shape[0] // heads
    span = count * requests
    here = lax.broadcasted_iota(jnp.int32, (span, tokens), 0) == code_ref[0:1, :]
    parts = [ref[...] for ref in score_refs]
    while len(parts) > 1:
        parts = [parts[i] + parts[i + 1] for i in range(0, len(parts), 2)]
    scores = parts[0]
    mixed = []
    for k in range(heads):
        weights = []
        for g in range(group):
            row = k * group + g
            line = jnp.broadcast_to(scores[row : row + 1, :], (span, tokens))
            top = jnp.max(jnp.where(here, line, LOWEST), axis=1, keepdims=True)
            probs = jnp.where(here, jnp.exp(line - top), 0.0)
            total = jnp.sum(probs, axis=1, keepdims=True)
            weights.append(probs)
            column = slice(row * size, (row + 1) * size)
            tops_ref[:, column] = jnp.broadcast_to(top[:requests], (requests, size))
            totals_ref[:, column] = jnp.broadcast_to(total[:requests], (requests, size))
        weights = jnp.concatenate(weights, axis=0).astype(jnp.bfloat16)
        values = values_ref[:, k * size : (k + 1) * size]
        mixed.append(jnp.dot(weights, values, preferred_element_type=jnp.float32))
    half = heads // 2
    for k in range(half):
        for g in range(group):
            at = (k * group + g) * size
            for d in range(count):
                rows = slice(g * span + d * requests, g * span + (d + 1) * requests)
                pair = jnp.concatenate([mixed[k][rows], mixed[k + half][rows]], axis=0)
                mixed_refs[d][:, at : at + size] = pair.astype(jnp.bfloat16)


def mix(heads, width, requests, code, partials, scores):
    count = len(scores)
    tokens = partials.shape[0]
    columns = scores[0].shape[0] * (width // heads)
    whole = lambda shape: pl.BlockSpec(shape, lambda i: (0, 0))
    return pl.pallas_call(
        functools.partial(mix_kernel, heads, count),
        grid=(1,),
        in_specs=[whole(code.shape), pl.BlockSpec((tokens, width), lambda i: (0, 1))]
        + [whole(s.shape) for s in scores],
        out_specs=[whole((2 * requests, columns // 2))] * count + [whole((requests, columns))] * 2,
        out_shape=[jax.ShapeDtypeStruct((2 * requests, columns // 2), jnp.bfloat16)] * count
        + [jax.ShapeDtypeStruct((requests, columns), jnp.float32)] * 2,
        compiler_params=params(),
        name="mix",
    )(code, partials, *scores)


def merge_kernel(count, cache_ref, stats_ref, factor_ref, *refs):
    mixed_refs, out_ref = refs[:count], refs[count]
    requests, columns = cache_ref.shape
    half = columns // 2
    new = sum(ref[...].astype(jnp.float32) for ref in mixed_refs)
    for side in range(2):
        at = slice(side * half, (side + 1) * half)
        own = cache_ref[:, at] + new[side * requests : (side + 1) * requests] * factor_ref[:, at]
        out_ref[:, at] = own.astype(out_ref.dtype)
    out_ref[:, columns:] = stats_ref[...]


def merge(cache_mixed, stats, factor, mixed):
    requests, columns = cache_mixed.shape
    return pl.pallas_call(
        functools.partial(merge_kernel, len(mixed)),
        out_shape=jax.ShapeDtypeStruct((requests, columns + stats.shape[1]), jnp.bfloat16),
        compiler_params=params(),
        name="merge",
    )(cache_mixed, stats, factor, *mixed)


def finish_kernel(own_ref, far_ref, out_ref):
    requests, columns = out_ref.shape
    first = lax.axis_index("tp") == 0
    own, far = own_ref[...].astype(jnp.float32), far_ref[...].astype(jnp.float32)
    low, high = jnp.where(first, own, far), jnp.where(first, far, own)
    count = (own.shape[1] - columns) // 8
    size = columns // count

    def read(message, start):
        at = columns + start * count
        parts = [message[:, at + part * count : at + (part + 1) * count] for part in range(3)]
        return parts[0] + parts[1] + parts[2]

    low_top, high_top = read(low, 0), read(high, 0)
    both = jnp.maximum(low_top, high_top)
    low_factor, high_factor = jnp.exp(low_top - both), jnp.exp(high_top - both)
    inverse = 1.0 / (read(low, 3) * low_factor + read(high, 3) * high_factor)
    low_factor, high_factor = low_factor * inverse, high_factor * inverse
    for h in range(count):
        at = slice(h * size, (h + 1) * size)
        out = low[:, at] * low_factor[:, h : h + 1] + high[:, at] * high_factor[:, h : h + 1]
        out_ref[:, at] = out.astype(out_ref.dtype)


def finish(own, far, columns):
    return pl.pallas_call(
        finish_kernel,
        out_shape=jax.ShapeDtypeStruct((own.shape[0], columns), jnp.bfloat16),
        compiler_params=params(),
        name="finish",
    )(own, far)


def from_partner(x, axis, distance):
    count = lax.axis_size(axis)
    return lax.ppermute(x, axis, [(i, i ^ distance) for i in range(count)])


def on_device(tokens, kv_weight, owners, requests, signs, queries, kv_cache, lengths):
    seq_count = lax.axis_size("seq")
    blocks, size = signs.shape
    heads = blocks // 2
    width = heads * size
    query = queries[0, 0]
    request_count, columns = query.shape
    message = make_message(query, owners[:, :, 0], requests, tokens.shape[0])
    messages = [message] + [from_partner(message, "seq", d) for d in range(1, seq_count)]
    partials = project(tokens, kv_weight)
    scores, code = partial_scores(heads, width, partials, messages)
    scores = [scores] + [from_partner(scores, "seq", d) for d in range(1, seq_count)]
    results = mix(heads, width, request_count, code, partials, scores)
    mixed, (tops, totals) = results[:seq_count], results[seq_count:]
    mixed = [mixed[0]] + [from_partner(mixed[d], "seq", d) for d in range(1, seq_count)]
    cache_mixed, stats, factor = cache_part(lengths, query, kv_cache[0, 0], signs, tops, totals)
    own = merge(cache_mixed, stats, factor, mixed)
    far = from_partner(own, "tp", 1)
    return finish(own, far, columns).reshape(1, 1, request_count, columns)


def hadamard(order):
    rows = lax.broadcasted_iota(jnp.int32, (order, order), 0)
    cols = lax.broadcasted_iota(jnp.int32, (order, order), 1)
    parity = jnp.zeros((order, order), jnp.int32)
    for bit_number in range(order.bit_length() - 1):
        parity = parity + rows // 2**bit_number % 2 * (cols // 2**bit_number % 2)
    return (1 - 2 * (parity % 2)).astype(jnp.float32)


def rotate(blocks, sign_rows, matrix):
    product = jnp.einsum(
        "...h,hk->...k", blocks * sign_rows, matrix, precision=lax.Precision.HIGHEST
    )
    return product / math.sqrt(matrix.shape[0])


def encode(rotated):
    largest = jnp.max(jnp.abs(rotated), axis=-1) + 1e-06
    scales = largest.astype(jnp.bfloat16)
    encoded = (rotated / scales.astype(jnp.float32)[..., None]).astype(jnp.bfloat16)
    return (encoded, scales)


def decode(encoded, scales):
    return (encoded.astype(jnp.float32) * scales.astype(jnp.float32)[..., None]).astype(
        jnp.bfloat16
    )


def slot_numbers(targets, count, room):
    onehot = (targets[:, None] == lax.iota(jnp.int32, count)[None, :]).astype(jnp.int32)
    within = jnp.sum((jnp.cumsum(onehot, axis=0) - 1) * onehot, axis=1)
    return targets * room + within


def on_device_long(tokens, kv_weight, owners, requests, signs, queries, kv_cache, lengths):
    seq_count = lax.axis_size("seq")
    per_device = owners.shape[1]
    slots = max(2, (2 * per_device + seq_count - 1) // seq_count)
    head_blocks = signs.shape[0]
    kv_heads = head_blocks // 2
    head_size = signs.shape[1]
    matrix = hadamard(head_size)
    sign_rows = (2 * signs - 1).astype(jnp.float32)
    summed = lax.psum_scatter(
        jnp.dot(tokens, kv_weight, preferred_element_type=jnp.float32).astype(jnp.bfloat16),
        "seq",
        scatter_dimension=0,
        tiled=True,
    ).astype(jnp.float32)
    encoded, scales = encode(
        rotate(summed.reshape(per_device, head_blocks, head_size), sign_rows, matrix)
    )
    slot_index = slot_numbers(owners[0, :, 0], seq_count, slots)
    slot_total = seq_count * slots
    send_values = (
        jnp.zeros((slot_total, head_blocks, head_size), jnp.bfloat16).at[slot_index].set(encoded)
    )
    send_scales = jnp.zeros((slot_total, head_blocks), jnp.bfloat16).at[slot_index].set(scales)
    send_codes = jnp.zeros((slot_total,), jnp.int32).at[slot_index].set(requests[0] + 1)
    got_values, got_scales, arrived_codes = (
        lax.all_to_all(send_values, "seq", split_axis=0, concat_axis=0, tiled=True),
        lax.all_to_all(send_scales, "seq", split_axis=0, concat_axis=0, tiled=True),
        lax.all_to_all(send_codes, "seq", split_axis=0, concat_axis=0, tiled=True),
    )
    arrived = decode(got_values, got_scales)
    query = queries[0, 0]
    request_count = query.shape[0]
    group = query.shape[1] // (kv_heads * head_size)
    query_blocks = query.astype(jnp.float32).reshape(request_count, kv_heads, group, head_size)
    query_rot = rotate(query_blocks, sign_rows[:kv_heads][:, None, :], matrix).astype(jnp.bfloat16)
    local_cache = kv_cache[0, 0]
    cache_span = local_cache.shape[1]
    local_cache = local_cache.reshape(request_count, cache_span, head_blocks, head_size)
    score_scale = 1.0 / math.sqrt(head_size)
    lowest = -1e30
    highest = lax.Precision.HIGHEST
    score_cache = (
        jnp.einsum(
            "rkgd,rckd->rkgc",
            query_rot,
            local_cache[:, :, :kv_heads],
            preferred_element_type=jnp.float32,
        )
        * score_scale
    )
    score_new = (
        jnp.einsum(
            "rkgd,nkd->rkgn", query_rot, arrived[:, :kv_heads], preferred_element_type=jnp.float32
        )
        * score_scale
    )
    positions = lax.axis_index("tp") * cache_span + lax.iota(jnp.int32, cache_span)
    mask_cache = (positions[None, :] < lengths[0, 0][:, None])[:, None, None, :]
    match = arrived_codes[None, :] == (lax.iota(jnp.int32, request_count) + 1)[:, None]
    mask_new = match[:, None, None, :]
    top = jnp.maximum(
        jnp.max(jnp.where(mask_cache, score_cache, lowest), axis=-1),
        jnp.max(jnp.where(mask_new, score_new, lowest), axis=-1),
    )
    probs_cache = jnp.where(mask_cache, jnp.exp(score_cache - top[..., None]), 0.0)
    probs_new = jnp.where(mask_new, jnp.exp(score_new - top[..., None]), 0.0)
    total = jnp.sum(probs_cache, axis=-1) + jnp.sum(probs_new, axis=-1)
    mixed = jnp.einsum(
        "rkgc,rckd->rkgd",
        probs_cache,
        local_cache[:, :, kv_heads:].astype(jnp.float32),
        precision=highest,
    )
    mixed = mixed + jnp.einsum(
        "rkgn,nkd->rkgd", probs_new, arrived[:, kv_heads:].astype(jnp.float32), precision=highest
    )
    shared_top = lax.pmax(top, "tp")
    factor = jnp.exp(top - shared_top)
    total, mixed = (
        lax.psum((total * factor).astype(jnp.bfloat16), "tp").astype(jnp.float32),
        lax.psum((mixed * factor[..., None]).astype(jnp.bfloat16), "tp").astype(jnp.float32),
    )
    mixed = mixed / total[..., None]
    output = rotate(mixed, 1.0, matrix) * sign_rows[kv_heads:][None, :, None, :]
    return output.reshape(1, 1, request_count, group * kv_heads * head_size).astype(jnp.bfloat16)


def solution(mesh):
    placed = (
        P(("groups", "tp", "section"), "seq"),
        P("seq", None),
        P(("groups", "tp", "section"), "seq", None),
        P(("groups", "tp", "section"), "seq"),
        P(),
        P(("groups", "seq"), "section", None, None),
        P(("groups", "seq"), "section", None, "tp", None),
        P(("groups", "seq"), "section", None),
    )
    short = mesh.shape["seq"] == 4 and mesh.shape["tp"] == 2
    return jax.shard_map(
        on_device if short else on_device_long,
        mesh=mesh,
        in_specs=placed,
        out_specs=P(("groups", "seq"), "section", None, None),
        check_vma=False,
    )
```

```python
import functools
import math

import jax
import jax.numpy as jnp
from jax import lax
from jax.experimental import pallas as pl
from jax.experimental.pallas import tpu as pltpu
from jax.sharding import PartitionSpec as P

LOWEST = -1e30
MIB = 1024 * 1024
NT = (((1,), (1,)), ((), ()))


def params(mib=32):
    return pltpu.CompilerParams(vmem_limit_bytes=mib * MIB)


def in_hbm(x):
    return pltpu.with_memory_space_constraint(x, pltpu.HBM)


def hadamard_tile(order):
    rows = lax.broadcasted_iota(jnp.int32, (order, order), 0)
    cols = lax.broadcasted_iota(jnp.int32, (order, order), 1)
    common = rows & cols
    parity = jnp.zeros((order, order), jnp.int32)
    for bit_number in range(order.bit_length() - 1):
        parity = parity ^ (common >> bit_number)
    return (1 - 2 * (parity & 1)).astype(jnp.float32).astype(jnp.bfloat16)


def project_kernel(tokens_ref, weight_ref, out_ref, tokens_buf, weight_buf, acc_ref, sems):
    steps, block, width = weight_buf.shape
    copies = []
    for step in range(steps):
        span = slice(step * block, (step + 1) * block)
        pair = (
            pltpu.make_async_copy(tokens_ref.at[:, span], tokens_buf.at[step], sems.at[0, step]),
            pltpu.make_async_copy(weight_ref.at[span, :], weight_buf.at[step], sems.at[1, step]),
        )
        for copy in pair:
            copy.start()
        copies.append(pair)
    for step in range(steps):
        for copy in copies[step]:
            copy.wait()
        part = jnp.dot(tokens_buf[step], weight_buf[step], preferred_element_type=jnp.float32)
        if step == 0:
            acc_ref[...] = part
        elif step < steps - 1:
            acc_ref[...] += part
        else:
            out_ref[...] = (acc_ref[...] + part).astype(out_ref.dtype)


def project(tokens, weight):
    rows, features = tokens.shape
    width = weight.shape[1]
    block = min(512, features // 2)
    steps = features // block
    return pl.pallas_call(
        project_kernel,
        in_specs=[pl.BlockSpec(memory_space=pl.ANY)] * 2,
        out_specs=pl.BlockSpec(memory_space=pltpu.VMEM),
        out_shape=jax.ShapeDtypeStruct((rows, width), jnp.bfloat16),
        scratch_shapes=[
            pltpu.VMEM((steps, rows, block), jnp.bfloat16),
            pltpu.VMEM((steps, block, width), jnp.bfloat16),
            pltpu.VMEM((rows, width), jnp.float32),
            pltpu.SemaphoreType.DMA((2, steps)),
        ],
        compiler_params=params(48),
        cost_estimate=pl.CostEstimate(
            flops=2 * rows * features * width,
            bytes_accessed=2 * (rows * features + features * width),
            transcendentals=0,
        ),
        name="project",
    )(in_hbm(tokens), in_hbm(weight))


def message_kernel(query_ref, owners_ref, requests_ref, out_ref, query_buf, owners_buf, requests_buf, sems):
    requests, columns = query_ref.shape
    per_device = owners_ref.shape[1]
    tokens = out_ref.shape[1] - columns
    copies = [
        pltpu.make_async_copy(source, target, sems.at[i])
        for i, (source, target) in enumerate(
            ((query_ref, query_buf), (owners_ref, owners_buf), (requests_ref, requests_buf))
        )
    ]
    for copy in copies:
        copy.start()
    for copy in copies:
        copy.wait()
    out_ref[:, :columns] = query_buf[...]
    code = (owners_buf[...] * requests + requests_buf[...]).astype(jnp.float32)
    spread = jnp.concatenate([code] * (tokens // per_device), axis=1)
    spread = jnp.broadcast_to(spread, (requests, tokens))
    start = lax.axis_index("seq") * per_device
    lane = lax.broadcasted_iota(jnp.int32, spread.shape, 1)
    mine = (lane >= start) & (lane < start + per_device)
    out_ref[:, columns:] = jnp.where(mine, spread, 0.0).astype(out_ref.dtype)


def make_message(query, owners, requests, tokens):
    count, columns = query.shape
    return pl.pallas_call(
        message_kernel,
        in_specs=[pl.BlockSpec(memory_space=pl.ANY)] * 3,
        out_specs=pl.BlockSpec(memory_space=pltpu.VMEM),
        out_shape=jax.ShapeDtypeStruct((count, columns + tokens), query.dtype),
        scratch_shapes=[
            pltpu.VMEM(query.shape, query.dtype),
            pltpu.VMEM(owners.shape, owners.dtype),
            pltpu.VMEM(requests.shape, requests.dtype),
            pltpu.SemaphoreType.DMA((3,)),
        ],
        compiler_params=params(48),
        name="make_message",
    )(in_hbm(query), in_hbm(owners), in_hbm(requests))


def cache_kernel(
    lengths_ref, query_ref, cache_ref, signs_ref, mixed_ref, tops_ref, totals_ref, query_buf, top_buf, total_buf, mixed_buf
):
    requests, span, _ = cache_ref.shape
    blocks, size = signs_ref.shape
    heads = blocks // 2
    width = heads * size
    count = query_ref.shape[1] // size
    group = count // heads
    norm = 1.0 / math.sqrt(size)
    matrix = hadamard_tile(size)
    signs = (2 * signs_ref[...] - 1).astype(jnp.float32)
    query = query_ref[...].astype(jnp.float32)
    query = jnp.concatenate(
        [query[:, h * size : (h + 1) * size] * signs[h // group : h // group + 1] for h in range(count)], axis=0
    )
    query_buf[...] = jnp.dot(query.astype(jnp.bfloat16), matrix, preferred_element_type=jnp.float32) * norm
    rows = 2 * count
    kv_head = lax.broadcasted_iota(jnp.int32, (rows, width), 0) // group & (heads - 1)
    own_head = kv_head == lax.broadcasted_iota(jnp.int32, (rows, width), 1) // size
    first = lax.broadcasted_iota(jnp.int32, (rows, span), 0) < count
    position = lax.axis_index("tp") * span + lax.broadcasted_iota(jnp.int32, (rows, span), 1)
    pairs = range(0, requests, 2)
    scores = []
    for r in pairs:
        both = [query_buf[pl.ds(r + i, count, stride=requests), :] for i in range(2)]
        wide = jnp.concatenate([jnp.concatenate(both, axis=0)] * heads, axis=1)
        wide = jnp.where(own_head, wide, 0.0).astype(jnp.bfloat16)
        keys = cache_ref[r : r + 2, :, :width].reshape(2 * span, width)
        scores.append(lax.dot_general(wide, keys, NT, preferred_element_type=jnp.float32))
    probs = []
    for r, score in zip(pairs, scores):
        score = jnp.where(first, score[:, :span], score[:, span:]) * norm
        live = position < jnp.where(first, lengths_ref[0, 0, r], lengths_ref[0, 0, r + 1])
        top = jnp.max(jnp.where(live, score, LOWEST), axis=1, keepdims=True)
        prob = jnp.where(live, jnp.exp(score - top), 0.0)
        total = jnp.sum(prob, axis=1, keepdims=True)
        at = slice(r * count, (r + 2) * count)
        top_buf[at, :] = jnp.broadcast_to(top, (rows, size))
        total_buf[at, :] = jnp.broadcast_to(total, (rows, size))
        probs.append(
            jnp.concatenate([jnp.where(first, prob, 0.0), jnp.where(first, 0.0, prob)], axis=1).astype(jnp.bfloat16)
        )
    mixed = []
    for r, prob in zip(pairs, probs):
        values = cache_ref[r : r + 2, :, width:].reshape(2 * span, width)
        wide = jnp.dot(prob, values, preferred_element_type=jnp.float32)
        wide = jnp.where(own_head, wide, 0.0)
        mixed.append(sum(wide[:, k * size : (k + 1) * size] for k in range(heads)))
    mixed = jnp.concatenate(mixed, axis=0)
    high = mixed.astype(jnp.bfloat16)
    low = (mixed - high.astype(jnp.float32)).astype(jnp.bfloat16)
    plain = jnp.dot(high, matrix, preferred_element_type=jnp.float32)
    mixed_buf[...] = plain + jnp.dot(low, matrix, preferred_element_type=jnp.float32)
    for h in range(count):
        pick = pl.ds(h, requests, stride=count)
        column = slice(h * size, (h + 1) * size)
        k = heads + h // group
        mixed_ref[:, column] = mixed_buf[pick, :] * (signs[k : k + 1] * norm)
        tops_ref[:, column] = top_buf[pick, :]
        totals_ref[:, column] = total_buf[pick, :]


def cache_part(lengths, query, cache, signs):
    requests, span, width = cache.shape
    size = signs.shape[1]
    columns = query.shape[1]
    vmem = pl.BlockSpec(memory_space=pltpu.VMEM)
    return pl.pallas_call(
        cache_kernel,
        in_specs=[pl.BlockSpec(memory_space=pltpu.SMEM)] + [vmem] * 3,
        out_shape=[jax.ShapeDtypeStruct(query.shape, jnp.float32)] * 3,
        scratch_shapes=[pltpu.VMEM((requests * columns // size, size), jnp.float32)] * 4,
        compiler_params=params(),
        cost_estimate=pl.CostEstimate(
            flops=4 * span * requests * columns,
            bytes_accessed=2 * requests * span * width,
            transcendentals=span * requests * columns // size,
        ),
        name="cache_part",
    )(lengths, query, cache, signs)


def stats_kernel(top_ref, total_ref, new_top_ref, new_total_ref, cache_ref, cache_out_ref, factor_ref, stats_ref):
    requests, columns = top_ref.shape
    size = 128
    count = columns // size
    top, new_top = top_ref[...], new_top_ref[...]
    both = jnp.maximum(top, new_top)
    cache_factor = jnp.exp(top - both)
    new_factor = jnp.exp(new_top - both)
    cache_out_ref[...] = cache_ref[...] * cache_factor
    factor_ref[...] = new_factor
    total = total_ref[...] * cache_factor + new_total_ref[...] * new_factor
    lane = lax.broadcasted_iota(jnp.int32, (requests, size), 1)
    packed = []
    for value in (both, total):
        narrow = jnp.zeros((requests, size), jnp.float32)
        for h in range(count):
            narrow = jnp.where(lane % count == h, value[:, h * size : (h + 1) * size], narrow)
        high = narrow.astype(jnp.bfloat16).astype(jnp.float32)
        middle = (narrow - high).astype(jnp.bfloat16).astype(jnp.float32)
        low = narrow - high - middle
        packed.append(jnp.where(lane < count, high, jnp.where(lane < 2 * count, middle, low)))
    stats_ref[...] = jnp.concatenate(packed, axis=1).astype(jnp.bfloat16)


def combine_stats(tops, totals, new_tops, new_totals, cache_mixed):
    shape = tops.shape
    return pl.pallas_call(
        stats_kernel,
        out_shape=[
            jax.ShapeDtypeStruct(shape, jnp.float32),
            jax.ShapeDtypeStruct(shape, jnp.float32),
            jax.ShapeDtypeStruct((shape[0], 256), jnp.bfloat16),
        ],
        compiler_params=params(),
        name="combine_stats",
    )(tops, totals, new_tops, new_totals, cache_mixed)


def code_row(message_refs, start, requests):
    code = sum(ref[0:1, start:].astype(jnp.float32) for ref in message_refs).astype(jnp.int32)
    me = lax.axis_index("seq")
    return ((code // requests) ^ me) * requests + code % requests


def score_kernel(heads, partial_ref, *refs):
    message_refs, (scores_ref, code_ref) = refs[:-2], refs[-2:]
    requests = message_refs[0].shape[0]
    size = partial_ref.shape[1] // heads
    tokens = partial_ref.shape[0]
    start = message_refs[0].shape[1] - tokens
    group = start // (heads * size)
    code = code_row(message_refs, start, requests)
    code_ref[...] = jnp.broadcast_to(code, code_ref.shape)
    span = len(message_refs) * requests
    here = lax.broadcasted_iota(jnp.int32, (span, tokens), 0) == code
    queries = [ref[:, :start].astype(jnp.float32) for ref in message_refs]
    for k in range(heads):
        rows = []
        for g in range(group):
            at = (k * group + g) * size
            rows += [query[:, at : at + size] for query in queries]
        query = jnp.concatenate(rows, axis=0).astype(jnp.bfloat16)
        keys = partial_ref[:, k * size : (k + 1) * size]
        scores = lax.dot_general(query, keys, NT, preferred_element_type=jnp.float32)
        lines = [
            jnp.sum(jnp.where(here, scores[g * span : (g + 1) * span], 0.0), axis=0, keepdims=True)
            for g in range(group)
        ]
        scores_ref[k * group : (k + 1) * group, :] = jnp.concatenate(lines, axis=0) * (
            1.0 / math.sqrt(size)
        )


def partial_scores(heads, width, partials, messages):
    tokens = partials.shape[0]
    size = width // heads
    query_heads = (messages[0].shape[1] - tokens) // size
    return pl.pallas_call(
        functools.partial(score_kernel, heads),
        grid=(1,),
        in_specs=[pl.BlockSpec((tokens, width), lambda i: (0, 0))]
        + [pl.BlockSpec(m.shape, lambda i: (0, 0)) for m in messages],
        out_specs=[
            pl.BlockSpec((query_heads, tokens), lambda i: (0, 0)),
            pl.BlockSpec((8, tokens), lambda i: (0, 0)),
        ],
        out_shape=[
            jax.ShapeDtypeStruct((query_heads, tokens), jnp.float32),
            jax.ShapeDtypeStruct((8, tokens), jnp.int32),
        ],
        compiler_params=params(),
        name="partial_scores",
    )(partials, *messages)


def add_kernel(left_ref, right_ref, out_ref):
    out_ref[...] = left_ref[...] + right_ref[...]


def add(left, right):
    return pl.pallas_call(
        add_kernel,
        out_shape=jax.ShapeDtypeStruct(left.shape, left.dtype),
        compiler_params=params(),
        name="add",
    )(left, right)


def mix_kernel(heads, count, code_ref, values_ref, near_ref, far_ref, *refs):
    mixed_refs, (tops_ref, totals_ref) = refs[:count], refs[count:]
    tokens = values_ref.shape[0]
    size = values_ref.shape[1] // heads
    requests = tops_ref.shape[0]
    group = near_ref.shape[0] // heads
    span = count * requests
    here = lax.broadcasted_iota(jnp.int32, (span, tokens), 0) == code_ref[0:1, :]
    scores = near_ref[...] + far_ref[...]
    mixed = []
    for k in range(heads):
        weights = []
        for g in range(group):
            row = k * group + g
            line = jnp.broadcast_to(scores[row : row + 1, :], (span, tokens))
            top = jnp.max(jnp.where(here, line, LOWEST), axis=1, keepdims=True)
            probs = jnp.where(here, jnp.exp(line - top), 0.0)
            total = jnp.sum(probs, axis=1, keepdims=True)
            weights.append(probs)
            column = slice(row * size, (row + 1) * size)
            tops_ref[:, column] = jnp.broadcast_to(top[:requests], (requests, size))
            totals_ref[:, column] = jnp.broadcast_to(total[:requests], (requests, size))
        weights = jnp.concatenate(weights, axis=0).astype(jnp.bfloat16)
        values = values_ref[:, k * size : (k + 1) * size]
        mixed.append(jnp.dot(weights, values, preferred_element_type=jnp.float32))
    half = heads // 2
    for k in range(half):
        for g in range(group):
            at = (k * group + g) * size
            for d in range(count):
                rows = slice(g * span + d * requests, g * span + (d + 1) * requests)
                pair = jnp.concatenate([mixed[k][rows], mixed[k + half][rows]], axis=0)
                mixed_refs[d][:, at : at + size] = pair.astype(jnp.bfloat16)


def mix(heads, width, requests, count, code, partials, scores):
    tokens = partials.shape[0]
    columns = scores[0].shape[0] * (width // heads)
    whole = lambda shape: pl.BlockSpec(shape, lambda i: (0, 0))
    return pl.pallas_call(
        functools.partial(mix_kernel, heads, count),
        grid=(1,),
        in_specs=[whole(code.shape), pl.BlockSpec((tokens, width), lambda i: (0, 1))]
        + [whole(s.shape) for s in scores],
        out_specs=[whole((2 * requests, columns // 2))] * count + [whole((requests, columns))] * 2,
        out_shape=[jax.ShapeDtypeStruct((2 * requests, columns // 2), jnp.bfloat16)] * count
        + [jax.ShapeDtypeStruct((requests, columns), jnp.float32)] * 2,
        compiler_params=params(),
        name="mix",
    )(code, partials, *scores)


def merge_kernel(count, cache_ref, stats_ref, factor_ref, *refs):
    mixed_refs, out_ref = refs[:count], refs[count]
    requests, columns = cache_ref.shape
    half = columns // 2
    new = sum(ref[...].astype(jnp.float32) for ref in mixed_refs)
    for side in range(2):
        at = slice(side * half, (side + 1) * half)
        own = cache_ref[:, at] + new[side * requests : (side + 1) * requests] * factor_ref[:, at]
        out_ref[:, at] = own.astype(out_ref.dtype)
    out_ref[:, columns:] = stats_ref[...]


def merge(cache_mixed, stats, factor, mixed):
    requests, columns = cache_mixed.shape
    return pl.pallas_call(
        functools.partial(merge_kernel, len(mixed)),
        out_shape=jax.ShapeDtypeStruct((requests, columns + stats.shape[1]), jnp.bfloat16),
        compiler_params=params(),
        name="merge",
    )(cache_mixed, stats, factor, *mixed)


def finish_kernel(own_ref, far_ref, out_ref):
    requests, columns = out_ref.shape
    first = lax.axis_index("tp") == 0
    own, far = own_ref[...].astype(jnp.float32), far_ref[...].astype(jnp.float32)
    low, high = jnp.where(first, own, far), jnp.where(first, far, own)
    size = 128
    count = columns // size

    def read(message, start):
        at = columns + start * size
        parts = [message[:, at + part * count : at + (part + 1) * count] for part in range(3)]
        return parts[0] + parts[1] + parts[2]

    low_top, high_top = read(low, 0), read(high, 0)
    both = jnp.maximum(low_top, high_top)
    low_factor, high_factor = jnp.exp(low_top - both), jnp.exp(high_top - both)
    inverse = 1.0 / (read(low, 1) * low_factor + read(high, 1) * high_factor)
    low_factor, high_factor = low_factor * inverse, high_factor * inverse
    for h in range(count):
        at = slice(h * size, (h + 1) * size)
        out = low[:, at] * low_factor[:, h : h + 1] + high[:, at] * high_factor[:, h : h + 1]
        out_ref[:, at] = out.astype(out_ref.dtype)


def finish(own, far, columns):
    return pl.pallas_call(
        finish_kernel,
        out_shape=jax.ShapeDtypeStruct((own.shape[0], columns), jnp.bfloat16),
        compiler_params=params(),
        name="finish",
    )(own, far)


def from_partner(x, axis, distance):
    count = lax.axis_size(axis)
    return lax.ppermute(x, axis, [(i, i ^ distance) for i in range(count)])


def on_device(tokens, kv_weight, owners, requests, signs, queries, kv_cache, lengths):
    seq_count = lax.axis_size("seq")
    blocks, size = signs.shape
    heads = blocks // 2
    width = heads * size
    query = queries[0, 0]
    request_count, columns = query.shape
    message = make_message(query, owners[:, :, 0], requests, tokens.shape[0])
    messages = [message] + [from_partner(message, "seq", d) for d in range(1, seq_count)]
    partials = project(tokens, kv_weight)
    scores, code = partial_scores(heads, width, partials, messages)
    distance = 1
    while distance < seq_count // 2:
        scores = add(scores, from_partner(scores, "seq", distance))
        distance *= 2
    scores = (scores, from_partner(scores, "seq", distance))
    cache_mixed, tops, totals = cache_part(lengths, query, kv_cache[0, 0], signs)
    results = mix(heads, width, request_count, seq_count, code, partials, scores)
    mixed, (new_tops, new_totals) = results[:seq_count], results[seq_count:]
    mixed = [mixed[0]] + [from_partner(mixed[d], "seq", d) for d in range(1, seq_count)]
    cache_mixed, factor, stats = combine_stats(tops, totals, new_tops, new_totals, cache_mixed)
    own = merge(cache_mixed, stats, factor, mixed)
    far = from_partner(own, "tp", 1)
    return finish(own, far, columns).reshape(1, 1, request_count, columns)


def hadamard(order):
    rows = lax.broadcasted_iota(jnp.int32, (order, order), 0)
    cols = lax.broadcasted_iota(jnp.int32, (order, order), 1)
    parity = jnp.zeros((order, order), jnp.int32)
    for bit_number in range(order.bit_length() - 1):
        parity = parity + rows // 2**bit_number % 2 * (cols // 2**bit_number % 2)
    return (1 - 2 * (parity % 2)).astype(jnp.float32)


def rotate(blocks, sign_rows, matrix):
    product = jnp.einsum(
        "...h,hk->...k", blocks * sign_rows, matrix, precision=lax.Precision.HIGHEST
    )
    return product / math.sqrt(matrix.shape[0])


def encode(rotated):
    largest = jnp.max(jnp.abs(rotated), axis=-1) + 1e-06
    scales = largest.astype(jnp.bfloat16)
    encoded = (rotated / scales.astype(jnp.float32)[..., None]).astype(jnp.bfloat16)
    return (encoded, scales)


def decode(encoded, scales):
    return (encoded.astype(jnp.float32) * scales.astype(jnp.float32)[..., None]).astype(
        jnp.bfloat16
    )


def slot_numbers(targets, count, room):
    onehot = (targets[:, None] == lax.iota(jnp.int32, count)[None, :]).astype(jnp.int32)
    within = jnp.sum((jnp.cumsum(onehot, axis=0) - 1) * onehot, axis=1)
    return targets * room + within


def on_device_long(tokens, kv_weight, owners, requests, signs, queries, kv_cache, lengths):
    seq_count = lax.axis_size("seq")
    per_device = owners.shape[1]
    slots = max(2, (2 * per_device + seq_count - 1) // seq_count)
    head_blocks = signs.shape[0]
    kv_heads = head_blocks // 2
    head_size = signs.shape[1]
    matrix = hadamard(head_size)
    sign_rows = (2 * signs - 1).astype(jnp.float32)
    summed = lax.psum_scatter(
        jnp.dot(tokens, kv_weight, preferred_element_type=jnp.float32).astype(jnp.bfloat16),
        "seq",
        scatter_dimension=0,
        tiled=True,
    ).astype(jnp.float32)
    encoded, scales = encode(
        rotate(summed.reshape(per_device, head_blocks, head_size), sign_rows, matrix)
    )
    slot_index = slot_numbers(owners[0, :, 0], seq_count, slots)
    slot_total = seq_count * slots
    send_values = (
        jnp.zeros((slot_total, head_blocks, head_size), jnp.bfloat16).at[slot_index].set(encoded)
    )
    send_scales = jnp.zeros((slot_total, head_blocks), jnp.bfloat16).at[slot_index].set(scales)
    send_codes = jnp.zeros((slot_total,), jnp.int32).at[slot_index].set(requests[0] + 1)
    got_values, got_scales, arrived_codes = (
        lax.all_to_all(send_values, "seq", split_axis=0, concat_axis=0, tiled=True),
        lax.all_to_all(send_scales, "seq", split_axis=0, concat_axis=0, tiled=True),
        lax.all_to_all(send_codes, "seq", split_axis=0, concat_axis=0, tiled=True),
    )
    arrived = decode(got_values, got_scales)
    query = queries[0, 0]
    request_count = query.shape[0]
    group = query.shape[1] // (kv_heads * head_size)
    query_blocks = query.astype(jnp.float32).reshape(request_count, kv_heads, group, head_size)
    query_rot = rotate(query_blocks, sign_rows[:kv_heads][:, None, :], matrix).astype(jnp.bfloat16)
    local_cache = kv_cache[0, 0]
    cache_span = local_cache.shape[1]
    local_cache = local_cache.reshape(request_count, cache_span, head_blocks, head_size)
    score_scale = 1.0 / math.sqrt(head_size)
    lowest = -1e30
    highest = lax.Precision.HIGHEST
    score_cache = (
        jnp.einsum(
            "rkgd,rckd->rkgc",
            query_rot,
            local_cache[:, :, :kv_heads],
            preferred_element_type=jnp.float32,
        )
        * score_scale
    )
    score_new = (
        jnp.einsum(
            "rkgd,nkd->rkgn", query_rot, arrived[:, :kv_heads], preferred_element_type=jnp.float32
        )
        * score_scale
    )
    positions = lax.axis_index("tp") * cache_span + lax.iota(jnp.int32, cache_span)
    mask_cache = (positions[None, :] < lengths[0, 0][:, None])[:, None, None, :]
    match = arrived_codes[None, :] == (lax.iota(jnp.int32, request_count) + 1)[:, None]
    mask_new = match[:, None, None, :]
    top = jnp.maximum(
        jnp.max(jnp.where(mask_cache, score_cache, lowest), axis=-1),
        jnp.max(jnp.where(mask_new, score_new, lowest), axis=-1),
    )
    probs_cache = jnp.where(mask_cache, jnp.exp(score_cache - top[..., None]), 0.0)
    probs_new = jnp.where(mask_new, jnp.exp(score_new - top[..., None]), 0.0)
    total = jnp.sum(probs_cache, axis=-1) + jnp.sum(probs_new, axis=-1)
    mixed = jnp.einsum(
        "rkgc,rckd->rkgd",
        probs_cache,
        local_cache[:, :, kv_heads:].astype(jnp.float32),
        precision=highest,
    )
    mixed = mixed + jnp.einsum(
        "rkgn,nkd->rkgd", probs_new, arrived[:, kv_heads:].astype(jnp.float32), precision=highest
    )
    shared_top = lax.pmax(top, "tp")
    factor = jnp.exp(top - shared_top)
    total, mixed = (
        lax.psum((total * factor).astype(jnp.bfloat16), "tp").astype(jnp.float32),
        lax.psum((mixed * factor[..., None]).astype(jnp.bfloat16), "tp").astype(jnp.float32),
    )
    mixed = mixed / total[..., None]
    output = rotate(mixed, 1.0, matrix) * sign_rows[kv_heads:][None, :, None, :]
    return output.reshape(1, 1, request_count, group * kv_heads * head_size).astype(jnp.bfloat16)


def solution(mesh):
    placed = (
        P(("groups", "tp", "section"), "seq"),
        P("seq", None),
        P(("groups", "tp", "section"), "seq", None),
        P(("groups", "tp", "section"), "seq"),
        P(),
        P(("groups", "seq"), "section", None, None),
        P(("groups", "seq"), "section", None, "tp", None),
        P(("groups", "seq"), "section", None),
    )
    short = mesh.shape["seq"] == 4 and mesh.shape["tp"] == 2
    return jax.shard_map(
        on_device if short else on_device_long,
        mesh=mesh,
        in_specs=placed,
        out_specs=P(("groups", "seq"), "section", None, None),
        check_vma=False,
    )
```

```python
import functools
import math

import jax
import jax.numpy as jnp
from jax import lax
from jax.experimental import pallas as pl
from jax.experimental.pallas import tpu as pltpu
from jax.sharding import PartitionSpec as P

LOWEST = -1e30
MIB = 1024 * 1024
NT = (((1,), (1,)), ((), ()))


def params(mib=32):
    return pltpu.CompilerParams(vmem_limit_bytes=mib * MIB)


def in_hbm(x):
    return pltpu.with_memory_space_constraint(x, pltpu.HBM)


def in_vmem(x):
    return pltpu.with_memory_space_constraint(x, pltpu.VMEM)


def hadamard_tile(order):
    rows = lax.broadcasted_iota(jnp.int32, (order, order), 0)
    cols = lax.broadcasted_iota(jnp.int32, (order, order), 1)
    common = rows & cols
    parity = jnp.zeros((order, order), jnp.int32)
    for bit_number in range(order.bit_length() - 1):
        parity = parity ^ (common >> bit_number)
    return (1 - 2 * (parity & 1)).astype(jnp.float32).astype(jnp.bfloat16)


def project_kernel(tokens_ref, weight_ref, out_ref):
    out_ref[...] = jnp.dot(tokens_ref[...], weight_ref[...], preferred_element_type=jnp.float32).astype(out_ref.dtype)


def project(tokens, weight):
    rows, features = tokens.shape
    width = weight.shape[1]
    return pl.pallas_call(
        project_kernel,
        in_specs=[pl.BlockSpec(memory_space=pltpu.VMEM)] * 2,
        out_specs=pl.BlockSpec(memory_space=pltpu.VMEM),
        out_shape=jax.ShapeDtypeStruct((rows, width), jnp.bfloat16),
        compiler_params=params(32),
        cost_estimate=pl.CostEstimate(
            flops=2 * rows * features * width,
            bytes_accessed=2 * (rows * features + features * width),
            transcendentals=0,
        ),
        name="project",
    )(in_vmem(tokens), in_vmem(weight))


def message_kernel(query_ref, owners_ref, requests_ref, out_ref, query_buf, owners_buf, requests_buf, sems):
    requests, columns = query_ref.shape
    per_device = owners_ref.shape[1]
    tokens = out_ref.shape[1] - columns
    copies = [
        pltpu.make_async_copy(source, target, sems.at[i])
        for i, (source, target) in enumerate(
            ((query_ref, query_buf), (owners_ref, owners_buf), (requests_ref, requests_buf))
        )
    ]
    for copy in copies:
        copy.start()
    for copy in copies:
        copy.wait()
    out_ref[:, :columns] = query_buf[...]
    code = (owners_buf[...] * requests + requests_buf[...]).astype(jnp.float32)
    spread = jnp.concatenate([code] * (tokens // per_device), axis=1)
    spread = jnp.broadcast_to(spread, (requests, tokens))
    start = lax.axis_index("seq") * per_device
    lane = lax.broadcasted_iota(jnp.int32, spread.shape, 1)
    mine = (lane >= start) & (lane < start + per_device)
    out_ref[:, columns:] = jnp.where(mine, spread, 0.0).astype(out_ref.dtype)


def make_message(query, owners, requests, tokens):
    count, columns = query.shape
    return pl.pallas_call(
        message_kernel,
        in_specs=[pl.BlockSpec(memory_space=pl.ANY)] * 3,
        out_specs=pl.BlockSpec(memory_space=pltpu.VMEM),
        out_shape=jax.ShapeDtypeStruct((count, columns + tokens), query.dtype),
        scratch_shapes=[
            pltpu.VMEM(query.shape, query.dtype),
            pltpu.VMEM(owners.shape, owners.dtype),
            pltpu.VMEM(requests.shape, requests.dtype),
            pltpu.SemaphoreType.DMA((3,)),
        ],
        compiler_params=params(16),
        cost_estimate=pl.CostEstimate(flops=10**11, bytes_accessed=10**4, transcendentals=0),
        name="make_message",
    )(in_hbm(query), in_hbm(owners), in_hbm(requests))


def cache_kernel(
    lengths_ref, query_ref, cache_ref, signs_ref, mixed_ref, tops_ref, totals_ref, query_buf, top_buf, total_buf, mixed_buf
):
    requests, span, _ = cache_ref.shape
    blocks, size = signs_ref.shape
    heads = blocks // 2
    width = heads * size
    count = query_ref.shape[1] // size
    group = count // heads
    norm = 1.0 / math.sqrt(size)
    matrix = hadamard_tile(size)
    signs = (2 * signs_ref[...] - 1).astype(jnp.float32)
    query = query_ref[...].astype(jnp.float32)
    query = jnp.concatenate(
        [query[:, h * size : (h + 1) * size] * signs[h // group : h // group + 1] for h in range(count)], axis=0
    )
    query_buf[...] = jnp.dot(query.astype(jnp.bfloat16), matrix, preferred_element_type=jnp.float32) * norm
    rows = 2 * count
    kv_head = lax.broadcasted_iota(jnp.int32, (rows, width), 0) // group & (heads - 1)
    own_head = kv_head == lax.broadcasted_iota(jnp.int32, (rows, width), 1) // size
    first = lax.broadcasted_iota(jnp.int32, (rows, span), 0) < count
    position = lax.axis_index("tp") * span + lax.broadcasted_iota(jnp.int32, (rows, span), 1)
    pairs = range(0, requests, 2)
    scores = []
    for r in pairs:
        both = [query_buf[pl.ds(r + i, count, stride=requests), :] for i in range(2)]
        wide = jnp.concatenate([jnp.concatenate(both, axis=0)] * heads, axis=1)
        wide = jnp.where(own_head, wide, 0.0).astype(jnp.bfloat16)
        keys = cache_ref[r : r + 2, :, :width].reshape(2 * span, width)
        scores.append(lax.dot_general(wide, keys, NT, preferred_element_type=jnp.float32))
    probs = []
    for r, score in zip(pairs, scores):
        score = jnp.where(first, score[:, :span], score[:, span:]) * norm
        live = position < jnp.where(first, lengths_ref[0, 0, r], lengths_ref[0, 0, r + 1])
        top = jnp.max(jnp.where(live, score, LOWEST), axis=1, keepdims=True)
        prob = jnp.where(live, jnp.exp(score - top), 0.0)
        total = jnp.sum(prob, axis=1, keepdims=True)
        at = slice(r * count, (r + 2) * count)
        top_buf[at, :] = jnp.broadcast_to(top, (rows, size))
        total_buf[at, :] = jnp.broadcast_to(total, (rows, size))
        probs.append(
            jnp.concatenate([jnp.where(first, prob, 0.0), jnp.where(first, 0.0, prob)], axis=1).astype(jnp.bfloat16)
        )
    mixed = []
    for r, prob in zip(pairs, probs):
        values = cache_ref[r : r + 2, :, width:].reshape(2 * span, width)
        wide = jnp.dot(prob, values, preferred_element_type=jnp.float32)
        wide = jnp.where(own_head, wide, 0.0)
        mixed.append(sum(wide[:, k * size : (k + 1) * size] for k in range(heads)))
    mixed = jnp.concatenate(mixed, axis=0)
    high = mixed.astype(jnp.bfloat16)
    low = (mixed - high.astype(jnp.float32)).astype(jnp.bfloat16)
    plain = jnp.dot(high, matrix, preferred_element_type=jnp.float32)
    mixed_buf[...] = plain + jnp.dot(low, matrix, preferred_element_type=jnp.float32)
    for h in range(count):
        pick = pl.ds(h, requests, stride=count)
        column = slice(h * size, (h + 1) * size)
        k = heads + h // group
        mixed_ref[:, column] = mixed_buf[pick, :] * (signs[k : k + 1] * norm)
        tops_ref[:, column] = top_buf[pick, :]
        totals_ref[:, column] = total_buf[pick, :]


def cache_part(lengths, query, cache, signs):
    requests, span, width = cache.shape
    size = signs.shape[1]
    columns = query.shape[1]
    vmem = pl.BlockSpec(memory_space=pltpu.VMEM)
    return pl.pallas_call(
        cache_kernel,
        in_specs=[pl.BlockSpec(memory_space=pltpu.SMEM)] + [vmem] * 3,
        out_shape=[jax.ShapeDtypeStruct(query.shape, jnp.float32)] * 3,
        scratch_shapes=[pltpu.VMEM((requests * columns // size, size), jnp.float32)] * 4,
        compiler_params=params(),
        cost_estimate=pl.CostEstimate(
            flops=4 * span * requests * columns,
            bytes_accessed=2 * requests * span * width,
            transcendentals=span * requests * columns // size,
        ),
        name="cache_part",
    )(lengths, query, cache, signs)


def stats_kernel(top_ref, total_ref, new_top_ref, new_total_ref, cache_ref, cache_out_ref, factor_ref, stats_ref):
    requests, columns = top_ref.shape
    size = 128
    count = columns // size
    top, new_top = top_ref[...], new_top_ref[...]
    both = jnp.maximum(top, new_top)
    cache_factor = jnp.exp(top - both)
    new_factor = jnp.exp(new_top - both)
    cache_out_ref[...] = cache_ref[...] * cache_factor
    factor_ref[...] = new_factor
    total = total_ref[...] * cache_factor + new_total_ref[...] * new_factor
    lane = lax.broadcasted_iota(jnp.int32, (requests, size), 1)
    packed = []
    for value in (both, total):
        narrow = jnp.zeros((requests, size), jnp.float32)
        for h in range(count):
            narrow = jnp.where(lane % count == h, value[:, h * size : (h + 1) * size], narrow)
        high = narrow.astype(jnp.bfloat16).astype(jnp.float32)
        middle = (narrow - high).astype(jnp.bfloat16).astype(jnp.float32)
        low = narrow - high - middle
        packed.append(jnp.where(lane < count, high, jnp.where(lane < 2 * count, middle, low)))
    stats_ref[...] = jnp.concatenate(packed, axis=1).astype(jnp.bfloat16)


def combine_stats(tops, totals, new_tops, new_totals, cache_mixed):
    shape = tops.shape
    return pl.pallas_call(
        stats_kernel,
        out_shape=[
            jax.ShapeDtypeStruct(shape, jnp.float32),
            jax.ShapeDtypeStruct(shape, jnp.float32),
            jax.ShapeDtypeStruct((shape[0], 256), jnp.bfloat16),
        ],
        compiler_params=params(),
        name="combine_stats",
    )(tops, totals, new_tops, new_totals, cache_mixed)


def code_row(message_refs, start, requests):
    code = sum(ref[0:1, start:].astype(jnp.float32) for ref in message_refs).astype(jnp.int32)
    me = lax.axis_index("seq")
    return ((code // requests) ^ me) * requests + code % requests


def score_kernel(heads, partial_ref, *refs):
    message_refs, (scores_ref, code_ref) = refs[:-2], refs[-2:]
    requests = message_refs[0].shape[0]
    size = partial_ref.shape[1] // heads
    tokens = partial_ref.shape[0]
    start = message_refs[0].shape[1] - tokens
    group = start // (heads * size)
    code = code_row(message_refs, start, requests)
    code_ref[...] = jnp.broadcast_to(code, code_ref.shape)
    span = len(message_refs) * requests
    here = lax.broadcasted_iota(jnp.int32, (span, tokens), 0) == code
    queries = [ref[:, :start].astype(jnp.float32) for ref in message_refs]
    for k in range(heads):
        rows = []
        for g in range(group):
            at = (k * group + g) * size
            rows += [query[:, at : at + size] for query in queries]
        query = jnp.concatenate(rows, axis=0).astype(jnp.bfloat16)
        keys = partial_ref[:, k * size : (k + 1) * size]
        scores = lax.dot_general(query, keys, NT, preferred_element_type=jnp.float32)
        lines = [
            jnp.sum(jnp.where(here, scores[g * span : (g + 1) * span], 0.0), axis=0, keepdims=True)
            for g in range(group)
        ]
        scores_ref[k * group : (k + 1) * group, :] = jnp.concatenate(lines, axis=0) * (
            1.0 / math.sqrt(size)
        )


def partial_scores(heads, width, partials, messages):
    tokens = partials.shape[0]
    size = width // heads
    query_heads = (messages[0].shape[1] - tokens) // size
    return pl.pallas_call(
        functools.partial(score_kernel, heads),
        grid=(1,),
        in_specs=[pl.BlockSpec((tokens, width), lambda i: (0, 0))]
        + [pl.BlockSpec(m.shape, lambda i: (0, 0)) for m in messages],
        out_specs=[
            pl.BlockSpec((query_heads, tokens), lambda i: (0, 0)),
            pl.BlockSpec((8, tokens), lambda i: (0, 0)),
        ],
        out_shape=[
            jax.ShapeDtypeStruct((query_heads, tokens), jnp.float32),
            jax.ShapeDtypeStruct((8, tokens), jnp.int32),
        ],
        compiler_params=params(),
        name="partial_scores",
    )(partials, *messages)


def add_kernel(left_ref, right_ref, out_ref):
    out_ref[...] = left_ref[...] + right_ref[...]


def add(left, right):
    return pl.pallas_call(
        add_kernel,
        out_shape=jax.ShapeDtypeStruct(left.shape, left.dtype),
        compiler_params=params(),
        name="add",
    )(left, right)


def mix_kernel(heads, count, code_ref, values_ref, near_ref, far_ref, *refs):
    mixed_refs, (tops_ref, totals_ref) = refs[:count], refs[count:]
    tokens = values_ref.shape[0]
    size = values_ref.shape[1] // heads
    requests = tops_ref.shape[0]
    group = near_ref.shape[0] // heads
    span = count * requests
    here = lax.broadcasted_iota(jnp.int32, (span, tokens), 0) == code_ref[0:1, :]
    scores = near_ref[...] + far_ref[...]
    mixed = []
    for k in range(heads):
        weights = []
        for g in range(group):
            row = k * group + g
            line = jnp.broadcast_to(scores[row : row + 1, :], (span, tokens))
            top = jnp.max(jnp.where(here, line, LOWEST), axis=1, keepdims=True)
            probs = jnp.where(here, jnp.exp(line - top), 0.0)
            total = jnp.sum(probs, axis=1, keepdims=True)
            weights.append(probs)
            column = slice(row * size, (row + 1) * size)
            tops_ref[:, column] = jnp.broadcast_to(top[:requests], (requests, size))
            totals_ref[:, column] = jnp.broadcast_to(total[:requests], (requests, size))
        weights = jnp.concatenate(weights, axis=0).astype(jnp.bfloat16)
        values = values_ref[:, k * size : (k + 1) * size]
        mixed.append(jnp.dot(weights, values, preferred_element_type=jnp.float32))
    half = heads // 2
    for k in range(half):
        for g in range(group):
            at = (k * group + g) * size
            for d in range(count):
                rows = slice(g * span + d * requests, g * span + (d + 1) * requests)
                pair = jnp.concatenate([mixed[k][rows], mixed[k + half][rows]], axis=0)
                mixed_refs[d][:, at : at + size] = pair.astype(jnp.bfloat16)


def mix(heads, width, requests, count, code, partials, scores):
    tokens = partials.shape[0]
    columns = scores[0].shape[0] * (width // heads)
    whole = lambda shape: pl.BlockSpec(shape, lambda i: (0, 0))
    return pl.pallas_call(
        functools.partial(mix_kernel, heads, count),
        grid=(1,),
        in_specs=[whole(code.shape), pl.BlockSpec((tokens, width), lambda i: (0, 1))]
        + [whole(s.shape) for s in scores],
        out_specs=[whole((2 * requests, columns // 2))] * count + [whole((requests, columns))] * 2,
        out_shape=[jax.ShapeDtypeStruct((2 * requests, columns // 2), jnp.bfloat16)] * count
        + [jax.ShapeDtypeStruct((requests, columns), jnp.float32)] * 2,
        compiler_params=params(),
        name="mix",
    )(code, partials, *scores)


def merge_kernel(count, cache_ref, stats_ref, factor_ref, *refs):
    mixed_refs, out_ref = refs[:count], refs[count]
    requests, columns = cache_ref.shape
    half = columns // 2
    new = sum(ref[...].astype(jnp.float32) for ref in mixed_refs)
    for side in range(2):
        at = slice(side * half, (side + 1) * half)
        own = cache_ref[:, at] + new[side * requests : (side + 1) * requests] * factor_ref[:, at]
        out_ref[:, at] = own.astype(out_ref.dtype)
    out_ref[:, columns:] = stats_ref[...]


def merge(cache_mixed, stats, factor, mixed):
    requests, columns = cache_mixed.shape
    return pl.pallas_call(
        functools.partial(merge_kernel, len(mixed)),
        out_shape=jax.ShapeDtypeStruct((requests, columns + stats.shape[1]), jnp.bfloat16),
        compiler_params=params(),
        name="merge",
    )(cache_mixed, stats, factor, *mixed)


def finish_kernel(own_ref, far_ref, out_ref):
    requests, columns = out_ref.shape
    first = lax.axis_index("tp") == 0
    own, far = own_ref[...].astype(jnp.float32), far_ref[...].astype(jnp.float32)
    low, high = jnp.where(first, own, far), jnp.where(first, far, own)
    size = 128
    count = columns // size

    def read(message, start):
        at = columns + start * size
        parts = [message[:, at + part * count : at + (part + 1) * count] for part in range(3)]
        return parts[0] + parts[1] + parts[2]

    low_top, high_top = read(low, 0), read(high, 0)
    both = jnp.maximum(low_top, high_top)
    low_factor, high_factor = jnp.exp(low_top - both), jnp.exp(high_top - both)
    inverse = 1.0 / (read(low, 1) * low_factor + read(high, 1) * high_factor)
    low_factor, high_factor = low_factor * inverse, high_factor * inverse
    for h in range(count):
        at = slice(h * size, (h + 1) * size)
        out = low[:, at] * low_factor[:, h : h + 1] + high[:, at] * high_factor[:, h : h + 1]
        out_ref[:, at] = out.astype(out_ref.dtype)


def finish(own, far, columns):
    return pl.pallas_call(
        finish_kernel,
        out_shape=jax.ShapeDtypeStruct((own.shape[0], columns), jnp.bfloat16),
        compiler_params=params(),
        name="finish",
    )(own, far)


def from_partner(x, axis, distance):
    count = lax.axis_size(axis)
    return lax.ppermute(x, axis, [(i, i ^ distance) for i in range(count)])


def on_device(tokens, kv_weight, owners, requests, signs, queries, kv_cache, lengths):
    seq_count = lax.axis_size("seq")
    blocks, size = signs.shape
    heads = blocks // 2
    width = heads * size
    query = queries[0, 0]
    request_count, columns = query.shape
    message = make_message(query, owners[:, :, 0], requests, tokens.shape[0])
    messages = [message] + [from_partner(message, "seq", d) for d in range(1, seq_count)]
    partials = project(tokens, kv_weight)
    scores, code = partial_scores(heads, width, partials, messages)
    distance = 1
    while distance < seq_count // 2:
        scores = add(scores, from_partner(scores, "seq", distance))
        distance *= 2
    scores = (scores, from_partner(scores, "seq", distance))
    cache_mixed, tops, totals = cache_part(lengths, query, kv_cache[0, 0], signs)
    results = mix(heads, width, request_count, seq_count, code, partials, scores)
    mixed, (new_tops, new_totals) = results[:seq_count], results[seq_count:]
    mixed = [mixed[0]] + [from_partner(mixed[d], "seq", d) for d in range(1, seq_count)]
    cache_mixed, factor, stats = combine_stats(tops, totals, new_tops, new_totals, cache_mixed)
    own = merge(cache_mixed, stats, factor, mixed)
    far = from_partner(own, "tp", 1)
    return finish(own, far, columns).reshape(1, 1, request_count, columns)


def hadamard(order):
    rows = lax.broadcasted_iota(jnp.int32, (order, order), 0)
    cols = lax.broadcasted_iota(jnp.int32, (order, order), 1)
    parity = jnp.zeros((order, order), jnp.int32)
    for bit_number in range(order.bit_length() - 1):
        parity = parity + rows // 2**bit_number % 2 * (cols // 2**bit_number % 2)
    return (1 - 2 * (parity % 2)).astype(jnp.float32)


def rotate(blocks, sign_rows, matrix):
    product = jnp.einsum(
        "...h,hk->...k", blocks * sign_rows, matrix, precision=lax.Precision.HIGHEST
    )
    return product / math.sqrt(matrix.shape[0])


def encode(rotated):
    largest = jnp.max(jnp.abs(rotated), axis=-1) + 1e-06
    scales = largest.astype(jnp.bfloat16)
    encoded = (rotated / scales.astype(jnp.float32)[..., None]).astype(jnp.bfloat16)
    return (encoded, scales)


def decode(encoded, scales):
    return (encoded.astype(jnp.float32) * scales.astype(jnp.float32)[..., None]).astype(
        jnp.bfloat16
    )


def slot_numbers(targets, count, room):
    onehot = (targets[:, None] == lax.iota(jnp.int32, count)[None, :]).astype(jnp.int32)
    within = jnp.sum((jnp.cumsum(onehot, axis=0) - 1) * onehot, axis=1)
    return targets * room + within


def on_device_long(tokens, kv_weight, owners, requests, signs, queries, kv_cache, lengths):
    seq_count = lax.axis_size("seq")
    per_device = owners.shape[1]
    slots = max(2, (2 * per_device + seq_count - 1) // seq_count)
    head_blocks = signs.shape[0]
    kv_heads = head_blocks // 2
    head_size = signs.shape[1]
    matrix = hadamard(head_size)
    sign_rows = (2 * signs - 1).astype(jnp.float32)
    summed = lax.psum_scatter(
        jnp.dot(tokens, kv_weight, preferred_element_type=jnp.float32).astype(jnp.bfloat16),
        "seq",
        scatter_dimension=0,
        tiled=True,
    ).astype(jnp.float32)
    encoded, scales = encode(
        rotate(summed.reshape(per_device, head_blocks, head_size), sign_rows, matrix)
    )
    slot_index = slot_numbers(owners[0, :, 0], seq_count, slots)
    slot_total = seq_count * slots
    send_values = (
        jnp.zeros((slot_total, head_blocks, head_size), jnp.bfloat16).at[slot_index].set(encoded)
    )
    send_scales = jnp.zeros((slot_total, head_blocks), jnp.bfloat16).at[slot_index].set(scales)
    send_codes = jnp.zeros((slot_total,), jnp.int32).at[slot_index].set(requests[0] + 1)
    got_values, got_scales, arrived_codes = (
        lax.all_to_all(send_values, "seq", split_axis=0, concat_axis=0, tiled=True),
        lax.all_to_all(send_scales, "seq", split_axis=0, concat_axis=0, tiled=True),
        lax.all_to_all(send_codes, "seq", split_axis=0, concat_axis=0, tiled=True),
    )
    arrived = decode(got_values, got_scales)
    query = queries[0, 0]
    request_count = query.shape[0]
    group = query.shape[1] // (kv_heads * head_size)
    query_blocks = query.astype(jnp.float32).reshape(request_count, kv_heads, group, head_size)
    query_rot = rotate(query_blocks, sign_rows[:kv_heads][:, None, :], matrix).astype(jnp.bfloat16)
    local_cache = kv_cache[0, 0]
    cache_span = local_cache.shape[1]
    local_cache = local_cache.reshape(request_count, cache_span, head_blocks, head_size)
    score_scale = 1.0 / math.sqrt(head_size)
    lowest = -1e30
    highest = lax.Precision.HIGHEST
    score_cache = (
        jnp.einsum(
            "rkgd,rckd->rkgc",
            query_rot,
            local_cache[:, :, :kv_heads],
            preferred_element_type=jnp.float32,
        )
        * score_scale
    )
    score_new = (
        jnp.einsum(
            "rkgd,nkd->rkgn", query_rot, arrived[:, :kv_heads], preferred_element_type=jnp.float32
        )
        * score_scale
    )
    positions = lax.axis_index("tp") * cache_span + lax.iota(jnp.int32, cache_span)
    mask_cache = (positions[None, :] < lengths[0, 0][:, None])[:, None, None, :]
    match = arrived_codes[None, :] == (lax.iota(jnp.int32, request_count) + 1)[:, None]
    mask_new = match[:, None, None, :]
    top = jnp.maximum(
        jnp.max(jnp.where(mask_cache, score_cache, lowest), axis=-1),
        jnp.max(jnp.where(mask_new, score_new, lowest), axis=-1),
    )
    probs_cache = jnp.where(mask_cache, jnp.exp(score_cache - top[..., None]), 0.0)
    probs_new = jnp.where(mask_new, jnp.exp(score_new - top[..., None]), 0.0)
    total = jnp.sum(probs_cache, axis=-1) + jnp.sum(probs_new, axis=-1)
    mixed = jnp.einsum(
        "rkgc,rckd->rkgd",
        probs_cache,
        local_cache[:, :, kv_heads:].astype(jnp.float32),
        precision=highest,
    )
    mixed = mixed + jnp.einsum(
        "rkgn,nkd->rkgd", probs_new, arrived[:, kv_heads:].astype(jnp.float32), precision=highest
    )
    shared_top = lax.pmax(top, "tp")
    factor = jnp.exp(top - shared_top)
    total, mixed = (
        lax.psum((total * factor).astype(jnp.bfloat16), "tp").astype(jnp.float32),
        lax.psum((mixed * factor[..., None]).astype(jnp.bfloat16), "tp").astype(jnp.float32),
    )
    mixed = mixed / total[..., None]
    output = rotate(mixed, 1.0, matrix) * sign_rows[kv_heads:][None, :, None, :]
    return output.reshape(1, 1, request_count, group * kv_heads * head_size).astype(jnp.bfloat16)


def solution(mesh):
    placed = (
        P(("groups", "tp", "section"), "seq"),
        P("seq", None),
        P(("groups", "tp", "section"), "seq", None),
        P(("groups", "tp", "section"), "seq"),
        P(),
        P(("groups", "seq"), "section", None, None),
        P(("groups", "seq"), "section", None, "tp", None),
        P(("groups", "seq"), "section", None),
    )
    short = mesh.shape["seq"] == 4 and mesh.shape["tp"] == 2
    return jax.shard_map(
        on_device if short else on_device_long,
        mesh=mesh,
        in_specs=placed,
        out_specs=P(("groups", "seq"), "section", None, None),
        check_vma=False,
    )
```

```python
import functools
import math

import jax
import jax.numpy as jnp
from jax import lax
from jax.experimental import pallas as pl
from jax.experimental.pallas import tpu as pltpu
from jax.sharding import PartitionSpec as P

LOWEST = -1e30
MIB = 1024 * 1024
NT = (((1,), (1,)), ((), ()))


def params(mib=32):
    return pltpu.CompilerParams(vmem_limit_bytes=mib * MIB)


def in_hbm(x):
    return pltpu.with_memory_space_constraint(x, pltpu.HBM)


def in_vmem(x):
    return pltpu.with_memory_space_constraint(x, pltpu.VMEM)


def hadamard_tile(order):
    rows = lax.broadcasted_iota(jnp.int32, (order, order), 0)
    cols = lax.broadcasted_iota(jnp.int32, (order, order), 1)
    common = rows & cols
    parity = jnp.zeros((order, order), jnp.int32)
    for bit_number in range(order.bit_length() - 1):
        parity = parity ^ (common >> bit_number)
    return (1 - 2 * (parity & 1)).astype(jnp.float32).astype(jnp.bfloat16)


def far_first(blocks):
    return [blocks[0]] + list(blocks[:0:-1])


def project_kernel(tokens_ref, weight_ref, out_ref):
    out_ref[...] = jnp.dot(tokens_ref[...], weight_ref[...], preferred_element_type=jnp.float32).astype(out_ref.dtype)


def project(tokens, weight):
    rows, features = tokens.shape
    width = weight.shape[1]
    return pl.pallas_call(
        project_kernel,
        in_specs=[pl.BlockSpec(memory_space=pltpu.VMEM)] * 2,
        out_specs=pl.BlockSpec(memory_space=pltpu.VMEM),
        out_shape=jax.ShapeDtypeStruct((rows, width), jnp.bfloat16),
        compiler_params=params(32),
        cost_estimate=pl.CostEstimate(
            flops=2 * rows * features * width,
            bytes_accessed=2 * (rows * features + features * width),
            transcendentals=0,
        ),
        name="project",
    )(in_vmem(tokens), in_vmem(weight))


def message_kernel(query_ref, owners_ref, requests_ref, out_ref, query_buf, owners_buf, requests_buf, sems):
    requests, columns = query_ref.shape
    per_device = owners_ref.shape[1]
    copies = [
        pltpu.make_async_copy(source, target, sems.at[i])
        for i, (source, target) in enumerate(
            ((query_ref, query_buf), (owners_ref, owners_buf), (requests_ref, requests_buf))
        )
    ]
    for copy in copies:
        copy.start()
    for copy in copies:
        copy.wait()
    out_ref[:, :columns] = query_buf[...]
    code = (owners_buf[...] * requests + requests_buf[...]).astype(jnp.float32)
    spare = jnp.zeros((1, out_ref.shape[1] - columns - per_device), jnp.float32)
    code = jnp.concatenate([code, spare], axis=1)
    out_ref[:, columns:] = jnp.broadcast_to(code, (requests, code.shape[1])).astype(out_ref.dtype)


def make_message(query, owners, requests):
    count, columns = query.shape
    lanes = -(-owners.shape[1] // 128) * 128
    return pl.pallas_call(
        message_kernel,
        in_specs=[pl.BlockSpec(memory_space=pl.ANY)] * 3,
        out_specs=pl.BlockSpec(memory_space=pltpu.VMEM),
        out_shape=jax.ShapeDtypeStruct((count, columns + lanes), query.dtype),
        scratch_shapes=[
            pltpu.VMEM(query.shape, query.dtype),
            pltpu.VMEM(owners.shape, owners.dtype),
            pltpu.VMEM(requests.shape, requests.dtype),
            pltpu.SemaphoreType.DMA((3,)),
        ],
        compiler_params=params(16),
        cost_estimate=pl.CostEstimate(flops=10**11, bytes_accessed=10**4, transcendentals=0),
        name="make_message",
    )(in_hbm(query), in_hbm(owners), in_hbm(requests))


def cache_kernel(
    lengths_ref, query_ref, cache_ref, signs_ref, mixed_ref, tops_ref, totals_ref, query_buf, top_buf, total_buf, mixed_buf
):
    requests, span, _ = cache_ref.shape
    blocks, size = signs_ref.shape
    heads = blocks // 2
    width = heads * size
    count = query_ref.shape[1] // size
    group = count // heads
    norm = 1.0 / math.sqrt(size)
    matrix = hadamard_tile(size)
    signs = (2 * signs_ref[...] - 1).astype(jnp.float32)
    query = query_ref[...].astype(jnp.float32)
    query = jnp.concatenate(
        [query[:, h * size : (h + 1) * size] * signs[h // group : h // group + 1] for h in range(count)], axis=0
    )
    query_buf[...] = jnp.dot(query.astype(jnp.bfloat16), matrix, preferred_element_type=jnp.float32) * norm
    rows = 2 * count
    kv_head = lax.broadcasted_iota(jnp.int32, (rows, width), 0) // group & (heads - 1)
    own_head = kv_head == lax.broadcasted_iota(jnp.int32, (rows, width), 1) // size
    first = lax.broadcasted_iota(jnp.int32, (rows, span), 0) < count
    position = lax.axis_index("tp") * span + lax.broadcasted_iota(jnp.int32, (rows, span), 1)
    pairs = range(0, requests, 2)
    scores = []
    for r in pairs:
        both = [query_buf[pl.ds(r + i, count, stride=requests), :] for i in range(2)]
        wide = jnp.concatenate([jnp.concatenate(both, axis=0)] * heads, axis=1)
        wide = jnp.where(own_head, wide, 0.0).astype(jnp.bfloat16)
        keys = cache_ref[r : r + 2, :, :width].reshape(2 * span, width)
        scores.append(lax.dot_general(wide, keys, NT, preferred_element_type=jnp.float32))
    probs = []
    for r, score in zip(pairs, scores):
        score = jnp.where(first, score[:, :span], score[:, span:]) * norm
        live = position < jnp.where(first, lengths_ref[0, 0, r], lengths_ref[0, 0, r + 1])
        top = jnp.max(jnp.where(live, score, LOWEST), axis=1, keepdims=True)
        prob = jnp.where(live, jnp.exp(score - top), 0.0)
        total = jnp.sum(prob, axis=1, keepdims=True)
        at = slice(r * count, (r + 2) * count)
        top_buf[at, :] = jnp.broadcast_to(top, (rows, size))
        total_buf[at, :] = jnp.broadcast_to(total, (rows, size))
        probs.append(
            jnp.concatenate([jnp.where(first, prob, 0.0), jnp.where(first, 0.0, prob)], axis=1).astype(jnp.bfloat16)
        )
    mixed = []
    for r, prob in zip(pairs, probs):
        values = cache_ref[r : r + 2, :, width:].reshape(2 * span, width)
        wide = jnp.dot(prob, values, preferred_element_type=jnp.float32)
        wide = jnp.where(own_head, wide, 0.0)
        mixed.append(sum(wide[:, k * size : (k + 1) * size] for k in range(heads)))
    mixed = jnp.concatenate(mixed, axis=0)
    high = mixed.astype(jnp.bfloat16)
    low = (mixed - high.astype(jnp.float32)).astype(jnp.bfloat16)
    plain = jnp.dot(high, matrix, preferred_element_type=jnp.float32)
    mixed_buf[...] = plain + jnp.dot(low, matrix, preferred_element_type=jnp.float32)
    for h in range(count):
        pick = pl.ds(h, requests, stride=count)
        column = slice(h * size, (h + 1) * size)
        k = heads + h // group
        mixed_ref[:, column] = mixed_buf[pick, :] * (signs[k : k + 1] * norm)
        tops_ref[:, column] = top_buf[pick, :]
        totals_ref[:, column] = total_buf[pick, :]


def cache_part(lengths, query, cache, signs):
    requests, span, width = cache.shape
    size = signs.shape[1]
    columns = query.shape[1]
    vmem = pl.BlockSpec(memory_space=pltpu.VMEM)
    return pl.pallas_call(
        cache_kernel,
        in_specs=[pl.BlockSpec(memory_space=pltpu.SMEM)] + [vmem] * 3,
        out_shape=[jax.ShapeDtypeStruct(query.shape, jnp.float32)] * 3,
        scratch_shapes=[pltpu.VMEM((requests * columns // size, size), jnp.float32)] * 4,
        compiler_params=params(),
        cost_estimate=pl.CostEstimate(
            flops=4 * span * requests * columns,
            bytes_accessed=2 * requests * span * width,
            transcendentals=span * requests * columns // size,
        ),
        name="cache_part",
    )(lengths, query, cache, signs)


def stats_kernel(top_ref, total_ref, new_top_ref, new_total_ref, cache_ref, cache_out_ref, factor_ref, stats_ref):
    requests, columns = top_ref.shape
    size = 128
    count = columns // size
    top, new_top = top_ref[...], new_top_ref[...]
    both = jnp.maximum(top, new_top)
    cache_factor = jnp.exp(top - both)
    new_factor = jnp.exp(new_top - both)
    cache_out_ref[...] = cache_ref[...] * cache_factor
    factor_ref[...] = new_factor
    total = total_ref[...] * cache_factor + new_total_ref[...] * new_factor
    lane = lax.broadcasted_iota(jnp.int32, (requests, size), 1)
    packed = []
    for value in (both, total):
        narrow = jnp.zeros((requests, size), jnp.float32)
        for h in range(count):
            narrow = jnp.where(lane % count == h, value[:, h * size : (h + 1) * size], narrow)
        high = narrow.astype(jnp.bfloat16).astype(jnp.float32)
        middle = (narrow - high).astype(jnp.bfloat16).astype(jnp.float32)
        low = narrow - high - middle
        packed.append(jnp.where(lane < count, high, jnp.where(lane < 2 * count, middle, low)))
    stats_ref[...] = jnp.concatenate(packed, axis=1).astype(jnp.bfloat16)


def combine_stats(tops, totals, new_tops, new_totals, cache_mixed):
    shape = tops.shape
    return pl.pallas_call(
        stats_kernel,
        out_shape=[
            jax.ShapeDtypeStruct(shape, jnp.float32),
            jax.ShapeDtypeStruct(shape, jnp.float32),
            jax.ShapeDtypeStruct((shape[0], 256), jnp.bfloat16),
        ],
        compiler_params=params(),
        name="combine_stats",
    )(tops, totals, new_tops, new_totals, cache_mixed)


def code_row(message_refs, start, requests, tokens):
    count = len(message_refs)
    me = lax.axis_index("seq")
    pieces = [ref[0:1, start : start + tokens // count].astype(jnp.float32) for ref in message_refs]
    row = [sum(jnp.where(me ^ d == at, pieces[d], 0.0) for d in range(count)) for at in range(count)]
    code = jnp.concatenate(row, axis=1).astype(jnp.int32)
    return ((code // requests) ^ me) * requests + code % requests


def score_kernel(heads, start, partial_ref, *refs):
    message_refs, (scores_ref, code_ref) = far_first(refs[:-2]), refs[-2:]
    requests = message_refs[0].shape[0]
    size = partial_ref.shape[1] // heads
    tokens = partial_ref.shape[0]
    group = start // (heads * size)
    code = code_row(message_refs, start, requests, tokens)
    code_ref[...] = jnp.broadcast_to(code, code_ref.shape)
    span = len(message_refs) * requests
    here = lax.broadcasted_iota(jnp.int32, (span, tokens), 0) == code
    queries = [ref[:, :start].astype(jnp.float32) for ref in message_refs]
    for k in range(heads):
        rows = []
        for g in range(group):
            at = (k * group + g) * size
            rows += [query[:, at : at + size] for query in queries]
        query = jnp.concatenate(rows, axis=0).astype(jnp.bfloat16)
        keys = partial_ref[:, k * size : (k + 1) * size]
        scores = lax.dot_general(query, keys, NT, preferred_element_type=jnp.float32)
        lines = [
            jnp.sum(jnp.where(here, scores[g * span : (g + 1) * span], 0.0), axis=0, keepdims=True)
            for g in range(group)
        ]
        scores_ref[k * group : (k + 1) * group, :] = jnp.concatenate(lines, axis=0) * (
            1.0 / math.sqrt(size)
        )


def partial_scores(heads, width, columns, partials, messages):
    tokens = partials.shape[0]
    size = width // heads
    query_heads = columns // size
    return pl.pallas_call(
        functools.partial(score_kernel, heads, columns),
        grid=(1,),
        in_specs=[pl.BlockSpec((tokens, width), lambda i: (0, 0))]
        + [pl.BlockSpec(m.shape, lambda i: (0, 0)) for m in messages],
        out_specs=[
            pl.BlockSpec((query_heads, tokens), lambda i: (0, 0)),
            pl.BlockSpec((8, tokens), lambda i: (0, 0)),
        ],
        out_shape=[
            jax.ShapeDtypeStruct((query_heads, tokens), jnp.float32),
            jax.ShapeDtypeStruct((8, tokens), jnp.int32),
        ],
        compiler_params=params(),
        name="partial_scores",
    )(partials, *far_first(messages))


def mix_kernel(heads, count, code_ref, values_ref, *refs):
    score_refs = far_first(refs[:count])
    mixed_refs = refs[count : 2 * count]
    tops_ref, totals_ref = refs[2 * count :]
    tokens = values_ref.shape[0]
    size = values_ref.shape[1] // heads
    requests = tops_ref.shape[0]
    group = score_refs[0].shape[0] // heads
    span = count * requests
    here = lax.broadcasted_iota(jnp.int32, (span, tokens), 0) == code_ref[0:1, :]
    parts = [ref[...] for ref in score_refs]
    while len(parts) > 1:
        parts = [parts[i] + parts[i + 1] for i in range(0, len(parts), 2)]
    scores = parts[0]
    mixed = []
    for k in range(heads):
        weights = []
        for g in range(group):
            row = k * group + g
            line = jnp.broadcast_to(scores[row : row + 1, :], (span, tokens))
            top = jnp.max(jnp.where(here, line, LOWEST), axis=1, keepdims=True)
            probs = jnp.where(here, jnp.exp(line - top), 0.0)
            total = jnp.sum(probs, axis=1, keepdims=True)
            weights.append(probs)
            column = slice(row * size, (row + 1) * size)
            tops_ref[:, column] = jnp.broadcast_to(top[:requests], (requests, size))
            totals_ref[:, column] = jnp.broadcast_to(total[:requests], (requests, size))
        weights = jnp.concatenate(weights, axis=0).astype(jnp.bfloat16)
        values = values_ref[:, k * size : (k + 1) * size]
        mixed.append(jnp.dot(weights, values, preferred_element_type=jnp.float32))
    half = heads // 2
    for k in range(half):
        for g in range(group):
            at = (k * group + g) * size
            for d in range(count):
                rows = slice(g * span + d * requests, g * span + (d + 1) * requests)
                pair = jnp.concatenate([mixed[k][rows], mixed[k + half][rows]], axis=0)
                mixed_refs[d][:, at : at + size] = pair.astype(jnp.bfloat16)


def mix(heads, width, requests, code, partials, scores):
    count = len(scores)
    tokens = partials.shape[0]
    columns = scores[0].shape[0] * (width // heads)
    whole = lambda shape: pl.BlockSpec(shape, lambda i: (0, 0))
    return pl.pallas_call(
        functools.partial(mix_kernel, heads, count),
        grid=(1,),
        in_specs=[whole(code.shape), pl.BlockSpec((tokens, width), lambda i: (0, 1))]
        + [whole(s.shape) for s in scores],
        out_specs=[whole((2 * requests, columns // 2))] * count + [whole((requests, columns))] * 2,
        out_shape=[jax.ShapeDtypeStruct((2 * requests, columns // 2), jnp.bfloat16)] * count
        + [jax.ShapeDtypeStruct((requests, columns), jnp.float32)] * 2,
        compiler_params=params(),
        name="mix",
    )(code, partials, *far_first(scores))


def merge_kernel(count, cache_ref, stats_ref, factor_ref, *refs):
    mixed_refs, out_ref = refs[:count], refs[count]
    requests, columns = cache_ref.shape
    half = columns // 2
    new = sum(ref[...].astype(jnp.float32) for ref in mixed_refs)
    for side in range(2):
        at = slice(side * half, (side + 1) * half)
        own = cache_ref[:, at] + new[side * requests : (side + 1) * requests] * factor_ref[:, at]
        out_ref[:, at] = own.astype(out_ref.dtype)
    out_ref[:, columns:] = stats_ref[...]


def merge(cache_mixed, stats, factor, mixed):
    requests, columns = cache_mixed.shape
    return pl.pallas_call(
        functools.partial(merge_kernel, len(mixed)),
        out_shape=jax.ShapeDtypeStruct((requests, columns + stats.shape[1]), jnp.bfloat16),
        compiler_params=params(),
        name="merge",
    )(cache_mixed, stats, factor, *far_first(mixed))


def finish_kernel(own_ref, far_ref, out_ref):
    requests, columns = out_ref.shape
    first = lax.axis_index("tp") == 0
    own, far = own_ref[...].astype(jnp.float32), far_ref[...].astype(jnp.float32)
    low, high = jnp.where(first, own, far), jnp.where(first, far, own)
    size = 128
    count = columns // size

    def read(message, start):
        at = columns + start * size
        parts = [message[:, at + part * count : at + (part + 1) * count] for part in range(3)]
        return parts[0] + parts[1] + parts[2]

    low_top, high_top = read(low, 0), read(high, 0)
    both = jnp.maximum(low_top, high_top)
    low_factor, high_factor = jnp.exp(low_top - both), jnp.exp(high_top - both)
    inverse = 1.0 / (read(low, 1) * low_factor + read(high, 1) * high_factor)
    low_factor, high_factor = low_factor * inverse, high_factor * inverse
    for h in range(count):
        at = slice(h * size, (h + 1) * size)
        out = low[:, at] * low_factor[:, h : h + 1] + high[:, at] * high_factor[:, h : h + 1]
        out_ref[:, at] = out.astype(out_ref.dtype)


def finish(own, far, columns):
    return pl.pallas_call(
        finish_kernel,
        out_shape=jax.ShapeDtypeStruct((own.shape[0], columns), jnp.bfloat16),
        compiler_params=params(),
        name="finish",
    )(own, far)


def from_partner(x, axis, distance):
    count = lax.axis_size(axis)
    return lax.ppermute(x, axis, [(i, i ^ distance) for i in range(count)])


def exchange(blocks):
    return [blocks[0]] + [from_partner(blocks[d], "seq", d) for d in range(1, len(blocks))]


def on_device(tokens, kv_weight, owners, requests, signs, queries, kv_cache, lengths):
    seq_count = lax.axis_size("seq")
    blocks, size = signs.shape
    heads = blocks // 2
    width = heads * size
    query = queries[0, 0]
    request_count, columns = query.shape
    message = make_message(query, owners[:, :, 0], requests)
    messages = exchange([message] * seq_count)
    partials = project(tokens, kv_weight)
    scores, code = partial_scores(heads, width, columns, partials, messages)
    scores = exchange([scores] * seq_count)
    cache_mixed, tops, totals = cache_part(lengths, query, kv_cache[0, 0], signs)
    results = mix(heads, width, request_count, code, partials, scores)
    mixed, (new_tops, new_totals) = results[:seq_count], results[seq_count:]
    mixed = exchange(mixed)
    cache_mixed, factor, stats = combine_stats(tops, totals, new_tops, new_totals, cache_mixed)
    own = merge(cache_mixed, stats, factor, mixed)
    far = from_partner(own, "tp", 1)
    return finish(own, far, columns).reshape(1, 1, request_count, columns)


def hadamard(order):
    rows = lax.broadcasted_iota(jnp.int32, (order, order), 0)
    cols = lax.broadcasted_iota(jnp.int32, (order, order), 1)
    parity = jnp.zeros((order, order), jnp.int32)
    for bit_number in range(order.bit_length() - 1):
        parity = parity + rows // 2**bit_number % 2 * (cols // 2**bit_number % 2)
    return (1 - 2 * (parity % 2)).astype(jnp.float32)


def rotate(blocks, sign_rows, matrix):
    product = jnp.einsum(
        "...h,hk->...k", blocks * sign_rows, matrix, precision=lax.Precision.HIGHEST
    )
    return product / math.sqrt(matrix.shape[0])


def encode(rotated):
    largest = jnp.max(jnp.abs(rotated), axis=-1) + 1e-06
    scales = largest.astype(jnp.bfloat16)
    encoded = (rotated / scales.astype(jnp.float32)[..., None]).astype(jnp.bfloat16)
    return (encoded, scales)


def decode(encoded, scales):
    return (encoded.astype(jnp.float32) * scales.astype(jnp.float32)[..., None]).astype(
        jnp.bfloat16
    )


def slot_numbers(targets, count, room):
    onehot = (targets[:, None] == lax.iota(jnp.int32, count)[None, :]).astype(jnp.int32)
    within = jnp.sum((jnp.cumsum(onehot, axis=0) - 1) * onehot, axis=1)
    return targets * room + within


def on_device_long(tokens, kv_weight, owners, requests, signs, queries, kv_cache, lengths):
    seq_count = lax.axis_size("seq")
    per_device = owners.shape[1]
    slots = max(2, (2 * per_device + seq_count - 1) // seq_count)
    head_blocks = signs.shape[0]
    kv_heads = head_blocks // 2
    head_size = signs.shape[1]
    matrix = hadamard(head_size)
    sign_rows = (2 * signs - 1).astype(jnp.float32)
    summed = lax.psum_scatter(
        jnp.dot(tokens, kv_weight, preferred_element_type=jnp.float32).astype(jnp.bfloat16),
        "seq",
        scatter_dimension=0,
        tiled=True,
    ).astype(jnp.float32)
    encoded, scales = encode(
        rotate(summed.reshape(per_device, head_blocks, head_size), sign_rows, matrix)
    )
    slot_index = slot_numbers(owners[0, :, 0], seq_count, slots)
    slot_total = seq_count * slots
    send_values = (
        jnp.zeros((slot_total, head_blocks, head_size), jnp.bfloat16).at[slot_index].set(encoded)
    )
    send_scales = jnp.zeros((slot_total, head_blocks), jnp.bfloat16).at[slot_index].set(scales)
    send_codes = jnp.zeros((slot_total,), jnp.int32).at[slot_index].set(requests[0] + 1)
    got_values, got_scales, arrived_codes = (
        lax.all_to_all(send_values, "seq", split_axis=0, concat_axis=0, tiled=True),
        lax.all_to_all(send_scales, "seq", split_axis=0, concat_axis=0, tiled=True),
        lax.all_to_all(send_codes, "seq", split_axis=0, concat_axis=0, tiled=True),
    )
    arrived = decode(got_values, got_scales)
    query = queries[0, 0]
    request_count = query.shape[0]
    group = query.shape[1] // (kv_heads * head_size)
    query_blocks = query.astype(jnp.float32).reshape(request_count, kv_heads, group, head_size)
    query_rot = rotate(query_blocks, sign_rows[:kv_heads][:, None, :], matrix).astype(jnp.bfloat16)
    local_cache = kv_cache[0, 0]
    cache_span = local_cache.shape[1]
    local_cache = local_cache.reshape(request_count, cache_span, head_blocks, head_size)
    score_scale = 1.0 / math.sqrt(head_size)
    lowest = -1e30
    highest = lax.Precision.HIGHEST
    score_cache = (
        jnp.einsum(
            "rkgd,rckd->rkgc",
            query_rot,
            local_cache[:, :, :kv_heads],
            preferred_element_type=jnp.float32,
        )
        * score_scale
    )
    score_new = (
        jnp.einsum(
            "rkgd,nkd->rkgn", query_rot, arrived[:, :kv_heads], preferred_element_type=jnp.float32
        )
        * score_scale
    )
    positions = lax.axis_index("tp") * cache_span + lax.iota(jnp.int32, cache_span)
    mask_cache = (positions[None, :] < lengths[0, 0][:, None])[:, None, None, :]
    match = arrived_codes[None, :] == (lax.iota(jnp.int32, request_count) + 1)[:, None]
    mask_new = match[:, None, None, :]
    top = jnp.maximum(
        jnp.max(jnp.where(mask_cache, score_cache, lowest), axis=-1),
        jnp.max(jnp.where(mask_new, score_new, lowest), axis=-1),
    )
    probs_cache = jnp.where(mask_cache, jnp.exp(score_cache - top[..., None]), 0.0)
    probs_new = jnp.where(mask_new, jnp.exp(score_new - top[..., None]), 0.0)
    total = jnp.sum(probs_cache, axis=-1) + jnp.sum(probs_new, axis=-1)
    mixed = jnp.einsum(
        "rkgc,rckd->rkgd",
        probs_cache,
        local_cache[:, :, kv_heads:].astype(jnp.float32),
        precision=highest,
    )
    mixed = mixed + jnp.einsum(
        "rkgn,nkd->rkgd", probs_new, arrived[:, kv_heads:].astype(jnp.float32), precision=highest
    )
    shared_top = lax.pmax(top, "tp")
    factor = jnp.exp(top - shared_top)
    total, mixed = (
        lax.psum((total * factor).astype(jnp.bfloat16), "tp").astype(jnp.float32),
        lax.psum((mixed * factor[..., None]).astype(jnp.bfloat16), "tp").astype(jnp.float32),
    )
    mixed = mixed / total[..., None]
    output = rotate(mixed, 1.0, matrix) * sign_rows[kv_heads:][None, :, None, :]
    return output.reshape(1, 1, request_count, group * kv_heads * head_size).astype(jnp.bfloat16)


def solution(mesh):
    placed = (
        P(("groups", "tp", "section"), "seq"),
        P("seq", None),
        P(("groups", "tp", "section"), "seq", None),
        P(("groups", "tp", "section"), "seq"),
        P(),
        P(("groups", "seq"), "section", None, None),
        P(("groups", "seq"), "section", None, "tp", None),
        P(("groups", "seq"), "section", None),
    )
    short = mesh.shape["seq"] == 4 and mesh.shape["tp"] == 2
    return jax.shard_map(
        on_device if short else on_device_long,
        mesh=mesh,
        in_specs=placed,
        out_specs=P(("groups", "seq"), "section", None, None),
        check_vma=False,
    )
```

```python
import functools
import math

import jax
import jax.numpy as jnp
from jax import lax
from jax.experimental import pallas as pl
from jax.experimental.pallas import tpu as pltpu
from jax.sharding import PartitionSpec as P

LOWEST = -1e30
MIB = 1024 * 1024
NT = (((1,), (1,)), ((), ()))


def params(mib=32):
    return pltpu.CompilerParams(vmem_limit_bytes=mib * MIB)


def in_hbm(x):
    return pltpu.with_memory_space_constraint(x, pltpu.HBM)


def in_vmem(x):
    return pltpu.with_memory_space_constraint(x, pltpu.VMEM)


def hadamard_tile(order):
    rows = lax.broadcasted_iota(jnp.int32, (order, order), 0)
    cols = lax.broadcasted_iota(jnp.int32, (order, order), 1)
    common = rows & cols
    parity = jnp.zeros((order, order), jnp.int32)
    for bit_number in range(order.bit_length() - 1):
        parity = parity ^ (common >> bit_number)
    return (1 - 2 * (parity & 1)).astype(jnp.float32).astype(jnp.bfloat16)


QUERY_ORDER = (3, 2, 1)
SCORE_ORDER = (2, 3, 1)
MIXED_ORDER = (3, 1, 2)


def arranged(blocks, order):
    return [blocks[0]] + [blocks[d] for d in order]


def by_distance(refs, order):
    return [refs[0]] + [refs[1 + order.index(d)] for d in range(1, len(refs))]


def project_kernel(tokens_ref, weight_ref, out_ref):
    out_ref[...] = jnp.dot(tokens_ref[...], weight_ref[...], preferred_element_type=jnp.float32).astype(out_ref.dtype)


def project(tokens, weight):
    rows, features = tokens.shape
    width = weight.shape[1]
    return pl.pallas_call(
        project_kernel,
        in_specs=[pl.BlockSpec(memory_space=pltpu.VMEM)] * 2,
        out_specs=pl.BlockSpec(memory_space=pltpu.VMEM),
        out_shape=jax.ShapeDtypeStruct((rows, width), jnp.bfloat16),
        compiler_params=params(32),
        cost_estimate=pl.CostEstimate(
            flops=2 * rows * features * width,
            bytes_accessed=2 * (rows * features + features * width),
            transcendentals=0,
        ),
        name="project",
    )(in_vmem(tokens), in_vmem(weight))


def message_kernel(query_ref, owners_ref, requests_ref, out_ref, query_buf, owners_buf, requests_buf, sems):
    requests, columns = query_ref.shape
    per_device = owners_ref.shape[1]
    copies = [
        pltpu.make_async_copy(source, target, sems.at[i])
        for i, (source, target) in enumerate(
            ((query_ref, query_buf), (owners_ref, owners_buf), (requests_ref, requests_buf))
        )
    ]
    for copy in copies:
        copy.start()
    for copy in copies:
        copy.wait()
    out_ref[:, :columns] = query_buf[...]
    code = (owners_buf[...] * requests + requests_buf[...]).astype(jnp.float32)
    spare = jnp.zeros((1, out_ref.shape[1] - columns - per_device), jnp.float32)
    code = jnp.concatenate([code, spare], axis=1)
    out_ref[:, columns:] = jnp.broadcast_to(code, (requests, code.shape[1])).astype(out_ref.dtype)


def make_message(query, owners, requests):
    count, columns = query.shape
    lanes = -(-owners.shape[1] // 128) * 128
    return pl.pallas_call(
        message_kernel,
        in_specs=[pl.BlockSpec(memory_space=pl.ANY)] * 3,
        out_specs=pl.BlockSpec(memory_space=pltpu.VMEM),
        out_shape=jax.ShapeDtypeStruct((count, columns + lanes), query.dtype),
        scratch_shapes=[
            pltpu.VMEM(query.shape, query.dtype),
            pltpu.VMEM(owners.shape, owners.dtype),
            pltpu.VMEM(requests.shape, requests.dtype),
            pltpu.SemaphoreType.DMA((3,)),
        ],
        compiler_params=params(16),
        cost_estimate=pl.CostEstimate(flops=10**11, bytes_accessed=10**4, transcendentals=0),
        name="make_message",
    )(in_hbm(query), in_hbm(owners), in_hbm(requests))


def cache_kernel(
    lengths_ref, query_ref, cache_ref, signs_ref, mixed_ref, tops_ref, totals_ref, query_buf, top_buf, total_buf, mixed_buf
):
    requests, span, _ = cache_ref.shape
    blocks, size = signs_ref.shape
    heads = blocks // 2
    width = heads * size
    count = query_ref.shape[1] // size
    group = count // heads
    norm = 1.0 / math.sqrt(size)
    matrix = hadamard_tile(size)
    signs = (2 * signs_ref[...] - 1).astype(jnp.float32)
    query = query_ref[...].astype(jnp.float32)
    query = jnp.concatenate(
        [query[:, h * size : (h + 1) * size] * signs[h // group : h // group + 1] for h in range(count)], axis=0
    )
    query_buf[...] = jnp.dot(query.astype(jnp.bfloat16), matrix, preferred_element_type=jnp.float32) * norm
    rows = 2 * count
    kv_head = lax.broadcasted_iota(jnp.int32, (rows, width), 0) // group & (heads - 1)
    own_head = kv_head == lax.broadcasted_iota(jnp.int32, (rows, width), 1) // size
    first = lax.broadcasted_iota(jnp.int32, (rows, span), 0) < count
    position = lax.axis_index("tp") * span + lax.broadcasted_iota(jnp.int32, (rows, span), 1)
    pairs = range(0, requests, 2)
    scores = []
    for r in pairs:
        both = [query_buf[pl.ds(r + i, count, stride=requests), :] for i in range(2)]
        wide = jnp.concatenate([jnp.concatenate(both, axis=0)] * heads, axis=1)
        wide = jnp.where(own_head, wide, 0.0).astype(jnp.bfloat16)
        keys = cache_ref[r : r + 2, :, :width].reshape(2 * span, width)
        scores.append(lax.dot_general(wide, keys, NT, preferred_element_type=jnp.float32))
    probs = []
    for r, score in zip(pairs, scores):
        score = jnp.where(first, score[:, :span], score[:, span:]) * norm
        live = position < jnp.where(first, lengths_ref[0, 0, r], lengths_ref[0, 0, r + 1])
        top = jnp.max(jnp.where(live, score, LOWEST), axis=1, keepdims=True)
        prob = jnp.where(live, jnp.exp(score - top), 0.0)
        total = jnp.sum(prob, axis=1, keepdims=True)
        at = slice(r * count, (r + 2) * count)
        top_buf[at, :] = jnp.broadcast_to(top, (rows, size))
        total_buf[at, :] = jnp.broadcast_to(total, (rows, size))
        probs.append(
            jnp.concatenate([jnp.where(first, prob, 0.0), jnp.where(first, 0.0, prob)], axis=1).astype(jnp.bfloat16)
        )
    mixed = []
    for r, prob in zip(pairs, probs):
        values = cache_ref[r : r + 2, :, width:].reshape(2 * span, width)
        wide = jnp.dot(prob, values, preferred_element_type=jnp.float32)
        wide = jnp.where(own_head, wide, 0.0)
        mixed.append(sum(wide[:, k * size : (k + 1) * size] for k in range(heads)))
    mixed = jnp.concatenate(mixed, axis=0)
    high = mixed.astype(jnp.bfloat16)
    low = (mixed - high.astype(jnp.float32)).astype(jnp.bfloat16)
    plain = jnp.dot(high, matrix, preferred_element_type=jnp.float32)
    mixed_buf[...] = plain + jnp.dot(low, matrix, preferred_element_type=jnp.float32)
    for h in range(count):
        pick = pl.ds(h, requests, stride=count)
        column = slice(h * size, (h + 1) * size)
        k = heads + h // group
        mixed_ref[:, column] = mixed_buf[pick, :] * (signs[k : k + 1] * norm)
        tops_ref[:, column] = top_buf[pick, :]
        totals_ref[:, column] = total_buf[pick, :]


def cache_part(lengths, query, cache, signs):
    requests, span, width = cache.shape
    size = signs.shape[1]
    columns = query.shape[1]
    vmem = pl.BlockSpec(memory_space=pltpu.VMEM)
    return pl.pallas_call(
        cache_kernel,
        in_specs=[pl.BlockSpec(memory_space=pltpu.SMEM)] + [vmem] * 3,
        out_shape=[jax.ShapeDtypeStruct(query.shape, jnp.float32)] * 3,
        scratch_shapes=[pltpu.VMEM((requests * columns // size, size), jnp.float32)] * 4,
        compiler_params=params(),
        cost_estimate=pl.CostEstimate(
            flops=4 * span * requests * columns,
            bytes_accessed=2 * requests * span * width,
            transcendentals=span * requests * columns // size,
        ),
        name="cache_part",
    )(lengths, query, cache, signs)


def stats_kernel(top_ref, total_ref, new_top_ref, new_total_ref, cache_ref, cache_out_ref, factor_ref, stats_ref):
    requests, columns = top_ref.shape
    size = 128
    count = columns // size
    top, new_top = top_ref[...], new_top_ref[...]
    both = jnp.maximum(top, new_top)
    cache_factor = jnp.exp(top - both)
    new_factor = jnp.exp(new_top - both)
    cache_out_ref[...] = cache_ref[...] * cache_factor
    factor_ref[...] = new_factor
    total = total_ref[...] * cache_factor + new_total_ref[...] * new_factor
    lane = lax.broadcasted_iota(jnp.int32, (requests, size), 1)
    packed = []
    for value in (both, total):
        narrow = jnp.zeros((requests, size), jnp.float32)
        for h in range(count):
            narrow = jnp.where(lane % count == h, value[:, h * size : (h + 1) * size], narrow)
        high = narrow.astype(jnp.bfloat16).astype(jnp.float32)
        middle = (narrow - high).astype(jnp.bfloat16).astype(jnp.float32)
        low = narrow - high - middle
        packed.append(jnp.where(lane < count, high, jnp.where(lane < 2 * count, middle, low)))
    stats_ref[...] = jnp.concatenate(packed, axis=1).astype(jnp.bfloat16)


def combine_stats(tops, totals, new_tops, new_totals, cache_mixed):
    shape = tops.shape
    return pl.pallas_call(
        stats_kernel,
        out_shape=[
            jax.ShapeDtypeStruct(shape, jnp.float32),
            jax.ShapeDtypeStruct(shape, jnp.float32),
            jax.ShapeDtypeStruct((shape[0], 256), jnp.bfloat16),
        ],
        compiler_params=params(),
        name="combine_stats",
    )(tops, totals, new_tops, new_totals, cache_mixed)


def code_row(message_refs, start, requests, tokens):
    count = len(message_refs)
    me = lax.axis_index("seq")
    pieces = [ref[0:1, start : start + tokens // count].astype(jnp.float32) for ref in message_refs]
    row = [sum(jnp.where(me ^ d == at, pieces[d], 0.0) for d in range(count)) for at in range(count)]
    code = jnp.concatenate(row, axis=1).astype(jnp.int32)
    return ((code // requests) ^ me) * requests + code % requests


def score_kernel(heads, start, partial_ref, *refs):
    message_refs, (scores_ref, code_ref) = by_distance(refs[:-2], QUERY_ORDER), refs[-2:]
    requests = message_refs[0].shape[0]
    size = partial_ref.shape[1] // heads
    tokens = partial_ref.shape[0]
    group = start // (heads * size)
    code = code_row(message_refs, start, requests, tokens)
    code_ref[...] = jnp.broadcast_to(code, code_ref.shape)
    span = len(message_refs) * requests
    here = lax.broadcasted_iota(jnp.int32, (span, tokens), 0) == code
    queries = [ref[:, :start].astype(jnp.float32) for ref in message_refs]
    for k in range(heads):
        rows = []
        for g in range(group):
            at = (k * group + g) * size
            rows += [query[:, at : at + size] for query in queries]
        query = jnp.concatenate(rows, axis=0).astype(jnp.bfloat16)
        keys = partial_ref[:, k * size : (k + 1) * size]
        scores = lax.dot_general(query, keys, NT, preferred_element_type=jnp.float32)
        lines = [
            jnp.sum(jnp.where(here, scores[g * span : (g + 1) * span], 0.0), axis=0, keepdims=True)
            for g in range(group)
        ]
        scores_ref[k * group : (k + 1) * group, :] = jnp.concatenate(lines, axis=0) * (
            1.0 / math.sqrt(size)
        )


def partial_scores(heads, width, columns, partials, messages):
    tokens = partials.shape[0]
    size = width // heads
    query_heads = columns // size
    return pl.pallas_call(
        functools.partial(score_kernel, heads, columns),
        grid=(1,),
        in_specs=[pl.BlockSpec((tokens, width), lambda i: (0, 0))]
        + [pl.BlockSpec(m.shape, lambda i: (0, 0)) for m in messages],
        out_specs=[
            pl.BlockSpec((query_heads, tokens), lambda i: (0, 0)),
            pl.BlockSpec((8, tokens), lambda i: (0, 0)),
        ],
        out_shape=[
            jax.ShapeDtypeStruct((query_heads, tokens), jnp.float32),
            jax.ShapeDtypeStruct((8, tokens), jnp.int32),
        ],
        compiler_params=params(),
        name="partial_scores",
    )(partials, *arranged(messages, QUERY_ORDER))


def mix_kernel(heads, count, code_ref, values_ref, *refs):
    score_refs = by_distance(refs[:count], SCORE_ORDER)
    mixed_refs = refs[count : 2 * count]
    tops_ref, totals_ref = refs[2 * count :]
    tokens = values_ref.shape[0]
    size = values_ref.shape[1] // heads
    requests = tops_ref.shape[0]
    group = score_refs[0].shape[0] // heads
    span = count * requests
    here = lax.broadcasted_iota(jnp.int32, (span, tokens), 0) == code_ref[0:1, :]
    parts = [ref[...] for ref in score_refs]
    while len(parts) > 1:
        parts = [parts[i] + parts[i + 1] for i in range(0, len(parts), 2)]
    scores = parts[0]
    mixed = []
    for k in range(heads):
        weights = []
        for g in range(group):
            row = k * group + g
            line = jnp.broadcast_to(scores[row : row + 1, :], (span, tokens))
            top = jnp.max(jnp.where(here, line, LOWEST), axis=1, keepdims=True)
            probs = jnp.where(here, jnp.exp(line - top), 0.0)
            total = jnp.sum(probs, axis=1, keepdims=True)
            weights.append(probs)
            column = slice(row * size, (row + 1) * size)
            tops_ref[:, column] = jnp.broadcast_to(top[:requests], (requests, size))
            totals_ref[:, column] = jnp.broadcast_to(total[:requests], (requests, size))
        weights = jnp.concatenate(weights, axis=0).astype(jnp.bfloat16)
        values = values_ref[:, k * size : (k + 1) * size]
        mixed.append(jnp.dot(weights, values, preferred_element_type=jnp.float32))
    half = heads // 2
    for k in range(half):
        for g in range(group):
            at = (k * group + g) * size
            for d in range(count):
                rows = slice(g * span + d * requests, g * span + (d + 1) * requests)
                pair = jnp.concatenate([mixed[k][rows], mixed[k + half][rows]], axis=0)
                mixed_refs[d][:, at : at + size] = pair.astype(jnp.bfloat16)


def mix(heads, width, requests, code, partials, scores):
    count = len(scores)
    tokens = partials.shape[0]
    columns = scores[0].shape[0] * (width // heads)
    whole = lambda shape: pl.BlockSpec(shape, lambda i: (0, 0))
    return pl.pallas_call(
        functools.partial(mix_kernel, heads, count),
        grid=(1,),
        in_specs=[whole(code.shape), pl.BlockSpec((tokens, width), lambda i: (0, 1))]
        + [whole(s.shape) for s in scores],
        out_specs=[whole((2 * requests, columns // 2))] * count + [whole((requests, columns))] * 2,
        out_shape=[jax.ShapeDtypeStruct((2 * requests, columns // 2), jnp.bfloat16)] * count
        + [jax.ShapeDtypeStruct((requests, columns), jnp.float32)] * 2,
        compiler_params=params(),
        name="mix",
    )(code, partials, *arranged(scores, SCORE_ORDER))


def merge_kernel(count, cache_ref, stats_ref, factor_ref, *refs):
    mixed_refs, out_ref = refs[:count], refs[count]
    requests, columns = cache_ref.shape
    half = columns // 2
    new = sum(ref[...].astype(jnp.float32) for ref in mixed_refs)
    for side in range(2):
        at = slice(side * half, (side + 1) * half)
        own = cache_ref[:, at] + new[side * requests : (side + 1) * requests] * factor_ref[:, at]
        out_ref[:, at] = own.astype(out_ref.dtype)
    out_ref[:, columns:] = stats_ref[...]


def merge(cache_mixed, stats, factor, mixed):
    requests, columns = cache_mixed.shape
    return pl.pallas_call(
        functools.partial(merge_kernel, len(mixed)),
        out_shape=jax.ShapeDtypeStruct((requests, columns + stats.shape[1]), jnp.bfloat16),
        compiler_params=params(),
        name="merge",
    )(cache_mixed, stats, factor, *arranged(mixed, MIXED_ORDER))


def finish_kernel(own_ref, far_ref, out_ref):
    requests, columns = out_ref.shape
    first = lax.axis_index("tp") == 0
    own, far = own_ref[...].astype(jnp.float32), far_ref[...].astype(jnp.float32)
    low, high = jnp.where(first, own, far), jnp.where(first, far, own)
    size = 128
    count = columns // size

    def read(message, start):
        at = columns + start * size
        parts = [message[:, at + part * count : at + (part + 1) * count] for part in range(3)]
        return parts[0] + parts[1] + parts[2]

    low_top, high_top = read(low, 0), read(high, 0)
    both = jnp.maximum(low_top, high_top)
    low_factor, high_factor = jnp.exp(low_top - both), jnp.exp(high_top - both)
    inverse = 1.0 / (read(low, 1) * low_factor + read(high, 1) * high_factor)
    low_factor, high_factor = low_factor * inverse, high_factor * inverse
    for h in range(count):
        at = slice(h * size, (h + 1) * size)
        out = low[:, at] * low_factor[:, h : h + 1] + high[:, at] * high_factor[:, h : h + 1]
        out_ref[:, at] = out.astype(out_ref.dtype)


def finish(own, far, columns):
    return pl.pallas_call(
        finish_kernel,
        out_shape=jax.ShapeDtypeStruct((own.shape[0], columns), jnp.bfloat16),
        compiler_params=params(),
        name="finish",
    )(own, far)


def from_partner(x, axis, distance):
    count = lax.axis_size(axis)
    return lax.ppermute(x, axis, [(i, i ^ distance) for i in range(count)])


def exchange(blocks):
    return [blocks[0]] + [from_partner(blocks[d], "seq", d) for d in range(1, len(blocks))]


def on_device(tokens, kv_weight, owners, requests, signs, queries, kv_cache, lengths):
    seq_count = lax.axis_size("seq")
    blocks, size = signs.shape
    heads = blocks // 2
    width = heads * size
    query = queries[0, 0]
    request_count, columns = query.shape
    message = make_message(query, owners[:, :, 0], requests)
    messages = exchange([message] * seq_count)
    partials = project(tokens, kv_weight)
    scores, code = partial_scores(heads, width, columns, partials, messages)
    scores = exchange([scores] * seq_count)
    cache_mixed, tops, totals = cache_part(lengths, query, kv_cache[0, 0], signs)
    results = mix(heads, width, request_count, code, partials, scores)
    mixed, (new_tops, new_totals) = results[:seq_count], results[seq_count:]
    mixed = exchange(mixed)
    cache_mixed, factor, stats = combine_stats(tops, totals, new_tops, new_totals, cache_mixed)
    own = merge(cache_mixed, stats, factor, mixed)
    far = from_partner(own, "tp", 1)
    return finish(own, far, columns).reshape(1, 1, request_count, columns)


def hadamard(order):
    rows = lax.broadcasted_iota(jnp.int32, (order, order), 0)
    cols = lax.broadcasted_iota(jnp.int32, (order, order), 1)
    parity = jnp.zeros((order, order), jnp.int32)
    for bit_number in range(order.bit_length() - 1):
        parity = parity + rows // 2**bit_number % 2 * (cols // 2**bit_number % 2)
    return (1 - 2 * (parity % 2)).astype(jnp.float32)


def rotate(blocks, sign_rows, matrix):
    product = jnp.einsum(
        "...h,hk->...k", blocks * sign_rows, matrix, precision=lax.Precision.HIGHEST
    )
    return product / math.sqrt(matrix.shape[0])


def encode(rotated):
    largest = jnp.max(jnp.abs(rotated), axis=-1) + 1e-06
    scales = largest.astype(jnp.bfloat16)
    encoded = (rotated / scales.astype(jnp.float32)[..., None]).astype(jnp.bfloat16)
    return (encoded, scales)


def decode(encoded, scales):
    return (encoded.astype(jnp.float32) * scales.astype(jnp.float32)[..., None]).astype(
        jnp.bfloat16
    )


def slot_numbers(targets, count, room):
    onehot = (targets[:, None] == lax.iota(jnp.int32, count)[None, :]).astype(jnp.int32)
    within = jnp.sum((jnp.cumsum(onehot, axis=0) - 1) * onehot, axis=1)
    return targets * room + within


def on_device_long(tokens, kv_weight, owners, requests, signs, queries, kv_cache, lengths):
    seq_count = lax.axis_size("seq")
    per_device = owners.shape[1]
    slots = max(2, (2 * per_device + seq_count - 1) // seq_count)
    head_blocks = signs.shape[0]
    kv_heads = head_blocks // 2
    head_size = signs.shape[1]
    matrix = hadamard(head_size)
    sign_rows = (2 * signs - 1).astype(jnp.float32)
    summed = lax.psum_scatter(
        jnp.dot(tokens, kv_weight, preferred_element_type=jnp.float32).astype(jnp.bfloat16),
        "seq",
        scatter_dimension=0,
        tiled=True,
    ).astype(jnp.float32)
    encoded, scales = encode(
        rotate(summed.reshape(per_device, head_blocks, head_size), sign_rows, matrix)
    )
    slot_index = slot_numbers(owners[0, :, 0], seq_count, slots)
    slot_total = seq_count * slots
    send_values = (
        jnp.zeros((slot_total, head_blocks, head_size), jnp.bfloat16).at[slot_index].set(encoded)
    )
    send_scales = jnp.zeros((slot_total, head_blocks), jnp.bfloat16).at[slot_index].set(scales)
    send_codes = jnp.zeros((slot_total,), jnp.int32).at[slot_index].set(requests[0] + 1)
    got_values, got_scales, arrived_codes = (
        lax.all_to_all(send_values, "seq", split_axis=0, concat_axis=0, tiled=True),
        lax.all_to_all(send_scales, "seq", split_axis=0, concat_axis=0, tiled=True),
        lax.all_to_all(send_codes, "seq", split_axis=0, concat_axis=0, tiled=True),
    )
    arrived = decode(got_values, got_scales)
    query = queries[0, 0]
    request_count = query.shape[0]
    group = query.shape[1] // (kv_heads * head_size)
    query_blocks = query.astype(jnp.float32).reshape(request_count, kv_heads, group, head_size)
    query_rot = rotate(query_blocks, sign_rows[:kv_heads][:, None, :], matrix).astype(jnp.bfloat16)
    local_cache = kv_cache[0, 0]
    cache_span = local_cache.shape[1]
    local_cache = local_cache.reshape(request_count, cache_span, head_blocks, head_size)
    score_scale = 1.0 / math.sqrt(head_size)
    lowest = -1e30
    highest = lax.Precision.HIGHEST
    score_cache = (
        jnp.einsum(
            "rkgd,rckd->rkgc",
            query_rot,
            local_cache[:, :, :kv_heads],
            preferred_element_type=jnp.float32,
        )
        * score_scale
    )
    score_new = (
        jnp.einsum(
            "rkgd,nkd->rkgn", query_rot, arrived[:, :kv_heads], preferred_element_type=jnp.float32
        )
        * score_scale
    )
    positions = lax.axis_index("tp") * cache_span + lax.iota(jnp.int32, cache_span)
    mask_cache = (positions[None, :] < lengths[0, 0][:, None])[:, None, None, :]
    match = arrived_codes[None, :] == (lax.iota(jnp.int32, request_count) + 1)[:, None]
    mask_new = match[:, None, None, :]
    top = jnp.maximum(
        jnp.max(jnp.where(mask_cache, score_cache, lowest), axis=-1),
        jnp.max(jnp.where(mask_new, score_new, lowest), axis=-1),
    )
    probs_cache = jnp.where(mask_cache, jnp.exp(score_cache - top[..., None]), 0.0)
    probs_new = jnp.where(mask_new, jnp.exp(score_new - top[..., None]), 0.0)
    total = jnp.sum(probs_cache, axis=-1) + jnp.sum(probs_new, axis=-1)
    mixed = jnp.einsum(
        "rkgc,rckd->rkgd",
        probs_cache,
        local_cache[:, :, kv_heads:].astype(jnp.float32),
        precision=highest,
    )
    mixed = mixed + jnp.einsum(
        "rkgn,nkd->rkgd", probs_new, arrived[:, kv_heads:].astype(jnp.float32), precision=highest
    )
    shared_top = lax.pmax(top, "tp")
    factor = jnp.exp(top - shared_top)
    total, mixed = (
        lax.psum((total * factor).astype(jnp.bfloat16), "tp").astype(jnp.float32),
        lax.psum((mixed * factor[..., None]).astype(jnp.bfloat16), "tp").astype(jnp.float32),
    )
    mixed = mixed / total[..., None]
    output = rotate(mixed, 1.0, matrix) * sign_rows[kv_heads:][None, :, None, :]
    return output.reshape(1, 1, request_count, group * kv_heads * head_size).astype(jnp.bfloat16)


def solution(mesh):
    placed = (
        P(("groups", "tp", "section"), "seq"),
        P("seq", None),
        P(("groups", "tp", "section"), "seq", None),
        P(("groups", "tp", "section"), "seq"),
        P(),
        P(("groups", "seq"), "section", None, None),
        P(("groups", "seq"), "section", None, "tp", None),
        P(("groups", "seq"), "section", None),
    )
    short = mesh.shape["seq"] == 4 and mesh.shape["tp"] == 2
    return jax.shard_map(
        on_device if short else on_device_long,
        mesh=mesh,
        in_specs=placed,
        out_specs=P(("groups", "seq"), "section", None, None),
        check_vma=False,
    )
```

```python
import functools
import math

import jax
import jax.numpy as jnp
from jax import lax
from jax.experimental import pallas as pl
from jax.experimental.pallas import tpu as pltpu
from jax.sharding import PartitionSpec as P

LOWEST = -1e30
MIB = 1024 * 1024
NT = (((1,), (1,)), ((), ()))


def params(mib=32):
    return pltpu.CompilerParams(vmem_limit_bytes=mib * MIB)


def in_hbm(x):
    return pltpu.with_memory_space_constraint(x, pltpu.HBM)


def in_vmem(x):
    return pltpu.with_memory_space_constraint(x, pltpu.VMEM)


def hadamard_tile(order):
    rows = lax.broadcasted_iota(jnp.int32, (order, order), 0)
    cols = lax.broadcasted_iota(jnp.int32, (order, order), 1)
    common = rows & cols
    parity = jnp.zeros((order, order), jnp.int32)
    for bit_number in range(order.bit_length() - 1):
        parity = parity ^ (common >> bit_number)
    return (1 - 2 * (parity & 1)).astype(jnp.float32).astype(jnp.bfloat16)


QUERY_ORDER = (3, 2, 1)
MIXED_ORDER = (3, 2, 1)


def arranged(blocks, order):
    return [blocks[0]] + [blocks[d] for d in order]


def by_distance(refs, order):
    return [refs[0]] + [refs[1 + order.index(d)] for d in range(1, len(refs))]


def project_kernel(tokens_ref, weight_ref, out_ref):
    out_ref[...] = jnp.dot(tokens_ref[...], weight_ref[...], preferred_element_type=jnp.float32).astype(out_ref.dtype)


def project(tokens, weight):
    rows, features = tokens.shape
    width = weight.shape[1]
    return pl.pallas_call(
        project_kernel,
        in_specs=[pl.BlockSpec(memory_space=pltpu.VMEM)] * 2,
        out_specs=pl.BlockSpec(memory_space=pltpu.VMEM),
        out_shape=jax.ShapeDtypeStruct((rows, width), jnp.bfloat16),
        compiler_params=params(32),
        cost_estimate=pl.CostEstimate(
            flops=2 * rows * features * width,
            bytes_accessed=2 * (rows * features + features * width),
            transcendentals=0,
        ),
        name="project",
    )(in_vmem(tokens), in_vmem(weight))


def message_kernel(query_ref, owners_ref, requests_ref, out_ref, query_buf, owners_buf, requests_buf, sems):
    requests, columns = query_ref.shape
    per_device = owners_ref.shape[1]
    copies = [
        pltpu.make_async_copy(source, target, sems.at[i])
        for i, (source, target) in enumerate(
            ((query_ref, query_buf), (owners_ref, owners_buf), (requests_ref, requests_buf))
        )
    ]
    for copy in copies:
        copy.start()
    for copy in copies:
        copy.wait()
    out_ref[:, :columns] = query_buf[...]
    code = (owners_buf[...] * requests + requests_buf[...]).astype(jnp.float32)
    spare = jnp.zeros((1, out_ref.shape[1] - columns - per_device), jnp.float32)
    code = jnp.concatenate([code, spare], axis=1)
    out_ref[:, columns:] = jnp.broadcast_to(code, (requests, code.shape[1])).astype(out_ref.dtype)


def make_message(query, owners, requests):
    count, columns = query.shape
    lanes = -(-owners.shape[1] // 128) * 128
    return pl.pallas_call(
        message_kernel,
        in_specs=[pl.BlockSpec(memory_space=pl.ANY)] * 3,
        out_specs=pl.BlockSpec(memory_space=pltpu.VMEM),
        out_shape=jax.ShapeDtypeStruct((count, columns + lanes), query.dtype),
        scratch_shapes=[
            pltpu.VMEM(query.shape, query.dtype),
            pltpu.VMEM(owners.shape, owners.dtype),
            pltpu.VMEM(requests.shape, requests.dtype),
            pltpu.SemaphoreType.DMA((3,)),
        ],
        compiler_params=params(16),
        cost_estimate=pl.CostEstimate(flops=10**11, bytes_accessed=10**4, transcendentals=0),
        name="make_message",
    )(in_hbm(query), in_hbm(owners), in_hbm(requests))


def cache_kernel(
    lengths_ref, query_ref, cache_ref, signs_ref, mixed_ref, tops_ref, totals_ref, query_buf, top_buf, total_buf, mixed_buf
):
    requests, span, _ = cache_ref.shape
    blocks, size = signs_ref.shape
    heads = blocks // 2
    width = heads * size
    count = query_ref.shape[1] // size
    group = count // heads
    norm = 1.0 / math.sqrt(size)
    matrix = hadamard_tile(size)
    signs = (2 * signs_ref[...] - 1).astype(jnp.float32)
    query = query_ref[...].astype(jnp.float32)
    query = jnp.concatenate(
        [query[:, h * size : (h + 1) * size] * signs[h // group : h // group + 1] for h in range(count)], axis=0
    )
    query_buf[...] = jnp.dot(query.astype(jnp.bfloat16), matrix, preferred_element_type=jnp.float32) * norm
    rows = 2 * count
    kv_head = lax.broadcasted_iota(jnp.int32, (rows, width), 0) // group & (heads - 1)
    own_head = kv_head == lax.broadcasted_iota(jnp.int32, (rows, width), 1) // size
    first = lax.broadcasted_iota(jnp.int32, (rows, span), 0) < count
    position = lax.axis_index("tp") * span + lax.broadcasted_iota(jnp.int32, (rows, span), 1)
    pairs = range(0, requests, 2)
    scores = []
    for r in pairs:
        both = [query_buf[pl.ds(r + i, count, stride=requests), :] for i in range(2)]
        wide = jnp.concatenate([jnp.concatenate(both, axis=0)] * heads, axis=1)
        wide = jnp.where(own_head, wide, 0.0).astype(jnp.bfloat16)
        keys = cache_ref[r : r + 2, :, :width].reshape(2 * span, width)
        scores.append(lax.dot_general(wide, keys, NT, preferred_element_type=jnp.float32))
    probs = []
    for r, score in zip(pairs, scores):
        score = jnp.where(first, score[:, :span], score[:, span:]) * norm
        live = position < jnp.where(first, lengths_ref[0, 0, r], lengths_ref[0, 0, r + 1])
        top = jnp.max(jnp.where(live, score, LOWEST), axis=1, keepdims=True)
        prob = jnp.where(live, jnp.exp(score - top), 0.0)
        total = jnp.sum(prob, axis=1, keepdims=True)
        at = slice(r * count, (r + 2) * count)
        top_buf[at, :] = jnp.broadcast_to(top, (rows, size))
        total_buf[at, :] = jnp.broadcast_to(total, (rows, size))
        probs.append(
            jnp.concatenate([jnp.where(first, prob, 0.0), jnp.where(first, 0.0, prob)], axis=1).astype(jnp.bfloat16)
        )
    mixed = []
    for r, prob in zip(pairs, probs):
        values = cache_ref[r : r + 2, :, width:].reshape(2 * span, width)
        wide = jnp.dot(prob, values, preferred_element_type=jnp.float32)
        wide = jnp.where(own_head, wide, 0.0)
        mixed.append(sum(wide[:, k * size : (k + 1) * size] for k in range(heads)))
    mixed = jnp.concatenate(mixed, axis=0)
    high = mixed.astype(jnp.bfloat16)
    low = (mixed - high.astype(jnp.float32)).astype(jnp.bfloat16)
    plain = jnp.dot(high, matrix, preferred_element_type=jnp.float32)
    mixed_buf[...] = plain + jnp.dot(low, matrix, preferred_element_type=jnp.float32)
    for h in range(count):
        pick = pl.ds(h, requests, stride=count)
        column = slice(h * size, (h + 1) * size)
        k = heads + h // group
        mixed_ref[:, column] = mixed_buf[pick, :] * (signs[k : k + 1] * norm)
        tops_ref[:, column] = top_buf[pick, :]
        totals_ref[:, column] = total_buf[pick, :]


def cache_part(lengths, query, cache, signs):
    requests, span, width = cache.shape
    size = signs.shape[1]
    columns = query.shape[1]
    vmem = pl.BlockSpec(memory_space=pltpu.VMEM)
    return pl.pallas_call(
        cache_kernel,
        in_specs=[pl.BlockSpec(memory_space=pltpu.SMEM)] + [vmem] * 3,
        out_shape=[jax.ShapeDtypeStruct(query.shape, jnp.float32)] * 3,
        scratch_shapes=[pltpu.VMEM((requests * columns // size, size), jnp.float32)] * 4,
        compiler_params=params(),
        cost_estimate=pl.CostEstimate(
            flops=4 * span * requests * columns,
            bytes_accessed=2 * requests * span * width,
            transcendentals=span * requests * columns // size,
        ),
        name="cache_part",
    )(lengths, query, cache, signs)


def stats_kernel(top_ref, total_ref, new_top_ref, new_total_ref, cache_ref, cache_out_ref, factor_ref, stats_ref):
    requests, columns = top_ref.shape
    size = 128
    count = columns // size
    top, new_top = top_ref[...], new_top_ref[...]
    both = jnp.maximum(top, new_top)
    cache_factor = jnp.exp(top - both)
    new_factor = jnp.exp(new_top - both)
    cache_out_ref[...] = cache_ref[...] * cache_factor
    factor_ref[...] = new_factor
    total = total_ref[...] * cache_factor + new_total_ref[...] * new_factor
    lane = lax.broadcasted_iota(jnp.int32, (requests, size), 1)
    packed = []
    for value in (both, total):
        narrow = jnp.zeros((requests, size), jnp.float32)
        for h in range(count):
            narrow = jnp.where(lane % count == h, value[:, h * size : (h + 1) * size], narrow)
        high = narrow.astype(jnp.bfloat16).astype(jnp.float32)
        middle = (narrow - high).astype(jnp.bfloat16).astype(jnp.float32)
        low = narrow - high - middle
        packed.append(jnp.where(lane < count, high, jnp.where(lane < 2 * count, middle, low)))
    stats_ref[...] = jnp.concatenate(packed, axis=1).astype(jnp.bfloat16)


def combine_stats(tops, totals, new_tops, new_totals, cache_mixed):
    shape = tops.shape
    return pl.pallas_call(
        stats_kernel,
        out_shape=[
            jax.ShapeDtypeStruct(shape, jnp.float32),
            jax.ShapeDtypeStruct(shape, jnp.float32),
            jax.ShapeDtypeStruct((shape[0], 256), jnp.bfloat16),
        ],
        compiler_params=params(),
        name="combine_stats",
    )(tops, totals, new_tops, new_totals, cache_mixed)


def code_row(message_refs, start, requests, tokens):
    count = len(message_refs)
    me = lax.axis_index("seq")
    pieces = [ref[0:1, start : start + tokens // count].astype(jnp.float32) for ref in message_refs]
    row = [sum(jnp.where(me ^ d == at, pieces[d], 0.0) for d in range(count)) for at in range(count)]
    code = jnp.concatenate(row, axis=1).astype(jnp.int32)
    return ((code // requests) ^ me) * requests + code % requests


def score_kernel(heads, start, partial_ref, *refs):
    message_refs, (scores_ref, code_ref) = by_distance(refs[:-2], QUERY_ORDER), refs[-2:]
    requests = message_refs[0].shape[0]
    size = partial_ref.shape[1] // heads
    tokens = partial_ref.shape[0]
    group = start // (heads * size)
    code = code_row(message_refs, start, requests, tokens)
    code_ref[...] = jnp.broadcast_to(code, code_ref.shape)
    span = len(message_refs) * requests
    here = lax.broadcasted_iota(jnp.int32, (span, tokens), 0) == code
    queries = [ref[:, :start].astype(jnp.float32) for ref in message_refs]
    for k in range(heads):
        rows = []
        for g in range(group):
            at = (k * group + g) * size
            rows += [query[:, at : at + size] for query in queries]
        query = jnp.concatenate(rows, axis=0).astype(jnp.bfloat16)
        keys = partial_ref[:, k * size : (k + 1) * size]
        scores = lax.dot_general(query, keys, NT, preferred_element_type=jnp.float32)
        lines = [
            jnp.sum(jnp.where(here, scores[g * span : (g + 1) * span], 0.0), axis=0, keepdims=True)
            for g in range(group)
        ]
        block = jnp.concatenate(lines, axis=0) * (1.0 / math.sqrt(size))
        for d in range(len(message_refs)):
            scores_ref[d, k * group : (k + 1) * group, :] = block


def partial_scores(heads, width, columns, partials, messages):
    tokens = partials.shape[0]
    size = width // heads
    query_heads = columns // size
    return pl.pallas_call(
        functools.partial(score_kernel, heads, columns),
        grid=(1,),
        in_specs=[pl.BlockSpec((tokens, width), lambda i: (0, 0))]
        + [pl.BlockSpec(m.shape, lambda i: (0, 0)) for m in messages],
        out_specs=[
            pl.BlockSpec((len(messages), query_heads, tokens), lambda i: (0, 0, 0)),
            pl.BlockSpec((8, tokens), lambda i: (0, 0)),
        ],
        out_shape=[
            jax.ShapeDtypeStruct((len(messages), query_heads, tokens), jnp.float32),
            jax.ShapeDtypeStruct((8, tokens), jnp.int32),
        ],
        compiler_params=params(),
        name="partial_scores",
    )(partials, *arranged(messages, QUERY_ORDER))


def mix_kernel(heads, code_ref, values_ref, scores_ref, *refs):
    mixed_refs, (tops_ref, totals_ref) = refs[:-2], refs[-2:]
    count = scores_ref.shape[0]
    tokens = values_ref.shape[0]
    size = values_ref.shape[1] // heads
    requests = tops_ref.shape[0]
    group = scores_ref.shape[1] // heads
    span = count * requests
    here = lax.broadcasted_iota(jnp.int32, (span, tokens), 0) == code_ref[0:1, :]
    scores = jnp.sum(scores_ref[...], axis=0)
    mixed = []
    for k in range(heads):
        weights = []
        for g in range(group):
            row = k * group + g
            line = jnp.broadcast_to(scores[row : row + 1, :], (span, tokens))
            top = jnp.max(jnp.where(here, line, LOWEST), axis=1, keepdims=True)
            probs = jnp.where(here, jnp.exp(line - top), 0.0)
            total = jnp.sum(probs, axis=1, keepdims=True)
            weights.append(probs)
            column = slice(row * size, (row + 1) * size)
            tops_ref[:, column] = jnp.broadcast_to(top[:requests], (requests, size))
            totals_ref[:, column] = jnp.broadcast_to(total[:requests], (requests, size))
        weights = jnp.concatenate(weights, axis=0).astype(jnp.bfloat16)
        values = values_ref[:, k * size : (k + 1) * size]
        mixed.append(jnp.dot(weights, values, preferred_element_type=jnp.float32))
    half = heads // 2
    for k in range(half):
        for g in range(group):
            at = (k * group + g) * size
            for d in range(count):
                rows = slice(g * span + d * requests, g * span + (d + 1) * requests)
                pair = jnp.concatenate([mixed[k][rows], mixed[k + half][rows]], axis=0)
                mixed_refs[d][:, at : at + size] = pair.astype(jnp.bfloat16)


def mix(heads, width, requests, code, partials, scores):
    count = scores.shape[0]
    tokens = partials.shape[0]
    columns = scores.shape[1] * (width // heads)
    whole = lambda shape: pl.BlockSpec(shape, lambda i: (0, 0))
    return pl.pallas_call(
        functools.partial(mix_kernel, heads),
        grid=(1,),
        in_specs=[whole(code.shape), pl.BlockSpec((tokens, width), lambda i: (0, 1))]
        + [pl.BlockSpec(scores.shape, lambda i: (0, 0, 0))],
        out_specs=[whole((2 * requests, columns // 2))] * count + [whole((requests, columns))] * 2,
        out_shape=[jax.ShapeDtypeStruct((2 * requests, columns // 2), jnp.bfloat16)] * count
        + [jax.ShapeDtypeStruct((requests, columns), jnp.float32)] * 2,
        compiler_params=params(),
        name="mix",
    )(code, partials, scores)


def merge_kernel(count, cache_ref, stats_ref, factor_ref, *refs):
    mixed_refs, out_ref = refs[:count], refs[count]
    requests, columns = cache_ref.shape
    half = columns // 2
    new = sum(ref[...].astype(jnp.float32) for ref in mixed_refs)
    for side in range(2):
        at = slice(side * half, (side + 1) * half)
        own = cache_ref[:, at] + new[side * requests : (side + 1) * requests] * factor_ref[:, at]
        out_ref[:, at] = own.astype(out_ref.dtype)
    out_ref[:, columns:] = stats_ref[...]


def merge(cache_mixed, stats, factor, mixed):
    requests, columns = cache_mixed.shape
    return pl.pallas_call(
        functools.partial(merge_kernel, len(mixed)),
        out_shape=jax.ShapeDtypeStruct((requests, columns + stats.shape[1]), jnp.bfloat16),
        compiler_params=params(),
        name="merge",
    )(cache_mixed, stats, factor, *arranged(mixed, MIXED_ORDER))


def finish_kernel(own_ref, far_ref, out_ref):
    requests, columns = out_ref.shape
    first = lax.axis_index("tp") == 0
    own, far = own_ref[...].astype(jnp.float32), far_ref[...].astype(jnp.float32)
    low, high = jnp.where(first, own, far), jnp.where(first, far, own)
    size = 128
    count = columns // size

    def read(message, start):
        at = columns + start * size
        parts = [message[:, at + part * count : at + (part + 1) * count] for part in range(3)]
        return parts[0] + parts[1] + parts[2]

    low_top, high_top = read(low, 0), read(high, 0)
    both = jnp.maximum(low_top, high_top)
    low_factor, high_factor = jnp.exp(low_top - both), jnp.exp(high_top - both)
    inverse = 1.0 / (read(low, 1) * low_factor + read(high, 1) * high_factor)
    low_factor, high_factor = low_factor * inverse, high_factor * inverse
    for h in range(count):
        at = slice(h * size, (h + 1) * size)
        out = low[:, at] * low_factor[:, h : h + 1] + high[:, at] * high_factor[:, h : h + 1]
        out_ref[:, at] = out.astype(out_ref.dtype)


def finish(own, far, columns):
    return pl.pallas_call(
        finish_kernel,
        out_shape=jax.ShapeDtypeStruct((own.shape[0], columns), jnp.bfloat16),
        compiler_params=params(),
        name="finish",
    )(own, far)


def from_partner(x, axis, distance):
    count = lax.axis_size(axis)
    return lax.ppermute(x, axis, [(i, i ^ distance) for i in range(count)])


def exchange(blocks):
    return [blocks[0]] + [from_partner(blocks[d], "seq", d) for d in range(1, len(blocks))]


def on_device(tokens, kv_weight, owners, requests, signs, queries, kv_cache, lengths):
    seq_count = lax.axis_size("seq")
    blocks, size = signs.shape
    heads = blocks // 2
    width = heads * size
    query = queries[0, 0]
    request_count, columns = query.shape
    message = make_message(query, owners[:, :, 0], requests)
    messages = exchange([message] * seq_count)
    partials = project(tokens, kv_weight)
    scores, code = partial_scores(heads, width, columns, partials, messages)
    scores = lax.all_to_all(scores, "seq", split_axis=0, concat_axis=0, tiled=True)
    cache_mixed, tops, totals = cache_part(lengths, query, kv_cache[0, 0], signs)
    results = mix(heads, width, request_count, code, partials, scores)
    mixed, (new_tops, new_totals) = results[:seq_count], results[seq_count:]
    mixed = exchange(mixed)
    cache_mixed, factor, stats = combine_stats(tops, totals, new_tops, new_totals, cache_mixed)
    own = merge(cache_mixed, stats, factor, mixed)
    far = from_partner(own, "tp", 1)
    return finish(own, far, columns).reshape(1, 1, request_count, columns)


def hadamard(order):
    rows = lax.broadcasted_iota(jnp.int32, (order, order), 0)
    cols = lax.broadcasted_iota(jnp.int32, (order, order), 1)
    parity = jnp.zeros((order, order), jnp.int32)
    for bit_number in range(order.bit_length() - 1):
        parity = parity + rows // 2**bit_number % 2 * (cols // 2**bit_number % 2)
    return (1 - 2 * (parity % 2)).astype(jnp.float32)


def rotate(blocks, sign_rows, matrix):
    product = jnp.einsum(
        "...h,hk->...k", blocks * sign_rows, matrix, precision=lax.Precision.HIGHEST
    )
    return product / math.sqrt(matrix.shape[0])


def encode(rotated):
    largest = jnp.max(jnp.abs(rotated), axis=-1) + 1e-06
    scales = largest.astype(jnp.bfloat16)
    encoded = (rotated / scales.astype(jnp.float32)[..., None]).astype(jnp.bfloat16)
    return (encoded, scales)


def decode(encoded, scales):
    return (encoded.astype(jnp.float32) * scales.astype(jnp.float32)[..., None]).astype(
        jnp.bfloat16
    )


def slot_numbers(targets, count, room):
    onehot = (targets[:, None] == lax.iota(jnp.int32, count)[None, :]).astype(jnp.int32)
    within = jnp.sum((jnp.cumsum(onehot, axis=0) - 1) * onehot, axis=1)
    return targets * room + within


def on_device_long(tokens, kv_weight, owners, requests, signs, queries, kv_cache, lengths):
    seq_count = lax.axis_size("seq")
    per_device = owners.shape[1]
    slots = max(2, (2 * per_device + seq_count - 1) // seq_count)
    head_blocks = signs.shape[0]
    kv_heads = head_blocks // 2
    head_size = signs.shape[1]
    matrix = hadamard(head_size)
    sign_rows = (2 * signs - 1).astype(jnp.float32)
    summed = lax.psum_scatter(
        jnp.dot(tokens, kv_weight, preferred_element_type=jnp.float32).astype(jnp.bfloat16),
        "seq",
        scatter_dimension=0,
        tiled=True,
    ).astype(jnp.float32)
    encoded, scales = encode(
        rotate(summed.reshape(per_device, head_blocks, head_size), sign_rows, matrix)
    )
    slot_index = slot_numbers(owners[0, :, 0], seq_count, slots)
    slot_total = seq_count * slots
    send_values = (
        jnp.zeros((slot_total, head_blocks, head_size), jnp.bfloat16).at[slot_index].set(encoded)
    )
    send_scales = jnp.zeros((slot_total, head_blocks), jnp.bfloat16).at[slot_index].set(scales)
    send_codes = jnp.zeros((slot_total,), jnp.int32).at[slot_index].set(requests[0] + 1)
    got_values, got_scales, arrived_codes = (
        lax.all_to_all(send_values, "seq", split_axis=0, concat_axis=0, tiled=True),
        lax.all_to_all(send_scales, "seq", split_axis=0, concat_axis=0, tiled=True),
        lax.all_to_all(send_codes, "seq", split_axis=0, concat_axis=0, tiled=True),
    )
    arrived = decode(got_values, got_scales)
    query = queries[0, 0]
    request_count = query.shape[0]
    group = query.shape[1] // (kv_heads * head_size)
    query_blocks = query.astype(jnp.float32).reshape(request_count, kv_heads, group, head_size)
    query_rot = rotate(query_blocks, sign_rows[:kv_heads][:, None, :], matrix).astype(jnp.bfloat16)
    local_cache = kv_cache[0, 0]
    cache_span = local_cache.shape[1]
    local_cache = local_cache.reshape(request_count, cache_span, head_blocks, head_size)
    score_scale = 1.0 / math.sqrt(head_size)
    lowest = -1e30
    highest = lax.Precision.HIGHEST
    score_cache = (
        jnp.einsum(
            "rkgd,rckd->rkgc",
            query_rot,
            local_cache[:, :, :kv_heads],
            preferred_element_type=jnp.float32,
        )
        * score_scale
    )
    score_new = (
        jnp.einsum(
            "rkgd,nkd->rkgn", query_rot, arrived[:, :kv_heads], preferred_element_type=jnp.float32
        )
        * score_scale
    )
    positions = lax.axis_index("tp") * cache_span + lax.iota(jnp.int32, cache_span)
    mask_cache = (positions[None, :] < lengths[0, 0][:, None])[:, None, None, :]
    match = arrived_codes[None, :] == (lax.iota(jnp.int32, request_count) + 1)[:, None]
    mask_new = match[:, None, None, :]
    top = jnp.maximum(
        jnp.max(jnp.where(mask_cache, score_cache, lowest), axis=-1),
        jnp.max(jnp.where(mask_new, score_new, lowest), axis=-1),
    )
    probs_cache = jnp.where(mask_cache, jnp.exp(score_cache - top[..., None]), 0.0)
    probs_new = jnp.where(mask_new, jnp.exp(score_new - top[..., None]), 0.0)
    total = jnp.sum(probs_cache, axis=-1) + jnp.sum(probs_new, axis=-1)
    mixed = jnp.einsum(
        "rkgc,rckd->rkgd",
        probs_cache,
        local_cache[:, :, kv_heads:].astype(jnp.float32),
        precision=highest,
    )
    mixed = mixed + jnp.einsum(
        "rkgn,nkd->rkgd", probs_new, arrived[:, kv_heads:].astype(jnp.float32), precision=highest
    )
    shared_top = lax.pmax(top, "tp")
    factor = jnp.exp(top - shared_top)
    total, mixed = (
        lax.psum((total * factor).astype(jnp.bfloat16), "tp").astype(jnp.float32),
        lax.psum((mixed * factor[..., None]).astype(jnp.bfloat16), "tp").astype(jnp.float32),
    )
    mixed = mixed / total[..., None]
    output = rotate(mixed, 1.0, matrix) * sign_rows[kv_heads:][None, :, None, :]
    return output.reshape(1, 1, request_count, group * kv_heads * head_size).astype(jnp.bfloat16)


def solution(mesh):
    placed = (
        P(("groups", "tp", "section"), "seq"),
        P("seq", None),
        P(("groups", "tp", "section"), "seq", None),
        P(("groups", "tp", "section"), "seq"),
        P(),
        P(("groups", "seq"), "section", None, None),
        P(("groups", "seq"), "section", None, "tp", None),
        P(("groups", "seq"), "section", None),
    )
    short = mesh.shape["seq"] == 4 and mesh.shape["tp"] == 2
    return jax.shard_map(
        on_device if short else on_device_long,
        mesh=mesh,
        in_specs=placed,
        out_specs=P(("groups", "seq"), "section", None, None),
        check_vma=False,
    )
```

```python
import functools
import math

import jax
import jax.numpy as jnp
from jax import lax
from jax.experimental import pallas as pl
from jax.experimental.pallas import tpu as pltpu
from jax.sharding import PartitionSpec as P

LOWEST = -1e30
MIB = 1024 * 1024
NT = (((1,), (1,)), ((), ()))


def params(mib=32):
    return pltpu.CompilerParams(vmem_limit_bytes=mib * MIB)


def in_hbm(x):
    return pltpu.with_memory_space_constraint(x, pltpu.HBM)


def in_vmem(x):
    return pltpu.with_memory_space_constraint(x, pltpu.VMEM)


def hadamard_tile(order):
    rows = lax.broadcasted_iota(jnp.int32, (order, order), 0)
    cols = lax.broadcasted_iota(jnp.int32, (order, order), 1)
    common = rows & cols
    parity = jnp.zeros((order, order), jnp.int32)
    for bit_number in range(order.bit_length() - 1):
        parity = parity ^ (common >> bit_number)
    return (1 - 2 * (parity & 1)).astype(jnp.float32).astype(jnp.bfloat16)


QUERY_ORDER = (3, 2, 1)
SCORE_ORDER = (2, 3, 1)
MIXED_ORDER = (3, 2, 1)


def arranged(blocks, order):
    return [blocks[0]] + [blocks[d] for d in order]


def by_distance(refs, order):
    return [refs[0]] + [refs[1 + order.index(d)] for d in range(1, len(refs))]


def project_kernel(tokens_ref, weight_ref, out_ref):
    out_ref[...] = jnp.dot(tokens_ref[...], weight_ref[...], preferred_element_type=jnp.float32).astype(out_ref.dtype)


def project(tokens, weight):
    rows, features = tokens.shape
    width = weight.shape[1]
    return pl.pallas_call(
        project_kernel,
        in_specs=[pl.BlockSpec(memory_space=pltpu.VMEM)] * 2,
        out_specs=pl.BlockSpec(memory_space=pltpu.VMEM),
        out_shape=jax.ShapeDtypeStruct((rows, width), jnp.bfloat16),
        compiler_params=params(32),
        cost_estimate=pl.CostEstimate(
            flops=2 * rows * features * width,
            bytes_accessed=2 * (rows * features + features * width),
            transcendentals=0,
        ),
        name="project",
    )(in_vmem(tokens), in_vmem(weight))


def message_kernel(query_ref, owners_ref, requests_ref, out_ref, query_buf, owners_buf, requests_buf, sems):
    requests, columns = query_ref.shape
    per_device = owners_ref.shape[1]
    copies = [
        pltpu.make_async_copy(source, target, sems.at[i])
        for i, (source, target) in enumerate(
            ((query_ref, query_buf), (owners_ref, owners_buf), (requests_ref, requests_buf))
        )
    ]
    for copy in copies:
        copy.start()
    for copy in copies:
        copy.wait()
    out_ref[:, :columns] = query_buf[...]
    code = (owners_buf[...] * requests + requests_buf[...]).astype(jnp.float32)
    spare = jnp.zeros((1, out_ref.shape[1] - columns - per_device), jnp.float32)
    code = jnp.concatenate([code, spare], axis=1)
    out_ref[:, columns:] = jnp.broadcast_to(code, (requests, code.shape[1])).astype(out_ref.dtype)


def make_message(query, owners, requests):
    count, columns = query.shape
    lanes = -(-owners.shape[1] // 128) * 128
    return pl.pallas_call(
        message_kernel,
        in_specs=[pl.BlockSpec(memory_space=pl.ANY)] * 3,
        out_specs=pl.BlockSpec(memory_space=pltpu.VMEM),
        out_shape=jax.ShapeDtypeStruct((count, columns + lanes), query.dtype),
        scratch_shapes=[
            pltpu.VMEM(query.shape, query.dtype),
            pltpu.VMEM(owners.shape, owners.dtype),
            pltpu.VMEM(requests.shape, requests.dtype),
            pltpu.SemaphoreType.DMA((3,)),
        ],
        compiler_params=params(16),
        cost_estimate=pl.CostEstimate(flops=10**11, bytes_accessed=10**4, transcendentals=0),
        name="make_message",
    )(in_hbm(query), in_hbm(owners), in_hbm(requests))


def cache_kernel(
    lengths_ref, query_ref, cache_ref, signs_ref, mixed_ref, tops_ref, totals_ref, query_buf, top_buf, total_buf, mixed_buf
):
    requests, span, _ = cache_ref.shape
    blocks, size = signs_ref.shape
    heads = blocks // 2
    width = heads * size
    count = query_ref.shape[1] // size
    group = count // heads
    norm = 1.0 / math.sqrt(size)
    matrix = hadamard_tile(size)
    signs = (2 * signs_ref[...] - 1).astype(jnp.float32)
    query = query_ref[...].astype(jnp.float32)
    query = jnp.concatenate(
        [query[:, h * size : (h + 1) * size] * signs[h // group : h // group + 1] for h in range(count)], axis=0
    )
    query_buf[...] = jnp.dot(query.astype(jnp.bfloat16), matrix, preferred_element_type=jnp.float32) * norm
    rows = 2 * count
    kv_head = lax.broadcasted_iota(jnp.int32, (rows, width), 0) // group & (heads - 1)
    own_head = kv_head == lax.broadcasted_iota(jnp.int32, (rows, width), 1) // size
    first = lax.broadcasted_iota(jnp.int32, (rows, span), 0) < count
    position = lax.axis_index("tp") * span + lax.broadcasted_iota(jnp.int32, (rows, span), 1)
    pairs = range(0, requests, 2)
    scores = []
    for r in pairs:
        both = [query_buf[pl.ds(r + i, count, stride=requests), :] for i in range(2)]
        wide = jnp.concatenate([jnp.concatenate(both, axis=0)] * heads, axis=1)
        wide = jnp.where(own_head, wide, 0.0).astype(jnp.bfloat16)
        keys = cache_ref[r : r + 2, :, :width].reshape(2 * span, width)
        scores.append(lax.dot_general(wide, keys, NT, preferred_element_type=jnp.float32))
    probs = []
    for r, score in zip(pairs, scores):
        score = jnp.where(first, score[:, :span], score[:, span:]) * norm
        live = position < jnp.where(first, lengths_ref[0, 0, r], lengths_ref[0, 0, r + 1])
        top = jnp.max(jnp.where(live, score, LOWEST), axis=1, keepdims=True)
        prob = jnp.where(live, jnp.exp(score - top), 0.0)
        total = jnp.sum(prob, axis=1, keepdims=True)
        at = slice(r * count, (r + 2) * count)
        top_buf[at, :] = jnp.broadcast_to(top, (rows, size))
        total_buf[at, :] = jnp.broadcast_to(total, (rows, size))
        probs.append(
            jnp.concatenate([jnp.where(first, prob, 0.0), jnp.where(first, 0.0, prob)], axis=1).astype(jnp.bfloat16)
        )
    mixed = []
    for r, prob in zip(pairs, probs):
        values = cache_ref[r : r + 2, :, width:].reshape(2 * span, width)
        wide = jnp.dot(prob, values, preferred_element_type=jnp.float32)
        wide = jnp.where(own_head, wide, 0.0)
        mixed.append(sum(wide[:, k * size : (k + 1) * size] for k in range(heads)))
    mixed = jnp.concatenate(mixed, axis=0)
    high = mixed.astype(jnp.bfloat16)
    low = (mixed - high.astype(jnp.float32)).astype(jnp.bfloat16)
    plain = jnp.dot(high, matrix, preferred_element_type=jnp.float32)
    mixed_buf[...] = plain + jnp.dot(low, matrix, preferred_element_type=jnp.float32)
    for h in range(count):
        pick = pl.ds(h, requests, stride=count)
        column = slice(h * size, (h + 1) * size)
        k = heads + h // group
        mixed_ref[:, column] = mixed_buf[pick, :] * (signs[k : k + 1] * norm)
        tops_ref[:, column] = top_buf[pick, :]
        totals_ref[:, column] = total_buf[pick, :]


def cache_part(lengths, query, cache, signs):
    requests, span, width = cache.shape
    size = signs.shape[1]
    columns = query.shape[1]
    vmem = pl.BlockSpec(memory_space=pltpu.VMEM)
    return pl.pallas_call(
        cache_kernel,
        in_specs=[pl.BlockSpec(memory_space=pltpu.SMEM)] + [vmem] * 3,
        out_shape=[jax.ShapeDtypeStruct(query.shape, jnp.float32)] * 3,
        scratch_shapes=[pltpu.VMEM((requests * columns // size, size), jnp.float32)] * 4,
        compiler_params=params(),
        cost_estimate=pl.CostEstimate(
            flops=4 * span * requests * columns,
            bytes_accessed=2 * requests * span * width,
            transcendentals=span * requests * columns // size,
        ),
        name="cache_part",
    )(lengths, query, cache, signs)


def stats_kernel(top_ref, total_ref, new_top_ref, new_total_ref, cache_ref, cache_out_ref, factor_ref, stats_ref):
    requests, columns = top_ref.shape
    size = 128
    count = columns // size
    top, new_top = top_ref[...], new_top_ref[...]
    both = jnp.maximum(top, new_top)
    cache_factor = jnp.exp(top - both)
    new_factor = jnp.exp(new_top - both)
    cache_out_ref[...] = cache_ref[...] * cache_factor
    factor_ref[...] = new_factor
    total = total_ref[...] * cache_factor + new_total_ref[...] * new_factor
    lane = lax.broadcasted_iota(jnp.int32, (requests, size), 1)
    packed = []
    for value in (both, total):
        narrow = jnp.zeros((requests, size), jnp.float32)
        for h in range(count):
            narrow = jnp.where(lane % count == h, value[:, h * size : (h + 1) * size], narrow)
        high = narrow.astype(jnp.bfloat16).astype(jnp.float32)
        middle = (narrow - high).astype(jnp.bfloat16).astype(jnp.float32)
        low = narrow - high - middle
        packed.append(jnp.where(lane < count, high, jnp.where(lane < 2 * count, middle, low)))
    stats_ref[...] = jnp.concatenate(packed, axis=1).astype(jnp.bfloat16)


def combine_stats(tops, totals, new_tops, new_totals, cache_mixed):
    shape = tops.shape
    return pl.pallas_call(
        stats_kernel,
        out_shape=[
            jax.ShapeDtypeStruct(shape, jnp.float32),
            jax.ShapeDtypeStruct(shape, jnp.float32),
            jax.ShapeDtypeStruct((shape[0], 256), jnp.bfloat16),
        ],
        compiler_params=params(),
        name="combine_stats",
    )(tops, totals, new_tops, new_totals, cache_mixed)


def code_row(message_refs, start, requests, tokens):
    count = len(message_refs)
    me = lax.axis_index("seq")
    pieces = [ref[0:1, start : start + tokens // count].astype(jnp.float32) for ref in message_refs]
    row = [sum(jnp.where(me ^ d == at, pieces[d], 0.0) for d in range(count)) for at in range(count)]
    code = jnp.concatenate(row, axis=1).astype(jnp.int32)
    return ((code // requests) ^ me) * requests + code % requests


def score_kernel(heads, start, partial_ref, *refs):
    message_refs, (scores_ref, code_ref) = by_distance(refs[:-2], QUERY_ORDER), refs[-2:]
    requests = message_refs[0].shape[0]
    size = partial_ref.shape[1] // heads
    tokens = partial_ref.shape[0]
    group = start // (heads * size)
    code = code_row(message_refs, start, requests, tokens)
    code_ref[...] = jnp.broadcast_to(code, code_ref.shape)
    span = len(message_refs) * requests
    here = lax.broadcasted_iota(jnp.int32, (span, tokens), 0) == code
    queries = [ref[:, :start].astype(jnp.float32) for ref in message_refs]
    for k in range(heads):
        rows = []
        for g in range(group):
            at = (k * group + g) * size
            rows += [query[:, at : at + size] for query in queries]
        query = jnp.concatenate(rows, axis=0).astype(jnp.bfloat16)
        keys = partial_ref[:, k * size : (k + 1) * size]
        scores = lax.dot_general(query, keys, NT, preferred_element_type=jnp.float32)
        lines = [
            jnp.sum(jnp.where(here, scores[g * span : (g + 1) * span], 0.0), axis=0, keepdims=True)
            for g in range(group)
        ]
        scores_ref[k * group : (k + 1) * group, :] = jnp.concatenate(lines, axis=0) * (
            1.0 / math.sqrt(size)
        )


def partial_scores(heads, width, columns, partials, messages):
    tokens = partials.shape[0]
    size = width // heads
    query_heads = columns // size
    return pl.pallas_call(
        functools.partial(score_kernel, heads, columns),
        grid=(1,),
        in_specs=[pl.BlockSpec((tokens, width), lambda i: (0, 0))]
        + [pl.BlockSpec(m.shape, lambda i: (0, 0)) for m in messages],
        out_specs=[
            pl.BlockSpec((query_heads, tokens), lambda i: (0, 0)),
            pl.BlockSpec((8, tokens), lambda i: (0, 0)),
        ],
        out_shape=[
            jax.ShapeDtypeStruct((query_heads, tokens), jnp.float32),
            jax.ShapeDtypeStruct((8, tokens), jnp.int32),
        ],
        compiler_params=params(),
        name="partial_scores",
    )(partials, *arranged(messages, QUERY_ORDER))


def mix_kernel(heads, count, code_ref, values_ref, *refs):
    score_refs = by_distance(refs[:count], SCORE_ORDER)
    mixed_refs = refs[count : 2 * count]
    tops_ref, totals_ref = refs[2 * count :]
    tokens = values_ref.shape[0]
    size = values_ref.shape[1] // heads
    requests = tops_ref.shape[0]
    group = score_refs[0].shape[0] // heads
    span = count * requests
    here = lax.broadcasted_iota(jnp.int32, (span, tokens), 0) == code_ref[0:1, :]
    parts = [ref[...] for ref in score_refs]
    while len(parts) > 1:
        parts = [parts[i] + parts[i + 1] for i in range(0, len(parts), 2)]
    scores = parts[0]
    mixed = []
    for k in range(heads):
        weights = []
        for g in range(group):
            row = k * group + g
            line = jnp.broadcast_to(scores[row : row + 1, :], (span, tokens))
            top = jnp.max(jnp.where(here, line, LOWEST), axis=1, keepdims=True)
            probs = jnp.where(here, jnp.exp(line - top), 0.0)
            total = jnp.sum(probs, axis=1, keepdims=True)
            weights.append(probs)
            column = slice(row * size, (row + 1) * size)
            tops_ref[:, column] = jnp.broadcast_to(top[:requests], (requests, size))
            totals_ref[:, column] = jnp.broadcast_to(total[:requests], (requests, size))
        weights = jnp.concatenate(weights, axis=0).astype(jnp.bfloat16)
        values = values_ref[:, k * size : (k + 1) * size]
        mixed.append(jnp.dot(weights, values, preferred_element_type=jnp.float32))
    half = heads // 2
    for k in range(half):
        for g in range(group):
            at = (k * group + g) * size
            for d in range(count):
                rows = slice(g * span + d * requests, g * span + (d + 1) * requests)
                pair = jnp.concatenate([mixed[k][rows], mixed[k + half][rows]], axis=0)
                mixed_refs[d][:, at : at + size] = pair.astype(jnp.bfloat16)


def mix(heads, width, requests, code, partials, scores):
    count = len(scores)
    tokens = partials.shape[0]
    columns = scores[0].shape[0] * (width // heads)
    whole = lambda shape: pl.BlockSpec(shape, lambda i: (0, 0))
    return pl.pallas_call(
        functools.partial(mix_kernel, heads, count),
        grid=(1,),
        in_specs=[whole(code.shape), pl.BlockSpec((tokens, width), lambda i: (0, 1))]
        + [whole(s.shape) for s in scores],
        out_specs=[whole((2 * requests, columns // 2))] * count + [whole((requests, columns))] * 2,
        out_shape=[jax.ShapeDtypeStruct((2 * requests, columns // 2), jnp.bfloat16)] * count
        + [jax.ShapeDtypeStruct((requests, columns), jnp.float32)] * 2,
        compiler_params=params(),
        name="mix",
    )(code, partials, *arranged(scores, SCORE_ORDER))


def merge_kernel(count, cache_ref, stats_ref, factor_ref, *refs):
    mixed_refs, out_ref = refs[:count], refs[count]
    requests, columns = cache_ref.shape
    half = columns // 2
    new = sum(ref[...].astype(jnp.float32) for ref in mixed_refs)
    for side in range(2):
        at = slice(side * half, (side + 1) * half)
        own = cache_ref[:, at] + new[side * requests : (side + 1) * requests] * factor_ref[:, at]
        out_ref[:, at] = own.astype(out_ref.dtype)
    out_ref[:, columns:] = stats_ref[...]


def merge(cache_mixed, stats, factor, mixed):
    requests, columns = cache_mixed.shape
    return pl.pallas_call(
        functools.partial(merge_kernel, len(mixed)),
        out_shape=jax.ShapeDtypeStruct((requests, columns + stats.shape[1]), jnp.bfloat16),
        compiler_params=params(),
        name="merge",
    )(cache_mixed, stats, factor, *arranged(mixed, MIXED_ORDER))


def finish_kernel(own_ref, far_ref, out_ref):
    requests, columns = out_ref.shape
    first = lax.axis_index("tp") == 0
    own, far = own_ref[...].astype(jnp.float32), far_ref[...].astype(jnp.float32)
    low, high = jnp.where(first, own, far), jnp.where(first, far, own)
    size = 128
    count = columns // size

    def read(message, start):
        at = columns + start * size
        parts = [message[:, at + part * count : at + (part + 1) * count] for part in range(3)]
        return parts[0] + parts[1] + parts[2]

    low_top, high_top = read(low, 0), read(high, 0)
    both = jnp.maximum(low_top, high_top)
    low_factor, high_factor = jnp.exp(low_top - both), jnp.exp(high_top - both)
    inverse = 1.0 / (read(low, 1) * low_factor + read(high, 1) * high_factor)
    low_factor, high_factor = low_factor * inverse, high_factor * inverse
    for h in range(count):
        at = slice(h * size, (h + 1) * size)
        out = low[:, at] * low_factor[:, h : h + 1] + high[:, at] * high_factor[:, h : h + 1]
        out_ref[:, at] = out.astype(out_ref.dtype)


def finish(own, far, columns):
    return pl.pallas_call(
        finish_kernel,
        out_shape=jax.ShapeDtypeStruct((own.shape[0], columns), jnp.bfloat16),
        compiler_params=params(),
        name="finish",
    )(own, far)


def from_partner(x, axis, distance):
    count = lax.axis_size(axis)
    return lax.ppermute(x, axis, [(i, i ^ distance) for i in range(count)])


def exchange(blocks):
    return [blocks[0]] + [from_partner(blocks[d], "seq", d) for d in range(1, len(blocks))]


def on_device(tokens, kv_weight, owners, requests, signs, queries, kv_cache, lengths):
    seq_count = lax.axis_size("seq")
    blocks, size = signs.shape
    heads = blocks // 2
    width = heads * size
    query = queries[0, 0]
    request_count, columns = query.shape
    message = make_message(query, owners[:, :, 0], requests)
    messages = exchange([message] * seq_count)
    partials = project(tokens, kv_weight)
    scores, code = partial_scores(heads, width, columns, partials, messages)
    scores = exchange([scores] * seq_count)
    cache_mixed, tops, totals = cache_part(lengths, query, kv_cache[0, 0], signs)
    results = mix(heads, width, request_count, code, partials, scores)
    mixed, (new_tops, new_totals) = results[:seq_count], results[seq_count:]
    mixed = exchange(mixed)
    cache_mixed, factor, stats = combine_stats(tops, totals, new_tops, new_totals, cache_mixed)
    own = merge(cache_mixed, stats, factor, mixed)
    far = from_partner(own, "tp", 1)
    return finish(own, far, columns).reshape(1, 1, request_count, columns)


def hadamard(order):
    rows = lax.broadcasted_iota(jnp.int32, (order, order), 0)
    cols = lax.broadcasted_iota(jnp.int32, (order, order), 1)
    parity = jnp.zeros((order, order), jnp.int32)
    for bit_number in range(order.bit_length() - 1):
        parity = parity + rows // 2**bit_number % 2 * (cols // 2**bit_number % 2)
    return (1 - 2 * (parity % 2)).astype(jnp.float32)


def rotate(blocks, sign_rows, matrix):
    product = jnp.einsum(
        "...h,hk->...k", blocks * sign_rows, matrix, precision=lax.Precision.HIGHEST
    )
    return product / math.sqrt(matrix.shape[0])


def encode(rotated):
    largest = jnp.max(jnp.abs(rotated), axis=-1) + 1e-06
    scales = largest.astype(jnp.bfloat16)
    encoded = (rotated / scales.astype(jnp.float32)[..., None]).astype(jnp.bfloat16)
    return (encoded, scales)


def decode(encoded, scales):
    return (encoded.astype(jnp.float32) * scales.astype(jnp.float32)[..., None]).astype(
        jnp.bfloat16
    )


def slot_numbers(targets, count, room):
    onehot = (targets[:, None] == lax.iota(jnp.int32, count)[None, :]).astype(jnp.int32)
    within = jnp.sum((jnp.cumsum(onehot, axis=0) - 1) * onehot, axis=1)
    return targets * room + within


def on_device_long(tokens, kv_weight, owners, requests, signs, queries, kv_cache, lengths):
    seq_count = lax.axis_size("seq")
    per_device = owners.shape[1]
    slots = max(2, (2 * per_device + seq_count - 1) // seq_count)
    head_blocks = signs.shape[0]
    kv_heads = head_blocks // 2
    head_size = signs.shape[1]
    matrix = hadamard(head_size)
    sign_rows = (2 * signs - 1).astype(jnp.float32)
    summed = lax.psum_scatter(
        jnp.dot(tokens, kv_weight, preferred_element_type=jnp.float32).astype(jnp.bfloat16),
        "seq",
        scatter_dimension=0,
        tiled=True,
    ).astype(jnp.float32)
    encoded, scales = encode(
        rotate(summed.reshape(per_device, head_blocks, head_size), sign_rows, matrix)
    )
    slot_index = slot_numbers(owners[0, :, 0], seq_count, slots)
    slot_total = seq_count * slots
    send_values = (
        jnp.zeros((slot_total, head_blocks, head_size), jnp.bfloat16).at[slot_index].set(encoded)
    )
    send_scales = jnp.zeros((slot_total, head_blocks), jnp.bfloat16).at[slot_index].set(scales)
    send_codes = jnp.zeros((slot_total,), jnp.int32).at[slot_index].set(requests[0] + 1)
    got_values, got_scales, arrived_codes = (
        lax.all_to_all(send_values, "seq", split_axis=0, concat_axis=0, tiled=True),
        lax.all_to_all(send_scales, "seq", split_axis=0, concat_axis=0, tiled=True),
        lax.all_to_all(send_codes, "seq", split_axis=0, concat_axis=0, tiled=True),
    )
    arrived = decode(got_values, got_scales)
    query = queries[0, 0]
    request_count = query.shape[0]
    group = query.shape[1] // (kv_heads * head_size)
    query_blocks = query.astype(jnp.float32).reshape(request_count, kv_heads, group, head_size)
    query_rot = rotate(query_blocks, sign_rows[:kv_heads][:, None, :], matrix).astype(jnp.bfloat16)
    local_cache = kv_cache[0, 0]
    cache_span = local_cache.shape[1]
    local_cache = local_cache.reshape(request_count, cache_span, head_blocks, head_size)
    score_scale = 1.0 / math.sqrt(head_size)
    lowest = -1e30
    highest = lax.Precision.HIGHEST
    score_cache = (
        jnp.einsum(
            "rkgd,rckd->rkgc",
            query_rot,
            local_cache[:, :, :kv_heads],
            preferred_element_type=jnp.float32,
        )
        * score_scale
    )
    score_new = (
        jnp.einsum(
            "rkgd,nkd->rkgn", query_rot, arrived[:, :kv_heads], preferred_element_type=jnp.float32
        )
        * score_scale
    )
    positions = lax.axis_index("tp") * cache_span + lax.iota(jnp.int32, cache_span)
    mask_cache = (positions[None, :] < lengths[0, 0][:, None])[:, None, None, :]
    match = arrived_codes[None, :] == (lax.iota(jnp.int32, request_count) + 1)[:, None]
    mask_new = match[:, None, None, :]
    top = jnp.maximum(
        jnp.max(jnp.where(mask_cache, score_cache, lowest), axis=-1),
        jnp.max(jnp.where(mask_new, score_new, lowest), axis=-1),
    )
    probs_cache = jnp.where(mask_cache, jnp.exp(score_cache - top[..., None]), 0.0)
    probs_new = jnp.where(mask_new, jnp.exp(score_new - top[..., None]), 0.0)
    total = jnp.sum(probs_cache, axis=-1) + jnp.sum(probs_new, axis=-1)
    mixed = jnp.einsum(
        "rkgc,rckd->rkgd",
        probs_cache,
        local_cache[:, :, kv_heads:].astype(jnp.float32),
        precision=highest,
    )
    mixed = mixed + jnp.einsum(
        "rkgn,nkd->rkgd", probs_new, arrived[:, kv_heads:].astype(jnp.float32), precision=highest
    )
    shared_top = lax.pmax(top, "tp")
    factor = jnp.exp(top - shared_top)
    total, mixed = (
        lax.psum((total * factor).astype(jnp.bfloat16), "tp").astype(jnp.float32),
        lax.psum((mixed * factor[..., None]).astype(jnp.bfloat16), "tp").astype(jnp.float32),
    )
    mixed = mixed / total[..., None]
    output = rotate(mixed, 1.0, matrix) * sign_rows[kv_heads:][None, :, None, :]
    return output.reshape(1, 1, request_count, group * kv_heads * head_size).astype(jnp.bfloat16)


def solution(mesh):
    placed = (
        P(("groups", "tp", "section"), "seq"),
        P("seq", None),
        P(("groups", "tp", "section"), "seq", None),
        P(("groups", "tp", "section"), "seq"),
        P(),
        P(("groups", "seq"), "section", None, None),
        P(("groups", "seq"), "section", None, "tp", None),
        P(("groups", "seq"), "section", None),
    )
    short = mesh.shape["seq"] == 4 and mesh.shape["tp"] == 2
    return jax.shard_map(
        on_device if short else on_device_long,
        mesh=mesh,
        in_specs=placed,
        out_specs=P(("groups", "seq"), "section", None, None),
        check_vma=False,
    )
```

```python
import functools
import math

import jax
import jax.numpy as jnp
from jax import lax
from jax.experimental import pallas as pl
from jax.experimental.pallas import tpu as pltpu
from jax.sharding import PartitionSpec as P

LOWEST = -1e30
MIB = 1024 * 1024
NT = (((1,), (1,)), ((), ()))


def params(mib=32):
    return pltpu.CompilerParams(vmem_limit_bytes=mib * MIB)


def in_hbm(x):
    return pltpu.with_memory_space_constraint(x, pltpu.HBM)


def hadamard_tile(order):
    rows = lax.broadcasted_iota(jnp.int32, (order, order), 0)
    cols = lax.broadcasted_iota(jnp.int32, (order, order), 1)
    common = rows & cols
    parity = jnp.zeros((order, order), jnp.int32)
    for bit_number in range(order.bit_length() - 1):
        parity = parity ^ (common >> bit_number)
    return (1 - 2 * (parity & 1)).astype(jnp.float32).astype(jnp.bfloat16)


QUERY_ORDER = (1, 3, 2)
MIXED_ORDER = (3, 2, 1)


def arranged(blocks, order):
    return [blocks[0]] + [blocks[d] for d in order]


def by_distance(refs, order):
    return [refs[0]] + [refs[1 + order.index(d)] for d in range(1, len(refs))]


def side():
    return lax.axis_index("seq") & 1


def start_all(copies):
    for copy in copies:
        copy.start()
    return copies


def accumulate(tokens_ref, weight_buf, acc_ref, copies):
    steps, block, _ = weight_buf.shape
    for step in range(steps):
        for copy in copies[step]:
            copy.wait()
        tokens = tokens_ref[:, step * block : (step + 1) * block]
        part = jnp.dot(tokens, weight_buf[step], preferred_element_type=jnp.float32)
        acc_ref[...] = part if step == 0 else acc_ref[...] + part


def halves(acc_ref):
    width = acc_ref.shape[1] // 2
    mine = pl.multiple_of(side() * width, width)
    other = pl.multiple_of((1 - side()) * width, width)
    return acc_ref[:, pl.ds(mine, width)], acc_ref[:, pl.ds(other, width)]


def keys_kernel(
    query_ref, owners_ref, requests_ref, tokens_ref, weight_ref,
    tokens_out, own_ref, near_ref, same_ref, other_ref,
    query_buf, owners_buf, requests_buf, weight_buf, acc_ref, small_sems, sems,
):
    requests, columns = query_ref.shape
    per_device = owners_ref.shape[1]
    rows = tokens_ref.shape[0]
    steps, block, width = weight_buf.shape
    half = columns // 2
    small = start_all(
        [
            pltpu.make_async_copy(query_ref, query_buf, small_sems.at[0]),
            pltpu.make_async_copy(owners_ref, owners_buf, small_sems.at[1]),
            pltpu.make_async_copy(requests_ref, requests_buf, small_sems.at[2]),
        ]
    )
    copies = []
    for step in range(steps):
        span = slice(step * block, (step + 1) * block)
        copies.append(
            start_all(
                [
                    pltpu.make_async_copy(tokens_ref.at[:, span], tokens_out.at[:, span], sems.at[0, step]),
                    pltpu.make_async_copy(weight_ref.at[span, :width], weight_buf.at[step], sems.at[1, step]),
                ]
            )
        )
    for copy in small:
        copy.wait()
    code = (owners_buf[...] * requests + requests_buf[...]).astype(jnp.float32)
    near_width = near_ref.shape[1]
    spare = jnp.zeros((1, near_width - per_device), jnp.float32)
    code = jnp.broadcast_to(jnp.concatenate([code, spare], axis=1), (2 * requests, near_width))
    lanes = same_ref.shape[1] - half
    mine = pl.multiple_of(side() * half, half)
    other = pl.multiple_of((1 - side()) * half, half)
    same_ref[:, :half] = query_buf[:, pl.ds(mine, half)]
    same_ref[:, half:] = code[:requests, :lanes].astype(same_ref.dtype)
    far_query = query_buf[:, pl.ds(other, half)]
    other_ref[:, :half] = far_query
    other_ref[:, half:] = code[:requests, :lanes].astype(same_ref.dtype)
    stacked = far_query.astype(jnp.float32)
    stacked = jnp.concatenate([stacked[:, at : at + near_width] for at in range(0, half, near_width)], axis=0)
    near_ref[rows : rows + stacked.shape[0], :] = stacked.astype(near_ref.dtype)
    near_ref[rows + stacked.shape[0] :, :] = code.astype(near_ref.dtype)
    accumulate(tokens_out, weight_buf, acc_ref, copies)
    kept, sent = halves(acc_ref)
    own_ref[...] = kept.astype(own_ref.dtype)
    near_ref[:rows, :] = sent.astype(near_ref.dtype)


def project_keys(query, owners, requests, tokens, weight):
    count, columns = query.shape
    rows, features = tokens.shape
    width = weight.shape[1] // 2
    block = min(512, features // 2)
    steps = features // block
    half = columns // 2
    lanes = -(-owners.shape[1] // 128) * 128
    near_rows = rows + count * half // (width // 2) + 2 * count
    vmem = pl.BlockSpec(memory_space=pltpu.VMEM)
    return pl.pallas_call(
        keys_kernel,
        in_specs=[pl.BlockSpec(memory_space=pl.ANY)] * 5,
        out_specs=[vmem] * 5,
        out_shape=[
            jax.ShapeDtypeStruct(tokens.shape, tokens.dtype),
            jax.ShapeDtypeStruct((rows, width // 2), jnp.bfloat16),
            jax.ShapeDtypeStruct((near_rows, width // 2), jnp.bfloat16),
            jax.ShapeDtypeStruct((count, half + lanes), query.dtype),
            jax.ShapeDtypeStruct((count, half + lanes), query.dtype),
        ],
        scratch_shapes=[
            pltpu.VMEM(query.shape, query.dtype),
            pltpu.VMEM(owners.shape, owners.dtype),
            pltpu.VMEM(requests.shape, requests.dtype),
            pltpu.VMEM((steps, block, width), weight.dtype),
            pltpu.VMEM((rows, width), jnp.float32),
            pltpu.SemaphoreType.DMA((3,)),
            pltpu.SemaphoreType.DMA((2, steps)),
        ],
        compiler_params=params(),
        name="project_keys",
    )(in_hbm(query), in_hbm(owners), in_hbm(requests), in_hbm(tokens), in_hbm(weight))


def values_kernel(tokens_ref, weight_ref, own_ref, near_ref, weight_buf, acc_ref, sems):
    steps, block, width = weight_buf.shape
    copies = []
    for step in range(steps):
        span = slice(step * block, (step + 1) * block)
        copies.append(
            start_all([pltpu.make_async_copy(weight_ref.at[span, width:], weight_buf.at[step], sems.at[step])])
        )
    accumulate(tokens_ref, weight_buf, acc_ref, copies)
    kept, sent = halves(acc_ref)
    own_ref[...] = kept.astype(own_ref.dtype)
    near_ref[...] = sent.astype(near_ref.dtype)


def project_values(tokens, weight):
    rows, features = tokens.shape
    width = weight.shape[1] // 2
    block = min(512, features // 2)
    steps = features // block
    vmem = pl.BlockSpec(memory_space=pltpu.VMEM)
    return pl.pallas_call(
        values_kernel,
        in_specs=[vmem, pl.BlockSpec(memory_space=pl.ANY)],
        out_specs=[vmem] * 2,
        out_shape=[jax.ShapeDtypeStruct((rows, width // 2), jnp.bfloat16)] * 2,
        scratch_shapes=[
            pltpu.VMEM((steps, block, width), weight.dtype),
            pltpu.VMEM((rows, width), jnp.float32),
            pltpu.SemaphoreType.DMA((steps,)),
        ],
        compiler_params=params(),
        cost_estimate=pl.CostEstimate(
            flops=2 * rows * features * width,
            bytes_accessed=2 * features * width,
            transcendentals=0,
        ),
        name="project_values",
    )(tokens, in_hbm(weight))


def cache_kernel(
    lengths_ref, query_ref, cache_ref, signs_ref, mixed_ref, tops_ref, totals_ref, query_buf, top_buf, total_buf, mixed_buf
):
    requests, span, _ = cache_ref.shape
    blocks, size = signs_ref.shape
    heads = blocks // 2
    width = heads * size
    count = query_ref.shape[1] // size
    group = count // heads
    norm = 1.0 / math.sqrt(size)
    matrix = hadamard_tile(size)
    signs = (2 * signs_ref[...] - 1).astype(jnp.float32)
    query = query_ref[...].astype(jnp.float32)
    query = jnp.concatenate(
        [query[:, h * size : (h + 1) * size] * signs[h // group : h // group + 1] for h in range(count)], axis=0
    )
    query_buf[...] = jnp.dot(query.astype(jnp.bfloat16), matrix, preferred_element_type=jnp.float32) * norm
    rows = 2 * count
    kv_head = lax.broadcasted_iota(jnp.int32, (rows, width), 0) // group & (heads - 1)
    own_head = kv_head == lax.broadcasted_iota(jnp.int32, (rows, width), 1) // size
    first = lax.broadcasted_iota(jnp.int32, (rows, span), 0) < count
    position = lax.axis_index("tp") * span + lax.broadcasted_iota(jnp.int32, (rows, span), 1)
    pairs = range(0, requests, 2)
    scores = []
    for r in pairs:
        both = [query_buf[pl.ds(r + i, count, stride=requests), :] for i in range(2)]
        wide = jnp.concatenate([jnp.concatenate(both, axis=0)] * heads, axis=1)
        wide = jnp.where(own_head, wide, 0.0).astype(jnp.bfloat16)
        keys = cache_ref[r : r + 2, :, :width].reshape(2 * span, width)
        scores.append(lax.dot_general(wide, keys, NT, preferred_element_type=jnp.float32))
    probs = []
    for r, score in zip(pairs, scores):
        score = jnp.where(first, score[:, :span], score[:, span:]) * norm
        live = position < jnp.where(first, lengths_ref[0, 0, r], lengths_ref[0, 0, r + 1])
        top = jnp.max(jnp.where(live, score, LOWEST), axis=1, keepdims=True)
        prob = jnp.where(live, jnp.exp(score - top), 0.0)
        total = jnp.sum(prob, axis=1, keepdims=True)
        at = slice(r * count, (r + 2) * count)
        top_buf[at, :] = jnp.broadcast_to(top, (rows, size))
        total_buf[at, :] = jnp.broadcast_to(total, (rows, size))
        probs.append(
            jnp.concatenate([jnp.where(first, prob, 0.0), jnp.where(first, 0.0, prob)], axis=1).astype(jnp.bfloat16)
        )
    mixed = []
    for r, prob in zip(pairs, probs):
        values = cache_ref[r : r + 2, :, width:].reshape(2 * span, width)
        wide = jnp.dot(prob, values, preferred_element_type=jnp.float32)
        wide = jnp.where(own_head, wide, 0.0)
        mixed.append(sum(wide[:, k * size : (k + 1) * size] for k in range(heads)))
    mixed = jnp.concatenate(mixed, axis=0)
    high = mixed.astype(jnp.bfloat16)
    low = (mixed - high.astype(jnp.float32)).astype(jnp.bfloat16)
    plain = jnp.dot(high, matrix, preferred_element_type=jnp.float32)
    mixed_buf[...] = plain + jnp.dot(low, matrix, preferred_element_type=jnp.float32)
    for h in range(count):
        pick = pl.ds(h, requests, stride=count)
        k = h // group
        at = slice(k * requests, (k + 1) * requests)
        column = slice(h % group * size, (h % group + 1) * size)
        mixed_ref[at, column] = mixed_buf[pick, :] * (signs[heads + k : heads + k + 1] * norm)
        tops_ref[at, column] = top_buf[pick, :]
        totals_ref[at, column] = total_buf[pick, :]


def cache_part(lengths, query, cache, signs):
    requests, span, width = cache.shape
    size = signs.shape[1]
    heads = signs.shape[0] // 2
    columns = query.shape[1]
    vmem = pl.BlockSpec(memory_space=pltpu.VMEM)
    return pl.pallas_call(
        cache_kernel,
        in_specs=[pl.BlockSpec(memory_space=pltpu.SMEM)] + [vmem] * 3,
        out_shape=[jax.ShapeDtypeStruct((heads * requests, columns // heads), jnp.float32)] * 3,
        scratch_shapes=[pltpu.VMEM((requests * columns // size, size), jnp.float32)] * 4,
        compiler_params=params(),
        cost_estimate=pl.CostEstimate(
            flops=4 * span * requests * columns,
            bytes_accessed=2 * requests * span * width,
            transcendentals=span * requests * columns // size,
        ),
        name="cache_part",
    )(lengths, query, cache, signs)


def score_kernel(heads, keys_ref, own_ref, *refs):
    message_refs, (scores_ref, code_ref) = by_distance((own_ref,) + refs[:-2], QUERY_ORDER), refs[-2:]
    near_ref = message_refs[1]
    requests = own_ref.shape[0]
    tokens, width = keys_ref.shape
    size = width // heads
    count = len(message_refs)
    half = scores_ref.shape[0] * size
    group = scores_ref.shape[0] // heads
    stacked = near_ref[tokens:, :].astype(jnp.float32)
    spread = requests * half // width
    near_query = jnp.concatenate(
        [stacked[at * requests : (at + 1) * requests] for at in range(half // width)], axis=1
    )
    queries, codes = [], []
    for d, ref in enumerate(message_refs):
        if d == 1:
            queries.append(near_query)
            codes.append(stacked[spread : spread + 1, : tokens // count])
        else:
            queries.append(ref[:, :half].astype(jnp.float32))
            codes.append(ref[0:1, half : half + tokens // count].astype(jnp.float32))
    me = lax.axis_index("seq")
    row = [sum(jnp.where(me ^ d == at, codes[d], 0.0) for d in range(count)) for at in range(count)]
    code = jnp.concatenate(row, axis=1).astype(jnp.int32)
    code = ((code // requests) ^ me) * requests + code % requests
    code_ref[...] = jnp.broadcast_to(code, code_ref.shape)
    span = count * requests
    here = lax.broadcasted_iota(jnp.int32, (span, tokens), 0) == code
    for k in range(heads):
        rows = []
        for g in range(group):
            at = (k * group + g) * size
            rows += [query[:, at : at + size] for query in queries]
        query = jnp.concatenate(rows, axis=0).astype(jnp.bfloat16)
        columns = slice(k * size, (k + 1) * size)
        scores = lax.dot_general(query, keys_ref[:, columns], NT, preferred_element_type=jnp.float32)
        scores = scores + lax.dot_general(
            query, near_ref[:tokens, columns], NT, preferred_element_type=jnp.float32
        )
        lines = [
            jnp.sum(jnp.where(here, scores[g * span : (g + 1) * span], 0.0), axis=0, keepdims=True)
            for g in range(group)
        ]
        scores_ref[k * group : (k + 1) * group, :] = jnp.concatenate(lines, axis=0) * (
            1.0 / math.sqrt(size)
        )


def pair_scores(heads, half, keys, messages):
    tokens, width = keys.shape
    return pl.pallas_call(
        functools.partial(score_kernel, heads),
        out_shape=[
            jax.ShapeDtypeStruct((half * heads // width, tokens), jnp.float32),
            jax.ShapeDtypeStruct((8, tokens), jnp.int32),
        ],
        compiler_params=params(),
        name="pair_scores",
    )(keys, *arranged(messages, QUERY_ORDER))


def packed(value, group, size):
    lane = lax.broadcasted_iota(jnp.int32, (value.shape[0], size), 1)
    narrow = jnp.zeros(lane.shape, jnp.float32)
    for g in range(group):
        narrow = jnp.where(lane % group == g, value[:, g * size : (g + 1) * size], narrow)
    high = narrow.astype(jnp.bfloat16).astype(jnp.float32)
    middle = (narrow - high).astype(jnp.bfloat16).astype(jnp.float32)
    return jnp.where(lane < group, high, jnp.where(lane < 2 * group, middle, narrow - high - middle))


def packed_stats(tops, totals, group):
    size = tops.shape[1] // group
    lane = lax.broadcasted_iota(jnp.int32, (tops.shape[0], size), 1)
    totals = pltpu.roll(packed(totals, group, size), 3 * group, 1)
    return jnp.where(lane < 3 * group, packed(tops, group, size), totals)


def unpacked_stats(stats, group):
    parts = [stats[:, at * group : (at + 1) * group] for at in range(6)]
    return parts[0] + parts[1] + parts[2], parts[3] + parts[4] + parts[5]


def broad(narrow, size):
    rows, group = narrow.shape
    return jnp.concatenate([jnp.broadcast_to(narrow[:, g : g + 1], (rows, size)) for g in range(group)], axis=1)


def mix_kernel(heads, count, requests, code_ref, own_ref, near_ref, scores_ref, far_scores_ref, *refs):
    mixed_refs, (tops_ref, totals_ref) = refs[:count], refs[count:]
    tokens, width = own_ref.shape
    size = width // heads
    group = scores_ref.shape[0] // heads
    span = count * requests
    here = lax.broadcasted_iota(jnp.int32, (span, tokens), 0) == code_ref[0:1, :]
    scores = scores_ref[...] + far_scores_ref[...]
    mixed, tops, totals = [], [], []
    for k in range(heads):
        weights = []
        for g in range(group):
            row = k * group + g
            line = jnp.broadcast_to(scores[row : row + 1, :], (span, tokens))
            top = jnp.max(jnp.where(here, line, LOWEST), axis=1, keepdims=True)
            probs = jnp.where(here, jnp.exp(line - top), 0.0)
            weights.append(probs)
            tops.append(jnp.broadcast_to(top, (span, size)))
            totals.append(jnp.broadcast_to(jnp.sum(probs, axis=1, keepdims=True), (span, size)))
        weights = jnp.concatenate(weights, axis=0).astype(jnp.bfloat16)
        columns = slice(k * size, (k + 1) * size)
        sums = jnp.dot(weights, own_ref[:, columns], preferred_element_type=jnp.float32)
        mixed.append(sums + jnp.dot(weights, near_ref[:, columns], preferred_element_type=jnp.float32))

    def block(parts, d):
        rows = slice(d * requests, (d + 1) * requests)
        lines = [
            jnp.concatenate([parts[k * group + g][rows] for g in range(group)], axis=1) for k in range(heads)
        ]
        return jnp.concatenate(lines, axis=0)

    pieces = [mixed[k][g * span : (g + 1) * span] for k in range(heads) for g in range(group)]
    for d in range(count):
        mixed_refs[d][:, : group * size] = block(pieces, d).astype(jnp.bfloat16)
    stats = packed_stats(block(tops, 1), block(totals, 1), group)
    mixed_refs[1][:, group * size :] = stats.astype(jnp.bfloat16)
    tops_ref[...] = block(tops, 0)
    totals_ref[...] = block(totals, 0)


def mix(heads, count, requests, code, values, near_values, scores, far_scores):
    size = values.shape[1] // heads
    columns = scores.shape[0] // heads * size
    shape = (heads * requests, columns)
    wide = (heads * requests, columns + size)
    return pl.pallas_call(
        functools.partial(mix_kernel, heads, count, requests),
        out_shape=[jax.ShapeDtypeStruct(wide if d == 1 else shape, jnp.bfloat16) for d in range(count)]
        + [jax.ShapeDtypeStruct(shape, jnp.float32)] * 2,
        compiler_params=params(),
        name="mix",
    )(code, values, near_values, scores, far_scores)


def merge_kernel(cache_ref, top_ref, total_ref, new_top_ref, new_total_ref, *refs):
    mixed_refs, out_ref = by_distance(refs[:-1], MIXED_ORDER), refs[-1]
    rows, columns = new_top_ref.shape
    size = out_ref.shape[1] - columns
    group = columns // size
    near = mixed_refs[1][...].astype(jnp.float32)
    near_top, near_total = unpacked_stats(near[:, columns:], group)
    own = mixed_refs[0][...].astype(jnp.float32) + mixed_refs[2][...].astype(jnp.float32)
    other = near[:, :columns] + mixed_refs[3][...].astype(jnp.float32)
    parts = (
        (side(), own, new_top_ref[...], new_total_ref[...]),
        (1 - side(), other, broad(near_top, size), broad(near_total, size)),
    )
    for place, new, new_top, new_total in parts:
        at = pl.ds(pl.multiple_of(place * rows, rows), rows)
        top = top_ref[at, :]
        both = jnp.maximum(top, new_top)
        cache_factor = jnp.exp(top - both)
        new_factor = jnp.exp(new_top - both)
        out_ref[at, :columns] = (cache_ref[at, :] * cache_factor + new * new_factor).astype(out_ref.dtype)
        total = total_ref[at, :] * cache_factor + new_total * new_factor
        out_ref[at, columns:] = packed_stats(both, total, group).astype(out_ref.dtype)


def merge(size, cache_mixed, tops, totals, new_tops, new_totals, mixed):
    rows, columns = cache_mixed.shape
    return pl.pallas_call(
        merge_kernel,
        out_shape=jax.ShapeDtypeStruct((rows, columns + size), jnp.bfloat16),
        compiler_params=params(),
        name="merge",
    )(cache_mixed, tops, totals, new_tops, new_totals, *arranged(mixed, MIXED_ORDER))


def finish_kernel(own_ref, far_ref, out_ref):
    requests = out_ref.shape[0]
    rows, wide = own_ref.shape
    heads = rows // requests
    columns = out_ref.shape[1] // heads
    size = wide - columns
    group = columns // size
    first = lax.axis_index("tp") == 0
    own, far = own_ref[...].astype(jnp.float32), far_ref[...].astype(jnp.float32)
    low, high = jnp.where(first, own, far), jnp.where(first, far, own)
    low_top, low_total = unpacked_stats(low[:, columns:], group)
    high_top, high_total = unpacked_stats(high[:, columns:], group)
    both = jnp.maximum(low_top, high_top)
    low_factor, high_factor = jnp.exp(low_top - both), jnp.exp(high_top - both)
    inverse = 1.0 / (low_total * low_factor + high_total * high_factor)
    low_factor, high_factor = low_factor * inverse, high_factor * inverse
    for g in range(group):
        at = slice(g * size, (g + 1) * size)
        out = low[:, at] * low_factor[:, g : g + 1] + high[:, at] * high_factor[:, g : g + 1]
        for k in range(heads):
            column = slice((k * group + g) * size, (k * group + g + 1) * size)
            out_ref[:, column] = out[k * requests : (k + 1) * requests].astype(out_ref.dtype)


def finish(requests, own, far, columns):
    return pl.pallas_call(
        finish_kernel,
        out_shape=jax.ShapeDtypeStruct((requests, columns), jnp.bfloat16),
        compiler_params=params(),
        name="finish",
    )(own, far)


def from_partner(x, axis, distance):
    count = lax.axis_size(axis)
    return lax.ppermute(x, axis, [(i, i ^ distance) for i in range(count)])


def on_device(tokens, kv_weight, owners, requests, signs, queries, kv_cache, lengths):
    seq_count = lax.axis_size("seq")
    blocks, size = signs.shape
    kept_heads = blocks // 4
    query = queries[0, 0]
    request_count, columns = query.shape
    tokens, keys, near, same, other = project_keys(query, owners[:, :, 0], requests, tokens, kv_weight)
    messages = [
        same,
        from_partner(near, "seq", 1),
        from_partner(same, "seq", 2),
        from_partner(other, "seq", 3),
    ]
    values, far_values = project_values(tokens, kv_weight)
    near_values = from_partner(far_values, "seq", 1)
    scores, code = pair_scores(kept_heads, columns // 2, keys, messages)
    far_scores = from_partner(scores, "seq", 2)
    results = mix(kept_heads, seq_count, request_count, code, values, near_values, scores, far_scores)
    mixed, (new_tops, new_totals) = results[:seq_count], results[seq_count:]
    mixed = [mixed[0]] + [from_partner(mixed[d], "seq", d) for d in range(1, seq_count)]
    cache_mixed, tops, totals = cache_part(lengths, query, kv_cache[0, 0], signs)
    own = merge(size, cache_mixed, tops, totals, new_tops, new_totals, mixed)
    far = from_partner(own, "tp", 1)
    return finish(request_count, own, far, columns).reshape(1, 1, request_count, columns)


def hadamard(order):
    rows = lax.broadcasted_iota(jnp.int32, (order, order), 0)
    cols = lax.broadcasted_iota(jnp.int32, (order, order), 1)
    parity = jnp.zeros((order, order), jnp.int32)
    for bit_number in range(order.bit_length() - 1):
        parity = parity + rows // 2**bit_number % 2 * (cols // 2**bit_number % 2)
    return (1 - 2 * (parity % 2)).astype(jnp.float32)


def rotate(blocks, sign_rows, matrix):
    product = jnp.einsum(
        "...h,hk->...k", blocks * sign_rows, matrix, precision=lax.Precision.HIGHEST
    )
    return product / math.sqrt(matrix.shape[0])


def encode(rotated):
    largest = jnp.max(jnp.abs(rotated), axis=-1) + 1e-06
    scales = largest.astype(jnp.bfloat16)
    encoded = (rotated / scales.astype(jnp.float32)[..., None]).astype(jnp.bfloat16)
    return (encoded, scales)


def decode(encoded, scales):
    return (encoded.astype(jnp.float32) * scales.astype(jnp.float32)[..., None]).astype(
        jnp.bfloat16
    )


def slot_numbers(targets, count, room):
    onehot = (targets[:, None] == lax.iota(jnp.int32, count)[None, :]).astype(jnp.int32)
    within = jnp.sum((jnp.cumsum(onehot, axis=0) - 1) * onehot, axis=1)
    return targets * room + within


def on_device_long(tokens, kv_weight, owners, requests, signs, queries, kv_cache, lengths):
    seq_count = lax.axis_size("seq")
    per_device = owners.shape[1]
    slots = max(2, (2 * per_device + seq_count - 1) // seq_count)
    head_blocks = signs.shape[0]
    kv_heads = head_blocks // 2
    head_size = signs.shape[1]
    matrix = hadamard(head_size)
    sign_rows = (2 * signs - 1).astype(jnp.float32)
    summed = lax.psum_scatter(
        jnp.dot(tokens, kv_weight, preferred_element_type=jnp.float32).astype(jnp.bfloat16),
        "seq",
        scatter_dimension=0,
        tiled=True,
    ).astype(jnp.float32)
    encoded, scales = encode(
        rotate(summed.reshape(per_device, head_blocks, head_size), sign_rows, matrix)
    )
    slot_index = slot_numbers(owners[0, :, 0], seq_count, slots)
    slot_total = seq_count * slots
    send_values = (
        jnp.zeros((slot_total, head_blocks, head_size), jnp.bfloat16).at[slot_index].set(encoded)
    )
    send_scales = jnp.zeros((slot_total, head_blocks), jnp.bfloat16).at[slot_index].set(scales)
    send_codes = jnp.zeros((slot_total,), jnp.int32).at[slot_index].set(requests[0] + 1)
    got_values, got_scales, arrived_codes = (
        lax.all_to_all(send_values, "seq", split_axis=0, concat_axis=0, tiled=True),
        lax.all_to_all(send_scales, "seq", split_axis=0, concat_axis=0, tiled=True),
        lax.all_to_all(send_codes, "seq", split_axis=0, concat_axis=0, tiled=True),
    )
    arrived = decode(got_values, got_scales)
    query = queries[0, 0]
    request_count = query.shape[0]
    group = query.shape[1] // (kv_heads * head_size)
    query_blocks = query.astype(jnp.float32).reshape(request_count, kv_heads, group, head_size)
    query_rot = rotate(query_blocks, sign_rows[:kv_heads][:, None, :], matrix).astype(jnp.bfloat16)
    local_cache = kv_cache[0, 0]
    cache_span = local_cache.shape[1]
    local_cache = local_cache.reshape(request_count, cache_span, head_blocks, head_size)
    score_scale = 1.0 / math.sqrt(head_size)
    lowest = -1e30
    highest = lax.Precision.HIGHEST
    score_cache = (
        jnp.einsum(
            "rkgd,rckd->rkgc",
            query_rot,
            local_cache[:, :, :kv_heads],
            preferred_element_type=jnp.float32,
        )
        * score_scale
    )
    score_new = (
        jnp.einsum(
            "rkgd,nkd->rkgn", query_rot, arrived[:, :kv_heads], preferred_element_type=jnp.float32
        )
        * score_scale
    )
    positions = lax.axis_index("tp") * cache_span + lax.iota(jnp.int32, cache_span)
    mask_cache = (positions[None, :] < lengths[0, 0][:, None])[:, None, None, :]
    match = arrived_codes[None, :] == (lax.iota(jnp.int32, request_count) + 1)[:, None]
    mask_new = match[:, None, None, :]
    top = jnp.maximum(
        jnp.max(jnp.where(mask_cache, score_cache, lowest), axis=-1),
        jnp.max(jnp.where(mask_new, score_new, lowest), axis=-1),
    )
    probs_cache = jnp.where(mask_cache, jnp.exp(score_cache - top[..., None]), 0.0)
    probs_new = jnp.where(mask_new, jnp.exp(score_new - top[..., None]), 0.0)
    total = jnp.sum(probs_cache, axis=-1) + jnp.sum(probs_new, axis=-1)
    mixed = jnp.einsum(
        "rkgc,rckd->rkgd",
        probs_cache,
        local_cache[:, :, kv_heads:].astype(jnp.float32),
        precision=highest,
    )
    mixed = mixed + jnp.einsum(
        "rkgn,nkd->rkgd", probs_new, arrived[:, kv_heads:].astype(jnp.float32), precision=highest
    )
    shared_top = lax.pmax(top, "tp")
    factor = jnp.exp(top - shared_top)
    total, mixed = (
        lax.psum((total * factor).astype(jnp.bfloat16), "tp").astype(jnp.float32),
        lax.psum((mixed * factor[..., None]).astype(jnp.bfloat16), "tp").astype(jnp.float32),
    )
    mixed = mixed / total[..., None]
    output = rotate(mixed, 1.0, matrix) * sign_rows[kv_heads:][None, :, None, :]
    return output.reshape(1, 1, request_count, group * kv_heads * head_size).astype(jnp.bfloat16)


def solution(mesh):
    placed = (
        P(("groups", "tp", "section"), "seq"),
        P("seq", None),
        P(("groups", "tp", "section"), "seq", None),
        P(("groups", "tp", "section"), "seq"),
        P(),
        P(("groups", "seq"), "section", None, None),
        P(("groups", "seq"), "section", None, "tp", None),
        P(("groups", "seq"), "section", None),
    )
    short = mesh.shape["seq"] == 4 and mesh.shape["tp"] == 2
    return jax.shard_map(
        on_device if short else on_device_long,
        mesh=mesh,
        in_specs=placed,
        out_specs=P(("groups", "seq"), "section", None, None),
        check_vma=False,
    )
```

```python
import functools
import math

import jax
import jax.numpy as jnp
from jax import lax
from jax.experimental import pallas as pl
from jax.experimental.pallas import tpu as pltpu
from jax.sharding import PartitionSpec as P

LOWEST = -1e30
MIB = 1024 * 1024
NT = (((1,), (1,)), ((), ()))


def params(mib=32):
    return pltpu.CompilerParams(vmem_limit_bytes=mib * MIB)


def in_hbm(x):
    return pltpu.with_memory_space_constraint(x, pltpu.HBM)


def in_vmem(x):
    return pltpu.with_memory_space_constraint(x, pltpu.VMEM)


def hadamard_tile(order):
    rows = lax.broadcasted_iota(jnp.int32, (order, order), 0)
    cols = lax.broadcasted_iota(jnp.int32, (order, order), 1)
    common = rows & cols
    parity = jnp.zeros((order, order), jnp.int32)
    for bit_number in range(order.bit_length() - 1):
        parity = parity ^ (common >> bit_number)
    return (1 - 2 * (parity & 1)).astype(jnp.float32).astype(jnp.bfloat16)


QUERY_ORDER = (3, 2, 1)
SCORE_ORDER = (1, 3, 2)
MIXED_ORDER = (3, 2, 1)


def arranged(blocks, order):
    return [blocks[0]] + [blocks[d] for d in order]


def by_distance(refs, order):
    return [refs[0]] + [refs[1 + order.index(d)] for d in range(1, len(refs))]


def side():
    return lax.axis_index("seq") & 1


def project_kernel(tokens_ref, weight_ref, keys_ref, own_ref, near_ref, acc_ref):
    width = keys_ref.shape[1]
    half = own_ref.shape[1]
    keys_ref[...] = jnp.dot(
        tokens_ref[...], weight_ref[:, :width], preferred_element_type=jnp.float32
    ).astype(keys_ref.dtype)
    acc_ref[...] = jnp.dot(tokens_ref[...], weight_ref[:, width:], preferred_element_type=jnp.float32)
    mine = pl.multiple_of(side() * half, half)
    other = pl.multiple_of((1 - side()) * half, half)
    own_ref[...] = acc_ref[:, pl.ds(mine, half)].astype(own_ref.dtype)
    near_ref[...] = acc_ref[:, pl.ds(other, half)].astype(near_ref.dtype)


def project(tokens, weight):
    rows, features = tokens.shape
    width = weight.shape[1] // 2
    vmem = pl.BlockSpec(memory_space=pltpu.VMEM)
    return pl.pallas_call(
        project_kernel,
        in_specs=[vmem] * 2,
        out_specs=[vmem] * 3,
        out_shape=[jax.ShapeDtypeStruct((rows, columns), jnp.bfloat16) for columns in (width, width // 2, width // 2)],
        scratch_shapes=[pltpu.VMEM((rows, width), jnp.float32)],
        compiler_params=params(32),
        cost_estimate=pl.CostEstimate(
            flops=4 * rows * features * width,
            bytes_accessed=2 * (rows * features + 2 * features * width),
            transcendentals=0,
        ),
        name="project",
    )(in_vmem(tokens), in_vmem(weight))


def message_kernel(query_ref, owners_ref, requests_ref, out_ref, query_buf, owners_buf, requests_buf, sems):
    requests, columns = query_ref.shape
    per_device = owners_ref.shape[1]
    copies = [
        pltpu.make_async_copy(source, target, sems.at[i])
        for i, (source, target) in enumerate(
            ((query_ref, query_buf), (owners_ref, owners_buf), (requests_ref, requests_buf))
        )
    ]
    for copy in copies:
        copy.start()
    for copy in copies:
        copy.wait()
    out_ref[:, :columns] = query_buf[...]
    code = (owners_buf[...] * requests + requests_buf[...]).astype(jnp.float32)
    spare = jnp.zeros((1, out_ref.shape[1] - columns - per_device), jnp.float32)
    code = jnp.concatenate([code, spare], axis=1)
    out_ref[:, columns:] = jnp.broadcast_to(code, (requests, code.shape[1])).astype(out_ref.dtype)


def make_message(query, owners, requests):
    count, columns = query.shape
    lanes = -(-owners.shape[1] // 128) * 128
    return pl.pallas_call(
        message_kernel,
        in_specs=[pl.BlockSpec(memory_space=pl.ANY)] * 3,
        out_specs=pl.BlockSpec(memory_space=pltpu.VMEM),
        out_shape=jax.ShapeDtypeStruct((count, columns + lanes), query.dtype),
        scratch_shapes=[
            pltpu.VMEM(query.shape, query.dtype),
            pltpu.VMEM(owners.shape, owners.dtype),
            pltpu.VMEM(requests.shape, requests.dtype),
            pltpu.SemaphoreType.DMA((3,)),
        ],
        compiler_params=params(16),
        cost_estimate=pl.CostEstimate(flops=10**11, bytes_accessed=10**4, transcendentals=0),
        name="make_message",
    )(in_hbm(query), in_hbm(owners), in_hbm(requests))


def cache_kernel(
    lengths_ref, query_ref, cache_ref, signs_ref, mixed_ref, tops_ref, totals_ref, query_buf, top_buf, total_buf, mixed_buf
):
    requests, span, _ = cache_ref.shape
    blocks, size = signs_ref.shape
    heads = blocks // 2
    width = heads * size
    count = query_ref.shape[1] // size
    group = count // heads
    norm = 1.0 / math.sqrt(size)
    matrix = hadamard_tile(size)
    signs = (2 * signs_ref[...] - 1).astype(jnp.float32)
    query = query_ref[...].astype(jnp.float32)
    query = jnp.concatenate(
        [query[:, h * size : (h + 1) * size] * signs[h // group : h // group + 1] for h in range(count)], axis=0
    )
    query_buf[...] = jnp.dot(query.astype(jnp.bfloat16), matrix, preferred_element_type=jnp.float32) * norm
    rows = 2 * count
    kv_head = lax.broadcasted_iota(jnp.int32, (rows, width), 0) // group & (heads - 1)
    own_head = kv_head == lax.broadcasted_iota(jnp.int32, (rows, width), 1) // size
    first = lax.broadcasted_iota(jnp.int32, (rows, span), 0) < count
    position = lax.axis_index("tp") * span + lax.broadcasted_iota(jnp.int32, (rows, span), 1)
    pairs = range(0, requests, 2)
    scores = []
    for r in pairs:
        both = [query_buf[pl.ds(r + i, count, stride=requests), :] for i in range(2)]
        wide = jnp.concatenate([jnp.concatenate(both, axis=0)] * heads, axis=1)
        wide = jnp.where(own_head, wide, 0.0).astype(jnp.bfloat16)
        keys = cache_ref[r : r + 2, :, :width].reshape(2 * span, width)
        scores.append(lax.dot_general(wide, keys, NT, preferred_element_type=jnp.float32))
    probs = []
    for r, score in zip(pairs, scores):
        score = jnp.where(first, score[:, :span], score[:, span:]) * norm
        live = position < jnp.where(first, lengths_ref[0, 0, r], lengths_ref[0, 0, r + 1])
        top = jnp.max(jnp.where(live, score, LOWEST), axis=1, keepdims=True)
        prob = jnp.where(live, jnp.exp(score - top), 0.0)
        total = jnp.sum(prob, axis=1, keepdims=True)
        at = slice(r * count, (r + 2) * count)
        top_buf[at, :] = jnp.broadcast_to(top, (rows, size))
        total_buf[at, :] = jnp.broadcast_to(total, (rows, size))
        probs.append(
            jnp.concatenate([jnp.where(first, prob, 0.0), jnp.where(first, 0.0, prob)], axis=1).astype(jnp.bfloat16)
        )
    mixed = []
    for r, prob in zip(pairs, probs):
        values = cache_ref[r : r + 2, :, width:].reshape(2 * span, width)
        wide = jnp.dot(prob, values, preferred_element_type=jnp.float32)
        wide = jnp.where(own_head, wide, 0.0)
        mixed.append(sum(wide[:, k * size : (k + 1) * size] for k in range(heads)))
    mixed = jnp.concatenate(mixed, axis=0)
    high = mixed.astype(jnp.bfloat16)
    low = (mixed - high.astype(jnp.float32)).astype(jnp.bfloat16)
    plain = jnp.dot(high, matrix, preferred_element_type=jnp.float32)
    mixed_buf[...] = plain + jnp.dot(low, matrix, preferred_element_type=jnp.float32)
    for h in range(count):
        pick = pl.ds(h, requests, stride=count)
        k = h // group
        at = slice(k * requests, (k + 1) * requests)
        column = slice(h % group * size, (h % group + 1) * size)
        mixed_ref[at, column] = mixed_buf[pick, :] * (signs[heads + k : heads + k + 1] * norm)
        tops_ref[at, column] = top_buf[pick, :]
        totals_ref[at, column] = total_buf[pick, :]


def cache_part(lengths, query, cache, signs):
    requests, span, width = cache.shape
    size = signs.shape[1]
    heads = signs.shape[0] // 2
    columns = query.shape[1]
    vmem = pl.BlockSpec(memory_space=pltpu.VMEM)
    return pl.pallas_call(
        cache_kernel,
        in_specs=[pl.BlockSpec(memory_space=pltpu.SMEM)] + [vmem] * 3,
        out_shape=[jax.ShapeDtypeStruct((heads * requests, columns // heads), jnp.float32)] * 3,
        scratch_shapes=[pltpu.VMEM((requests * columns // size, size), jnp.float32)] * 4,
        compiler_params=params(),
        cost_estimate=pl.CostEstimate(
            flops=4 * span * requests * columns,
            bytes_accessed=2 * requests * span * width,
            transcendentals=span * requests * columns // size,
        ),
        name="cache_part",
    )(lengths, query, cache, signs)


def code_row(message_refs, start, requests, tokens):
    count = len(message_refs)
    me = lax.axis_index("seq")
    pieces = [ref[0:1, start : start + tokens // count].astype(jnp.float32) for ref in message_refs]
    row = [sum(jnp.where(me ^ d == at, pieces[d], 0.0) for d in range(count)) for at in range(count)]
    code = jnp.concatenate(row, axis=1).astype(jnp.int32)
    return ((code // requests) ^ me) * requests + code % requests


def score_kernel(heads, start, keys_ref, values_ref, *refs):
    message_refs, refs = by_distance(refs[:-5], QUERY_ORDER), refs[-5:]
    scores_ref, same_ref, other_ref, near_ref, code_ref = refs
    requests = message_refs[0].shape[0]
    tokens, width = keys_ref.shape
    size = width // heads
    group = start // width
    half = same_ref.shape[0]
    code = code_row(message_refs, start, requests, tokens)
    code_ref[...] = jnp.broadcast_to(code, code_ref.shape)
    span = len(message_refs) * requests
    here = lax.broadcasted_iota(jnp.int32, (span, tokens), 0) == code
    queries = [ref[:, :start].astype(jnp.float32) for ref in message_refs]
    for k in range(heads):
        rows = []
        for g in range(group):
            at = (k * group + g) * size
            rows += [query[:, at : at + size] for query in queries]
        query = jnp.concatenate(rows, axis=0).astype(jnp.bfloat16)
        keys = keys_ref[:, k * size : (k + 1) * size]
        scores = lax.dot_general(query, keys, NT, preferred_element_type=jnp.float32)
        lines = [
            jnp.sum(jnp.where(here, scores[g * span : (g + 1) * span], 0.0), axis=0, keepdims=True)
            for g in range(group)
        ]
        scores_ref[k * group : (k + 1) * group, :] = jnp.concatenate(lines, axis=0) * (
            1.0 / math.sqrt(size)
        )
    same_ref[...] = scores_ref[pl.ds(pl.multiple_of(side() * half, half), half), :]
    other = scores_ref[pl.ds(pl.multiple_of((1 - side()) * half, half), half), :]
    other_ref[...] = other
    near_ref[:tokens, :] = values_ref[...]
    for part in range(3):
        piece = other.astype(near_ref.dtype)
        near_ref[tokens + part * half : tokens + (part + 1) * half, :] = piece
        other = other - piece.astype(jnp.float32)


def partial_scores(heads, columns, keys, values, messages):
    tokens, width = keys.shape
    query_heads = columns * heads // width
    vmem = pl.BlockSpec(memory_space=pltpu.VMEM)
    return pl.pallas_call(
        functools.partial(score_kernel, heads, columns),
        in_specs=[vmem] * (2 + len(messages)),
        out_specs=[vmem] * 5,
        out_shape=[
            jax.ShapeDtypeStruct((query_heads, tokens), jnp.float32),
            jax.ShapeDtypeStruct((query_heads // 2, tokens), jnp.float32),
            jax.ShapeDtypeStruct((query_heads // 2, tokens), jnp.float32),
            jax.ShapeDtypeStruct((tokens + 3 * query_heads // 2, values.shape[1]), values.dtype),
            jax.ShapeDtypeStruct((8, tokens), jnp.int32),
        ],
        compiler_params=params(),
        name="partial_scores",
    )(keys, values, *arranged(messages, QUERY_ORDER))[1:]


def packed(value, group, size):
    lane = lax.broadcasted_iota(jnp.int32, (value.shape[0], size), 1)
    narrow = jnp.zeros(lane.shape, jnp.float32)
    for g in range(group):
        narrow = jnp.where(lane % group == g, value[:, g * size : (g + 1) * size], narrow)
    high = narrow.astype(jnp.bfloat16).astype(jnp.float32)
    middle = (narrow - high).astype(jnp.bfloat16).astype(jnp.float32)
    return jnp.where(lane < group, high, jnp.where(lane < 2 * group, middle, narrow - high - middle))


def packed_stats(tops, totals, group):
    size = tops.shape[1] // group
    lane = lax.broadcasted_iota(jnp.int32, (tops.shape[0], size), 1)
    totals = pltpu.roll(packed(totals, group, size), 3 * group, 1)
    return jnp.where(lane < 3 * group, packed(tops, group, size), totals)


def unpacked_stats(stats, group):
    parts = [stats[:, at * group : (at + 1) * group] for at in range(6)]
    return parts[0] + parts[1] + parts[2], parts[3] + parts[4] + parts[5]


def broad(narrow, size):
    rows, group = narrow.shape
    return jnp.concatenate([jnp.broadcast_to(narrow[:, g : g + 1], (rows, size)) for g in range(group)], axis=1)


def mix_kernel(heads, count, requests, code_ref, own_ref, *refs):
    score_refs = by_distance(refs[:count], SCORE_ORDER)
    mixed_refs, (tops_ref, totals_ref) = refs[count : 2 * count], refs[2 * count :]
    tokens, width = own_ref.shape
    size = width // heads
    group = score_refs[0].shape[0] // heads
    span = count * requests
    here = lax.broadcasted_iota(jnp.int32, (span, tokens), 0) == code_ref[0:1, :]
    near_ref, half = score_refs[1], score_refs[0].shape[0]
    parts = [
        near_ref[tokens + part * half : tokens + (part + 1) * half, :].astype(jnp.float32) for part in range(3)
    ]
    near_scores = (parts[0] + parts[1]) + parts[2]
    scores = (score_refs[0][...] + score_refs[2][...]) + (near_scores + score_refs[3][...])
    mixed, tops, totals = [], [], []
    for k in range(heads):
        weights = []
        for g in range(group):
            row = k * group + g
            line = jnp.broadcast_to(scores[row : row + 1, :], (span, tokens))
            top = jnp.max(jnp.where(here, line, LOWEST), axis=1, keepdims=True)
            probs = jnp.where(here, jnp.exp(line - top), 0.0)
            weights.append(probs)
            tops.append(jnp.broadcast_to(top, (span, size)))
            totals.append(jnp.broadcast_to(jnp.sum(probs, axis=1, keepdims=True), (span, size)))
        weights = jnp.concatenate(weights, axis=0).astype(jnp.bfloat16)
        columns = slice(k * size, (k + 1) * size)
        sums = jnp.dot(weights, own_ref[:, columns], preferred_element_type=jnp.float32)
        mixed.append(sums + jnp.dot(weights, near_ref[:tokens, columns], preferred_element_type=jnp.float32))

    def block(parts, d):
        rows = slice(d * requests, (d + 1) * requests)
        lines = [
            jnp.concatenate([parts[k * group + g][rows] for g in range(group)], axis=1) for k in range(heads)
        ]
        return jnp.concatenate(lines, axis=0)

    pieces = [mixed[k][g * span : (g + 1) * span] for k in range(heads) for g in range(group)]
    for d in range(count):
        mixed_refs[d][:, : group * size] = block(pieces, d).astype(jnp.bfloat16)
    stats = packed_stats(block(tops, 1), block(totals, 1), group)
    mixed_refs[1][:, group * size :] = stats.astype(jnp.bfloat16)
    tops_ref[...] = block(tops, 0)
    totals_ref[...] = block(totals, 0)


def mix(heads, requests, code, values, scores):
    count = len(scores)
    size = values.shape[1] // heads
    columns = scores[0].shape[0] // heads * size
    shape = (heads * requests, columns)
    wide = (heads * requests, columns + size)
    return pl.pallas_call(
        functools.partial(mix_kernel, heads, count, requests),
        out_shape=[jax.ShapeDtypeStruct(wide if d == 1 else shape, jnp.bfloat16) for d in range(count)]
        + [jax.ShapeDtypeStruct(shape, jnp.float32)] * 2,
        compiler_params=params(),
        name="mix",
    )(code, values, *arranged(scores, SCORE_ORDER))


def merge_kernel(cache_ref, top_ref, total_ref, new_top_ref, new_total_ref, *refs):
    mixed_refs, out_ref = by_distance(refs[:-1], MIXED_ORDER), refs[-1]
    rows, columns = new_top_ref.shape
    size = out_ref.shape[1] - columns
    group = columns // size
    near = mixed_refs[1][...].astype(jnp.float32)
    near_top, near_total = unpacked_stats(near[:, columns:], group)
    own = mixed_refs[0][...].astype(jnp.float32) + mixed_refs[2][...].astype(jnp.float32)
    other = near[:, :columns] + mixed_refs[3][...].astype(jnp.float32)
    parts = (
        (side(), own, new_top_ref[...], new_total_ref[...]),
        (1 - side(), other, broad(near_top, size), broad(near_total, size)),
    )
    for place, new, new_top, new_total in parts:
        at = pl.ds(pl.multiple_of(place * rows, rows), rows)
        top = top_ref[at, :]
        both = jnp.maximum(top, new_top)
        cache_factor = jnp.exp(top - both)
        new_factor = jnp.exp(new_top - both)
        out_ref[at, :columns] = (cache_ref[at, :] * cache_factor + new * new_factor).astype(out_ref.dtype)
        total = total_ref[at, :] * cache_factor + new_total * new_factor
        out_ref[at, columns:] = packed_stats(both, total, group).astype(out_ref.dtype)


def merge(size, cache_mixed, tops, totals, new_tops, new_totals, mixed):
    rows, columns = cache_mixed.shape
    return pl.pallas_call(
        merge_kernel,
        out_shape=jax.ShapeDtypeStruct((rows, columns + size), jnp.bfloat16),
        compiler_params=params(),
        name="merge",
    )(cache_mixed, tops, totals, new_tops, new_totals, *arranged(mixed, MIXED_ORDER))


def finish_kernel(own_ref, far_ref, out_ref):
    requests = out_ref.shape[0]
    rows, wide = own_ref.shape
    heads = rows // requests
    columns = out_ref.shape[1] // heads
    size = wide - columns
    group = columns // size
    first = lax.axis_index("tp") == 0
    own, far = own_ref[...].astype(jnp.float32), far_ref[...].astype(jnp.float32)
    low, high = jnp.where(first, own, far), jnp.where(first, far, own)
    low_top, low_total = unpacked_stats(low[:, columns:], group)
    high_top, high_total = unpacked_stats(high[:, columns:], group)
    both = jnp.maximum(low_top, high_top)
    low_factor, high_factor = jnp.exp(low_top - both), jnp.exp(high_top - both)
    inverse = 1.0 / (low_total * low_factor + high_total * high_factor)
    low_factor, high_factor = low_factor * inverse, high_factor * inverse
    for g in range(group):
        at = slice(g * size, (g + 1) * size)
        out = low[:, at] * low_factor[:, g : g + 1] + high[:, at] * high_factor[:, g : g + 1]
        for k in range(heads):
            column = slice((k * group + g) * size, (k * group + g + 1) * size)
            out_ref[:, column] = out[k * requests : (k + 1) * requests].astype(out_ref.dtype)


def finish(requests, own, far, columns):
    return pl.pallas_call(
        finish_kernel,
        out_shape=jax.ShapeDtypeStruct((requests, columns), jnp.bfloat16),
        compiler_params=params(),
        name="finish",
    )(own, far)


def from_partner(x, axis, distance):
    count = lax.axis_size(axis)
    return lax.ppermute(x, axis, [(i, i ^ distance) for i in range(count)])


def exchange(blocks):
    return [blocks[0]] + [from_partner(blocks[d], "seq", d) for d in range(1, len(blocks))]


def on_device(tokens, kv_weight, owners, requests, signs, queries, kv_cache, lengths):
    seq_count = lax.axis_size("seq")
    blocks, size = signs.shape
    heads = blocks // 2
    query = queries[0, 0]
    request_count, columns = query.shape
    message = make_message(query, owners[:, :, 0], requests)
    messages = exchange([message] * seq_count)
    keys, values, far_values = project(tokens, kv_weight)
    same, other, near, code = partial_scores(heads, columns, keys, far_values, messages)
    scores = exchange([same, near, same, other])
    results = mix(heads // 2, request_count, code, values, scores)
    mixed, (new_tops, new_totals) = results[:seq_count], results[seq_count:]
    mixed = exchange(mixed)
    cache_mixed, tops, totals = cache_part(lengths, query, kv_cache[0, 0], signs)
    own = merge(size, cache_mixed, tops, totals, new_tops, new_totals, mixed)
    far = from_partner(own, "tp", 1)
    return finish(request_count, own, far, columns).reshape(1, 1, request_count, columns)


def hadamard(order):
    rows = lax.broadcasted_iota(jnp.int32, (order, order), 0)
    cols = lax.broadcasted_iota(jnp.int32, (order, order), 1)
    parity = jnp.zeros((order, order), jnp.int32)
    for bit_number in range(order.bit_length() - 1):
        parity = parity + rows // 2**bit_number % 2 * (cols // 2**bit_number % 2)
    return (1 - 2 * (parity % 2)).astype(jnp.float32)


def rotate(blocks, sign_rows, matrix):
    product = jnp.einsum(
        "...h,hk->...k", blocks * sign_rows, matrix, precision=lax.Precision.HIGHEST
    )
    return product / math.sqrt(matrix.shape[0])


def encode(rotated):
    largest = jnp.max(jnp.abs(rotated), axis=-1) + 1e-06
    scales = largest.astype(jnp.bfloat16)
    encoded = (rotated / scales.astype(jnp.float32)[..., None]).astype(jnp.bfloat16)
    return (encoded, scales)


def decode(encoded, scales):
    return (encoded.astype(jnp.float32) * scales.astype(jnp.float32)[..., None]).astype(
        jnp.bfloat16
    )


def slot_numbers(targets, count, room):
    onehot = (targets[:, None] == lax.iota(jnp.int32, count)[None, :]).astype(jnp.int32)
    within = jnp.sum((jnp.cumsum(onehot, axis=0) - 1) * onehot, axis=1)
    return targets * room + within


def on_device_long(tokens, kv_weight, owners, requests, signs, queries, kv_cache, lengths):
    seq_count = lax.axis_size("seq")
    per_device = owners.shape[1]
    slots = max(2, (2 * per_device + seq_count - 1) // seq_count)
    head_blocks = signs.shape[0]
    kv_heads = head_blocks // 2
    head_size = signs.shape[1]
    matrix = hadamard(head_size)
    sign_rows = (2 * signs - 1).astype(jnp.float32)
    summed = lax.psum_scatter(
        jnp.dot(tokens, kv_weight, preferred_element_type=jnp.float32).astype(jnp.bfloat16),
        "seq",
        scatter_dimension=0,
        tiled=True,
    ).astype(jnp.float32)
    encoded, scales = encode(
        rotate(summed.reshape(per_device, head_blocks, head_size), sign_rows, matrix)
    )
    slot_index = slot_numbers(owners[0, :, 0], seq_count, slots)
    slot_total = seq_count * slots
    send_values = (
        jnp.zeros((slot_total, head_blocks, head_size), jnp.bfloat16).at[slot_index].set(encoded)
    )
    send_scales = jnp.zeros((slot_total, head_blocks), jnp.bfloat16).at[slot_index].set(scales)
    send_codes = jnp.zeros((slot_total,), jnp.int32).at[slot_index].set(requests[0] + 1)
    got_values, got_scales, arrived_codes = (
        lax.all_to_all(send_values, "seq", split_axis=0, concat_axis=0, tiled=True),
        lax.all_to_all(send_scales, "seq", split_axis=0, concat_axis=0, tiled=True),
        lax.all_to_all(send_codes, "seq", split_axis=0, concat_axis=0, tiled=True),
    )
    arrived = decode(got_values, got_scales)
    query = queries[0, 0]
    request_count = query.shape[0]
    group = query.shape[1] // (kv_heads * head_size)
    query_blocks = query.astype(jnp.float32).reshape(request_count, kv_heads, group, head_size)
    query_rot = rotate(query_blocks, sign_rows[:kv_heads][:, None, :], matrix).astype(jnp.bfloat16)
    local_cache = kv_cache[0, 0]
    cache_span = local_cache.shape[1]
    local_cache = local_cache.reshape(request_count, cache_span, head_blocks, head_size)
    score_scale = 1.0 / math.sqrt(head_size)
    lowest = -1e30
    highest = lax.Precision.HIGHEST
    score_cache = (
        jnp.einsum(
            "rkgd,rckd->rkgc",
            query_rot,
            local_cache[:, :, :kv_heads],
            preferred_element_type=jnp.float32,
        )
        * score_scale
    )
    score_new = (
        jnp.einsum(
            "rkgd,nkd->rkgn", query_rot, arrived[:, :kv_heads], preferred_element_type=jnp.float32
        )
        * score_scale
    )
    positions = lax.axis_index("tp") * cache_span + lax.iota(jnp.int32, cache_span)
    mask_cache = (positions[None, :] < lengths[0, 0][:, None])[:, None, None, :]
    match = arrived_codes[None, :] == (lax.iota(jnp.int32, request_count) + 1)[:, None]
    mask_new = match[:, None, None, :]
    top = jnp.maximum(
        jnp.max(jnp.where(mask_cache, score_cache, lowest), axis=-1),
        jnp.max(jnp.where(mask_new, score_new, lowest), axis=-1),
    )
    probs_cache = jnp.where(mask_cache, jnp.exp(score_cache - top[..., None]), 0.0)
    probs_new = jnp.where(mask_new, jnp.exp(score_new - top[..., None]), 0.0)
    total = jnp.sum(probs_cache, axis=-1) + jnp.sum(probs_new, axis=-1)
    mixed = jnp.einsum(
        "rkgc,rckd->rkgd",
        probs_cache,
        local_cache[:, :, kv_heads:].astype(jnp.float32),
        precision=highest,
    )
    mixed = mixed + jnp.einsum(
        "rkgn,nkd->rkgd", probs_new, arrived[:, kv_heads:].astype(jnp.float32), precision=highest
    )
    shared_top = lax.pmax(top, "tp")
    factor = jnp.exp(top - shared_top)
    total, mixed = (
        lax.psum((total * factor).astype(jnp.bfloat16), "tp").astype(jnp.float32),
        lax.psum((mixed * factor[..., None]).astype(jnp.bfloat16), "tp").astype(jnp.float32),
    )
    mixed = mixed / total[..., None]
    output = rotate(mixed, 1.0, matrix) * sign_rows[kv_heads:][None, :, None, :]
    return output.reshape(1, 1, request_count, group * kv_heads * head_size).astype(jnp.bfloat16)


def solution(mesh):
    placed = (
        P(("groups", "tp", "section"), "seq"),
        P("seq", None),
        P(("groups", "tp", "section"), "seq", None),
        P(("groups", "tp", "section"), "seq"),
        P(),
        P(("groups", "seq"), "section", None, None),
        P(("groups", "seq"), "section", None, "tp", None),
        P(("groups", "seq"), "section", None),
    )
    short = mesh.shape["seq"] == 4 and mesh.shape["tp"] == 2
    return jax.shard_map(
        on_device if short else on_device_long,
        mesh=mesh,
        in_specs=placed,
        out_specs=P(("groups", "seq"), "section", None, None),
        check_vma=False,
    )
```

```python
import functools
import math

import jax
import jax.numpy as jnp
from jax import lax
from jax.experimental import pallas as pl
from jax.experimental.pallas import tpu as pltpu
from jax.sharding import PartitionSpec as P

LOWEST = -1e30
MIB = 1024 * 1024
NT = (((1,), (1,)), ((), ()))


def params(mib=32):
    return pltpu.CompilerParams(vmem_limit_bytes=mib * MIB)


def in_hbm(x):
    return pltpu.with_memory_space_constraint(x, pltpu.HBM)


def in_vmem(x):
    return pltpu.with_memory_space_constraint(x, pltpu.VMEM)


def hadamard_tile(order):
    rows = lax.broadcasted_iota(jnp.int32, (order, order), 0)
    cols = lax.broadcasted_iota(jnp.int32, (order, order), 1)
    common = rows & cols
    parity = jnp.zeros((order, order), jnp.int32)
    for bit_number in range(order.bit_length() - 1):
        parity = parity ^ (common >> bit_number)
    return (1 - 2 * (parity & 1)).astype(jnp.float32).astype(jnp.bfloat16)


QUERY_ORDER = (3, 2, 1)
SCORE_ORDER = (2, 3, 1)
MIXED_ORDER = (3, 2, 1)


def arranged(blocks, order):
    return [blocks[0]] + [blocks[d] for d in order]


def by_distance(refs, order):
    return [refs[0]] + [refs[1 + order.index(d)] for d in range(1, len(refs))]


def side():
    return lax.axis_index("seq") & 1


def project_kernel(tokens_ref, weight_ref, keys_ref, own_ref, near_ref, acc_ref):
    width = keys_ref.shape[1]
    half = own_ref.shape[1]
    keys_ref[...] = jnp.dot(
        tokens_ref[...], weight_ref[:, :width], preferred_element_type=jnp.float32
    ).astype(keys_ref.dtype)
    acc_ref[...] = jnp.dot(tokens_ref[...], weight_ref[:, width:], preferred_element_type=jnp.float32)
    mine = pl.multiple_of(side() * half, half)
    other = pl.multiple_of((1 - side()) * half, half)
    own_ref[...] = acc_ref[:, pl.ds(mine, half)].astype(own_ref.dtype)
    near_ref[...] = acc_ref[:, pl.ds(other, half)].astype(near_ref.dtype)


def project(tokens, weight):
    rows, features = tokens.shape
    width = weight.shape[1] // 2
    vmem = pl.BlockSpec(memory_space=pltpu.VMEM)
    return pl.pallas_call(
        project_kernel,
        in_specs=[vmem] * 2,
        out_specs=[vmem] * 3,
        out_shape=[jax.ShapeDtypeStruct((rows, columns), jnp.bfloat16) for columns in (width, width // 2, width // 2)],
        scratch_shapes=[pltpu.VMEM((rows, width), jnp.float32)],
        compiler_params=params(32),
        cost_estimate=pl.CostEstimate(
            flops=4 * rows * features * width,
            bytes_accessed=2 * (rows * features + 2 * features * width),
            transcendentals=0,
        ),
        name="project",
    )(in_vmem(tokens), in_vmem(weight))


def message_kernel(query_ref, owners_ref, requests_ref, out_ref, query_buf, owners_buf, requests_buf, sems):
    requests, columns = query_ref.shape
    per_device = owners_ref.shape[1]
    copies = [
        pltpu.make_async_copy(source, target, sems.at[i])
        for i, (source, target) in enumerate(
            ((query_ref, query_buf), (owners_ref, owners_buf), (requests_ref, requests_buf))
        )
    ]
    for copy in copies:
        copy.start()
    for copy in copies:
        copy.wait()
    out_ref[:, :columns] = query_buf[...]
    code = (owners_buf[...] * requests + requests_buf[...]).astype(jnp.float32)
    spare = jnp.zeros((1, out_ref.shape[1] - columns - per_device), jnp.float32)
    code = jnp.concatenate([code, spare], axis=1)
    out_ref[:, columns:] = jnp.broadcast_to(code, (requests, code.shape[1])).astype(out_ref.dtype)


def make_message(query, owners, requests):
    count, columns = query.shape
    lanes = -(-owners.shape[1] // 128) * 128
    return pl.pallas_call(
        message_kernel,
        in_specs=[pl.BlockSpec(memory_space=pl.ANY)] * 3,
        out_specs=pl.BlockSpec(memory_space=pltpu.VMEM),
        out_shape=jax.ShapeDtypeStruct((count, columns + lanes), query.dtype),
        scratch_shapes=[
            pltpu.VMEM(query.shape, query.dtype),
            pltpu.VMEM(owners.shape, owners.dtype),
            pltpu.VMEM(requests.shape, requests.dtype),
            pltpu.SemaphoreType.DMA((3,)),
        ],
        compiler_params=params(16),
        cost_estimate=pl.CostEstimate(flops=10**11, bytes_accessed=10**4, transcendentals=0),
        name="make_message",
    )(in_hbm(query), in_hbm(owners), in_hbm(requests))


def cache_kernel(
    lengths_ref, query_ref, cache_ref, signs_ref, mixed_ref, tops_ref, totals_ref, query_buf, top_buf, total_buf, mixed_buf
):
    requests, span, _ = cache_ref.shape
    blocks, size = signs_ref.shape
    heads = blocks // 2
    width = heads * size
    count = query_ref.shape[1] // size
    group = count // heads
    norm = 1.0 / math.sqrt(size)
    matrix = hadamard_tile(size)
    signs = (2 * signs_ref[...] - 1).astype(jnp.float32)
    query = query_ref[...].astype(jnp.float32)
    query = jnp.concatenate(
        [query[:, h * size : (h + 1) * size] * signs[h // group : h // group + 1] for h in range(count)], axis=0
    )
    query_buf[...] = jnp.dot(query.astype(jnp.bfloat16), matrix, preferred_element_type=jnp.float32) * norm
    rows = 2 * count
    kv_head = lax.broadcasted_iota(jnp.int32, (rows, width), 0) // group & (heads - 1)
    own_head = kv_head == lax.broadcasted_iota(jnp.int32, (rows, width), 1) // size
    first = lax.broadcasted_iota(jnp.int32, (rows, span), 0) < count
    position = lax.axis_index("tp") * span + lax.broadcasted_iota(jnp.int32, (rows, span), 1)
    pairs = range(0, requests, 2)
    scores = []
    for r in pairs:
        both = [query_buf[pl.ds(r + i, count, stride=requests), :] for i in range(2)]
        wide = jnp.concatenate([jnp.concatenate(both, axis=0)] * heads, axis=1)
        wide = jnp.where(own_head, wide, 0.0).astype(jnp.bfloat16)
        keys = cache_ref[r : r + 2, :, :width].reshape(2 * span, width)
        scores.append(lax.dot_general(wide, keys, NT, preferred_element_type=jnp.float32))
    probs = []
    for r, score in zip(pairs, scores):
        score = jnp.where(first, score[:, :span], score[:, span:]) * norm
        live = position < jnp.where(first, lengths_ref[0, 0, r], lengths_ref[0, 0, r + 1])
        top = jnp.max(jnp.where(live, score, LOWEST), axis=1, keepdims=True)
        prob = jnp.where(live, jnp.exp(score - top), 0.0)
        total = jnp.sum(prob, axis=1, keepdims=True)
        at = slice(r * count, (r + 2) * count)
        top_buf[at, :] = jnp.broadcast_to(top, (rows, size))
        total_buf[at, :] = jnp.broadcast_to(total, (rows, size))
        probs.append(
            jnp.concatenate([jnp.where(first, prob, 0.0), jnp.where(first, 0.0, prob)], axis=1).astype(jnp.bfloat16)
        )
    mixed = []
    for r, prob in zip(pairs, probs):
        values = cache_ref[r : r + 2, :, width:].reshape(2 * span, width)
        wide = jnp.dot(prob, values, preferred_element_type=jnp.float32)
        wide = jnp.where(own_head, wide, 0.0)
        mixed.append(sum(wide[:, k * size : (k + 1) * size] for k in range(heads)))
    mixed = jnp.concatenate(mixed, axis=0)
    high = mixed.astype(jnp.bfloat16)
    low = (mixed - high.astype(jnp.float32)).astype(jnp.bfloat16)
    plain = jnp.dot(high, matrix, preferred_element_type=jnp.float32)
    mixed_buf[...] = plain + jnp.dot(low, matrix, preferred_element_type=jnp.float32)
    for h in range(count):
        pick = pl.ds(h, requests, stride=count)
        k = h // group
        at = slice(k * requests, (k + 1) * requests)
        column = slice(h % group * size, (h % group + 1) * size)
        mixed_ref[at, column] = mixed_buf[pick, :] * (signs[heads + k : heads + k + 1] * norm)
        tops_ref[at, column] = top_buf[pick, :]
        totals_ref[at, column] = total_buf[pick, :]


def cache_part(lengths, query, cache, signs):
    requests, span, width = cache.shape
    size = signs.shape[1]
    heads = signs.shape[0] // 2
    columns = query.shape[1]
    vmem = pl.BlockSpec(memory_space=pltpu.VMEM)
    return pl.pallas_call(
        cache_kernel,
        in_specs=[pl.BlockSpec(memory_space=pltpu.SMEM)] + [vmem] * 3,
        out_shape=[jax.ShapeDtypeStruct((heads * requests, columns // heads), jnp.float32)] * 3,
        scratch_shapes=[pltpu.VMEM((requests * columns // size, size), jnp.float32)] * 4,
        compiler_params=params(),
        cost_estimate=pl.CostEstimate(
            flops=4 * span * requests * columns,
            bytes_accessed=2 * requests * span * width,
            transcendentals=span * requests * columns // size,
        ),
        name="cache_part",
    )(lengths, query, cache, signs)


def code_row(message_refs, start, requests, tokens):
    count = len(message_refs)
    me = lax.axis_index("seq")
    pieces = [ref[0:1, start : start + tokens // count].astype(jnp.float32) for ref in message_refs]
    row = [sum(jnp.where(me ^ d == at, pieces[d], 0.0) for d in range(count)) for at in range(count)]
    code = jnp.concatenate(row, axis=1).astype(jnp.int32)
    return ((code // requests) ^ me) * requests + code % requests


def score_kernel(heads, start, keys_ref, *refs):
    message_refs, refs = by_distance(refs[:-4], QUERY_ORDER), refs[-4:]
    same_ref, other_ref, code_ref, scores_ref = refs
    requests = message_refs[0].shape[0]
    tokens, width = keys_ref.shape
    size = width // heads
    group = start // width
    half = same_ref.shape[0]
    code = code_row(message_refs, start, requests, tokens)
    code_ref[...] = jnp.broadcast_to(code, code_ref.shape)
    span = len(message_refs) * requests
    here = lax.broadcasted_iota(jnp.int32, (span, tokens), 0) == code
    queries = [ref[:, :start].astype(jnp.float32) for ref in message_refs]
    for k in range(heads):
        rows = []
        for g in range(group):
            at = (k * group + g) * size
            rows += [query[:, at : at + size] for query in queries]
        query = jnp.concatenate(rows, axis=0).astype(jnp.bfloat16)
        keys = keys_ref[:, k * size : (k + 1) * size]
        scores = lax.dot_general(query, keys, NT, preferred_element_type=jnp.float32)
        lines = [
            jnp.sum(jnp.where(here, scores[g * span : (g + 1) * span], 0.0), axis=0, keepdims=True)
            for g in range(group)
        ]
        scores_ref[k * group : (k + 1) * group, :] = jnp.concatenate(lines, axis=0) * (
            1.0 / math.sqrt(size)
        )
    same_ref[...] = scores_ref[pl.ds(pl.multiple_of(side() * half, half), half), :]
    other_ref[...] = scores_ref[pl.ds(pl.multiple_of((1 - side()) * half, half), half), :]


def partial_scores(heads, columns, keys, messages):
    tokens, width = keys.shape
    query_heads = columns * heads // width
    vmem = pl.BlockSpec(memory_space=pltpu.VMEM)
    return pl.pallas_call(
        functools.partial(score_kernel, heads, columns),
        in_specs=[vmem] * (1 + len(messages)),
        out_specs=[vmem] * 3,
        out_shape=[
            jax.ShapeDtypeStruct((query_heads // 2, tokens), jnp.float32),
            jax.ShapeDtypeStruct((query_heads // 2, tokens), jnp.float32),
            jax.ShapeDtypeStruct((8, tokens), jnp.int32),
        ],
        scratch_shapes=[pltpu.VMEM((query_heads, tokens), jnp.float32)],
        compiler_params=params(),
        cost_estimate=pl.CostEstimate(flops=10**11, bytes_accessed=10**4, transcendentals=0),
        name="partial_scores",
    )(keys, *arranged(messages, QUERY_ORDER))


def packed(value, group, size):
    lane = lax.broadcasted_iota(jnp.int32, (value.shape[0], size), 1)
    narrow = jnp.zeros(lane.shape, jnp.float32)
    for g in range(group):
        narrow = jnp.where(lane % group == g, value[:, g * size : (g + 1) * size], narrow)
    high = narrow.astype(jnp.bfloat16).astype(jnp.float32)
    middle = (narrow - high).astype(jnp.bfloat16).astype(jnp.float32)
    return jnp.where(lane < group, high, jnp.where(lane < 2 * group, middle, narrow - high - middle))


def packed_stats(tops, totals, group):
    size = tops.shape[1] // group
    lane = lax.broadcasted_iota(jnp.int32, (tops.shape[0], size), 1)
    totals = pltpu.roll(packed(totals, group, size), 3 * group, 1)
    return jnp.where(lane < 3 * group, packed(tops, group, size), totals)


def unpacked_stats(stats, group):
    parts = [stats[:, at * group : (at + 1) * group] for at in range(6)]
    return parts[0] + parts[1] + parts[2], parts[3] + parts[4] + parts[5]


def broad(narrow, size):
    rows, group = narrow.shape
    return jnp.concatenate([jnp.broadcast_to(narrow[:, g : g + 1], (rows, size)) for g in range(group)], axis=1)


def mix_kernel(heads, count, requests, code_ref, own_ref, near_ref, *refs):
    score_refs = by_distance(refs[:count], SCORE_ORDER)
    mixed_refs, (tops_ref, totals_ref) = refs[count : 2 * count], refs[2 * count :]
    tokens, width = own_ref.shape
    size = width // heads
    group = score_refs[0].shape[0] // heads
    span = count * requests
    here = lax.broadcasted_iota(jnp.int32, (span, tokens), 0) == code_ref[0:1, :]
    scores = (score_refs[0][...] + score_refs[2][...]) + (score_refs[1][...] + score_refs[3][...])
    mixed, tops, totals = [], [], []
    for k in range(heads):
        weights = []
        for g in range(group):
            row = k * group + g
            line = jnp.broadcast_to(scores[row : row + 1, :], (span, tokens))
            top = jnp.max(jnp.where(here, line, LOWEST), axis=1, keepdims=True)
            probs = jnp.where(here, jnp.exp(line - top), 0.0)
            weights.append(probs)
            tops.append(jnp.broadcast_to(top, (span, size)))
            totals.append(jnp.broadcast_to(jnp.sum(probs, axis=1, keepdims=True), (span, size)))
        weights = jnp.concatenate(weights, axis=0).astype(jnp.bfloat16)
        columns = slice(k * size, (k + 1) * size)
        sums = jnp.dot(weights, own_ref[:, columns], preferred_element_type=jnp.float32)
        mixed.append(sums + jnp.dot(weights, near_ref[:, columns], preferred_element_type=jnp.float32))

    def block(parts, d):
        rows = slice(d * requests, (d + 1) * requests)
        lines = [
            jnp.concatenate([parts[k * group + g][rows] for g in range(group)], axis=1) for k in range(heads)
        ]
        return jnp.concatenate(lines, axis=0)

    pieces = [mixed[k][g * span : (g + 1) * span] for k in range(heads) for g in range(group)]
    for d in range(count):
        mixed_refs[d][:, : group * size] = block(pieces, d).astype(jnp.bfloat16)
    stats = packed_stats(block(tops, 1), block(totals, 1), group)
    mixed_refs[1][:, group * size :] = stats.astype(jnp.bfloat16)
    tops_ref[...] = block(tops, 0)
    totals_ref[...] = block(totals, 0)


def mix(heads, requests, code, values, near_values, scores):
    count = len(scores)
    size = values.shape[1] // heads
    columns = scores[0].shape[0] // heads * size
    shape = (heads * requests, columns)
    wide = (heads * requests, columns + size)
    return pl.pallas_call(
        functools.partial(mix_kernel, heads, count, requests),
        out_shape=[jax.ShapeDtypeStruct(wide if d == 1 else shape, jnp.bfloat16) for d in range(count)]
        + [jax.ShapeDtypeStruct(shape, jnp.float32)] * 2,
        compiler_params=params(),
        name="mix",
    )(code, values, near_values, *arranged(scores, SCORE_ORDER))


def merge_kernel(cache_ref, top_ref, total_ref, new_top_ref, new_total_ref, *refs):
    mixed_refs, out_ref = by_distance(refs[:-1], MIXED_ORDER), refs[-1]
    rows, columns = new_top_ref.shape
    size = out_ref.shape[1] - columns
    group = columns // size
    near = mixed_refs[1][...].astype(jnp.float32)
    near_top, near_total = unpacked_stats(near[:, columns:], group)
    own = mixed_refs[0][...].astype(jnp.float32) + mixed_refs[2][...].astype(jnp.float32)
    other = near[:, :columns] + mixed_refs[3][...].astype(jnp.float32)
    parts = (
        (side(), own, new_top_ref[...], new_total_ref[...]),
        (1 - side(), other, broad(near_top, size), broad(near_total, size)),
    )
    for place, new, new_top, new_total in parts:
        at = pl.ds(pl.multiple_of(place * rows, rows), rows)
        top = top_ref[at, :]
        both = jnp.maximum(top, new_top)
        cache_factor = jnp.exp(top - both)
        new_factor = jnp.exp(new_top - both)
        out_ref[at, :columns] = (cache_ref[at, :] * cache_factor + new * new_factor).astype(out_ref.dtype)
        total = total_ref[at, :] * cache_factor + new_total * new_factor
        out_ref[at, columns:] = packed_stats(both, total, group).astype(out_ref.dtype)


def merge(size, cache_mixed, tops, totals, new_tops, new_totals, mixed):
    rows, columns = cache_mixed.shape
    return pl.pallas_call(
        merge_kernel,
        out_shape=jax.ShapeDtypeStruct((rows, columns + size), jnp.bfloat16),
        compiler_params=params(),
        name="merge",
    )(cache_mixed, tops, totals, new_tops, new_totals, *arranged(mixed, MIXED_ORDER))


def finish_kernel(own_ref, far_ref, out_ref):
    requests = out_ref.shape[0]
    rows, wide = own_ref.shape
    heads = rows // requests
    columns = out_ref.shape[1] // heads
    size = wide - columns
    group = columns // size
    first = lax.axis_index("tp") == 0
    own, far = own_ref[...].astype(jnp.float32), far_ref[...].astype(jnp.float32)
    low, high = jnp.where(first, own, far), jnp.where(first, far, own)
    low_top, low_total = unpacked_stats(low[:, columns:], group)
    high_top, high_total = unpacked_stats(high[:, columns:], group)
    both = jnp.maximum(low_top, high_top)
    low_factor, high_factor = jnp.exp(low_top - both), jnp.exp(high_top - both)
    inverse = 1.0 / (low_total * low_factor + high_total * high_factor)
    low_factor, high_factor = low_factor * inverse, high_factor * inverse
    for g in range(group):
        at = slice(g * size, (g + 1) * size)
        out = low[:, at] * low_factor[:, g : g + 1] + high[:, at] * high_factor[:, g : g + 1]
        for k in range(heads):
            column = slice((k * group + g) * size, (k * group + g + 1) * size)
            out_ref[:, column] = out[k * requests : (k + 1) * requests].astype(out_ref.dtype)


def finish(requests, own, far, columns):
    return pl.pallas_call(
        finish_kernel,
        out_shape=jax.ShapeDtypeStruct((requests, columns), jnp.bfloat16),
        compiler_params=params(),
        name="finish",
    )(own, far)


def from_partner(x, axis, distance):
    count = lax.axis_size(axis)
    return lax.ppermute(x, axis, [(i, i ^ distance) for i in range(count)])


def exchange(blocks):
    return [blocks[0]] + [from_partner(blocks[d], "seq", d) for d in range(1, len(blocks))]


def on_device(tokens, kv_weight, owners, requests, signs, queries, kv_cache, lengths):
    seq_count = lax.axis_size("seq")
    blocks, size = signs.shape
    heads = blocks // 2
    query = queries[0, 0]
    request_count, columns = query.shape
    message = make_message(query, owners[:, :, 0], requests)
    messages = exchange([message] * seq_count)
    keys, values, far_values = project(tokens, kv_weight)
    near_values = from_partner(far_values, "seq", 1)
    same, other, code = partial_scores(heads, columns, keys, messages)
    scores = exchange([same, other, same, other])
    results = mix(heads // 2, request_count, code, values, near_values, scores)
    mixed, (new_tops, new_totals) = results[:seq_count], results[seq_count:]
    mixed = exchange(mixed)
    cache_mixed, tops, totals = cache_part(lengths, query, kv_cache[0, 0], signs)
    own = merge(size, cache_mixed, tops, totals, new_tops, new_totals, mixed)
    far = from_partner(own, "tp", 1)
    return finish(request_count, own, far, columns).reshape(1, 1, request_count, columns)


def hadamard(order):
    rows = lax.broadcasted_iota(jnp.int32, (order, order), 0)
    cols = lax.broadcasted_iota(jnp.int32, (order, order), 1)
    parity = jnp.zeros((order, order), jnp.int32)
    for bit_number in range(order.bit_length() - 1):
        parity = parity + rows // 2**bit_number % 2 * (cols // 2**bit_number % 2)
    return (1 - 2 * (parity % 2)).astype(jnp.float32)


def rotate(blocks, sign_rows, matrix):
    product = jnp.einsum(
        "...h,hk->...k", blocks * sign_rows, matrix, precision=lax.Precision.HIGHEST
    )
    return product / math.sqrt(matrix.shape[0])


def encode(rotated):
    largest = jnp.max(jnp.abs(rotated), axis=-1) + 1e-06
    scales = largest.astype(jnp.bfloat16)
    encoded = (rotated / scales.astype(jnp.float32)[..., None]).astype(jnp.bfloat16)
    return (encoded, scales)


def decode(encoded, scales):
    return (encoded.astype(jnp.float32) * scales.astype(jnp.float32)[..., None]).astype(
        jnp.bfloat16
    )


def slot_numbers(targets, count, room):
    onehot = (targets[:, None] == lax.iota(jnp.int32, count)[None, :]).astype(jnp.int32)
    within = jnp.sum((jnp.cumsum(onehot, axis=0) - 1) * onehot, axis=1)
    return targets * room + within


def on_device_long(tokens, kv_weight, owners, requests, signs, queries, kv_cache, lengths):
    seq_count = lax.axis_size("seq")
    per_device = owners.shape[1]
    slots = max(2, (2 * per_device + seq_count - 1) // seq_count)
    head_blocks = signs.shape[0]
    kv_heads = head_blocks // 2
    head_size = signs.shape[1]
    matrix = hadamard(head_size)
    sign_rows = (2 * signs - 1).astype(jnp.float32)
    summed = lax.psum_scatter(
        jnp.dot(tokens, kv_weight, preferred_element_type=jnp.float32).astype(jnp.bfloat16),
        "seq",
        scatter_dimension=0,
        tiled=True,
    ).astype(jnp.float32)
    encoded, scales = encode(
        rotate(summed.reshape(per_device, head_blocks, head_size), sign_rows, matrix)
    )
    slot_index = slot_numbers(owners[0, :, 0], seq_count, slots)
    slot_total = seq_count * slots
    send_values = (
        jnp.zeros((slot_total, head_blocks, head_size), jnp.bfloat16).at[slot_index].set(encoded)
    )
    send_scales = jnp.zeros((slot_total, head_blocks), jnp.bfloat16).at[slot_index].set(scales)
    send_codes = jnp.zeros((slot_total,), jnp.int32).at[slot_index].set(requests[0] + 1)
    got_values, got_scales, arrived_codes = (
        lax.all_to_all(send_values, "seq", split_axis=0, concat_axis=0, tiled=True),
        lax.all_to_all(send_scales, "seq", split_axis=0, concat_axis=0, tiled=True),
        lax.all_to_all(send_codes, "seq", split_axis=0, concat_axis=0, tiled=True),
    )
    arrived = decode(got_values, got_scales)
    query = queries[0, 0]
    request_count = query.shape[0]
    group = query.shape[1] // (kv_heads * head_size)
    query_blocks = query.astype(jnp.float32).reshape(request_count, kv_heads, group, head_size)
    query_rot = rotate(query_blocks, sign_rows[:kv_heads][:, None, :], matrix).astype(jnp.bfloat16)
    local_cache = kv_cache[0, 0]
    cache_span = local_cache.shape[1]
    local_cache = local_cache.reshape(request_count, cache_span, head_blocks, head_size)
    score_scale = 1.0 / math.sqrt(head_size)
    lowest = -1e30
    highest = lax.Precision.HIGHEST
    score_cache = (
        jnp.einsum(
            "rkgd,rckd->rkgc",
            query_rot,
            local_cache[:, :, :kv_heads],
            preferred_element_type=jnp.float32,
        )
        * score_scale
    )
    score_new = (
        jnp.einsum(
            "rkgd,nkd->rkgn", query_rot, arrived[:, :kv_heads], preferred_element_type=jnp.float32
        )
        * score_scale
    )
    positions = lax.axis_index("tp") * cache_span + lax.iota(jnp.int32, cache_span)
    mask_cache = (positions[None, :] < lengths[0, 0][:, None])[:, None, None, :]
    match = arrived_codes[None, :] == (lax.iota(jnp.int32, request_count) + 1)[:, None]
    mask_new = match[:, None, None, :]
    top = jnp.maximum(
        jnp.max(jnp.where(mask_cache, score_cache, lowest), axis=-1),
        jnp.max(jnp.where(mask_new, score_new, lowest), axis=-1),
    )
    probs_cache = jnp.where(mask_cache, jnp.exp(score_cache - top[..., None]), 0.0)
    probs_new = jnp.where(mask_new, jnp.exp(score_new - top[..., None]), 0.0)
    total = jnp.sum(probs_cache, axis=-1) + jnp.sum(probs_new, axis=-1)
    mixed = jnp.einsum(
        "rkgc,rckd->rkgd",
        probs_cache,
        local_cache[:, :, kv_heads:].astype(jnp.float32),
        precision=highest,
    )
    mixed = mixed + jnp.einsum(
        "rkgn,nkd->rkgd", probs_new, arrived[:, kv_heads:].astype(jnp.float32), precision=highest
    )
    shared_top = lax.pmax(top, "tp")
    factor = jnp.exp(top - shared_top)
    total, mixed = (
        lax.psum((total * factor).astype(jnp.bfloat16), "tp").astype(jnp.float32),
        lax.psum((mixed * factor[..., None]).astype(jnp.bfloat16), "tp").astype(jnp.float32),
    )
    mixed = mixed / total[..., None]
    output = rotate(mixed, 1.0, matrix) * sign_rows[kv_heads:][None, :, None, :]
    return output.reshape(1, 1, request_count, group * kv_heads * head_size).astype(jnp.bfloat16)


def solution(mesh):
    placed = (
        P(("groups", "tp", "section"), "seq"),
        P("seq", None),
        P(("groups", "tp", "section"), "seq", None),
        P(("groups", "tp", "section"), "seq"),
        P(),
        P(("groups", "seq"), "section", None, None),
        P(("groups", "seq"), "section", None, "tp", None),
        P(("groups", "seq"), "section", None),
    )
    short = mesh.shape["seq"] == 4 and mesh.shape["tp"] == 2
    return jax.shard_map(
        on_device if short else on_device_long,
        mesh=mesh,
        in_specs=placed,
        out_specs=P(("groups", "seq"), "section", None, None),
        check_vma=False,
    )
```

```python
import functools
import math

import jax
import jax.numpy as jnp
from jax import lax
from jax.experimental import pallas as pl
from jax.experimental.pallas import tpu as pltpu
from jax.sharding import PartitionSpec as P

LOWEST = -1e30
MIB = 1024 * 1024
NT = (((1,), (1,)), ((), ()))


def params(mib=32):
    return pltpu.CompilerParams(vmem_limit_bytes=mib * MIB)


def in_hbm(x):
    return pltpu.with_memory_space_constraint(x, pltpu.HBM)


def in_vmem(x):
    return pltpu.with_memory_space_constraint(x, pltpu.VMEM)


def hadamard_tile(order):
    rows = lax.broadcasted_iota(jnp.int32, (order, order), 0)
    cols = lax.broadcasted_iota(jnp.int32, (order, order), 1)
    common = rows & cols
    parity = jnp.zeros((order, order), jnp.int32)
    for bit_number in range(order.bit_length() - 1):
        parity = parity ^ (common >> bit_number)
    return (1 - 2 * (parity & 1)).astype(jnp.float32).astype(jnp.bfloat16)


QUERY_ORDER = (3, 2, 1)
SCORE_ORDER = (3, 2, 1)
MIXED_ORDER = (3, 2, 1)


def arranged(blocks, order):
    return [blocks[0]] + [blocks[d] for d in order]


def by_distance(refs, order):
    return [refs[0]] + [refs[1 + order.index(d)] for d in range(1, len(refs))]


def side():
    return lax.axis_index("seq") & 1


def project_kernel(tokens_ref, weight_ref, keys_ref, own_ref, near_ref, acc_ref):
    width = keys_ref.shape[1]
    half = own_ref.shape[1]
    keys_ref[...] = jnp.dot(
        tokens_ref[...], weight_ref[:, :width], preferred_element_type=jnp.float32
    ).astype(keys_ref.dtype)
    acc_ref[...] = jnp.dot(tokens_ref[...], weight_ref[:, width:], preferred_element_type=jnp.float32)
    mine = pl.multiple_of(side() * half, half)
    other = pl.multiple_of((1 - side()) * half, half)
    own_ref[...] = acc_ref[:, pl.ds(mine, half)].astype(own_ref.dtype)
    near_ref[...] = acc_ref[:, pl.ds(other, half)].astype(near_ref.dtype)


def project(tokens, weight):
    rows, features = tokens.shape
    width = weight.shape[1] // 2
    vmem = pl.BlockSpec(memory_space=pltpu.VMEM)
    return pl.pallas_call(
        project_kernel,
        in_specs=[vmem] * 2,
        out_specs=[vmem] * 3,
        out_shape=[jax.ShapeDtypeStruct((rows, columns), jnp.bfloat16) for columns in (width, width // 2, width // 2)],
        scratch_shapes=[pltpu.VMEM((rows, width), jnp.float32)],
        compiler_params=params(32),
        cost_estimate=pl.CostEstimate(
            flops=4 * rows * features * width,
            bytes_accessed=2 * (rows * features + 2 * features * width),
            transcendentals=0,
        ),
        name="project",
    )(in_vmem(tokens), in_vmem(weight))


def message_kernel(query_ref, owners_ref, requests_ref, out_ref, query_buf, owners_buf, requests_buf, sems):
    requests, columns = query_ref.shape
    per_device = owners_ref.shape[1]
    copies = [
        pltpu.make_async_copy(source, target, sems.at[i])
        for i, (source, target) in enumerate(
            ((query_ref, query_buf), (owners_ref, owners_buf), (requests_ref, requests_buf))
        )
    ]
    for copy in copies:
        copy.start()
    for copy in copies:
        copy.wait()
    out_ref[:, :columns] = query_buf[...]
    code = (owners_buf[...] * requests + requests_buf[...]).astype(jnp.float32)
    spare = jnp.zeros((1, out_ref.shape[1] - columns - per_device), jnp.float32)
    code = jnp.concatenate([code, spare], axis=1)
    out_ref[:, columns:] = jnp.broadcast_to(code, (requests, code.shape[1])).astype(out_ref.dtype)


def make_message(query, owners, requests):
    count, columns = query.shape
    lanes = -(-owners.shape[1] // 128) * 128
    return pl.pallas_call(
        message_kernel,
        in_specs=[pl.BlockSpec(memory_space=pl.ANY)] * 3,
        out_specs=pl.BlockSpec(memory_space=pltpu.VMEM),
        out_shape=jax.ShapeDtypeStruct((count, columns + lanes), query.dtype),
        scratch_shapes=[
            pltpu.VMEM(query.shape, query.dtype),
            pltpu.VMEM(owners.shape, owners.dtype),
            pltpu.VMEM(requests.shape, requests.dtype),
            pltpu.SemaphoreType.DMA((3,)),
        ],
        compiler_params=params(16),
        cost_estimate=pl.CostEstimate(flops=10**11, bytes_accessed=10**4, transcendentals=0),
        name="make_message",
    )(in_hbm(query), in_hbm(owners), in_hbm(requests))


def cache_kernel(
    lengths_ref, query_ref, cache_ref, signs_ref, mixed_ref, tops_ref, totals_ref, query_buf, top_buf, total_buf, mixed_buf
):
    requests, span, _ = cache_ref.shape
    blocks, size = signs_ref.shape
    heads = blocks // 2
    width = heads * size
    count = query_ref.shape[1] // size
    group = count // heads
    norm = 1.0 / math.sqrt(size)
    matrix = hadamard_tile(size)
    signs = (2 * signs_ref[...] - 1).astype(jnp.float32)
    query = query_ref[...].astype(jnp.float32)
    query = jnp.concatenate(
        [query[:, h * size : (h + 1) * size] * signs[h // group : h // group + 1] for h in range(count)], axis=0
    )
    query_buf[...] = jnp.dot(query.astype(jnp.bfloat16), matrix, preferred_element_type=jnp.float32) * norm
    rows = 2 * count
    kv_head = lax.broadcasted_iota(jnp.int32, (rows, width), 0) // group & (heads - 1)
    own_head = kv_head == lax.broadcasted_iota(jnp.int32, (rows, width), 1) // size
    first = lax.broadcasted_iota(jnp.int32, (rows, span), 0) < count
    position = lax.axis_index("tp") * span + lax.broadcasted_iota(jnp.int32, (rows, span), 1)
    pairs = range(0, requests, 2)
    scores = []
    for r in pairs:
        both = [query_buf[pl.ds(r + i, count, stride=requests), :] for i in range(2)]
        wide = jnp.concatenate([jnp.concatenate(both, axis=0)] * heads, axis=1)
        wide = jnp.where(own_head, wide, 0.0).astype(jnp.bfloat16)
        keys = cache_ref[r : r + 2, :, :width].reshape(2 * span, width)
        scores.append(lax.dot_general(wide, keys, NT, preferred_element_type=jnp.float32))
    probs = []
    for r, score in zip(pairs, scores):
        score = jnp.where(first, score[:, :span], score[:, span:]) * norm
        live = position < jnp.where(first, lengths_ref[0, 0, r], lengths_ref[0, 0, r + 1])
        top = jnp.max(jnp.where(live, score, LOWEST), axis=1, keepdims=True)
        prob = jnp.where(live, jnp.exp(score - top), 0.0)
        total = jnp.sum(prob, axis=1, keepdims=True)
        at = slice(r * count, (r + 2) * count)
        top_buf[at, :] = jnp.broadcast_to(top, (rows, size))
        total_buf[at, :] = jnp.broadcast_to(total, (rows, size))
        probs.append(
            jnp.concatenate([jnp.where(first, prob, 0.0), jnp.where(first, 0.0, prob)], axis=1).astype(jnp.bfloat16)
        )
    mixed = []
    for r, prob in zip(pairs, probs):
        values = cache_ref[r : r + 2, :, width:].reshape(2 * span, width)
        wide = jnp.dot(prob, values, preferred_element_type=jnp.float32)
        wide = jnp.where(own_head, wide, 0.0)
        mixed.append(sum(wide[:, k * size : (k + 1) * size] for k in range(heads)))
    mixed = jnp.concatenate(mixed, axis=0)
    high = mixed.astype(jnp.bfloat16)
    low = (mixed - high.astype(jnp.float32)).astype(jnp.bfloat16)
    plain = jnp.dot(high, matrix, preferred_element_type=jnp.float32)
    mixed_buf[...] = plain + jnp.dot(low, matrix, preferred_element_type=jnp.float32)
    for h in range(count):
        pick = pl.ds(h, requests, stride=count)
        k = h // group
        at = slice(k * requests, (k + 1) * requests)
        column = slice(h % group * size, (h % group + 1) * size)
        mixed_ref[at, column] = mixed_buf[pick, :] * (signs[heads + k : heads + k + 1] * norm)
        tops_ref[at, column] = top_buf[pick, :]
        totals_ref[at, column] = total_buf[pick, :]


def cache_part(lengths, query, cache, signs):
    requests, span, width = cache.shape
    size = signs.shape[1]
    heads = signs.shape[0] // 2
    columns = query.shape[1]
    vmem = pl.BlockSpec(memory_space=pltpu.VMEM)
    return pl.pallas_call(
        cache_kernel,
        in_specs=[pl.BlockSpec(memory_space=pltpu.SMEM)] + [vmem] * 3,
        out_shape=[jax.ShapeDtypeStruct((heads * requests, columns // heads), jnp.float32)] * 3,
        scratch_shapes=[pltpu.VMEM((requests * columns // size, size), jnp.float32)] * 4,
        compiler_params=params(),
        cost_estimate=pl.CostEstimate(
            flops=4 * span * requests * columns,
            bytes_accessed=2 * requests * span * width,
            transcendentals=span * requests * columns // size,
        ),
        name="cache_part",
    )(lengths, query, cache, signs)


def code_row(message_refs, start, requests, tokens):
    count = len(message_refs)
    me = lax.axis_index("seq")
    pieces = [ref[0:1, start : start + tokens // count].astype(jnp.float32) for ref in message_refs]
    row = [sum(jnp.where(me ^ d == at, pieces[d], 0.0) for d in range(count)) for at in range(count)]
    code = jnp.concatenate(row, axis=1).astype(jnp.int32)
    return ((code // requests) ^ me) * requests + code % requests


def score_kernel(heads, start, keys_ref, *refs):
    message_refs, refs = by_distance(refs[:-4], QUERY_ORDER), refs[-4:]
    same_ref, other_ref, code_ref, scores_ref = refs
    requests = message_refs[0].shape[0]
    tokens, width = keys_ref.shape
    size = width // heads
    group = start // width
    half = same_ref.shape[0]
    code = code_row(message_refs, start, requests, tokens)
    code_ref[...] = jnp.broadcast_to(code, code_ref.shape)
    span = len(message_refs) * requests
    here = lax.broadcasted_iota(jnp.int32, (span, tokens), 0) == code
    queries = [ref[:, :start].astype(jnp.float32) for ref in message_refs]
    for k in range(heads):
        rows = []
        for g in range(group):
            at = (k * group + g) * size
            rows += [query[:, at : at + size] for query in queries]
        query = jnp.concatenate(rows, axis=0).astype(jnp.bfloat16)
        keys = keys_ref[:, k * size : (k + 1) * size]
        scores = lax.dot_general(query, keys, NT, preferred_element_type=jnp.float32)
        lines = [
            jnp.sum(jnp.where(here, scores[g * span : (g + 1) * span], 0.0), axis=0, keepdims=True)
            for g in range(group)
        ]
        scores_ref[k * group : (k + 1) * group, :] = jnp.concatenate(lines, axis=0) * (
            1.0 / math.sqrt(size)
        )
    same_ref[...] = scores_ref[pl.ds(pl.multiple_of(side() * half, half), half), :]
    other_ref[...] = scores_ref[pl.ds(pl.multiple_of((1 - side()) * half, half), half), :]


def partial_scores(heads, columns, keys, messages):
    tokens, width = keys.shape
    query_heads = columns * heads // width
    vmem = pl.BlockSpec(memory_space=pltpu.VMEM)
    return pl.pallas_call(
        functools.partial(score_kernel, heads, columns),
        in_specs=[vmem] * (1 + len(messages)),
        out_specs=[vmem] * 3,
        out_shape=[
            jax.ShapeDtypeStruct((query_heads // 2, tokens), jnp.float32),
            jax.ShapeDtypeStruct((query_heads // 2, tokens), jnp.float32),
            jax.ShapeDtypeStruct((8, tokens), jnp.int32),
        ],
        scratch_shapes=[pltpu.VMEM((query_heads, tokens), jnp.float32)],
        compiler_params=params(),
        cost_estimate=pl.CostEstimate(flops=10**11, bytes_accessed=10**4, transcendentals=0),
        name="partial_scores",
    )(keys, *arranged(messages, QUERY_ORDER))


def packed(value, group, size):
    lane = lax.broadcasted_iota(jnp.int32, (value.shape[0], size), 1)
    narrow = jnp.zeros(lane.shape, jnp.float32)
    for g in range(group):
        narrow = jnp.where(lane % group == g, value[:, g * size : (g + 1) * size], narrow)
    high = narrow.astype(jnp.bfloat16).astype(jnp.float32)
    middle = (narrow - high).astype(jnp.bfloat16).astype(jnp.float32)
    return jnp.where(lane < group, high, jnp.where(lane < 2 * group, middle, narrow - high - middle))


def packed_stats(tops, totals, group):
    size = tops.shape[1] // group
    lane = lax.broadcasted_iota(jnp.int32, (tops.shape[0], size), 1)
    totals = pltpu.roll(packed(totals, group, size), 3 * group, 1)
    return jnp.where(lane < 3 * group, packed(tops, group, size), totals)


def unpacked_stats(stats, group):
    parts = [stats[:, at * group : (at + 1) * group] for at in range(6)]
    return parts[0] + parts[1] + parts[2], parts[3] + parts[4] + parts[5]


def broad(narrow, size):
    rows, group = narrow.shape
    return jnp.concatenate([jnp.broadcast_to(narrow[:, g : g + 1], (rows, size)) for g in range(group)], axis=1)


def mix_kernel(heads, count, requests, code_ref, own_ref, near_ref, *refs):
    score_refs = by_distance(refs[:count], SCORE_ORDER)
    mixed_refs, (tops_ref, totals_ref) = refs[count : 2 * count], refs[2 * count :]
    tokens, width = own_ref.shape
    size = width // heads
    group = score_refs[0].shape[0] // heads
    span = count * requests
    here = lax.broadcasted_iota(jnp.int32, (span, tokens), 0) == code_ref[0:1, :]
    scores = (score_refs[0][...] + score_refs[2][...]) + (score_refs[1][...] + score_refs[3][...])
    mixed, tops, totals = [], [], []
    for k in range(heads):
        weights = []
        for g in range(group):
            row = k * group + g
            line = jnp.broadcast_to(scores[row : row + 1, :], (span, tokens))
            top = jnp.max(jnp.where(here, line, LOWEST), axis=1, keepdims=True)
            probs = jnp.where(here, jnp.exp(line - top), 0.0)
            weights.append(probs)
            tops.append(jnp.broadcast_to(top, (span, size)))
            totals.append(jnp.broadcast_to(jnp.sum(probs, axis=1, keepdims=True), (span, size)))
        weights = jnp.concatenate(weights, axis=0).astype(jnp.bfloat16)
        columns = slice(k * size, (k + 1) * size)
        sums = jnp.dot(weights, own_ref[:, columns], preferred_element_type=jnp.float32)
        mixed.append(sums + jnp.dot(weights, near_ref[:, columns], preferred_element_type=jnp.float32))

    def block(parts, d):
        rows = slice(d * requests, (d + 1) * requests)
        lines = [
            jnp.concatenate([parts[k * group + g][rows] for g in range(group)], axis=1) for k in range(heads)
        ]
        return jnp.concatenate(lines, axis=0)

    pieces = [mixed[k][g * span : (g + 1) * span] for k in range(heads) for g in range(group)]
    for d in range(count):
        mixed_refs[d][:, : group * size] = block(pieces, d).astype(jnp.bfloat16)
    stats = packed_stats(block(tops, 3), block(totals, 3), group)
    mixed_refs[3][:, group * size :] = stats.astype(jnp.bfloat16)
    tops_ref[...] = block(tops, 0)
    totals_ref[...] = block(totals, 0)


def mix(heads, requests, code, values, near_values, scores):
    count = len(scores)
    size = values.shape[1] // heads
    columns = scores[0].shape[0] // heads * size
    shape = (heads * requests, columns)
    wide = (heads * requests, columns + size)
    return pl.pallas_call(
        functools.partial(mix_kernel, heads, count, requests),
        out_shape=[jax.ShapeDtypeStruct(wide if d == 3 else shape, jnp.bfloat16) for d in range(count)]
        + [jax.ShapeDtypeStruct(shape, jnp.float32)] * 2,
        compiler_params=params(),
        name="mix",
    )(code, values, near_values, *arranged(scores, SCORE_ORDER))


def merge_kernel(cache_ref, top_ref, total_ref, new_top_ref, new_total_ref, *refs):
    mixed_refs, out_ref = by_distance(refs[:-1], MIXED_ORDER), refs[-1]
    rows, columns = new_top_ref.shape
    size = out_ref.shape[1] - columns
    group = columns // size
    far = mixed_refs[3][...].astype(jnp.float32)
    far_top, far_total = unpacked_stats(far[:, columns:], group)
    own = mixed_refs[0][...].astype(jnp.float32) + mixed_refs[2][...].astype(jnp.float32)
    other = mixed_refs[1][...].astype(jnp.float32) + far[:, :columns]
    parts = (
        (side(), own, new_top_ref[...], new_total_ref[...]),
        (1 - side(), other, broad(far_top, size), broad(far_total, size)),
    )
    for place, new, new_top, new_total in parts:
        at = pl.ds(pl.multiple_of(place * rows, rows), rows)
        top = top_ref[at, :]
        both = jnp.maximum(top, new_top)
        cache_factor = jnp.exp(top - both)
        new_factor = jnp.exp(new_top - both)
        out_ref[at, :columns] = (cache_ref[at, :] * cache_factor + new * new_factor).astype(out_ref.dtype)
        total = total_ref[at, :] * cache_factor + new_total * new_factor
        out_ref[at, columns:] = packed_stats(both, total, group).astype(out_ref.dtype)


def merge(size, cache_mixed, tops, totals, new_tops, new_totals, mixed):
    rows, columns = cache_mixed.shape
    return pl.pallas_call(
        merge_kernel,
        out_shape=jax.ShapeDtypeStruct((rows, columns + size), jnp.bfloat16),
        compiler_params=params(),
        name="merge",
    )(cache_mixed, tops, totals, new_tops, new_totals, *arranged(mixed, MIXED_ORDER))


def finish_kernel(own_ref, far_ref, out_ref):
    requests = out_ref.shape[0]
    rows, wide = own_ref.shape
    heads = rows // requests
    columns = out_ref.shape[1] // heads
    size = wide - columns
    group = columns // size
    first = lax.axis_index("tp") == 0
    own, far = own_ref[...].astype(jnp.float32), far_ref[...].astype(jnp.float32)
    low, high = jnp.where(first, own, far), jnp.where(first, far, own)
    low_top, low_total = unpacked_stats(low[:, columns:], group)
    high_top, high_total = unpacked_stats(high[:, columns:], group)
    both = jnp.maximum(low_top, high_top)
    low_factor, high_factor = jnp.exp(low_top - both), jnp.exp(high_top - both)
    inverse = 1.0 / (low_total * low_factor + high_total * high_factor)
    low_factor, high_factor = low_factor * inverse, high_factor * inverse
    for g in range(group):
        at = slice(g * size, (g + 1) * size)
        out = low[:, at] * low_factor[:, g : g + 1] + high[:, at] * high_factor[:, g : g + 1]
        for k in range(heads):
            column = slice((k * group + g) * size, (k * group + g + 1) * size)
            out_ref[:, column] = out[k * requests : (k + 1) * requests].astype(out_ref.dtype)


def finish(requests, own, far, columns):
    return pl.pallas_call(
        finish_kernel,
        out_shape=jax.ShapeDtypeStruct((requests, columns), jnp.bfloat16),
        compiler_params=params(),
        name="finish",
    )(own, far)


def from_partner(x, axis, distance):
    count = lax.axis_size(axis)
    return lax.ppermute(x, axis, [(i, i ^ distance) for i in range(count)])


def exchange(blocks):
    return [blocks[0]] + [from_partner(blocks[d], "seq", d) for d in range(1, len(blocks))]


def on_device(tokens, kv_weight, owners, requests, signs, queries, kv_cache, lengths):
    seq_count = lax.axis_size("seq")
    blocks, size = signs.shape
    heads = blocks // 2
    query = queries[0, 0]
    request_count, columns = query.shape
    message = make_message(query, owners[:, :, 0], requests)
    messages = exchange([message] * seq_count)
    keys, values, far_values = project(tokens, kv_weight)
    near_values = from_partner(far_values, "seq", 1)
    same, other, code = partial_scores(heads, columns, keys, messages)
    scores = exchange([same, other, same, other])
    results = mix(heads // 2, request_count, code, values, near_values, scores)
    mixed, (new_tops, new_totals) = results[:seq_count], results[seq_count:]
    mixed = exchange(mixed)
    cache_mixed, tops, totals = cache_part(lengths, query, kv_cache[0, 0], signs)
    own = merge(size, cache_mixed, tops, totals, new_tops, new_totals, mixed)
    far = from_partner(own, "tp", 1)
    return finish(request_count, own, far, columns).reshape(1, 1, request_count, columns)


def hadamard(order):
    rows = lax.broadcasted_iota(jnp.int32, (order, order), 0)
    cols = lax.broadcasted_iota(jnp.int32, (order, order), 1)
    parity = jnp.zeros((order, order), jnp.int32)
    for bit_number in range(order.bit_length() - 1):
        parity = parity + rows // 2**bit_number % 2 * (cols // 2**bit_number % 2)
    return (1 - 2 * (parity % 2)).astype(jnp.float32)


def rotate(blocks, sign_rows, matrix):
    product = jnp.einsum(
        "...h,hk->...k", blocks * sign_rows, matrix, precision=lax.Precision.HIGHEST
    )
    return product / math.sqrt(matrix.shape[0])


def encode(rotated):
    largest = jnp.max(jnp.abs(rotated), axis=-1) + 1e-06
    scales = largest.astype(jnp.bfloat16)
    encoded = (rotated / scales.astype(jnp.float32)[..., None]).astype(jnp.bfloat16)
    return (encoded, scales)


def decode(encoded, scales):
    return (encoded.astype(jnp.float32) * scales.astype(jnp.float32)[..., None]).astype(
        jnp.bfloat16
    )


def slot_numbers(targets, count, room):
    onehot = (targets[:, None] == lax.iota(jnp.int32, count)[None, :]).astype(jnp.int32)
    within = jnp.sum((jnp.cumsum(onehot, axis=0) - 1) * onehot, axis=1)
    return targets * room + within


def on_device_long(tokens, kv_weight, owners, requests, signs, queries, kv_cache, lengths):
    seq_count = lax.axis_size("seq")
    per_device = owners.shape[1]
    slots = max(2, (2 * per_device + seq_count - 1) // seq_count)
    head_blocks = signs.shape[0]
    kv_heads = head_blocks // 2
    head_size = signs.shape[1]
    matrix = hadamard(head_size)
    sign_rows = (2 * signs - 1).astype(jnp.float32)
    summed = lax.psum_scatter(
        jnp.dot(tokens, kv_weight, preferred_element_type=jnp.float32).astype(jnp.bfloat16),
        "seq",
        scatter_dimension=0,
        tiled=True,
    ).astype(jnp.float32)
    encoded, scales = encode(
        rotate(summed.reshape(per_device, head_blocks, head_size), sign_rows, matrix)
    )
    slot_index = slot_numbers(owners[0, :, 0], seq_count, slots)
    slot_total = seq_count * slots
    send_values = (
        jnp.zeros((slot_total, head_blocks, head_size), jnp.bfloat16).at[slot_index].set(encoded)
    )
    send_scales = jnp.zeros((slot_total, head_blocks), jnp.bfloat16).at[slot_index].set(scales)
    send_codes = jnp.zeros((slot_total,), jnp.int32).at[slot_index].set(requests[0] + 1)
    got_values, got_scales, arrived_codes = (
        lax.all_to_all(send_values, "seq", split_axis=0, concat_axis=0, tiled=True),
        lax.all_to_all(send_scales, "seq", split_axis=0, concat_axis=0, tiled=True),
        lax.all_to_all(send_codes, "seq", split_axis=0, concat_axis=0, tiled=True),
    )
    arrived = decode(got_values, got_scales)
    query = queries[0, 0]
    request_count = query.shape[0]
    group = query.shape[1] // (kv_heads * head_size)
    query_blocks = query.astype(jnp.float32).reshape(request_count, kv_heads, group, head_size)
    query_rot = rotate(query_blocks, sign_rows[:kv_heads][:, None, :], matrix).astype(jnp.bfloat16)
    local_cache = kv_cache[0, 0]
    cache_span = local_cache.shape[1]
    local_cache = local_cache.reshape(request_count, cache_span, head_blocks, head_size)
    score_scale = 1.0 / math.sqrt(head_size)
    lowest = -1e30
    highest = lax.Precision.HIGHEST
    score_cache = (
        jnp.einsum(
            "rkgd,rckd->rkgc",
            query_rot,
            local_cache[:, :, :kv_heads],
            preferred_element_type=jnp.float32,
        )
        * score_scale
    )
    score_new = (
        jnp.einsum(
            "rkgd,nkd->rkgn", query_rot, arrived[:, :kv_heads], preferred_element_type=jnp.float32
        )
        * score_scale
    )
    positions = lax.axis_index("tp") * cache_span + lax.iota(jnp.int32, cache_span)
    mask_cache = (positions[None, :] < lengths[0, 0][:, None])[:, None, None, :]
    match = arrived_codes[None, :] == (lax.iota(jnp.int32, request_count) + 1)[:, None]
    mask_new = match[:, None, None, :]
    top = jnp.maximum(
        jnp.max(jnp.where(mask_cache, score_cache, lowest), axis=-1),
        jnp.max(jnp.where(mask_new, score_new, lowest), axis=-1),
    )
    probs_cache = jnp.where(mask_cache, jnp.exp(score_cache - top[..., None]), 0.0)
    probs_new = jnp.where(mask_new, jnp.exp(score_new - top[..., None]), 0.0)
    total = jnp.sum(probs_cache, axis=-1) + jnp.sum(probs_new, axis=-1)
    mixed = jnp.einsum(
        "rkgc,rckd->rkgd",
        probs_cache,
        local_cache[:, :, kv_heads:].astype(jnp.float32),
        precision=highest,
    )
    mixed = mixed + jnp.einsum(
        "rkgn,nkd->rkgd", probs_new, arrived[:, kv_heads:].astype(jnp.float32), precision=highest
    )
    shared_top = lax.pmax(top, "tp")
    factor = jnp.exp(top - shared_top)
    total, mixed = (
        lax.psum((total * factor).astype(jnp.bfloat16), "tp").astype(jnp.float32),
        lax.psum((mixed * factor[..., None]).astype(jnp.bfloat16), "tp").astype(jnp.float32),
    )
    mixed = mixed / total[..., None]
    output = rotate(mixed, 1.0, matrix) * sign_rows[kv_heads:][None, :, None, :]
    return output.reshape(1, 1, request_count, group * kv_heads * head_size).astype(jnp.bfloat16)


def solution(mesh):
    placed = (
        P(("groups", "tp", "section"), "seq"),
        P("seq", None),
        P(("groups", "tp", "section"), "seq", None),
        P(("groups", "tp", "section"), "seq"),
        P(),
        P(("groups", "seq"), "section", None, None),
        P(("groups", "seq"), "section", None, "tp", None),
        P(("groups", "seq"), "section", None),
    )
    short = mesh.shape["seq"] == 4 and mesh.shape["tp"] == 2
    return jax.shard_map(
        on_device if short else on_device_long,
        mesh=mesh,
        in_specs=placed,
        out_specs=P(("groups", "seq"), "section", None, None),
        check_vma=False,
    )
```

```python
import functools
import math

import jax
import jax.numpy as jnp
from jax import lax
from jax.experimental import pallas as pl
from jax.experimental.pallas import tpu as pltpu
from jax.sharding import PartitionSpec as P

LOWEST = -1e30
MIB = 1024 * 1024
NT = (((1,), (1,)), ((), ()))


def params(mib=32):
    return pltpu.CompilerParams(vmem_limit_bytes=mib * MIB)


def in_hbm(x):
    return pltpu.with_memory_space_constraint(x, pltpu.HBM)


def in_vmem(x):
    return pltpu.with_memory_space_constraint(x, pltpu.VMEM)


def hadamard_tile(order):
    rows = lax.broadcasted_iota(jnp.int32, (order, order), 0)
    cols = lax.broadcasted_iota(jnp.int32, (order, order), 1)
    common = rows & cols
    parity = jnp.zeros((order, order), jnp.int32)
    for bit_number in range(order.bit_length() - 1):
        parity = parity ^ (common >> bit_number)
    return (1 - 2 * (parity & 1)).astype(jnp.float32).astype(jnp.bfloat16)


QUERY_ORDER = (1, 2, 3)
SCORE_ORDER = (3, 2, 1)


def arranged(blocks, order):
    return [blocks[0]] + [blocks[d] for d in order]


def by_distance(refs, order):
    return [refs[0]] + [refs[1 + order.index(d)] for d in range(1, len(refs))]


def project_kernel(tokens_ref, weight_ref, keys_ref, values_ref):
    width = keys_ref.shape[1]
    for out_ref, columns in ((keys_ref, slice(0, width)), (values_ref, slice(width, 2 * width))):
        out_ref[...] = jnp.dot(
            tokens_ref[...], weight_ref[:, columns], preferred_element_type=jnp.float32
        ).astype(out_ref.dtype)


def project(tokens, weight):
    rows, features = tokens.shape
    width = weight.shape[1] // 2
    vmem = pl.BlockSpec(memory_space=pltpu.VMEM)
    return pl.pallas_call(
        project_kernel,
        in_specs=[vmem] * 2,
        out_specs=[vmem] * 2,
        out_shape=[jax.ShapeDtypeStruct((rows, width), jnp.bfloat16)] * 2,
        compiler_params=params(32),
        cost_estimate=pl.CostEstimate(
            flops=4 * rows * features * width,
            bytes_accessed=2 * (rows * features + 2 * features * width),
            transcendentals=0,
        ),
        name="project",
    )(in_vmem(tokens), in_vmem(weight))


def message_kernel(query_ref, owners_ref, requests_ref, out_ref, query_buf, owners_buf, requests_buf, sems):
    requests, columns = query_ref.shape
    per_device = owners_ref.shape[1]
    copies = [
        pltpu.make_async_copy(source, target, sems.at[i])
        for i, (source, target) in enumerate(
            ((query_ref, query_buf), (owners_ref, owners_buf), (requests_ref, requests_buf))
        )
    ]
    for copy in copies:
        copy.start()
    for copy in copies:
        copy.wait()
    out_ref[:, :columns] = query_buf[...]
    code = (owners_buf[...] * requests + requests_buf[...]).astype(jnp.float32)
    spare = jnp.zeros((1, out_ref.shape[1] - columns - per_device), jnp.float32)
    code = jnp.concatenate([code, spare], axis=1)
    out_ref[:, columns:] = jnp.broadcast_to(code, (requests, code.shape[1])).astype(out_ref.dtype)


def make_message(query, owners, requests):
    count, columns = query.shape
    lanes = -(-owners.shape[1] // 128) * 128
    return pl.pallas_call(
        message_kernel,
        in_specs=[pl.BlockSpec(memory_space=pl.ANY)] * 3,
        out_specs=pl.BlockSpec(memory_space=pltpu.VMEM),
        out_shape=jax.ShapeDtypeStruct((count, columns + lanes), query.dtype),
        scratch_shapes=[
            pltpu.VMEM(query.shape, query.dtype),
            pltpu.VMEM(owners.shape, owners.dtype),
            pltpu.VMEM(requests.shape, requests.dtype),
            pltpu.SemaphoreType.DMA((3,)),
        ],
        compiler_params=params(16),
        cost_estimate=pl.CostEstimate(flops=10**11, bytes_accessed=10**4, transcendentals=0),
        name="make_message",
    )(in_hbm(query), in_hbm(owners), in_hbm(requests))


def cache_kernel(
    lengths_ref, query_ref, cache_ref, signs_ref, mixed_ref, stats_ref, query_buf, top_buf, total_buf, mixed_buf
):
    requests, span, _ = cache_ref.shape
    blocks, size = signs_ref.shape
    heads = blocks // 2
    width = heads * size
    count = query_ref.shape[1] // size
    group = count // heads
    norm = 1.0 / math.sqrt(size)
    matrix = hadamard_tile(size)
    signs = (2 * signs_ref[...] - 1).astype(jnp.float32)
    query = query_ref[...].astype(jnp.float32)
    query = jnp.concatenate(
        [query[:, h * size : (h + 1) * size] * signs[h // group : h // group + 1] for h in range(count)], axis=0
    )
    query_buf[...] = jnp.dot(query.astype(jnp.bfloat16), matrix, preferred_element_type=jnp.float32) * norm
    rows = 2 * count
    kv_head = lax.broadcasted_iota(jnp.int32, (rows, width), 0) // group & (heads - 1)
    own_head = kv_head == lax.broadcasted_iota(jnp.int32, (rows, width), 1) // size
    first = lax.broadcasted_iota(jnp.int32, (rows, span), 0) < count
    position = lax.axis_index("tp") * span + lax.broadcasted_iota(jnp.int32, (rows, span), 1)
    pairs = range(0, requests, 2)
    scores = []
    for r in pairs:
        both = [query_buf[pl.ds(r + i, count, stride=requests), :] for i in range(2)]
        wide = jnp.concatenate([jnp.concatenate(both, axis=0)] * heads, axis=1)
        wide = jnp.where(own_head, wide, 0.0).astype(jnp.bfloat16)
        keys = cache_ref[r : r + 2, :, :width].reshape(2 * span, width)
        scores.append(lax.dot_general(wide, keys, NT, preferred_element_type=jnp.float32))
    probs = []
    for r, score in zip(pairs, scores):
        score = jnp.where(first, score[:, :span], score[:, span:]) * norm
        live = position < jnp.where(first, lengths_ref[0, 0, r], lengths_ref[0, 0, r + 1])
        top = jnp.max(jnp.where(live, score, LOWEST), axis=1, keepdims=True)
        prob = jnp.where(live, jnp.exp(score - top), 0.0)
        total = jnp.sum(prob, axis=1, keepdims=True)
        at = slice(r * count, (r + 2) * count)
        top_buf[at, :] = jnp.broadcast_to(top, (rows, size))
        total_buf[at, :] = jnp.broadcast_to(total, (rows, size))
        probs.append(
            jnp.concatenate([jnp.where(first, prob, 0.0), jnp.where(first, 0.0, prob)], axis=1).astype(jnp.bfloat16)
        )
    mixed = []
    for r, prob in zip(pairs, probs):
        values = cache_ref[r : r + 2, :, width:].reshape(2 * span, width)
        wide = jnp.dot(prob, values, preferred_element_type=jnp.float32)
        wide = jnp.where(own_head, wide, 0.0)
        mixed.append(sum(wide[:, k * size : (k + 1) * size] for k in range(heads)))
    mixed = jnp.concatenate(mixed, axis=0)
    high = mixed.astype(jnp.bfloat16)
    low = (mixed - high.astype(jnp.float32)).astype(jnp.bfloat16)
    plain = jnp.dot(high, matrix, preferred_element_type=jnp.float32)
    mixed_buf[...] = plain + jnp.dot(low, matrix, preferred_element_type=jnp.float32)
    lane = lax.broadcasted_iota(jnp.int32, (requests, stats_ref.shape[1]), 1)
    tops = jnp.full(lane.shape, 0.0, jnp.float32)
    totals = jnp.ones(lane.shape, jnp.float32)
    for h in range(count):
        pick = pl.ds(h, requests, stride=count)
        column = slice(h * size, (h + 1) * size)
        k = heads + h // group
        mixed_ref[:, column] = mixed_buf[pick, :] * (signs[k : k + 1] * norm)
        tops = jnp.where(lane == h, top_buf[pick, :], tops)
        totals = jnp.where(lane == h, total_buf[pick, :], totals)
    stats_ref[:requests, :] = tops
    stats_ref[requests:, :] = totals


def cache_part(lengths, query, cache, signs):
    requests, span, width = cache.shape
    size = signs.shape[1]
    columns = query.shape[1]
    vmem = pl.BlockSpec(memory_space=pltpu.VMEM)
    return pl.pallas_call(
        cache_kernel,
        in_specs=[pl.BlockSpec(memory_space=pltpu.SMEM)] + [vmem] * 3,
        out_shape=[
            jax.ShapeDtypeStruct(query.shape, jnp.float32),
            jax.ShapeDtypeStruct((2 * requests, size), jnp.float32),
        ],
        scratch_shapes=[pltpu.VMEM((requests * columns // size, size), jnp.float32)] * 4,
        compiler_params=params(),
        cost_estimate=pl.CostEstimate(
            flops=4 * span * requests * columns,
            bytes_accessed=2 * requests * span * width,
            transcendentals=span * requests * columns // size,
        ),
        name="cache_part",
    )(lengths, query, cache, signs)


def code_row(message_refs, start, requests, tokens):
    count = len(message_refs)
    me = lax.axis_index("seq")
    pieces = [ref[0:1, start : start + tokens // count].astype(jnp.float32) for ref in message_refs]
    row = [sum(jnp.where(me ^ d == at, pieces[d], 0.0) for d in range(count)) for at in range(count)]
    code = jnp.concatenate(row, axis=1).astype(jnp.int32)
    return ((code // requests) ^ me) * requests + code % requests


def score_kernel(heads, start, keys_ref, *refs):
    message_refs, (scores_ref, code_ref) = by_distance(refs[:-2], QUERY_ORDER), refs[-2:]
    requests = message_refs[0].shape[0]
    tokens, width = keys_ref.shape
    size = width // heads
    group = start // width
    code = code_row(message_refs, start, requests, tokens)
    code_ref[...] = jnp.broadcast_to(code, code_ref.shape)
    span = len(message_refs) * requests
    here = lax.broadcasted_iota(jnp.int32, (span, tokens), 0) == code
    queries = [ref[:, :start].astype(jnp.float32) for ref in message_refs]
    for k in range(heads):
        rows = []
        for g in range(group):
            at = (k * group + g) * size
            rows += [query[:, at : at + size] for query in queries]
        query = jnp.concatenate(rows, axis=0).astype(jnp.bfloat16)
        keys = keys_ref[:, k * size : (k + 1) * size]
        scores = lax.dot_general(query, keys, NT, preferred_element_type=jnp.float32)
        lines = [
            jnp.sum(jnp.where(here, scores[g * span : (g + 1) * span], 0.0), axis=0, keepdims=True)
            for g in range(group)
        ]
        scores_ref[k * group : (k + 1) * group, :] = jnp.concatenate(lines, axis=0) * (
            1.0 / math.sqrt(size)
        )


def partial_scores(heads, columns, keys, messages):
    tokens, width = keys.shape
    return pl.pallas_call(
        functools.partial(score_kernel, heads, columns),
        out_shape=[
            jax.ShapeDtypeStruct((columns * heads // width, tokens), jnp.float32),
            jax.ShapeDtypeStruct((8, tokens), jnp.int32),
        ],
        compiler_params=params(),
        cost_estimate=pl.CostEstimate(flops=10**11, bytes_accessed=10**4, transcendentals=0),
        name="partial_scores",
    )(keys, *arranged(messages, QUERY_ORDER))


def mix_kernel(heads, requests, code_ref, values_ref, near_ref, cache_stats_ref, *refs):
    score_refs, (own_ref, far_ref, new_stats_ref, stats_ref) = refs[:4], refs[4:]
    own, after, across, before = [ref[...] for ref in score_refs]
    scores = (own + across) + (before + after)
    tokens, width = values_ref.shape
    size = width // heads
    group = scores.shape[0] // heads
    span = 2 * requests
    row = lax.broadcasted_iota(jnp.int32, (span, tokens), 0)
    here = jnp.where(row < requests, row, row + requests) == code_ref[0:1, :]
    lane = lax.broadcasted_iota(jnp.int32, (requests, stats_ref.shape[1]), 1)
    tops = jnp.full(lane.shape, 0.0, jnp.float32)
    totals = jnp.zeros(lane.shape, jnp.float32)
    for k in range(heads):
        weights = []
        for g in range(group):
            h = k * group + g
            line = jnp.broadcast_to(scores[h : h + 1, :], (span, tokens))
            top = jnp.max(jnp.where(here, line, LOWEST), axis=1, keepdims=True)
            probs = jnp.where(here, jnp.exp(line - top), 0.0)
            total = jnp.sum(probs, axis=1, keepdims=True)
            weights.append(probs)
            tops = jnp.where(lane == h, top[:requests], tops)
            totals = jnp.where(lane == h, total[:requests], totals)
        weights = jnp.concatenate(weights, axis=0).astype(jnp.bfloat16)
        columns = slice(k * size, (k + 1) * size)
        mixed = jnp.dot(weights, values_ref[:, columns], preferred_element_type=jnp.float32)
        mixed = mixed + jnp.dot(weights, near_ref[:, columns], preferred_element_type=jnp.float32)
        for g in range(group):
            at = slice((k * group + g) * size, (k * group + g + 1) * size)
            own_ref[:, at] = mixed[g * span : g * span + requests]
            far_ref[:, at] = mixed[g * span + requests : (g + 1) * span].astype(far_ref.dtype)
    new_stats_ref[...] = tops
    cache_tops = cache_stats_ref[:requests, :]
    both = jnp.maximum(cache_tops, tops)
    stats_ref[:requests, :] = both
    stats_ref[requests:, :] = cache_stats_ref[requests:, :] * jnp.exp(cache_tops - both) + totals * jnp.exp(
        tops - both
    )


def mix(heads, code, values, near_values, cache_stats, scores):
    requests, lanes = cache_stats.shape[0] // 2, cache_stats.shape[1]
    size = values.shape[1] // heads
    shape = (requests, scores[0].shape[0] * size)
    return pl.pallas_call(
        functools.partial(mix_kernel, heads, requests),
        out_shape=[
            jax.ShapeDtypeStruct(shape, jnp.float32),
            jax.ShapeDtypeStruct(shape, jnp.bfloat16),
            jax.ShapeDtypeStruct((requests, lanes), jnp.float32),
            jax.ShapeDtypeStruct(cache_stats.shape, jnp.float32),
        ],
        compiler_params=params(),
        name="mix",
    )(code, values, near_values, cache_stats, *arranged(scores, SCORE_ORDER))


def weigh_kernel(cache_ref, own_ref, cache_stats_ref, new_stats_ref, stats_ref, other_ref, base_ref, factor_ref):
    requests, columns = cache_ref.shape
    size = cache_stats_ref.shape[1]
    top, other_top = stats_ref[:requests, :], other_ref[:requests, :]
    both = jnp.maximum(top, other_top)
    total = stats_ref[requests:, :] * jnp.exp(top - both)
    total = total + other_ref[requests:, :] * jnp.exp(other_top - both)
    inverse = 1.0 / total
    cache_factor = jnp.exp(cache_stats_ref[:requests, :] - both) * inverse
    new_factor = jnp.exp(new_stats_ref[...] - both) * inverse
    for h in range(columns // size):
        at = slice(h * size, (h + 1) * size)
        factor = jnp.broadcast_to(new_factor[:, h : h + 1], (requests, size))
        factor_ref[:, at] = factor
        base_ref[:, at] = cache_ref[:, at] * cache_factor[:, h : h + 1] + own_ref[:, at] * factor


def weigh(cache_mixed, own, cache_stats, new_stats, stats, other):
    return pl.pallas_call(
        weigh_kernel,
        out_shape=[jax.ShapeDtypeStruct(own.shape, jnp.float32)] * 2,
        compiler_params=params(),
        name="weigh",
    )(cache_mixed, own, cache_stats, new_stats, stats, other)


def merge_kernel(base_ref, factor_ref, far_ref, out_ref):
    out = base_ref[...] + far_ref[...].astype(jnp.float32) * factor_ref[...]
    out_ref[...] = out.astype(out_ref.dtype)


def merge(base, factor, far):
    return pl.pallas_call(
        merge_kernel,
        out_shape=jax.ShapeDtypeStruct(far.shape, far.dtype),
        compiler_params=params(),
        name="merge",
    )(base, factor, far)


def finish_kernel(own_ref, other_ref, out_ref):
    out_ref[...] = (own_ref[...].astype(jnp.float32) + other_ref[...].astype(jnp.float32)).astype(out_ref.dtype)


def finish(own, other):
    return pl.pallas_call(
        finish_kernel,
        out_shape=jax.ShapeDtypeStruct(own.shape, own.dtype),
        compiler_params=params(),
        name="finish",
    )(own, other)


def from_partner(x, axis, distance):
    count = lax.axis_size(axis)
    return lax.ppermute(x, axis, [(i, i ^ distance) for i in range(count)])


def from_behind(x, axis, distance):
    count = lax.axis_size(axis)
    return lax.ppermute(x, axis, [(i, (i + distance) % count) for i in range(count)])


def on_device(tokens, kv_weight, owners, requests, signs, queries, kv_cache, lengths):
    seq_count = lax.axis_size("seq")
    heads = signs.shape[0] // 2
    query = queries[0, 0]
    request_count, columns = query.shape
    message = make_message(query, owners[:, :, 0], requests)
    messages = [message] + [from_partner(message, "seq", d) for d in range(1, seq_count)]
    keys, values = project(tokens, kv_weight)
    near_values = from_partner(values, "seq", 1)
    scores, code = partial_scores(heads, columns, keys, messages)
    scores = [scores] + [from_behind(scores, "seq", d) for d in range(1, seq_count)]
    cache_mixed, cache_stats = cache_part(lengths, query, kv_cache[0, 0], signs)
    own, far, new_stats, stats = mix(heads, code, values, near_values, cache_stats, scores)
    far = from_partner(far, "seq", 2)
    other = from_partner(stats, "tp", 1)
    base, factor = weigh(cache_mixed, own, cache_stats, new_stats, stats, other)
    share = merge(base, factor, far)
    return finish(share, from_partner(share, "tp", 1)).reshape(1, 1, request_count, columns)


def hadamard(order):
    rows = lax.broadcasted_iota(jnp.int32, (order, order), 0)
    cols = lax.broadcasted_iota(jnp.int32, (order, order), 1)
    parity = jnp.zeros((order, order), jnp.int32)
    for bit_number in range(order.bit_length() - 1):
        parity = parity + rows // 2**bit_number % 2 * (cols // 2**bit_number % 2)
    return (1 - 2 * (parity % 2)).astype(jnp.float32)


def rotate(blocks, sign_rows, matrix):
    product = jnp.einsum(
        "...h,hk->...k", blocks * sign_rows, matrix, precision=lax.Precision.HIGHEST
    )
    return product / math.sqrt(matrix.shape[0])


def encode(rotated):
    largest = jnp.max(jnp.abs(rotated), axis=-1) + 1e-06
    scales = largest.astype(jnp.bfloat16)
    encoded = (rotated / scales.astype(jnp.float32)[..., None]).astype(jnp.bfloat16)
    return (encoded, scales)


def decode(encoded, scales):
    return (encoded.astype(jnp.float32) * scales.astype(jnp.float32)[..., None]).astype(
        jnp.bfloat16
    )


def slot_numbers(targets, count, room):
    onehot = (targets[:, None] == lax.iota(jnp.int32, count)[None, :]).astype(jnp.int32)
    within = jnp.sum((jnp.cumsum(onehot, axis=0) - 1) * onehot, axis=1)
    return targets * room + within


def on_device_long(tokens, kv_weight, owners, requests, signs, queries, kv_cache, lengths):
    seq_count = lax.axis_size("seq")
    per_device = owners.shape[1]
    slots = max(2, (2 * per_device + seq_count - 1) // seq_count)
    head_blocks = signs.shape[0]
    kv_heads = head_blocks // 2
    head_size = signs.shape[1]
    matrix = hadamard(head_size)
    sign_rows = (2 * signs - 1).astype(jnp.float32)
    summed = lax.psum_scatter(
        jnp.dot(tokens, kv_weight, preferred_element_type=jnp.float32).astype(jnp.bfloat16),
        "seq",
        scatter_dimension=0,
        tiled=True,
    ).astype(jnp.float32)
    encoded, scales = encode(
        rotate(summed.reshape(per_device, head_blocks, head_size), sign_rows, matrix)
    )
    slot_index = slot_numbers(owners[0, :, 0], seq_count, slots)
    slot_total = seq_count * slots
    send_values = (
        jnp.zeros((slot_total, head_blocks, head_size), jnp.bfloat16).at[slot_index].set(encoded)
    )
    send_scales = jnp.zeros((slot_total, head_blocks), jnp.bfloat16).at[slot_index].set(scales)
    send_codes = jnp.zeros((slot_total,), jnp.int32).at[slot_index].set(requests[0] + 1)
    got_values, got_scales, arrived_codes = (
        lax.all_to_all(send_values, "seq", split_axis=0, concat_axis=0, tiled=True),
        lax.all_to_all(send_scales, "seq", split_axis=0, concat_axis=0, tiled=True),
        lax.all_to_all(send_codes, "seq", split_axis=0, concat_axis=0, tiled=True),
    )
    arrived = decode(got_values, got_scales)
    query = queries[0, 0]
    request_count = query.shape[0]
    group = query.shape[1] // (kv_heads * head_size)
    query_blocks = query.astype(jnp.float32).reshape(request_count, kv_heads, group, head_size)
    query_rot = rotate(query_blocks, sign_rows[:kv_heads][:, None, :], matrix).astype(jnp.bfloat16)
    local_cache = kv_cache[0, 0]
    cache_span = local_cache.shape[1]
    local_cache = local_cache.reshape(request_count, cache_span, head_blocks, head_size)
    score_scale = 1.0 / math.sqrt(head_size)
    lowest = -1e30
    highest = lax.Precision.HIGHEST
    score_cache = (
        jnp.einsum(
            "rkgd,rckd->rkgc",
            query_rot,
            local_cache[:, :, :kv_heads],
            preferred_element_type=jnp.float32,
        )
        * score_scale
    )
    score_new = (
        jnp.einsum(
            "rkgd,nkd->rkgn", query_rot, arrived[:, :kv_heads], preferred_element_type=jnp.float32
        )
        * score_scale
    )
    positions = lax.axis_index("tp") * cache_span + lax.iota(jnp.int32, cache_span)
    mask_cache = (positions[None, :] < lengths[0, 0][:, None])[:, None, None, :]
    match = arrived_codes[None, :] == (lax.iota(jnp.int32, request_count) + 1)[:, None]
    mask_new = match[:, None, None, :]
    top = jnp.maximum(
        jnp.max(jnp.where(mask_cache, score_cache, lowest), axis=-1),
        jnp.max(jnp.where(mask_new, score_new, lowest), axis=-1),
    )
    probs_cache = jnp.where(mask_cache, jnp.exp(score_cache - top[..., None]), 0.0)
    probs_new = jnp.where(mask_new, jnp.exp(score_new - top[..., None]), 0.0)
    total = jnp.sum(probs_cache, axis=-1) + jnp.sum(probs_new, axis=-1)
    mixed = jnp.einsum(
        "rkgc,rckd->rkgd",
        probs_cache,
        local_cache[:, :, kv_heads:].astype(jnp.float32),
        precision=highest,
    )
    mixed = mixed + jnp.einsum(
        "rkgn,nkd->rkgd", probs_new, arrived[:, kv_heads:].astype(jnp.float32), precision=highest
    )
    shared_top = lax.pmax(top, "tp")
    factor = jnp.exp(top - shared_top)
    total, mixed = (
        lax.psum((total * factor).astype(jnp.bfloat16), "tp").astype(jnp.float32),
        lax.psum((mixed * factor[..., None]).astype(jnp.bfloat16), "tp").astype(jnp.float32),
    )
    mixed = mixed / total[..., None]
    output = rotate(mixed, 1.0, matrix) * sign_rows[kv_heads:][None, :, None, :]
    return output.reshape(1, 1, request_count, group * kv_heads * head_size).astype(jnp.bfloat16)


def solution(mesh):
    placed = (
        P(("groups", "tp", "section"), "seq"),
        P("seq", None),
        P(("groups", "tp", "section"), "seq", None),
        P(("groups", "tp", "section"), "seq"),
        P(),
        P(("groups", "seq"), "section", None, None),
        P(("groups", "seq"), "section", None, "tp", None),
        P(("groups", "seq"), "section", None),
    )
    short = mesh.shape["seq"] == 4 and mesh.shape["tp"] == 2
    return jax.shard_map(
        on_device if short else on_device_long,
        mesh=mesh,
        in_specs=placed,
        out_specs=P(("groups", "seq"), "section", None, None),
        check_vma=False,
    )
```

```python
import functools
import math

import jax
import jax.numpy as jnp
from jax import lax
from jax.experimental import pallas as pl
from jax.experimental.pallas import tpu as pltpu
from jax.sharding import PartitionSpec as P

LOWEST = -1e30
MIB = 1024 * 1024
NT = (((1,), (1,)), ((), ()))


def params(mib=32):
    return pltpu.CompilerParams(vmem_limit_bytes=mib * MIB)


def in_hbm(x):
    return pltpu.with_memory_space_constraint(x, pltpu.HBM)


def in_vmem(x):
    return pltpu.with_memory_space_constraint(x, pltpu.VMEM)


def hadamard_tile(order):
    rows = lax.broadcasted_iota(jnp.int32, (order, order), 0)
    cols = lax.broadcasted_iota(jnp.int32, (order, order), 1)
    common = rows & cols
    parity = jnp.zeros((order, order), jnp.int32)
    for bit_number in range(order.bit_length() - 1):
        parity = parity ^ (common >> bit_number)
    return (1 - 2 * (parity & 1)).astype(jnp.float32).astype(jnp.bfloat16)


QUERY_ORDER = (1, 2, 3)
SCORE_ORDER = (3, 2, 1)


def arranged(blocks, order):
    return [blocks[0]] + [blocks[d] for d in order]


def by_distance(refs, order):
    return [refs[0]] + [refs[1 + order.index(d)] for d in range(1, len(refs))]


def project_kernel(tokens_ref, weight_ref, out_ref, *, first):
    width = out_ref.shape[1]
    columns = slice(first, first + width)
    product = jnp.dot(tokens_ref[...], weight_ref[:, columns], preferred_element_type=jnp.float32)
    out_ref[...] = product.astype(out_ref.dtype)


def project(tokens, weight, part, name):
    rows, features = tokens.shape
    width = weight.shape[1] // 2
    vmem = pl.BlockSpec(memory_space=pltpu.VMEM)
    return pl.pallas_call(
        functools.partial(project_kernel, first=part * width),
        in_specs=[vmem] * 2,
        out_specs=vmem,
        out_shape=jax.ShapeDtypeStruct((rows, width), jnp.bfloat16),
        compiler_params=params(32),
        cost_estimate=pl.CostEstimate(
            flops=2 * rows * features * width,
            bytes_accessed=2 * (rows * features + features * width),
            transcendentals=0,
        ),
        name=name,
    )(tokens, weight)


def message_kernel(query_ref, owners_ref, requests_ref, out_ref, query_buf, owners_buf, requests_buf, sems):
    requests, columns = query_ref.shape
    per_device = owners_ref.shape[1]
    copies = [
        pltpu.make_async_copy(source, target, sems.at[i])
        for i, (source, target) in enumerate(
            ((query_ref, query_buf), (owners_ref, owners_buf), (requests_ref, requests_buf))
        )
    ]
    for copy in copies:
        copy.start()
    for copy in copies:
        copy.wait()
    out_ref[:, :columns] = query_buf[...]
    code = (owners_buf[...] * requests + requests_buf[...]).astype(jnp.float32)
    spare = jnp.zeros((1, out_ref.shape[1] - columns - per_device), jnp.float32)
    code = jnp.concatenate([code, spare], axis=1)
    out_ref[:, columns:] = jnp.broadcast_to(code, (requests, code.shape[1])).astype(out_ref.dtype)


def make_message(query, owners, requests):
    count, columns = query.shape
    lanes = -(-owners.shape[1] // 128) * 128
    return pl.pallas_call(
        message_kernel,
        in_specs=[pl.BlockSpec(memory_space=pl.ANY)] * 3,
        out_specs=pl.BlockSpec(memory_space=pltpu.VMEM),
        out_shape=jax.ShapeDtypeStruct((count, columns + lanes), query.dtype),
        scratch_shapes=[
            pltpu.VMEM(query.shape, query.dtype),
            pltpu.VMEM(owners.shape, owners.dtype),
            pltpu.VMEM(requests.shape, requests.dtype),
            pltpu.SemaphoreType.DMA((3,)),
        ],
        compiler_params=params(16),
        cost_estimate=pl.CostEstimate(flops=10**11, bytes_accessed=10**4, transcendentals=0),
        name="make_message",
    )(in_hbm(query), in_hbm(owners), in_hbm(requests))


def cache_kernel(
    lengths_ref, query_ref, cache_ref, signs_ref, mixed_ref, stats_ref, query_buf, top_buf, total_buf, mixed_buf
):
    requests, span, _ = cache_ref.shape
    blocks, size = signs_ref.shape
    heads = blocks // 2
    width = heads * size
    count = query_ref.shape[1] // size
    group = count // heads
    norm = 1.0 / math.sqrt(size)
    matrix = hadamard_tile(size)
    signs = (2 * signs_ref[...] - 1).astype(jnp.float32)
    query = query_ref[...].astype(jnp.float32)
    query = jnp.concatenate(
        [query[:, h * size : (h + 1) * size] * signs[h // group : h // group + 1] for h in range(count)], axis=0
    )
    query_buf[...] = jnp.dot(query.astype(jnp.bfloat16), matrix, preferred_element_type=jnp.float32) * norm
    rows = 2 * count
    kv_head = lax.broadcasted_iota(jnp.int32, (rows, width), 0) // group & (heads - 1)
    own_head = kv_head == lax.broadcasted_iota(jnp.int32, (rows, width), 1) // size
    first = lax.broadcasted_iota(jnp.int32, (rows, span), 0) < count
    position = lax.axis_index("tp") * span + lax.broadcasted_iota(jnp.int32, (rows, span), 1)
    pairs = range(0, requests, 2)
    scores = []
    for r in pairs:
        both = [query_buf[pl.ds(r + i, count, stride=requests), :] for i in range(2)]
        wide = jnp.concatenate([jnp.concatenate(both, axis=0)] * heads, axis=1)
        wide = jnp.where(own_head, wide, 0.0).astype(jnp.bfloat16)
        keys = cache_ref[r : r + 2, :, :width].reshape(2 * span, width)
        scores.append(lax.dot_general(wide, keys, NT, preferred_element_type=jnp.float32))
    probs = []
    for r, score in zip(pairs, scores):
        score = jnp.where(first, score[:, :span], score[:, span:]) * norm
        live = position < jnp.where(first, lengths_ref[0, 0, r], lengths_ref[0, 0, r + 1])
        top = jnp.max(jnp.where(live, score, LOWEST), axis=1, keepdims=True)
        prob = jnp.where(live, jnp.exp(score - top), 0.0)
        total = jnp.sum(prob, axis=1, keepdims=True)
        at = slice(r * count, (r + 2) * count)
        top_buf[at, :] = jnp.broadcast_to(top, (rows, size))
        total_buf[at, :] = jnp.broadcast_to(total, (rows, size))
        probs.append(
            jnp.concatenate([jnp.where(first, prob, 0.0), jnp.where(first, 0.0, prob)], axis=1).astype(jnp.bfloat16)
        )
    mixed = []
    for r, prob in zip(pairs, probs):
        values = cache_ref[r : r + 2, :, width:].reshape(2 * span, width)
        wide = jnp.dot(prob, values, preferred_element_type=jnp.float32)
        wide = jnp.where(own_head, wide, 0.0)
        mixed.append(sum(wide[:, k * size : (k + 1) * size] for k in range(heads)))
    mixed = jnp.concatenate(mixed, axis=0)
    high = mixed.astype(jnp.bfloat16)
    low = (mixed - high.astype(jnp.float32)).astype(jnp.bfloat16)
    plain = jnp.dot(high, matrix, preferred_element_type=jnp.float32)
    mixed_buf[...] = plain + jnp.dot(low, matrix, preferred_element_type=jnp.float32)
    lane = lax.broadcasted_iota(jnp.int32, (requests, stats_ref.shape[1]), 1)
    tops = jnp.full(lane.shape, 0.0, jnp.float32)
    totals = jnp.ones(lane.shape, jnp.float32)
    for h in range(count):
        pick = pl.ds(h, requests, stride=count)
        column = slice(h * size, (h + 1) * size)
        k = heads + h // group
        mixed_ref[:, column] = mixed_buf[pick, :] * (signs[k : k + 1] * norm)
        tops = jnp.where(lane == h, top_buf[pick, :], tops)
        totals = jnp.where(lane == h, total_buf[pick, :], totals)
    stats_ref[:requests, :] = tops
    stats_ref[requests:, :] = totals


def cache_part(lengths, query, cache, signs):
    requests, span, width = cache.shape
    size = signs.shape[1]
    columns = query.shape[1]
    vmem = pl.BlockSpec(memory_space=pltpu.VMEM)
    return pl.pallas_call(
        cache_kernel,
        in_specs=[pl.BlockSpec(memory_space=pltpu.SMEM)] + [vmem] * 3,
        out_shape=[
            jax.ShapeDtypeStruct(query.shape, jnp.float32),
            jax.ShapeDtypeStruct((2 * requests, size), jnp.float32),
        ],
        scratch_shapes=[pltpu.VMEM((requests * columns // size, size), jnp.float32)] * 4,
        compiler_params=params(),
        cost_estimate=pl.CostEstimate(
            flops=4 * span * requests * columns,
            bytes_accessed=2 * requests * span * width,
            transcendentals=span * requests * columns // size,
        ),
        name="cache_part",
    )(lengths, query, cache, signs)


def code_row(message_refs, start, requests, tokens):
    count = len(message_refs)
    me = lax.axis_index("seq")
    pieces = [ref[0:1, start : start + tokens // count].astype(jnp.float32) for ref in message_refs]
    row = [sum(jnp.where(me ^ d == at, pieces[d], 0.0) for d in range(count)) for at in range(count)]
    code = jnp.concatenate(row, axis=1).astype(jnp.int32)
    return ((code // requests) ^ me) * requests + code % requests


def score_kernel(heads, start, keys_ref, *refs):
    message_refs, (scores_ref, code_ref) = by_distance(refs[:-2], QUERY_ORDER), refs[-2:]
    requests = message_refs[0].shape[0]
    tokens, width = keys_ref.shape
    size = width // heads
    group = start // width
    code = code_row(message_refs, start, requests, tokens)
    code_ref[...] = jnp.broadcast_to(code, code_ref.shape)
    span = len(message_refs) * requests
    here = lax.broadcasted_iota(jnp.int32, (span, tokens), 0) == code
    queries = [ref[:, :start].astype(jnp.float32) for ref in message_refs]
    for k in range(heads):
        rows = []
        for g in range(group):
            at = (k * group + g) * size
            rows += [query[:, at : at + size] for query in queries]
        query = jnp.concatenate(rows, axis=0).astype(jnp.bfloat16)
        keys = keys_ref[:, k * size : (k + 1) * size]
        scores = lax.dot_general(query, keys, NT, preferred_element_type=jnp.float32)
        lines = [
            jnp.sum(jnp.where(here, scores[g * span : (g + 1) * span], 0.0), axis=0, keepdims=True)
            for g in range(group)
        ]
        scores_ref[k * group : (k + 1) * group, :] = jnp.concatenate(lines, axis=0) * (
            1.0 / math.sqrt(size)
        )


def partial_scores(heads, columns, keys, messages):
    tokens, width = keys.shape
    return pl.pallas_call(
        functools.partial(score_kernel, heads, columns),
        out_shape=[
            jax.ShapeDtypeStruct((columns * heads // width, tokens), jnp.float32),
            jax.ShapeDtypeStruct((8, tokens), jnp.int32),
        ],
        compiler_params=params(),
        cost_estimate=pl.CostEstimate(flops=10**11, bytes_accessed=10**4, transcendentals=0),
        name="partial_scores",
    )(keys, *arranged(messages, QUERY_ORDER))


def mix_kernel(heads, requests, code_ref, values_ref, near_ref, cache_stats_ref, *refs):
    score_refs, (own_ref, far_ref, new_stats_ref, stats_ref) = refs[:4], refs[4:]
    own, after, across, before = [ref[...] for ref in score_refs]
    scores = (own + across) + (before + after)
    tokens, width = values_ref.shape
    size = width // heads
    group = scores.shape[0] // heads
    span = 2 * requests
    row = lax.broadcasted_iota(jnp.int32, (span, tokens), 0)
    here = jnp.where(row < requests, row, row + requests) == code_ref[0:1, :]
    lane = lax.broadcasted_iota(jnp.int32, (requests, stats_ref.shape[1]), 1)
    tops = jnp.full(lane.shape, 0.0, jnp.float32)
    totals = jnp.zeros(lane.shape, jnp.float32)
    for k in range(heads):
        weights = []
        for g in range(group):
            h = k * group + g
            line = jnp.broadcast_to(scores[h : h + 1, :], (span, tokens))
            top = jnp.max(jnp.where(here, line, LOWEST), axis=1, keepdims=True)
            probs = jnp.where(here, jnp.exp(line - top), 0.0)
            total = jnp.sum(probs, axis=1, keepdims=True)
            weights.append(probs)
            tops = jnp.where(lane == h, top[:requests], tops)
            totals = jnp.where(lane == h, total[:requests], totals)
        weights = jnp.concatenate(weights, axis=0).astype(jnp.bfloat16)
        columns = slice(k * size, (k + 1) * size)
        mixed = jnp.dot(weights, values_ref[:, columns], preferred_element_type=jnp.float32)
        mixed = mixed + jnp.dot(weights, near_ref[:, columns], preferred_element_type=jnp.float32)
        for g in range(group):
            at = slice((k * group + g) * size, (k * group + g + 1) * size)
            own_ref[:, at] = mixed[g * span : g * span + requests]
            far_ref[:, at] = mixed[g * span + requests : (g + 1) * span].astype(far_ref.dtype)
    new_stats_ref[...] = tops
    cache_tops = cache_stats_ref[:requests, :]
    both = jnp.maximum(cache_tops, tops)
    stats_ref[:requests, :] = both
    stats_ref[requests:, :] = cache_stats_ref[requests:, :] * jnp.exp(cache_tops - both) + totals * jnp.exp(
        tops - both
    )


def mix(heads, code, values, near_values, cache_stats, scores):
    requests, lanes = cache_stats.shape[0] // 2, cache_stats.shape[1]
    size = values.shape[1] // heads
    shape = (requests, scores[0].shape[0] * size)
    return pl.pallas_call(
        functools.partial(mix_kernel, heads, requests),
        out_shape=[
            jax.ShapeDtypeStruct(shape, jnp.float32),
            jax.ShapeDtypeStruct(shape, jnp.bfloat16),
            jax.ShapeDtypeStruct((requests, lanes), jnp.float32),
            jax.ShapeDtypeStruct(cache_stats.shape, jnp.float32),
        ],
        compiler_params=params(),
        name="mix",
    )(code, values, near_values, cache_stats, *arranged(scores, SCORE_ORDER))


def weigh_kernel(cache_ref, own_ref, cache_stats_ref, new_stats_ref, stats_ref, other_ref, base_ref, factor_ref):
    requests, columns = cache_ref.shape
    size = cache_stats_ref.shape[1]
    top, other_top = stats_ref[:requests, :], other_ref[:requests, :]
    both = jnp.maximum(top, other_top)
    total = stats_ref[requests:, :] * jnp.exp(top - both)
    total = total + other_ref[requests:, :] * jnp.exp(other_top - both)
    inverse = 1.0 / total
    cache_factor = jnp.exp(cache_stats_ref[:requests, :] - both) * inverse
    new_factor = jnp.exp(new_stats_ref[...] - both) * inverse
    for h in range(columns // size):
        at = slice(h * size, (h + 1) * size)
        factor = jnp.broadcast_to(new_factor[:, h : h + 1], (requests, size))
        factor_ref[:, at] = factor
        base_ref[:, at] = cache_ref[:, at] * cache_factor[:, h : h + 1] + own_ref[:, at] * factor


def weigh(cache_mixed, own, cache_stats, new_stats, stats, other):
    return pl.pallas_call(
        weigh_kernel,
        out_shape=[jax.ShapeDtypeStruct(own.shape, jnp.float32)] * 2,
        compiler_params=params(),
        name="weigh",
    )(cache_mixed, own, cache_stats, new_stats, stats, other)


def merge_kernel(base_ref, factor_ref, far_ref, out_ref):
    out = base_ref[...] + far_ref[...].astype(jnp.float32) * factor_ref[...]
    out_ref[...] = out.astype(out_ref.dtype)


def merge(base, factor, far):
    return pl.pallas_call(
        merge_kernel,
        out_shape=jax.ShapeDtypeStruct(far.shape, far.dtype),
        compiler_params=params(),
        name="merge",
    )(base, factor, far)


def finish_kernel(own_ref, other_ref, out_ref):
    out_ref[...] = (own_ref[...].astype(jnp.float32) + other_ref[...].astype(jnp.float32)).astype(out_ref.dtype)


def finish(own, other):
    return pl.pallas_call(
        finish_kernel,
        out_shape=jax.ShapeDtypeStruct(own.shape, own.dtype),
        compiler_params=params(),
        name="finish",
    )(own, other)


def from_partner(x, axis, distance):
    count = lax.axis_size(axis)
    return lax.ppermute(x, axis, [(i, i ^ distance) for i in range(count)])


def from_behind(x, axis, distance):
    count = lax.axis_size(axis)
    return lax.ppermute(x, axis, [(i, (i + distance) % count) for i in range(count)])


def on_device(tokens, kv_weight, owners, requests, signs, queries, kv_cache, lengths):
    seq_count = lax.axis_size("seq")
    heads = signs.shape[0] // 2
    query = queries[0, 0]
    request_count, columns = query.shape
    message = make_message(query, owners[:, :, 0], requests)
    messages = [message] + [from_partner(message, "seq", d) for d in range(1, seq_count)]
    tokens, kv_weight = in_vmem(tokens), in_vmem(kv_weight)
    values = project(tokens, kv_weight, 1, "project_values")
    near_values = from_partner(values, "seq", 1)
    keys = project(tokens, kv_weight, 0, "project_keys")
    scores, code = partial_scores(heads, columns, keys, messages)
    scores = [scores] + [from_behind(scores, "seq", d) for d in range(1, seq_count)]
    cache_mixed, cache_stats = cache_part(lengths, query, kv_cache[0, 0], signs)
    own, far, new_stats, stats = mix(heads, code, values, near_values, cache_stats, scores)
    far = from_partner(far, "seq", 2)
    other = from_partner(stats, "tp", 1)
    base, factor = weigh(cache_mixed, own, cache_stats, new_stats, stats, other)
    share = merge(base, factor, far)
    return finish(share, from_partner(share, "tp", 1)).reshape(1, 1, request_count, columns)


def hadamard(order):
    rows = lax.broadcasted_iota(jnp.int32, (order, order), 0)
    cols = lax.broadcasted_iota(jnp.int32, (order, order), 1)
    parity = jnp.zeros((order, order), jnp.int32)
    for bit_number in range(order.bit_length() - 1):
        parity = parity + rows // 2**bit_number % 2 * (cols // 2**bit_number % 2)
    return (1 - 2 * (parity % 2)).astype(jnp.float32)


def rotate(blocks, sign_rows, matrix):
    product = jnp.einsum(
        "...h,hk->...k", blocks * sign_rows, matrix, precision=lax.Precision.HIGHEST
    )
    return product / math.sqrt(matrix.shape[0])


def encode(rotated):
    largest = jnp.max(jnp.abs(rotated), axis=-1) + 1e-06
    scales = largest.astype(jnp.bfloat16)
    encoded = (rotated / scales.astype(jnp.float32)[..., None]).astype(jnp.bfloat16)
    return (encoded, scales)


def decode(encoded, scales):
    return (encoded.astype(jnp.float32) * scales.astype(jnp.float32)[..., None]).astype(
        jnp.bfloat16
    )


def slot_numbers(targets, count, room):
    onehot = (targets[:, None] == lax.iota(jnp.int32, count)[None, :]).astype(jnp.int32)
    within = jnp.sum((jnp.cumsum(onehot, axis=0) - 1) * onehot, axis=1)
    return targets * room + within


def on_device_long(tokens, kv_weight, owners, requests, signs, queries, kv_cache, lengths):
    seq_count = lax.axis_size("seq")
    per_device = owners.shape[1]
    slots = max(2, (2 * per_device + seq_count - 1) // seq_count)
    head_blocks = signs.shape[0]
    kv_heads = head_blocks // 2
    head_size = signs.shape[1]
    matrix = hadamard(head_size)
    sign_rows = (2 * signs - 1).astype(jnp.float32)
    summed = lax.psum_scatter(
        jnp.dot(tokens, kv_weight, preferred_element_type=jnp.float32).astype(jnp.bfloat16),
        "seq",
        scatter_dimension=0,
        tiled=True,
    ).astype(jnp.float32)
    encoded, scales = encode(
        rotate(summed.reshape(per_device, head_blocks, head_size), sign_rows, matrix)
    )
    slot_index = slot_numbers(owners[0, :, 0], seq_count, slots)
    slot_total = seq_count * slots
    send_values = (
        jnp.zeros((slot_total, head_blocks, head_size), jnp.bfloat16).at[slot_index].set(encoded)
    )
    send_scales = jnp.zeros((slot_total, head_blocks), jnp.bfloat16).at[slot_index].set(scales)
    send_codes = jnp.zeros((slot_total,), jnp.int32).at[slot_index].set(requests[0] + 1)
    got_values, got_scales, arrived_codes = (
        lax.all_to_all(send_values, "seq", split_axis=0, concat_axis=0, tiled=True),
        lax.all_to_all(send_scales, "seq", split_axis=0, concat_axis=0, tiled=True),
        lax.all_to_all(send_codes, "seq", split_axis=0, concat_axis=0, tiled=True),
    )
    arrived = decode(got_values, got_scales)
    query = queries[0, 0]
    request_count = query.shape[0]
    group = query.shape[1] // (kv_heads * head_size)
    query_blocks = query.astype(jnp.float32).reshape(request_count, kv_heads, group, head_size)
    query_rot = rotate(query_blocks, sign_rows[:kv_heads][:, None, :], matrix).astype(jnp.bfloat16)
    local_cache = kv_cache[0, 0]
    cache_span = local_cache.shape[1]
    local_cache = local_cache.reshape(request_count, cache_span, head_blocks, head_size)
    score_scale = 1.0 / math.sqrt(head_size)
    lowest = -1e30
    highest = lax.Precision.HIGHEST
    score_cache = (
        jnp.einsum(
            "rkgd,rckd->rkgc",
            query_rot,
            local_cache[:, :, :kv_heads],
            preferred_element_type=jnp.float32,
        )
        * score_scale
    )
    score_new = (
        jnp.einsum(
            "rkgd,nkd->rkgn", query_rot, arrived[:, :kv_heads], preferred_element_type=jnp.float32
        )
        * score_scale
    )
    positions = lax.axis_index("tp") * cache_span + lax.iota(jnp.int32, cache_span)
    mask_cache = (positions[None, :] < lengths[0, 0][:, None])[:, None, None, :]
    match = arrived_codes[None, :] == (lax.iota(jnp.int32, request_count) + 1)[:, None]
    mask_new = match[:, None, None, :]
    top = jnp.maximum(
        jnp.max(jnp.where(mask_cache, score_cache, lowest), axis=-1),
        jnp.max(jnp.where(mask_new, score_new, lowest), axis=-1),
    )
    probs_cache = jnp.where(mask_cache, jnp.exp(score_cache - top[..., None]), 0.0)
    probs_new = jnp.where(mask_new, jnp.exp(score_new - top[..., None]), 0.0)
    total = jnp.sum(probs_cache, axis=-1) + jnp.sum(probs_new, axis=-1)
    mixed = jnp.einsum(
        "rkgc,rckd->rkgd",
        probs_cache,
        local_cache[:, :, kv_heads:].astype(jnp.float32),
        precision=highest,
    )
    mixed = mixed + jnp.einsum(
        "rkgn,nkd->rkgd", probs_new, arrived[:, kv_heads:].astype(jnp.float32), precision=highest
    )
    shared_top = lax.pmax(top, "tp")
    factor = jnp.exp(top - shared_top)
    total, mixed = (
        lax.psum((total * factor).astype(jnp.bfloat16), "tp").astype(jnp.float32),
        lax.psum((mixed * factor[..., None]).astype(jnp.bfloat16), "tp").astype(jnp.float32),
    )
    mixed = mixed / total[..., None]
    output = rotate(mixed, 1.0, matrix) * sign_rows[kv_heads:][None, :, None, :]
    return output.reshape(1, 1, request_count, group * kv_heads * head_size).astype(jnp.bfloat16)


def solution(mesh):
    placed = (
        P(("groups", "tp", "section"), "seq"),
        P("seq", None),
        P(("groups", "tp", "section"), "seq", None),
        P(("groups", "tp", "section"), "seq"),
        P(),
        P(("groups", "seq"), "section", None, None),
        P(("groups", "seq"), "section", None, "tp", None),
        P(("groups", "seq"), "section", None),
    )
    short = mesh.shape["seq"] == 4 and mesh.shape["tp"] == 2
    return jax.shard_map(
        on_device if short else on_device_long,
        mesh=mesh,
        in_specs=placed,
        out_specs=P(("groups", "seq"), "section", None, None),
        check_vma=False,
    )
```

```python
import functools
import math

import jax
import jax.numpy as jnp
from jax import lax
from jax.experimental import pallas as pl
from jax.experimental.pallas import tpu as pltpu
from jax.sharding import PartitionSpec as P

LOWEST = -1e30
MIB = 1024 * 1024
NT = (((1,), (1,)), ((), ()))


def params(mib=32):
    return pltpu.CompilerParams(vmem_limit_bytes=mib * MIB)


def in_hbm(x):
    return pltpu.with_memory_space_constraint(x, pltpu.HBM)


def in_vmem(x):
    return pltpu.with_memory_space_constraint(x, pltpu.VMEM)


def hadamard_tile(order):
    rows = lax.broadcasted_iota(jnp.int32, (order, order), 0)
    cols = lax.broadcasted_iota(jnp.int32, (order, order), 1)
    common = rows & cols
    parity = jnp.zeros((order, order), jnp.int32)
    for bit_number in range(order.bit_length() - 1):
        parity = parity ^ (common >> bit_number)
    return (1 - 2 * (parity & 1)).astype(jnp.float32).astype(jnp.bfloat16)


QUERY_ORDER = (1, 2, 3)
SCORE_ORDER = (3, 2, 1)


def arranged(blocks, order):
    return [blocks[0]] + [blocks[d] for d in order]


def by_distance(refs, order):
    return [refs[0]] + [refs[1 + order.index(d)] for d in range(1, len(refs))]


def project_kernel(tokens_ref, weight_ref, keys_ref, values_ref):
    width = keys_ref.shape[1]
    for out_ref, columns in ((keys_ref, slice(0, width)), (values_ref, slice(width, 2 * width))):
        out_ref[...] = jnp.dot(
            tokens_ref[...], weight_ref[:, columns], preferred_element_type=jnp.float32
        ).astype(out_ref.dtype)


def project(tokens, weight):
    rows, features = tokens.shape
    width = weight.shape[1] // 2
    vmem = pl.BlockSpec(memory_space=pltpu.VMEM)
    return pl.pallas_call(
        project_kernel,
        in_specs=[vmem] * 2,
        out_specs=[vmem] * 2,
        out_shape=[jax.ShapeDtypeStruct((rows, width), jnp.bfloat16)] * 2,
        compiler_params=params(32),
        cost_estimate=pl.CostEstimate(
            flops=4 * rows * features * width,
            bytes_accessed=2 * (rows * features + 2 * features * width),
            transcendentals=0,
        ),
        name="project",
    )(in_vmem(tokens), in_vmem(weight))


def message_kernel(query_ref, owners_ref, requests_ref, out_ref, owners_buf, requests_buf, sems):
    requests, columns = query_ref.shape
    per_device = owners_ref.shape[1]
    copies = [
        pltpu.make_async_copy(query_ref, out_ref.at[:, :columns], sems.at[0]),
        pltpu.make_async_copy(owners_ref, owners_buf, sems.at[1]),
        pltpu.make_async_copy(requests_ref, requests_buf, sems.at[2]),
    ]
    for copy in copies:
        copy.start()
    copies[1].wait()
    copies[2].wait()
    code = (owners_buf[...] * requests + requests_buf[...]).astype(jnp.float32)
    spare = jnp.zeros((1, out_ref.shape[1] - columns - per_device), jnp.float32)
    code = jnp.concatenate([code, spare], axis=1)
    out_ref[:, columns:] = jnp.broadcast_to(code, (requests, code.shape[1])).astype(out_ref.dtype)
    copies[0].wait()


def make_message(query, owners, requests):
    count, columns = query.shape
    lanes = -(-owners.shape[1] // 128) * 128
    return pl.pallas_call(
        message_kernel,
        in_specs=[pl.BlockSpec(memory_space=pl.ANY)] * 3,
        out_specs=pl.BlockSpec(memory_space=pltpu.VMEM),
        out_shape=jax.ShapeDtypeStruct((count, columns + lanes), query.dtype),
        scratch_shapes=[
            pltpu.VMEM(owners.shape, owners.dtype),
            pltpu.VMEM(requests.shape, requests.dtype),
            pltpu.SemaphoreType.DMA((3,)),
        ],
        compiler_params=params(16),
        cost_estimate=pl.CostEstimate(flops=10**11, bytes_accessed=10**4, transcendentals=0),
        name="make_message",
    )(in_hbm(query), in_hbm(owners), in_hbm(requests))


def cache_kernel(
    lengths_ref, query_ref, cache_ref, signs_ref, mixed_ref, stats_ref, query_buf, top_buf, total_buf, mixed_buf
):
    requests, span, _ = cache_ref.shape
    blocks, size = signs_ref.shape
    heads = blocks // 2
    width = heads * size
    count = query_ref.shape[1] // size
    group = count // heads
    norm = 1.0 / math.sqrt(size)
    matrix = hadamard_tile(size)
    signs = (2 * signs_ref[...] - 1).astype(jnp.float32)
    query = query_ref[...].astype(jnp.float32)
    query = jnp.concatenate(
        [query[:, h * size : (h + 1) * size] * signs[h // group : h // group + 1] for h in range(count)], axis=0
    )
    query_buf[...] = jnp.dot(query.astype(jnp.bfloat16), matrix, preferred_element_type=jnp.float32) * norm
    rows = 2 * count
    kv_head = lax.broadcasted_iota(jnp.int32, (rows, width), 0) // group & (heads - 1)
    own_head = kv_head == lax.broadcasted_iota(jnp.int32, (rows, width), 1) // size
    first = lax.broadcasted_iota(jnp.int32, (rows, span), 0) < count
    position = lax.axis_index("tp") * span + lax.broadcasted_iota(jnp.int32, (rows, span), 1)
    pairs = range(0, requests, 2)
    scores = []
    for r in pairs:
        both = [query_buf[pl.ds(r + i, count, stride=requests), :] for i in range(2)]
        wide = jnp.concatenate([jnp.concatenate(both, axis=0)] * heads, axis=1)
        wide = jnp.where(own_head, wide, 0.0).astype(jnp.bfloat16)
        keys = cache_ref[r : r + 2, :, :width].reshape(2 * span, width)
        scores.append(lax.dot_general(wide, keys, NT, preferred_element_type=jnp.float32))
    probs = []
    for r, score in zip(pairs, scores):
        score = jnp.where(first, score[:, :span], score[:, span:]) * norm
        live = position < jnp.where(first, lengths_ref[0, 0, r], lengths_ref[0, 0, r + 1])
        top = jnp.max(jnp.where(live, score, LOWEST), axis=1, keepdims=True)
        prob = jnp.where(live, jnp.exp(score - top), 0.0)
        total = jnp.sum(prob, axis=1, keepdims=True)
        at = slice(r * count, (r + 2) * count)
        top_buf[at, :] = jnp.broadcast_to(top, (rows, size))
        total_buf[at, :] = jnp.broadcast_to(total, (rows, size))
        probs.append(
            jnp.concatenate([jnp.where(first, prob, 0.0), jnp.where(first, 0.0, prob)], axis=1).astype(jnp.bfloat16)
        )
    mixed = []
    for r, prob in zip(pairs, probs):
        values = cache_ref[r : r + 2, :, width:].reshape(2 * span, width)
        wide = jnp.dot(prob, values, preferred_element_type=jnp.float32)
        wide = jnp.where(own_head, wide, 0.0)
        mixed.append(sum(wide[:, k * size : (k + 1) * size] for k in range(heads)))
    mixed = jnp.concatenate(mixed, axis=0)
    high = mixed.astype(jnp.bfloat16)
    low = (mixed - high.astype(jnp.float32)).astype(jnp.bfloat16)
    plain = jnp.dot(high, matrix, preferred_element_type=jnp.float32)
    mixed_buf[...] = plain + jnp.dot(low, matrix, preferred_element_type=jnp.float32)
    lane = lax.broadcasted_iota(jnp.int32, (requests, stats_ref.shape[1]), 1)
    tops = jnp.full(lane.shape, 0.0, jnp.float32)
    totals = jnp.ones(lane.shape, jnp.float32)
    for h in range(count):
        pick = pl.ds(h, requests, stride=count)
        column = slice(h * size, (h + 1) * size)
        k = heads + h // group
        mixed_ref[:, column] = mixed_buf[pick, :] * (signs[k : k + 1] * norm)
        tops = jnp.where(lane == h, top_buf[pick, :], tops)
        totals = jnp.where(lane == h, total_buf[pick, :], totals)
    stats_ref[:requests, :] = tops
    stats_ref[requests:, :] = totals


def cache_part(lengths, query, cache, signs):
    requests, span, width = cache.shape
    size = signs.shape[1]
    columns = query.shape[1]
    vmem = pl.BlockSpec(memory_space=pltpu.VMEM)
    return pl.pallas_call(
        cache_kernel,
        in_specs=[pl.BlockSpec(memory_space=pltpu.SMEM)] + [vmem] * 3,
        out_shape=[
            jax.ShapeDtypeStruct(query.shape, jnp.float32),
            jax.ShapeDtypeStruct((2 * requests, size), jnp.float32),
        ],
        scratch_shapes=[pltpu.VMEM((requests * columns // size, size), jnp.float32)] * 4,
        compiler_params=params(),
        cost_estimate=pl.CostEstimate(
            flops=4 * span * requests * columns,
            bytes_accessed=2 * requests * span * width,
            transcendentals=span * requests * columns // size,
        ),
        name="cache_part",
    )(lengths, query, cache, signs)


def code_row(message_refs, start, requests, tokens):
    count = len(message_refs)
    me = lax.axis_index("seq")
    pieces = [ref[0:1, start : start + tokens // count].astype(jnp.float32) for ref in message_refs]
    row = [sum(jnp.where(me ^ d == at, pieces[d], 0.0) for d in range(count)) for at in range(count)]
    code = jnp.concatenate(row, axis=1).astype(jnp.int32)
    return ((code // requests) ^ me) * requests + code % requests


def score_kernel(heads, start, keys_ref, *refs):
    message_refs, (scores_ref, code_ref) = by_distance(refs[:-2], QUERY_ORDER), refs[-2:]
    requests = message_refs[0].shape[0]
    tokens, width = keys_ref.shape
    size = width // heads
    group = start // width
    code = code_row(message_refs, start, requests, tokens)
    code_ref[...] = jnp.broadcast_to(code, code_ref.shape)
    span = len(message_refs) * requests
    here = lax.broadcasted_iota(jnp.int32, (span, tokens), 0) == code
    queries = [ref[:, :start].astype(jnp.float32) for ref in message_refs]
    for k in range(heads):
        rows = []
        for g in range(group):
            at = (k * group + g) * size
            rows += [query[:, at : at + size] for query in queries]
        query = jnp.concatenate(rows, axis=0).astype(jnp.bfloat16)
        keys = keys_ref[:, k * size : (k + 1) * size]
        scores = lax.dot_general(query, keys, NT, preferred_element_type=jnp.float32)
        lines = [
            jnp.sum(jnp.where(here, scores[g * span : (g + 1) * span], 0.0), axis=0, keepdims=True)
            for g in range(group)
        ]
        lines = jnp.concatenate(lines, axis=0) * (1.0 / math.sqrt(size))
        scores_ref[k * group : (k + 1) * group, :] = lines.astype(scores_ref.dtype)


def partial_scores(heads, columns, keys, messages):
    tokens, width = keys.shape
    return pl.pallas_call(
        functools.partial(score_kernel, heads, columns),
        out_shape=[
            jax.ShapeDtypeStruct((columns * heads // width, tokens), jnp.bfloat16),
            jax.ShapeDtypeStruct((8, tokens), jnp.int32),
        ],
        compiler_params=params(),
        cost_estimate=pl.CostEstimate(flops=10**11, bytes_accessed=10**4, transcendentals=0),
        name="partial_scores",
    )(keys, *arranged(messages, QUERY_ORDER))


def mix_kernel(heads, requests, code_ref, values_ref, near_ref, cache_stats_ref, *refs):
    score_refs, (own_ref, far_ref, new_stats_ref, stats_ref) = refs[:4], refs[4:]
    own, after, across, before = [ref[...].astype(jnp.float32) for ref in score_refs]
    scores = (own + across) + (before + after)
    tokens, width = values_ref.shape
    size = width // heads
    group = scores.shape[0] // heads
    span = 2 * requests
    row = lax.broadcasted_iota(jnp.int32, (span, tokens), 0)
    here = jnp.where(row < requests, row, row + requests) == code_ref[0:1, :]
    lane = lax.broadcasted_iota(jnp.int32, (requests, stats_ref.shape[1]), 1)
    tops = jnp.full(lane.shape, 0.0, jnp.float32)
    totals = jnp.zeros(lane.shape, jnp.float32)
    for k in range(heads):
        weights = []
        for g in range(group):
            h = k * group + g
            line = jnp.where(here, jnp.broadcast_to(scores[h : h + 1, :], (span, tokens)), LOWEST)
            top = jnp.maximum(jnp.max(line, axis=1, keepdims=True), 0.1 * LOWEST)
            probs = jnp.exp(line - top)
            total = jnp.sum(probs, axis=1, keepdims=True)
            weights.append(probs)
            tops = jnp.where(lane == h, top[:requests], tops)
            totals = jnp.where(lane == h, total[:requests], totals)
        weights = jnp.concatenate(weights, axis=0).astype(jnp.bfloat16)
        columns = slice(k * size, (k + 1) * size)
        mixed = jnp.dot(weights, values_ref[:, columns], preferred_element_type=jnp.float32)
        mixed = mixed + jnp.dot(weights, near_ref[:, columns], preferred_element_type=jnp.float32)
        for g in range(group):
            at = slice((k * group + g) * size, (k * group + g + 1) * size)
            own_ref[:, at] = mixed[g * span : g * span + requests]
            far_ref[:, at] = mixed[g * span + requests : (g + 1) * span].astype(far_ref.dtype)
    new_stats_ref[...] = tops
    cache_tops = cache_stats_ref[:requests, :]
    both = jnp.maximum(cache_tops, tops)
    stats_ref[:requests, :] = both
    stats_ref[requests:, :] = cache_stats_ref[requests:, :] * jnp.exp(cache_tops - both) + totals * jnp.exp(
        tops - both
    )


def mix(heads, code, values, near_values, cache_stats, scores):
    requests, lanes = cache_stats.shape[0] // 2, cache_stats.shape[1]
    size = values.shape[1] // heads
    shape = (requests, scores[0].shape[0] * size)
    return pl.pallas_call(
        functools.partial(mix_kernel, heads, requests),
        out_shape=[
            jax.ShapeDtypeStruct(shape, jnp.float32),
            jax.ShapeDtypeStruct(shape, jnp.bfloat16),
            jax.ShapeDtypeStruct((requests, lanes), jnp.float32),
            jax.ShapeDtypeStruct(cache_stats.shape, jnp.float32),
        ],
        compiler_params=params(),
        name="mix",
    )(code, values, near_values, cache_stats, *arranged(scores, SCORE_ORDER))


def weigh_kernel(cache_ref, own_ref, cache_stats_ref, new_stats_ref, stats_ref, other_ref, base_ref, factor_ref):
    requests, columns = cache_ref.shape
    size = cache_stats_ref.shape[1]
    top, other_top = stats_ref[:requests, :], other_ref[:requests, :]
    both = jnp.maximum(top, other_top)
    total = stats_ref[requests:, :] * jnp.exp(top - both)
    total = total + other_ref[requests:, :] * jnp.exp(other_top - both)
    inverse = 1.0 / total
    cache_factor = jnp.exp(cache_stats_ref[:requests, :] - both) * inverse
    new_factor = jnp.exp(new_stats_ref[...] - both) * inverse
    for h in range(columns // size):
        at = slice(h * size, (h + 1) * size)
        factor = jnp.broadcast_to(new_factor[:, h : h + 1], (requests, size))
        factor_ref[:, at] = factor
        base_ref[:, at] = cache_ref[:, at] * cache_factor[:, h : h + 1] + own_ref[:, at] * factor


def weigh(cache_mixed, own, cache_stats, new_stats, stats, other):
    return pl.pallas_call(
        weigh_kernel,
        out_shape=[jax.ShapeDtypeStruct(own.shape, jnp.float32)] * 2,
        compiler_params=params(),
        name="weigh",
    )(cache_mixed, own, cache_stats, new_stats, stats, other)


def merge_kernel(base_ref, factor_ref, far_ref, out_ref):
    out = base_ref[...] + far_ref[...].astype(jnp.float32) * factor_ref[...]
    out_ref[...] = out.astype(out_ref.dtype)


def merge(base, factor, far):
    return pl.pallas_call(
        merge_kernel,
        out_shape=jax.ShapeDtypeStruct(far.shape, far.dtype),
        compiler_params=params(),
        name="merge",
    )(base, factor, far)


def finish_kernel(own_ref, other_ref, out_ref):
    out_ref[...] = (own_ref[...].astype(jnp.float32) + other_ref[...].astype(jnp.float32)).astype(out_ref.dtype)


def finish(own, other):
    return pl.pallas_call(
        finish_kernel,
        out_shape=jax.ShapeDtypeStruct(own.shape, own.dtype),
        compiler_params=params(),
        name="finish",
    )(own, other)


def from_partner(x, axis, distance):
    count = lax.axis_size(axis)
    return lax.ppermute(x, axis, [(i, i ^ distance) for i in range(count)])


def from_behind(x, axis, distance):
    count = lax.axis_size(axis)
    return lax.ppermute(x, axis, [(i, (i + distance) % count) for i in range(count)])


def on_device(tokens, kv_weight, owners, requests, signs, queries, kv_cache, lengths):
    seq_count = lax.axis_size("seq")
    heads = signs.shape[0] // 2
    query = queries[0, 0]
    request_count, columns = query.shape
    message = make_message(query, owners[:, :, 0], requests)
    messages = [message] + [from_partner(message, "seq", d) for d in range(1, seq_count)]
    keys, values = project(tokens, kv_weight)
    near_values = from_partner(values, "seq", 1)
    scores, code = partial_scores(heads, columns, keys, messages)
    scores = [scores] + [from_behind(scores, "seq", d) for d in range(1, seq_count)]
    cache_mixed, cache_stats = cache_part(lengths, query, kv_cache[0, 0], signs)
    own, far, new_stats, stats = mix(heads, code, values, near_values, cache_stats, scores)
    far = from_partner(far, "seq", 2)
    other = from_partner(stats, "tp", 1)
    base, factor = weigh(cache_mixed, own, cache_stats, new_stats, stats, other)
    share = merge(base, factor, far)
    return finish(share, from_partner(share, "tp", 1)).reshape(1, 1, request_count, columns)


def hadamard(order):
    rows = lax.broadcasted_iota(jnp.int32, (order, order), 0)
    cols = lax.broadcasted_iota(jnp.int32, (order, order), 1)
    parity = jnp.zeros((order, order), jnp.int32)
    for bit_number in range(order.bit_length() - 1):
        parity = parity + rows // 2**bit_number % 2 * (cols // 2**bit_number % 2)
    return (1 - 2 * (parity % 2)).astype(jnp.float32)


def rotate(blocks, sign_rows, matrix):
    product = jnp.einsum(
        "...h,hk->...k", blocks * sign_rows, matrix, precision=lax.Precision.HIGHEST
    )
    return product / math.sqrt(matrix.shape[0])


def encode(rotated):
    largest = jnp.max(jnp.abs(rotated), axis=-1) + 1e-06
    scales = largest.astype(jnp.bfloat16)
    encoded = (rotated / scales.astype(jnp.float32)[..., None]).astype(jnp.bfloat16)
    return (encoded, scales)


def decode(encoded, scales):
    return (encoded.astype(jnp.float32) * scales.astype(jnp.float32)[..., None]).astype(
        jnp.bfloat16
    )


def slot_numbers(targets, count, room):
    onehot = (targets[:, None] == lax.iota(jnp.int32, count)[None, :]).astype(jnp.int32)
    within = jnp.sum((jnp.cumsum(onehot, axis=0) - 1) * onehot, axis=1)
    return targets * room + within


def on_device_long(tokens, kv_weight, owners, requests, signs, queries, kv_cache, lengths):
    seq_count = lax.axis_size("seq")
    per_device = owners.shape[1]
    slots = max(2, (2 * per_device + seq_count - 1) // seq_count)
    head_blocks = signs.shape[0]
    kv_heads = head_blocks // 2
    head_size = signs.shape[1]
    matrix = hadamard(head_size)
    sign_rows = (2 * signs - 1).astype(jnp.float32)
    summed = lax.psum_scatter(
        jnp.dot(tokens, kv_weight, preferred_element_type=jnp.float32).astype(jnp.bfloat16),
        "seq",
        scatter_dimension=0,
        tiled=True,
    ).astype(jnp.float32)
    encoded, scales = encode(
        rotate(summed.reshape(per_device, head_blocks, head_size), sign_rows, matrix)
    )
    slot_index = slot_numbers(owners[0, :, 0], seq_count, slots)
    slot_total = seq_count * slots
    send_values = (
        jnp.zeros((slot_total, head_blocks, head_size), jnp.bfloat16).at[slot_index].set(encoded)
    )
    send_scales = jnp.zeros((slot_total, head_blocks), jnp.bfloat16).at[slot_index].set(scales)
    send_codes = jnp.zeros((slot_total,), jnp.int32).at[slot_index].set(requests[0] + 1)
    got_values, got_scales, arrived_codes = (
        lax.all_to_all(send_values, "seq", split_axis=0, concat_axis=0, tiled=True),
        lax.all_to_all(send_scales, "seq", split_axis=0, concat_axis=0, tiled=True),
        lax.all_to_all(send_codes, "seq", split_axis=0, concat_axis=0, tiled=True),
    )
    arrived = decode(got_values, got_scales)
    query = queries[0, 0]
    request_count = query.shape[0]
    group = query.shape[1] // (kv_heads * head_size)
    query_blocks = query.astype(jnp.float32).reshape(request_count, kv_heads, group, head_size)
    query_rot = rotate(query_blocks, sign_rows[:kv_heads][:, None, :], matrix).astype(jnp.bfloat16)
    local_cache = kv_cache[0, 0]
    cache_span = local_cache.shape[1]
    local_cache = local_cache.reshape(request_count, cache_span, head_blocks, head_size)
    score_scale = 1.0 / math.sqrt(head_size)
    lowest = -1e30
    highest = lax.Precision.HIGHEST
    score_cache = (
        jnp.einsum(
            "rkgd,rckd->rkgc",
            query_rot,
            local_cache[:, :, :kv_heads],
            preferred_element_type=jnp.float32,
        )
        * score_scale
    )
    score_new = (
        jnp.einsum(
            "rkgd,nkd->rkgn", query_rot, arrived[:, :kv_heads], preferred_element_type=jnp.float32
        )
        * score_scale
    )
    positions = lax.axis_index("tp") * cache_span + lax.iota(jnp.int32, cache_span)
    mask_cache = (positions[None, :] < lengths[0, 0][:, None])[:, None, None, :]
    match = arrived_codes[None, :] == (lax.iota(jnp.int32, request_count) + 1)[:, None]
    mask_new = match[:, None, None, :]
    top = jnp.maximum(
        jnp.max(jnp.where(mask_cache, score_cache, lowest), axis=-1),
        jnp.max(jnp.where(mask_new, score_new, lowest), axis=-1),
    )
    probs_cache = jnp.where(mask_cache, jnp.exp(score_cache - top[..., None]), 0.0)
    probs_new = jnp.where(mask_new, jnp.exp(score_new - top[..., None]), 0.0)
    total = jnp.sum(probs_cache, axis=-1) + jnp.sum(probs_new, axis=-1)
    mixed = jnp.einsum(
        "rkgc,rckd->rkgd",
        probs_cache,
        local_cache[:, :, kv_heads:].astype(jnp.float32),
        precision=highest,
    )
    mixed = mixed + jnp.einsum(
        "rkgn,nkd->rkgd", probs_new, arrived[:, kv_heads:].astype(jnp.float32), precision=highest
    )
    shared_top = lax.pmax(top, "tp")
    factor = jnp.exp(top - shared_top)
    total, mixed = (
        lax.psum((total * factor).astype(jnp.bfloat16), "tp").astype(jnp.float32),
        lax.psum((mixed * factor[..., None]).astype(jnp.bfloat16), "tp").astype(jnp.float32),
    )
    mixed = mixed / total[..., None]
    output = rotate(mixed, 1.0, matrix) * sign_rows[kv_heads:][None, :, None, :]
    return output.reshape(1, 1, request_count, group * kv_heads * head_size).astype(jnp.bfloat16)


def solution(mesh):
    placed = (
        P(("groups", "tp", "section"), "seq"),
        P("seq", None),
        P(("groups", "tp", "section"), "seq", None),
        P(("groups", "tp", "section"), "seq"),
        P(),
        P(("groups", "seq"), "section", None, None),
        P(("groups", "seq"), "section", None, "tp", None),
        P(("groups", "seq"), "section", None),
    )
    short = mesh.shape["seq"] == 4 and mesh.shape["tp"] == 2
    return jax.shard_map(
        on_device if short else on_device_long,
        mesh=mesh,
        in_specs=placed,
        out_specs=P(("groups", "seq"), "section", None, None),
        check_vma=False,
    )
```

```python
import functools
import math

import jax
import jax.numpy as jnp
from jax import lax
from jax.experimental import pallas as pl
from jax.experimental.pallas import tpu as pltpu
from jax.sharding import PartitionSpec as P

LOWEST = -1e30
MIB = 1024 * 1024
NT = (((1,), (1,)), ((), ()))


def params(mib=32):
    return pltpu.CompilerParams(vmem_limit_bytes=mib * MIB)


def in_hbm(x):
    return pltpu.with_memory_space_constraint(x, pltpu.HBM)


def in_vmem(x):
    return pltpu.with_memory_space_constraint(x, pltpu.VMEM)


def hadamard_tile(order):
    rows = lax.broadcasted_iota(jnp.int32, (order, order), 0)
    cols = lax.broadcasted_iota(jnp.int32, (order, order), 1)
    common = rows & cols
    parity = jnp.zeros((order, order), jnp.int32)
    for bit_number in range(order.bit_length() - 1):
        parity = parity ^ (common >> bit_number)
    return (1 - 2 * (parity & 1)).astype(jnp.float32).astype(jnp.bfloat16)


QUERY_ORDER = (3, 2, 1)
SCORE_ORDER = (1, 2, 3)


def arranged(blocks, order):
    return [blocks[0]] + [blocks[d] for d in order]


def by_distance(refs, order):
    return [refs[0]] + [refs[1 + order.index(d)] for d in range(1, len(refs))]


def project_kernel(tokens_ref, weight_ref, keys_ref, values_ref):
    width = keys_ref.shape[1]
    for out_ref, columns in ((keys_ref, slice(0, width)), (values_ref, slice(width, 2 * width))):
        out_ref[...] = jnp.dot(
            tokens_ref[...], weight_ref[:, columns], preferred_element_type=jnp.float32
        ).astype(out_ref.dtype)


def project(tokens, weight):
    rows, features = tokens.shape
    width = weight.shape[1] // 2
    vmem = pl.BlockSpec(memory_space=pltpu.VMEM)
    return pl.pallas_call(
        project_kernel,
        in_specs=[vmem] * 2,
        out_specs=[vmem] * 2,
        out_shape=[jax.ShapeDtypeStruct((rows, width), jnp.bfloat16)] * 2,
        compiler_params=params(32),
        cost_estimate=pl.CostEstimate(
            flops=4 * rows * features * width,
            bytes_accessed=2 * (rows * features + 2 * features * width),
            transcendentals=0,
        ),
        name="project",
    )(in_vmem(tokens), in_vmem(weight))


def message_kernel(query_ref, owners_ref, requests_ref, out_ref, owners_buf, requests_buf, sems):
    requests, columns = query_ref.shape
    per_device = owners_ref.shape[1]
    copies = [
        pltpu.make_async_copy(query_ref, out_ref.at[:, :columns], sems.at[0]),
        pltpu.make_async_copy(owners_ref, owners_buf, sems.at[1]),
        pltpu.make_async_copy(requests_ref, requests_buf, sems.at[2]),
    ]
    for copy in copies:
        copy.start()
    copies[1].wait()
    copies[2].wait()
    code = (owners_buf[...] * requests + requests_buf[...]).astype(jnp.float32)
    spare = jnp.zeros((1, out_ref.shape[1] - columns - per_device), jnp.float32)
    code = jnp.concatenate([code, spare], axis=1)
    out_ref[:, columns:] = jnp.broadcast_to(code, (requests, code.shape[1])).astype(out_ref.dtype)
    copies[0].wait()


def make_message(query, owners, requests):
    count, columns = query.shape
    lanes = -(-owners.shape[1] // 128) * 128
    return pl.pallas_call(
        message_kernel,
        in_specs=[pl.BlockSpec(memory_space=pl.ANY)] * 3,
        out_specs=pl.BlockSpec(memory_space=pltpu.VMEM),
        out_shape=jax.ShapeDtypeStruct((count, columns + lanes), query.dtype),
        scratch_shapes=[
            pltpu.VMEM(owners.shape, owners.dtype),
            pltpu.VMEM(requests.shape, requests.dtype),
            pltpu.SemaphoreType.DMA((3,)),
        ],
        compiler_params=params(16),
        cost_estimate=pl.CostEstimate(flops=10**11, bytes_accessed=10**4, transcendentals=0),
        name="make_message",
    )(in_hbm(query), in_hbm(owners), in_hbm(requests))


def cache_kernel(
    lengths_ref, query_ref, cache_ref, signs_ref, mixed_ref, stats_ref, query_buf, top_buf, total_buf, mixed_buf
):
    requests, span, _ = cache_ref.shape
    blocks, size = signs_ref.shape
    heads = blocks // 2
    width = heads * size
    count = query_ref.shape[1] // size
    group = count // heads
    norm = 1.0 / math.sqrt(size)
    matrix = hadamard_tile(size)
    signs = (2 * signs_ref[...] - 1).astype(jnp.float32)
    query = query_ref[...].astype(jnp.float32)
    query = jnp.concatenate(
        [query[:, h * size : (h + 1) * size] * signs[h // group : h // group + 1] for h in range(count)], axis=0
    )
    query_buf[...] = jnp.dot(query.astype(jnp.bfloat16), matrix, preferred_element_type=jnp.float32) * norm
    rows = 2 * count
    kv_head = lax.broadcasted_iota(jnp.int32, (rows, width), 0) // group & (heads - 1)
    own_head = kv_head == lax.broadcasted_iota(jnp.int32, (rows, width), 1) // size
    first = lax.broadcasted_iota(jnp.int32, (rows, span), 0) < count
    position = lax.axis_index("tp") * span + lax.broadcasted_iota(jnp.int32, (rows, span), 1)
    pairs = range(0, requests, 2)
    scores = []
    for r in pairs:
        both = [query_buf[pl.ds(r + i, count, stride=requests), :] for i in range(2)]
        wide = jnp.concatenate([jnp.concatenate(both, axis=0)] * heads, axis=1)
        wide = jnp.where(own_head, wide, 0.0).astype(jnp.bfloat16)
        keys = cache_ref[r : r + 2, :, :width].reshape(2 * span, width)
        scores.append(lax.dot_general(wide, keys, NT, preferred_element_type=jnp.float32))
    probs = []
    for r, score in zip(pairs, scores):
        score = jnp.where(first, score[:, :span], score[:, span:]) * norm
        live = position < jnp.where(first, lengths_ref[0, 0, r], lengths_ref[0, 0, r + 1])
        top = jnp.max(jnp.where(live, score, LOWEST), axis=1, keepdims=True)
        prob = jnp.where(live, jnp.exp(score - top), 0.0)
        total = jnp.sum(prob, axis=1, keepdims=True)
        at = slice(r * count, (r + 2) * count)
        top_buf[at, :] = jnp.broadcast_to(top, (rows, size))
        total_buf[at, :] = jnp.broadcast_to(total, (rows, size))
        probs.append(
            jnp.concatenate([jnp.where(first, prob, 0.0), jnp.where(first, 0.0, prob)], axis=1).astype(jnp.bfloat16)
        )
    mixed = []
    for r, prob in zip(pairs, probs):
        values = cache_ref[r : r + 2, :, width:].reshape(2 * span, width)
        wide = jnp.dot(prob, values, preferred_element_type=jnp.float32)
        wide = jnp.where(own_head, wide, 0.0)
        mixed.append(sum(wide[:, k * size : (k + 1) * size] for k in range(heads)))
    mixed = jnp.concatenate(mixed, axis=0)
    high = mixed.astype(jnp.bfloat16)
    low = (mixed - high.astype(jnp.float32)).astype(jnp.bfloat16)
    plain = jnp.dot(high, matrix, preferred_element_type=jnp.float32)
    mixed_buf[...] = plain + jnp.dot(low, matrix, preferred_element_type=jnp.float32)
    lane = lax.broadcasted_iota(jnp.int32, (requests, stats_ref.shape[1]), 1)
    tops = jnp.full(lane.shape, 0.0, jnp.float32)
    totals = jnp.ones(lane.shape, jnp.float32)
    for h in range(count):
        pick = pl.ds(h, requests, stride=count)
        column = slice(h * size, (h + 1) * size)
        k = heads + h // group
        mixed_ref[:, column] = mixed_buf[pick, :] * (signs[k : k + 1] * norm)
        tops = jnp.where(lane == h, top_buf[pick, :], tops)
        totals = jnp.where(lane == h, total_buf[pick, :], totals)
    stats_ref[:requests, :] = tops
    stats_ref[requests:, :] = totals


def cache_part(lengths, query, cache, signs):
    requests, span, width = cache.shape
    size = signs.shape[1]
    columns = query.shape[1]
    vmem = pl.BlockSpec(memory_space=pltpu.VMEM)
    return pl.pallas_call(
        cache_kernel,
        in_specs=[pl.BlockSpec(memory_space=pltpu.SMEM)] + [vmem] * 3,
        out_shape=[
            jax.ShapeDtypeStruct(query.shape, jnp.float32),
            jax.ShapeDtypeStruct((2 * requests, size), jnp.float32),
        ],
        scratch_shapes=[pltpu.VMEM((requests * columns // size, size), jnp.float32)] * 4,
        compiler_params=params(),
        cost_estimate=pl.CostEstimate(
            flops=4 * span * requests * columns,
            bytes_accessed=2 * requests * span * width,
            transcendentals=span * requests * columns // size,
        ),
        name="cache_part",
    )(lengths, query, cache, signs)


def code_row(message_refs, start, requests, tokens):
    count = len(message_refs)
    me = lax.axis_index("seq")
    pieces = [ref[0:1, start : start + tokens // count].astype(jnp.float32) for ref in message_refs]
    row = [sum(jnp.where(me ^ d == at, pieces[d], 0.0) for d in range(count)) for at in range(count)]
    code = jnp.concatenate(row, axis=1).astype(jnp.int32)
    return ((code // requests) ^ me) * requests + code % requests


def score_kernel(heads, start, keys_ref, *refs):
    message_refs, (scores_ref, code_ref) = by_distance(refs[:-2], QUERY_ORDER), refs[-2:]
    requests = message_refs[0].shape[0]
    tokens, width = keys_ref.shape
    size = width // heads
    group = start // width
    code = code_row(message_refs, start, requests, tokens)
    code_ref[...] = jnp.broadcast_to(code, code_ref.shape)
    span = len(message_refs) * requests
    here = lax.broadcasted_iota(jnp.int32, (span, tokens), 0) == code
    queries = [ref[:, :start].astype(jnp.float32) for ref in message_refs]
    for k in range(heads):
        rows = []
        for g in range(group):
            at = (k * group + g) * size
            rows += [query[:, at : at + size] for query in queries]
        query = jnp.concatenate(rows, axis=0).astype(jnp.bfloat16)
        keys = keys_ref[:, k * size : (k + 1) * size]
        scores = lax.dot_general(query, keys, NT, preferred_element_type=jnp.float32)
        lines = [
            jnp.sum(jnp.where(here, scores[g * span : (g + 1) * span], 0.0), axis=0, keepdims=True)
            for g in range(group)
        ]
        lines = jnp.concatenate(lines, axis=0) * (1.0 / math.sqrt(size))
        scores_ref[k * group : (k + 1) * group, :] = lines.astype(scores_ref.dtype)


def partial_scores(heads, columns, keys, messages):
    tokens, width = keys.shape
    return pl.pallas_call(
        functools.partial(score_kernel, heads, columns),
        out_shape=[
            jax.ShapeDtypeStruct((columns * heads // width, tokens), jnp.bfloat16),
            jax.ShapeDtypeStruct((8, tokens), jnp.int32),
        ],
        compiler_params=params(),
        cost_estimate=pl.CostEstimate(flops=10**11, bytes_accessed=10**4, transcendentals=0),
        name="partial_scores",
    )(keys, *arranged(messages, QUERY_ORDER))


def mix_kernel(heads, requests, code_ref, values_ref, near_ref, cache_stats_ref, *refs):
    score_refs, (own_ref, far_ref, new_stats_ref, stats_ref) = refs[:4], refs[4:]
    own, before, across, after = [ref[...].astype(jnp.float32) for ref in score_refs]
    scores = (own + across) + (before + after)
    tokens, width = values_ref.shape
    size = width // heads
    group = scores.shape[0] // heads
    span = 2 * requests
    row = lax.broadcasted_iota(jnp.int32, (span, tokens), 0)
    here = jnp.where(row < requests, row, row + requests) == code_ref[0:1, :]
    lane = lax.broadcasted_iota(jnp.int32, (requests, stats_ref.shape[1]), 1)
    tops = jnp.full(lane.shape, 0.0, jnp.float32)
    totals = jnp.zeros(lane.shape, jnp.float32)
    for k in range(heads):
        weights = []
        for g in range(group):
            h = k * group + g
            line = jnp.where(here, jnp.broadcast_to(scores[h : h + 1, :], (span, tokens)), LOWEST)
            top = jnp.maximum(jnp.max(line, axis=1, keepdims=True), 0.1 * LOWEST)
            probs = jnp.exp(line - top)
            total = jnp.sum(probs, axis=1, keepdims=True)
            weights.append(probs)
            tops = jnp.where(lane == h, top[:requests], tops)
            totals = jnp.where(lane == h, total[:requests], totals)
        weights = jnp.concatenate(weights, axis=0).astype(jnp.bfloat16)
        columns = slice(k * size, (k + 1) * size)
        mixed = jnp.dot(weights, values_ref[:, columns], preferred_element_type=jnp.float32)
        mixed = mixed + jnp.dot(weights, near_ref[:, columns], preferred_element_type=jnp.float32)
        for g in range(group):
            at = slice((k * group + g) * size, (k * group + g + 1) * size)
            own_ref[:, at] = mixed[g * span : g * span + requests]
            far_ref[:, at] = mixed[g * span + requests : (g + 1) * span].astype(far_ref.dtype)
    new_stats_ref[...] = tops
    cache_tops = cache_stats_ref[:requests, :]
    both = jnp.maximum(cache_tops, tops)
    stats_ref[:requests, :] = both
    stats_ref[requests:, :] = cache_stats_ref[requests:, :] * jnp.exp(cache_tops - both) + totals * jnp.exp(
        tops - both
    )


def mix(heads, code, values, near_values, cache_stats, scores):
    requests, lanes = cache_stats.shape[0] // 2, cache_stats.shape[1]
    size = values.shape[1] // heads
    shape = (requests, scores[0].shape[0] * size)
    return pl.pallas_call(
        functools.partial(mix_kernel, heads, requests),
        out_shape=[
            jax.ShapeDtypeStruct(shape, jnp.float32),
            jax.ShapeDtypeStruct(shape, jnp.bfloat16),
            jax.ShapeDtypeStruct((requests, lanes), jnp.float32),
            jax.ShapeDtypeStruct(cache_stats.shape, jnp.float32),
        ],
        compiler_params=params(),
        name="mix",
    )(code, values, near_values, cache_stats, *arranged(scores, SCORE_ORDER))


def weigh_kernel(cache_ref, own_ref, cache_stats_ref, new_stats_ref, stats_ref, other_ref, base_ref, factor_ref):
    requests, columns = cache_ref.shape
    size = cache_stats_ref.shape[1]
    top, other_top = stats_ref[:requests, :], other_ref[:requests, :]
    both = jnp.maximum(top, other_top)
    total = stats_ref[requests:, :] * jnp.exp(top - both)
    total = total + other_ref[requests:, :] * jnp.exp(other_top - both)
    inverse = 1.0 / total
    cache_factor = jnp.exp(cache_stats_ref[:requests, :] - both) * inverse
    new_factor = jnp.exp(new_stats_ref[...] - both) * inverse
    for h in range(columns // size):
        at = slice(h * size, (h + 1) * size)
        factor = jnp.broadcast_to(new_factor[:, h : h + 1], (requests, size))
        factor_ref[:, at] = factor
        base_ref[:, at] = cache_ref[:, at] * cache_factor[:, h : h + 1] + own_ref[:, at] * factor


def weigh(cache_mixed, own, cache_stats, new_stats, stats, other):
    return pl.pallas_call(
        weigh_kernel,
        out_shape=[jax.ShapeDtypeStruct(own.shape, jnp.float32)] * 2,
        compiler_params=params(),
        name="weigh",
    )(cache_mixed, own, cache_stats, new_stats, stats, other)


def merge_kernel(base_ref, factor_ref, far_ref, out_ref):
    out = base_ref[...] + far_ref[...].astype(jnp.float32) * factor_ref[...]
    out_ref[...] = out.astype(out_ref.dtype)


def merge(base, factor, far):
    return pl.pallas_call(
        merge_kernel,
        out_shape=jax.ShapeDtypeStruct(far.shape, far.dtype),
        compiler_params=params(),
        name="merge",
    )(base, factor, far)


def finish_kernel(own_ref, other_ref, out_ref):
    out_ref[...] = (own_ref[...].astype(jnp.float32) + other_ref[...].astype(jnp.float32)).astype(out_ref.dtype)


def finish(own, other):
    return pl.pallas_call(
        finish_kernel,
        out_shape=jax.ShapeDtypeStruct(own.shape, own.dtype),
        compiler_params=params(),
        name="finish",
    )(own, other)


def from_partner(x, axis, distance):
    count = lax.axis_size(axis)
    return lax.ppermute(x, axis, [(i, i ^ distance) for i in range(count)])


def from_behind(x, axis, distance):
    count = lax.axis_size(axis)
    return lax.ppermute(x, axis, [(i, (i + distance) % count) for i in range(count)])


def on_device(tokens, kv_weight, owners, requests, signs, queries, kv_cache, lengths):
    seq_count = lax.axis_size("seq")
    heads = signs.shape[0] // 2
    query = queries[0, 0]
    request_count, columns = query.shape
    message = make_message(query, owners[:, :, 0], requests)
    messages = [message] + [from_partner(message, "seq", d) for d in range(1, seq_count)]
    keys, values = project(tokens, kv_weight)
    near_values = from_partner(values, "seq", 1)
    scores, code = partial_scores(heads, columns, keys, messages)
    scores = [scores] + [from_behind(scores, "seq", d) for d in range(1, seq_count)]
    cache_mixed, cache_stats = cache_part(lengths, query, kv_cache[0, 0], signs)
    own, far, new_stats, stats = mix(heads, code, values, near_values, cache_stats, scores)
    far = from_partner(far, "seq", 2)
    other = from_partner(stats, "tp", 1)
    base, factor = weigh(cache_mixed, own, cache_stats, new_stats, stats, other)
    share = merge(base, factor, far)
    return finish(share, from_partner(share, "tp", 1)).reshape(1, 1, request_count, columns)


def hadamard(order):
    rows = lax.broadcasted_iota(jnp.int32, (order, order), 0)
    cols = lax.broadcasted_iota(jnp.int32, (order, order), 1)
    parity = jnp.zeros((order, order), jnp.int32)
    for bit_number in range(order.bit_length() - 1):
        parity = parity + rows // 2**bit_number % 2 * (cols // 2**bit_number % 2)
    return (1 - 2 * (parity % 2)).astype(jnp.float32)


def rotate(blocks, sign_rows, matrix):
    product = jnp.einsum(
        "...h,hk->...k", blocks * sign_rows, matrix, precision=lax.Precision.HIGHEST
    )
    return product / math.sqrt(matrix.shape[0])


def encode(rotated):
    largest = jnp.max(jnp.abs(rotated), axis=-1) + 1e-06
    scales = largest.astype(jnp.bfloat16)
    encoded = (rotated / scales.astype(jnp.float32)[..., None]).astype(jnp.bfloat16)
    return (encoded, scales)


def decode(encoded, scales):
    return (encoded.astype(jnp.float32) * scales.astype(jnp.float32)[..., None]).astype(
        jnp.bfloat16
    )


def slot_numbers(targets, count, room):
    onehot = (targets[:, None] == lax.iota(jnp.int32, count)[None, :]).astype(jnp.int32)
    within = jnp.sum((jnp.cumsum(onehot, axis=0) - 1) * onehot, axis=1)
    return targets * room + within


def on_device_long(tokens, kv_weight, owners, requests, signs, queries, kv_cache, lengths):
    seq_count = lax.axis_size("seq")
    per_device = owners.shape[1]
    slots = max(2, (2 * per_device + seq_count - 1) // seq_count)
    head_blocks = signs.shape[0]
    kv_heads = head_blocks // 2
    head_size = signs.shape[1]
    matrix = hadamard(head_size)
    sign_rows = (2 * signs - 1).astype(jnp.float32)
    summed = lax.psum_scatter(
        jnp.dot(tokens, kv_weight, preferred_element_type=jnp.float32).astype(jnp.bfloat16),
        "seq",
        scatter_dimension=0,
        tiled=True,
    ).astype(jnp.float32)
    encoded, scales = encode(
        rotate(summed.reshape(per_device, head_blocks, head_size), sign_rows, matrix)
    )
    slot_index = slot_numbers(owners[0, :, 0], seq_count, slots)
    slot_total = seq_count * slots
    send_values = (
        jnp.zeros((slot_total, head_blocks, head_size), jnp.bfloat16).at[slot_index].set(encoded)
    )
    send_scales = jnp.zeros((slot_total, head_blocks), jnp.bfloat16).at[slot_index].set(scales)
    send_codes = jnp.zeros((slot_total,), jnp.int32).at[slot_index].set(requests[0] + 1)
    got_values, got_scales, arrived_codes = (
        lax.all_to_all(send_values, "seq", split_axis=0, concat_axis=0, tiled=True),
        lax.all_to_all(send_scales, "seq", split_axis=0, concat_axis=0, tiled=True),
        lax.all_to_all(send_codes, "seq", split_axis=0, concat_axis=0, tiled=True),
    )
    arrived = decode(got_values, got_scales)
    query = queries[0, 0]
    request_count = query.shape[0]
    group = query.shape[1] // (kv_heads * head_size)
    query_blocks = query.astype(jnp.float32).reshape(request_count, kv_heads, group, head_size)
    query_rot = rotate(query_blocks, sign_rows[:kv_heads][:, None, :], matrix).astype(jnp.bfloat16)
    local_cache = kv_cache[0, 0]
    cache_span = local_cache.shape[1]
    local_cache = local_cache.reshape(request_count, cache_span, head_blocks, head_size)
    score_scale = 1.0 / math.sqrt(head_size)
    lowest = -1e30
    highest = lax.Precision.HIGHEST
    score_cache = (
        jnp.einsum(
            "rkgd,rckd->rkgc",
            query_rot,
            local_cache[:, :, :kv_heads],
            preferred_element_type=jnp.float32,
        )
        * score_scale
    )
    score_new = (
        jnp.einsum(
            "rkgd,nkd->rkgn", query_rot, arrived[:, :kv_heads], preferred_element_type=jnp.float32
        )
        * score_scale
    )
    positions = lax.axis_index("tp") * cache_span + lax.iota(jnp.int32, cache_span)
    mask_cache = (positions[None, :] < lengths[0, 0][:, None])[:, None, None, :]
    match = arrived_codes[None, :] == (lax.iota(jnp.int32, request_count) + 1)[:, None]
    mask_new = match[:, None, None, :]
    top = jnp.maximum(
        jnp.max(jnp.where(mask_cache, score_cache, lowest), axis=-1),
        jnp.max(jnp.where(mask_new, score_new, lowest), axis=-1),
    )
    probs_cache = jnp.where(mask_cache, jnp.exp(score_cache - top[..., None]), 0.0)
    probs_new = jnp.where(mask_new, jnp.exp(score_new - top[..., None]), 0.0)
    total = jnp.sum(probs_cache, axis=-1) + jnp.sum(probs_new, axis=-1)
    mixed = jnp.einsum(
        "rkgc,rckd->rkgd",
        probs_cache,
        local_cache[:, :, kv_heads:].astype(jnp.float32),
        precision=highest,
    )
    mixed = mixed + jnp.einsum(
        "rkgn,nkd->rkgd", probs_new, arrived[:, kv_heads:].astype(jnp.float32), precision=highest
    )
    shared_top = lax.pmax(top, "tp")
    factor = jnp.exp(top - shared_top)
    total, mixed = (
        lax.psum((total * factor).astype(jnp.bfloat16), "tp").astype(jnp.float32),
        lax.psum((mixed * factor[..., None]).astype(jnp.bfloat16), "tp").astype(jnp.float32),
    )
    mixed = mixed / total[..., None]
    output = rotate(mixed, 1.0, matrix) * sign_rows[kv_heads:][None, :, None, :]
    return output.reshape(1, 1, request_count, group * kv_heads * head_size).astype(jnp.bfloat16)


def solution(mesh):
    placed = (
        P(("groups", "tp", "section"), "seq"),
        P("seq", None),
        P(("groups", "tp", "section"), "seq", None),
        P(("groups", "tp", "section"), "seq"),
        P(),
        P(("groups", "seq"), "section", None, None),
        P(("groups", "seq"), "section", None, "tp", None),
        P(("groups", "seq"), "section", None),
    )
    short = mesh.shape["seq"] == 4 and mesh.shape["tp"] == 2
    return jax.shard_map(
        on_device if short else on_device_long,
        mesh=mesh,
        in_specs=placed,
        out_specs=P(("groups", "seq"), "section", None, None),
        check_vma=False,
    )
```

```python
import functools
import math

import jax
import jax.numpy as jnp
from jax import lax
from jax.experimental import pallas as pl
from jax.experimental.pallas import tpu as pltpu
from jax.sharding import PartitionSpec as P

LOWEST = -1e30
MIB = 1024 * 1024
NT = (((1,), (1,)), ((), ()))


def params(mib=32):
    return pltpu.CompilerParams(vmem_limit_bytes=mib * MIB)


def in_hbm(x):
    return pltpu.with_memory_space_constraint(x, pltpu.HBM)


def in_vmem(x):
    return pltpu.with_memory_space_constraint(x, pltpu.VMEM)


def hadamard_tile(order):
    rows = lax.broadcasted_iota(jnp.int32, (order, order), 0)
    cols = lax.broadcasted_iota(jnp.int32, (order, order), 1)
    common = rows & cols
    parity = jnp.zeros((order, order), jnp.int32)
    for bit_number in range(order.bit_length() - 1):
        parity = parity ^ (common >> bit_number)
    return (1 - 2 * (parity & 1)).astype(jnp.float32).astype(jnp.bfloat16)


QUERY_ORDER = (1, 2, 3)
SCORE_STEPS = (
    (3, ((3, 0), (1, 2))),
    (1, ((1, 0), (3, 2))),
    (2, ((0, 2), (2, 0))),
    (3, ((0, 3), (2, 1))),
    (1, ((0, 1), (2, 3))),
    (2, ((1, 3), (3, 1))),
)


def arranged(blocks, order):
    return [blocks[0]] + [blocks[d] for d in order]


def by_distance(refs, order):
    return [refs[0]] + [refs[1 + order.index(d)] for d in range(1, len(refs))]


def project_kernel(tokens_ref, weight_ref, keys_ref, values_ref):
    width = keys_ref.shape[1]
    for out_ref, columns in ((keys_ref, slice(0, width)), (values_ref, slice(width, 2 * width))):
        out_ref[...] = jnp.dot(
            tokens_ref[...], weight_ref[:, columns], preferred_element_type=jnp.float32
        ).astype(out_ref.dtype)


def project(tokens, weight):
    rows, features = tokens.shape
    width = weight.shape[1] // 2
    vmem = pl.BlockSpec(memory_space=pltpu.VMEM)
    return pl.pallas_call(
        project_kernel,
        in_specs=[vmem] * 2,
        out_specs=[vmem] * 2,
        out_shape=[jax.ShapeDtypeStruct((rows, width), jnp.bfloat16)] * 2,
        compiler_params=params(32),
        cost_estimate=pl.CostEstimate(
            flops=4 * rows * features * width,
            bytes_accessed=2 * (rows * features + 2 * features * width),
            transcendentals=0,
        ),
        name="project",
    )(in_vmem(tokens), in_vmem(weight))


def message_kernel(query_ref, owners_ref, requests_ref, out_ref, owners_buf, requests_buf, sems):
    requests, columns = query_ref.shape
    per_device = owners_ref.shape[1]
    copies = [
        pltpu.make_async_copy(query_ref, out_ref.at[:, :columns], sems.at[0]),
        pltpu.make_async_copy(owners_ref, owners_buf, sems.at[1]),
        pltpu.make_async_copy(requests_ref, requests_buf, sems.at[2]),
    ]
    for copy in copies:
        copy.start()
    copies[1].wait()
    copies[2].wait()
    code = (owners_buf[...] * requests + requests_buf[...]).astype(jnp.float32)
    spare = jnp.zeros((1, out_ref.shape[1] - columns - per_device), jnp.float32)
    code = jnp.concatenate([code, spare], axis=1)
    out_ref[:, columns:] = jnp.broadcast_to(code, (requests, code.shape[1])).astype(out_ref.dtype)
    copies[0].wait()


def make_message(query, owners, requests):
    count, columns = query.shape
    lanes = -(-owners.shape[1] // 128) * 128
    return pl.pallas_call(
        message_kernel,
        in_specs=[pl.BlockSpec(memory_space=pl.ANY)] * 3,
        out_specs=pl.BlockSpec(memory_space=pltpu.VMEM),
        out_shape=jax.ShapeDtypeStruct((count, columns + lanes), query.dtype),
        scratch_shapes=[
            pltpu.VMEM(owners.shape, owners.dtype),
            pltpu.VMEM(requests.shape, requests.dtype),
            pltpu.SemaphoreType.DMA((3,)),
        ],
        compiler_params=params(16),
        cost_estimate=pl.CostEstimate(flops=10**11, bytes_accessed=10**4, transcendentals=0),
        name="make_message",
    )(in_hbm(query), in_hbm(owners), in_hbm(requests))


def cache_kernel(
    lengths_ref, query_ref, cache_ref, signs_ref, mixed_ref, stats_ref, query_buf, top_buf, total_buf, mixed_buf
):
    requests, span, _ = cache_ref.shape
    blocks, size = signs_ref.shape
    heads = blocks // 2
    width = heads * size
    count = query_ref.shape[1] // size
    group = count // heads
    norm = 1.0 / math.sqrt(size)
    matrix = hadamard_tile(size)
    signs = (2 * signs_ref[...] - 1).astype(jnp.float32)
    query = query_ref[...].astype(jnp.float32)
    query = jnp.concatenate(
        [query[:, h * size : (h + 1) * size] * signs[h // group : h // group + 1] for h in range(count)], axis=0
    )
    query_buf[...] = jnp.dot(query.astype(jnp.bfloat16), matrix, preferred_element_type=jnp.float32) * norm
    rows = 2 * count
    kv_head = lax.broadcasted_iota(jnp.int32, (rows, width), 0) // group & (heads - 1)
    own_head = kv_head == lax.broadcasted_iota(jnp.int32, (rows, width), 1) // size
    first = lax.broadcasted_iota(jnp.int32, (rows, span), 0) < count
    position = lax.axis_index("tp") * span + lax.broadcasted_iota(jnp.int32, (rows, span), 1)
    pairs = range(0, requests, 2)
    scores = []
    for r in pairs:
        both = [query_buf[pl.ds(r + i, count, stride=requests), :] for i in range(2)]
        wide = jnp.concatenate([jnp.concatenate(both, axis=0)] * heads, axis=1)
        wide = jnp.where(own_head, wide, 0.0).astype(jnp.bfloat16)
        keys = cache_ref[r : r + 2, :, :width].reshape(2 * span, width)
        scores.append(lax.dot_general(wide, keys, NT, preferred_element_type=jnp.float32))
    probs = []
    for r, score in zip(pairs, scores):
        score = jnp.where(first, score[:, :span], score[:, span:]) * norm
        live = position < jnp.where(first, lengths_ref[0, 0, r], lengths_ref[0, 0, r + 1])
        top = jnp.max(jnp.where(live, score, LOWEST), axis=1, keepdims=True)
        prob = jnp.where(live, jnp.exp(score - top), 0.0)
        total = jnp.sum(prob, axis=1, keepdims=True)
        at = slice(r * count, (r + 2) * count)
        top_buf[at, :] = jnp.broadcast_to(top, (rows, size))
        total_buf[at, :] = jnp.broadcast_to(total, (rows, size))
        probs.append(
            jnp.concatenate([jnp.where(first, prob, 0.0), jnp.where(first, 0.0, prob)], axis=1).astype(jnp.bfloat16)
        )
    mixed = []
    for r, prob in zip(pairs, probs):
        values = cache_ref[r : r + 2, :, width:].reshape(2 * span, width)
        wide = jnp.dot(prob, values, preferred_element_type=jnp.float32)
        wide = jnp.where(own_head, wide, 0.0)
        mixed.append(sum(wide[:, k * size : (k + 1) * size] for k in range(heads)))
    mixed = jnp.concatenate(mixed, axis=0)
    high = mixed.astype(jnp.bfloat16)
    low = (mixed - high.astype(jnp.float32)).astype(jnp.bfloat16)
    plain = jnp.dot(high, matrix, preferred_element_type=jnp.float32)
    mixed_buf[...] = plain + jnp.dot(low, matrix, preferred_element_type=jnp.float32)
    lane = lax.broadcasted_iota(jnp.int32, (requests, stats_ref.shape[1]), 1)
    tops = jnp.full(lane.shape, 0.0, jnp.float32)
    totals = jnp.ones(lane.shape, jnp.float32)
    for h in range(count):
        pick = pl.ds(h, requests, stride=count)
        column = slice(h * size, (h + 1) * size)
        k = heads + h // group
        mixed_ref[:, column] = mixed_buf[pick, :] * (signs[k : k + 1] * norm)
        tops = jnp.where(lane == h, top_buf[pick, :], tops)
        totals = jnp.where(lane == h, total_buf[pick, :], totals)
    stats_ref[:requests, :] = tops
    stats_ref[requests:, :] = totals


def cache_part(lengths, query, cache, signs):
    requests, span, width = cache.shape
    size = signs.shape[1]
    columns = query.shape[1]
    vmem = pl.BlockSpec(memory_space=pltpu.VMEM)
    return pl.pallas_call(
        cache_kernel,
        in_specs=[pl.BlockSpec(memory_space=pltpu.SMEM)] + [vmem] * 3,
        out_shape=[
            jax.ShapeDtypeStruct(query.shape, jnp.float32),
            jax.ShapeDtypeStruct((2 * requests, size), jnp.float32),
        ],
        scratch_shapes=[pltpu.VMEM((requests * columns // size, size), jnp.float32)] * 4,
        compiler_params=params(),
        cost_estimate=pl.CostEstimate(
            flops=4 * span * requests * columns,
            bytes_accessed=2 * requests * span * width,
            transcendentals=span * requests * columns // size,
        ),
        name="cache_part",
    )(lengths, query, cache, signs)


def code_row(message_refs, start, requests, tokens):
    count = len(message_refs)
    me = lax.axis_index("seq")
    pieces = [ref[0:1, start : start + tokens // count].astype(jnp.float32) for ref in message_refs]
    row = [sum(jnp.where(me ^ d == at, pieces[d], 0.0) for d in range(count)) for at in range(count)]
    code = jnp.concatenate(row, axis=1).astype(jnp.int32)
    return ((code // requests) ^ me) * requests + code % requests


def score_kernel(heads, start, keys_ref, *refs):
    message_refs, (scores_ref, code_ref) = by_distance(refs[:-2], QUERY_ORDER), refs[-2:]
    requests = message_refs[0].shape[0]
    tokens, width = keys_ref.shape
    size = width // heads
    group = start // width
    code = code_row(message_refs, start, requests, tokens)
    code_ref[...] = jnp.broadcast_to(code, code_ref.shape)
    span = len(message_refs) * requests
    here = lax.broadcasted_iota(jnp.int32, (span, tokens), 0) == code
    queries = [ref[:, :start].astype(jnp.float32) for ref in message_refs]
    for k in range(heads):
        rows = []
        for g in range(group):
            at = (k * group + g) * size
            rows += [query[:, at : at + size] for query in queries]
        query = jnp.concatenate(rows, axis=0).astype(jnp.bfloat16)
        keys = keys_ref[:, k * size : (k + 1) * size]
        scores = lax.dot_general(query, keys, NT, preferred_element_type=jnp.float32)
        lines = [
            jnp.sum(jnp.where(here, scores[g * span : (g + 1) * span], 0.0), axis=0, keepdims=True)
            for g in range(group)
        ]
        lines = jnp.concatenate(lines, axis=0) * (1.0 / math.sqrt(size))
        scores_ref[k * group : (k + 1) * group, :] = lines.astype(scores_ref.dtype)


def partial_scores(heads, columns, keys, messages):
    tokens, width = keys.shape
    return pl.pallas_call(
        functools.partial(score_kernel, heads, columns),
        out_shape=[
            jax.ShapeDtypeStruct((columns * heads // width, tokens), jnp.bfloat16),
            jax.ShapeDtypeStruct((8, tokens), jnp.int32),
        ],
        compiler_params=params(),
        cost_estimate=pl.CostEstimate(flops=10**11, bytes_accessed=10**4, transcendentals=0),
        name="partial_scores",
    )(keys, *arranged(messages, QUERY_ORDER))


def mix_kernel(heads, requests, code_ref, values_ref, near_ref, cache_stats_ref, *refs):
    score_refs, (own_ref, far_ref, new_stats_ref, stats_ref) = refs[:-4], refs[-4:]
    parts = [ref[...].astype(jnp.float32) for ref in score_refs]
    by_xor = [parts[0]] + [
        sum(part for part, (d, _) in zip(parts[:0:-1], SCORE_STEPS) if d == distance) for distance in (1, 2, 3)
    ]
    scores = (by_xor[0] + by_xor[2]) + (by_xor[1] + by_xor[3])
    tokens, width = values_ref.shape
    size = width // heads
    group = scores.shape[0] // heads
    span = 2 * requests
    row = lax.broadcasted_iota(jnp.int32, (span, tokens), 0)
    here = jnp.where(row < requests, row, row + requests) == code_ref[0:1, :]
    lane = lax.broadcasted_iota(jnp.int32, (requests, stats_ref.shape[1]), 1)
    tops = jnp.full(lane.shape, 0.0, jnp.float32)
    totals = jnp.zeros(lane.shape, jnp.float32)
    for k in range(heads):
        weights = []
        for g in range(group):
            h = k * group + g
            line = jnp.where(here, jnp.broadcast_to(scores[h : h + 1, :], (span, tokens)), LOWEST)
            top = jnp.maximum(jnp.max(line, axis=1, keepdims=True), 0.1 * LOWEST)
            probs = jnp.exp(line - top)
            total = jnp.sum(probs, axis=1, keepdims=True)
            weights.append(probs)
            tops = jnp.where(lane == h, top[:requests], tops)
            totals = jnp.where(lane == h, total[:requests], totals)
        weights = jnp.concatenate(weights, axis=0).astype(jnp.bfloat16)
        columns = slice(k * size, (k + 1) * size)
        mixed = jnp.dot(weights, values_ref[:, columns], preferred_element_type=jnp.float32)
        mixed = mixed + jnp.dot(weights, near_ref[:, columns], preferred_element_type=jnp.float32)
        for g in range(group):
            at = slice((k * group + g) * size, (k * group + g + 1) * size)
            own_ref[:, at] = mixed[g * span : g * span + requests]
            far_ref[:, at] = mixed[g * span + requests : (g + 1) * span].astype(far_ref.dtype)
    new_stats_ref[...] = tops
    cache_tops = cache_stats_ref[:requests, :]
    both = jnp.maximum(cache_tops, tops)
    stats_ref[:requests, :] = both
    stats_ref[requests:, :] = cache_stats_ref[requests:, :] * jnp.exp(cache_tops - both) + totals * jnp.exp(
        tops - both
    )


def mix(heads, code, values, near_values, cache_stats, scores):
    requests, lanes = cache_stats.shape[0] // 2, cache_stats.shape[1]
    size = values.shape[1] // heads
    shape = (requests, scores[0].shape[0] * size)
    return pl.pallas_call(
        functools.partial(mix_kernel, heads, requests),
        out_shape=[
            jax.ShapeDtypeStruct(shape, jnp.float32),
            jax.ShapeDtypeStruct(shape, jnp.bfloat16),
            jax.ShapeDtypeStruct((requests, lanes), jnp.float32),
            jax.ShapeDtypeStruct(cache_stats.shape, jnp.float32),
        ],
        compiler_params=params(),
        name="mix",
    )(code, values, near_values, cache_stats, scores[0], *scores[:0:-1])


def weigh_kernel(cache_ref, own_ref, cache_stats_ref, new_stats_ref, stats_ref, other_ref, base_ref, factor_ref):
    requests, columns = cache_ref.shape
    size = cache_stats_ref.shape[1]
    top, other_top = stats_ref[:requests, :], other_ref[:requests, :]
    both = jnp.maximum(top, other_top)
    total = stats_ref[requests:, :] * jnp.exp(top - both)
    total = total + other_ref[requests:, :] * jnp.exp(other_top - both)
    inverse = 1.0 / total
    cache_factor = jnp.exp(cache_stats_ref[:requests, :] - both) * inverse
    new_factor = jnp.exp(new_stats_ref[...] - both) * inverse
    for h in range(columns // size):
        at = slice(h * size, (h + 1) * size)
        factor = jnp.broadcast_to(new_factor[:, h : h + 1], (requests, size))
        factor_ref[:, at] = factor
        base_ref[:, at] = cache_ref[:, at] * cache_factor[:, h : h + 1] + own_ref[:, at] * factor


def weigh(cache_mixed, own, cache_stats, new_stats, stats, other):
    return pl.pallas_call(
        weigh_kernel,
        out_shape=[jax.ShapeDtypeStruct(own.shape, jnp.float32)] * 2,
        compiler_params=params(),
        name="weigh",
    )(cache_mixed, own, cache_stats, new_stats, stats, other)


def merge_kernel(base_ref, factor_ref, far_ref, out_ref):
    out = base_ref[...] + far_ref[...].astype(jnp.float32) * factor_ref[...]
    out_ref[...] = out.astype(out_ref.dtype)


def merge(base, factor, far):
    return pl.pallas_call(
        merge_kernel,
        out_shape=jax.ShapeDtypeStruct(far.shape, far.dtype),
        compiler_params=params(),
        name="merge",
    )(base, factor, far)


def finish_kernel(own_ref, other_ref, out_ref):
    out_ref[...] = (own_ref[...].astype(jnp.float32) + other_ref[...].astype(jnp.float32)).astype(out_ref.dtype)


def finish(own, other):
    return pl.pallas_call(
        finish_kernel,
        out_shape=jax.ShapeDtypeStruct(own.shape, own.dtype),
        compiler_params=params(),
        name="finish",
    )(own, other)


def from_partner(x, axis, distance):
    count = lax.axis_size(axis)
    return lax.ppermute(x, axis, [(i, i ^ distance) for i in range(count)])


def on_device(tokens, kv_weight, owners, requests, signs, queries, kv_cache, lengths):
    seq_count = lax.axis_size("seq")
    heads = signs.shape[0] // 2
    query = queries[0, 0]
    request_count, columns = query.shape
    message = make_message(query, owners[:, :, 0], requests)
    messages = [message] + [from_partner(message, "seq", d) for d in range(1, seq_count)]
    keys, values = project(tokens, kv_weight)
    near_values = from_partner(values, "seq", 1)
    scores, code = partial_scores(heads, columns, keys, messages)
    scores = [scores] + [lax.ppermute(scores, "seq", pairs) for _, pairs in SCORE_STEPS]
    cache_mixed, cache_stats = cache_part(lengths, query, kv_cache[0, 0], signs)
    own, far, new_stats, stats = mix(heads, code, values, near_values, cache_stats, scores)
    far = from_partner(far, "seq", 2)
    other = from_partner(stats, "tp", 1)
    base, factor = weigh(cache_mixed, own, cache_stats, new_stats, stats, other)
    share = merge(base, factor, far)
    return finish(share, from_partner(share, "tp", 1)).reshape(1, 1, request_count, columns)


def hadamard(order):
    rows = lax.broadcasted_iota(jnp.int32, (order, order), 0)
    cols = lax.broadcasted_iota(jnp.int32, (order, order), 1)
    parity = jnp.zeros((order, order), jnp.int32)
    for bit_number in range(order.bit_length() - 1):
        parity = parity + rows // 2**bit_number % 2 * (cols // 2**bit_number % 2)
    return (1 - 2 * (parity % 2)).astype(jnp.float32)


def rotate(blocks, sign_rows, matrix):
    product = jnp.einsum(
        "...h,hk->...k", blocks * sign_rows, matrix, precision=lax.Precision.HIGHEST
    )
    return product / math.sqrt(matrix.shape[0])


def encode(rotated):
    largest = jnp.max(jnp.abs(rotated), axis=-1) + 1e-06
    scales = largest.astype(jnp.bfloat16)
    encoded = (rotated / scales.astype(jnp.float32)[..., None]).astype(jnp.bfloat16)
    return (encoded, scales)


def decode(encoded, scales):
    return (encoded.astype(jnp.float32) * scales.astype(jnp.float32)[..., None]).astype(
        jnp.bfloat16
    )


def slot_numbers(targets, count, room):
    onehot = (targets[:, None] == lax.iota(jnp.int32, count)[None, :]).astype(jnp.int32)
    within = jnp.sum((jnp.cumsum(onehot, axis=0) - 1) * onehot, axis=1)
    return targets * room + within


def on_device_long(tokens, kv_weight, owners, requests, signs, queries, kv_cache, lengths):
    seq_count = lax.axis_size("seq")
    per_device = owners.shape[1]
    slots = max(2, (2 * per_device + seq_count - 1) // seq_count)
    head_blocks = signs.shape[0]
    kv_heads = head_blocks // 2
    head_size = signs.shape[1]
    matrix = hadamard(head_size)
    sign_rows = (2 * signs - 1).astype(jnp.float32)
    summed = lax.psum_scatter(
        jnp.dot(tokens, kv_weight, preferred_element_type=jnp.float32).astype(jnp.bfloat16),
        "seq",
        scatter_dimension=0,
        tiled=True,
    ).astype(jnp.float32)
    encoded, scales = encode(
        rotate(summed.reshape(per_device, head_blocks, head_size), sign_rows, matrix)
    )
    slot_index = slot_numbers(owners[0, :, 0], seq_count, slots)
    slot_total = seq_count * slots
    send_values = (
        jnp.zeros((slot_total, head_blocks, head_size), jnp.bfloat16).at[slot_index].set(encoded)
    )
    send_scales = jnp.zeros((slot_total, head_blocks), jnp.bfloat16).at[slot_index].set(scales)
    send_codes = jnp.zeros((slot_total,), jnp.int32).at[slot_index].set(requests[0] + 1)
    got_values, got_scales, arrived_codes = (
        lax.all_to_all(send_values, "seq", split_axis=0, concat_axis=0, tiled=True),
        lax.all_to_all(send_scales, "seq", split_axis=0, concat_axis=0, tiled=True),
        lax.all_to_all(send_codes, "seq", split_axis=0, concat_axis=0, tiled=True),
    )
    arrived = decode(got_values, got_scales)
    query = queries[0, 0]
    request_count = query.shape[0]
    group = query.shape[1] // (kv_heads * head_size)
    query_blocks = query.astype(jnp.float32).reshape(request_count, kv_heads, group, head_size)
    query_rot = rotate(query_blocks, sign_rows[:kv_heads][:, None, :], matrix).astype(jnp.bfloat16)
    local_cache = kv_cache[0, 0]
    cache_span = local_cache.shape[1]
    local_cache = local_cache.reshape(request_count, cache_span, head_blocks, head_size)
    score_scale = 1.0 / math.sqrt(head_size)
    lowest = -1e30
    highest = lax.Precision.HIGHEST
    score_cache = (
        jnp.einsum(
            "rkgd,rckd->rkgc",
            query_rot,
            local_cache[:, :, :kv_heads],
            preferred_element_type=jnp.float32,
        )
        * score_scale
    )
    score_new = (
        jnp.einsum(
            "rkgd,nkd->rkgn", query_rot, arrived[:, :kv_heads], preferred_element_type=jnp.float32
        )
        * score_scale
    )
    positions = lax.axis_index("tp") * cache_span + lax.iota(jnp.int32, cache_span)
    mask_cache = (positions[None, :] < lengths[0, 0][:, None])[:, None, None, :]
    match = arrived_codes[None, :] == (lax.iota(jnp.int32, request_count) + 1)[:, None]
    mask_new = match[:, None, None, :]
    top = jnp.maximum(
        jnp.max(jnp.where(mask_cache, score_cache, lowest), axis=-1),
        jnp.max(jnp.where(mask_new, score_new, lowest), axis=-1),
    )
    probs_cache = jnp.where(mask_cache, jnp.exp(score_cache - top[..., None]), 0.0)
    probs_new = jnp.where(mask_new, jnp.exp(score_new - top[..., None]), 0.0)
    total = jnp.sum(probs_cache, axis=-1) + jnp.sum(probs_new, axis=-1)
    mixed = jnp.einsum(
        "rkgc,rckd->rkgd",
        probs_cache,
        local_cache[:, :, kv_heads:].astype(jnp.float32),
        precision=highest,
    )
    mixed = mixed + jnp.einsum(
        "rkgn,nkd->rkgd", probs_new, arrived[:, kv_heads:].astype(jnp.float32), precision=highest
    )
    shared_top = lax.pmax(top, "tp")
    factor = jnp.exp(top - shared_top)
    total, mixed = (
        lax.psum((total * factor).astype(jnp.bfloat16), "tp").astype(jnp.float32),
        lax.psum((mixed * factor[..., None]).astype(jnp.bfloat16), "tp").astype(jnp.float32),
    )
    mixed = mixed / total[..., None]
    output = rotate(mixed, 1.0, matrix) * sign_rows[kv_heads:][None, :, None, :]
    return output.reshape(1, 1, request_count, group * kv_heads * head_size).astype(jnp.bfloat16)


def solution(mesh):
    placed = (
        P(("groups", "tp", "section"), "seq"),
        P("seq", None),
        P(("groups", "tp", "section"), "seq", None),
        P(("groups", "tp", "section"), "seq"),
        P(),
        P(("groups", "seq"), "section", None, None),
        P(("groups", "seq"), "section", None, "tp", None),
        P(("groups", "seq"), "section", None),
    )
    short = mesh.shape["seq"] == 4 and mesh.shape["tp"] == 2
    return jax.shard_map(
        on_device if short else on_device_long,
        mesh=mesh,
        in_specs=placed,
        out_specs=P(("groups", "seq"), "section", None, None),
        check_vma=False,
    )
```

```python
import functools
import math

import jax
import jax.numpy as jnp
from jax import lax
from jax.experimental import pallas as pl
from jax.experimental.pallas import tpu as pltpu
from jax.sharding import PartitionSpec as P

LOWEST = -1e30
MIB = 1024 * 1024
NT = (((1,), (1,)), ((), ()))


def params(mib=32):
    return pltpu.CompilerParams(vmem_limit_bytes=mib * MIB)


def in_hbm(x):
    return pltpu.with_memory_space_constraint(x, pltpu.HBM)


def in_vmem(x):
    return pltpu.with_memory_space_constraint(x, pltpu.VMEM)


def hadamard_tile(order):
    rows = lax.broadcasted_iota(jnp.int32, (order, order), 0)
    cols = lax.broadcasted_iota(jnp.int32, (order, order), 1)
    common = rows & cols
    parity = jnp.zeros((order, order), jnp.int32)
    for bit_number in range(order.bit_length() - 1):
        parity = parity ^ (common >> bit_number)
    return (1 - 2 * (parity & 1)).astype(jnp.float32).astype(jnp.bfloat16)


QUERY_ORDER = (3, 2, 1)
SCORE_ORDER = (1, 2, 3)


def arranged(blocks, order):
    return [blocks[0]] + [blocks[d] for d in order]


def by_distance(refs, order):
    return [refs[0]] + [refs[1 + order.index(d)] for d in range(1, len(refs))]


def project_kernel(tokens_ref, weight_ref, keys_ref, values_ref):
    width = keys_ref.shape[1]
    for out_ref, columns in ((keys_ref, slice(0, width)), (values_ref, slice(width, 2 * width))):
        out_ref[...] = jnp.dot(
            tokens_ref[...], weight_ref[:, columns], preferred_element_type=jnp.float32
        ).astype(out_ref.dtype)


def project(tokens, weight):
    rows, features = tokens.shape
    width = weight.shape[1] // 2
    vmem = pl.BlockSpec(memory_space=pltpu.VMEM)
    return pl.pallas_call(
        project_kernel,
        in_specs=[vmem] * 2,
        out_specs=[vmem] * 2,
        out_shape=[jax.ShapeDtypeStruct((rows, width), jnp.bfloat16)] * 2,
        compiler_params=params(32),
        cost_estimate=pl.CostEstimate(
            flops=4 * rows * features * width,
            bytes_accessed=2 * (rows * features + 2 * features * width),
            transcendentals=0,
        ),
        name="project",
    )(in_vmem(tokens), in_vmem(weight))


def eighths(columns):
    step = columns // 8
    return [slice(at, at + step) for at in range(0, columns, step)]


def message_kernel(query_ref, owners_ref, requests_ref, out_ref, owners_buf, requests_buf, sems):
    requests, columns = query_ref.shape
    per_device = owners_ref.shape[1]
    small = [
        pltpu.make_async_copy(owners_ref, owners_buf, sems.at[0]),
        pltpu.make_async_copy(requests_ref, requests_buf, sems.at[1]),
    ]
    copies = []
    for i, span in enumerate(eighths(columns)):
        copies.append(pltpu.make_async_copy(query_ref.at[:, span], out_ref.at[:, span], sems.at[2 + i]))
    for copy in small + copies:
        copy.start()
    for copy in small:
        copy.wait()
    code = (owners_buf[...] * requests + requests_buf[...]).astype(jnp.float32)
    spare = jnp.zeros((1, out_ref.shape[1] - columns - per_device), jnp.float32)
    code = jnp.concatenate([code, spare], axis=1)
    out_ref[:, columns:] = jnp.broadcast_to(code, (requests, code.shape[1])).astype(out_ref.dtype)
    for copy in copies:
        copy.wait()


def make_message(query, owners, requests):
    count, columns = query.shape
    lanes = -(-owners.shape[1] // 128) * 128
    return pl.pallas_call(
        message_kernel,
        in_specs=[pl.BlockSpec(memory_space=pl.ANY)] * 3,
        out_specs=pl.BlockSpec(memory_space=pltpu.VMEM),
        out_shape=jax.ShapeDtypeStruct((count, columns + lanes), query.dtype),
        scratch_shapes=[
            pltpu.VMEM(owners.shape, owners.dtype),
            pltpu.VMEM(requests.shape, requests.dtype),
            pltpu.SemaphoreType.DMA((10,)),
        ],
        compiler_params=params(16),
        cost_estimate=pl.CostEstimate(flops=10**11, bytes_accessed=10**4, transcendentals=0),
        name="make_message",
    )(in_hbm(query), in_hbm(owners), in_hbm(requests))


def cache_kernel(
    lengths_ref, query_ref, cache_ref, signs_ref, mixed_ref, stats_ref, query_buf, top_buf, total_buf, mixed_buf
):
    requests, span, _ = cache_ref.shape
    blocks, size = signs_ref.shape
    heads = blocks // 2
    width = heads * size
    count = query_ref.shape[1] // size
    group = count // heads
    norm = 1.0 / math.sqrt(size)
    matrix = hadamard_tile(size)
    signs = (2 * signs_ref[...] - 1).astype(jnp.float32)
    query = query_ref[...].astype(jnp.float32)
    query = jnp.concatenate(
        [query[:, h * size : (h + 1) * size] * signs[h // group : h // group + 1] for h in range(count)], axis=0
    )
    query_buf[...] = jnp.dot(query.astype(jnp.bfloat16), matrix, preferred_element_type=jnp.float32) * norm
    rows = 2 * count
    kv_head = lax.broadcasted_iota(jnp.int32, (rows, width), 0) // group & (heads - 1)
    own_head = kv_head == lax.broadcasted_iota(jnp.int32, (rows, width), 1) // size
    first = lax.broadcasted_iota(jnp.int32, (rows, span), 0) < count
    position = lax.axis_index("tp") * span + lax.broadcasted_iota(jnp.int32, (rows, span), 1)
    pairs = range(0, requests, 2)
    scores = []
    for r in pairs:
        both = [query_buf[pl.ds(r + i, count, stride=requests), :] for i in range(2)]
        wide = jnp.concatenate([jnp.concatenate(both, axis=0)] * heads, axis=1)
        wide = jnp.where(own_head, wide, 0.0).astype(jnp.bfloat16)
        keys = cache_ref[r : r + 2, :, :width].reshape(2 * span, width)
        scores.append(lax.dot_general(wide, keys, NT, preferred_element_type=jnp.float32))
    probs = []
    for r, score in zip(pairs, scores):
        score = jnp.where(first, score[:, :span], score[:, span:]) * norm
        live = position < jnp.where(first, lengths_ref[0, 0, r], lengths_ref[0, 0, r + 1])
        top = jnp.max(jnp.where(live, score, LOWEST), axis=1, keepdims=True)
        prob = jnp.where(live, jnp.exp(score - top), 0.0)
        total = jnp.sum(prob, axis=1, keepdims=True)
        at = slice(r * count, (r + 2) * count)
        top_buf[at, :] = jnp.broadcast_to(top, (rows, size))
        total_buf[at, :] = jnp.broadcast_to(total, (rows, size))
        probs.append(
            jnp.concatenate([jnp.where(first, prob, 0.0), jnp.where(first, 0.0, prob)], axis=1).astype(jnp.bfloat16)
        )
    mixed = []
    for r, prob in zip(pairs, probs):
        values = cache_ref[r : r + 2, :, width:].reshape(2 * span, width)
        wide = jnp.dot(prob, values, preferred_element_type=jnp.float32)
        wide = jnp.where(own_head, wide, 0.0)
        mixed.append(sum(wide[:, k * size : (k + 1) * size] for k in range(heads)))
    mixed = jnp.concatenate(mixed, axis=0)
    high = mixed.astype(jnp.bfloat16)
    low = (mixed - high.astype(jnp.float32)).astype(jnp.bfloat16)
    plain = jnp.dot(high, matrix, preferred_element_type=jnp.float32)
    mixed_buf[...] = plain + jnp.dot(low, matrix, preferred_element_type=jnp.float32)
    lane = lax.broadcasted_iota(jnp.int32, (requests, stats_ref.shape[1]), 1)
    tops = jnp.full(lane.shape, 0.0, jnp.float32)
    totals = jnp.ones(lane.shape, jnp.float32)
    for h in range(count):
        pick = pl.ds(h, requests, stride=count)
        column = slice(h * size, (h + 1) * size)
        k = heads + h // group
        mixed_ref[:, column] = mixed_buf[pick, :] * (signs[k : k + 1] * norm)
        tops = jnp.where(lane == h, top_buf[pick, :], tops)
        totals = jnp.where(lane == h, total_buf[pick, :], totals)
    stats_ref[:requests, :] = tops
    stats_ref[requests:, :] = totals


def cache_part(lengths, query, cache, signs):
    requests, span, width = cache.shape
    size = signs.shape[1]
    columns = query.shape[1]
    vmem = pl.BlockSpec(memory_space=pltpu.VMEM)
    return pl.pallas_call(
        cache_kernel,
        in_specs=[pl.BlockSpec(memory_space=pltpu.SMEM)] + [vmem] * 3,
        out_shape=[
            jax.ShapeDtypeStruct(query.shape, jnp.float32),
            jax.ShapeDtypeStruct((2 * requests, size), jnp.float32),
        ],
        scratch_shapes=[pltpu.VMEM((requests * columns // size, size), jnp.float32)] * 4,
        compiler_params=params(),
        cost_estimate=pl.CostEstimate(
            flops=4 * span * requests * columns,
            bytes_accessed=2 * requests * span * width,
            transcendentals=span * requests * columns // size,
        ),
        name="cache_part",
    )(lengths, query, cache, signs)


def code_row(message_refs, start, requests, tokens):
    count = len(message_refs)
    me = lax.axis_index("seq")
    pieces = [ref[0:1, start : start + tokens // count].astype(jnp.float32) for ref in message_refs]
    row = [sum(jnp.where(me ^ d == at, pieces[d], 0.0) for d in range(count)) for at in range(count)]
    code = jnp.concatenate(row, axis=1).astype(jnp.int32)
    return ((code // requests) ^ me) * requests + code % requests


def score_kernel(heads, start, keys_ref, *refs):
    message_refs, (scores_ref, code_ref) = by_distance(refs[:-2], QUERY_ORDER), refs[-2:]
    requests = message_refs[0].shape[0]
    tokens, width = keys_ref.shape
    size = width // heads
    group = start // width
    code = code_row(message_refs, start, requests, tokens)
    code_ref[...] = jnp.broadcast_to(code, code_ref.shape)
    span = len(message_refs) * requests
    here = lax.broadcasted_iota(jnp.int32, (span, tokens), 0) == code
    queries = [ref[:, :start].astype(jnp.float32) for ref in message_refs]
    for k in range(heads):
        rows = []
        for g in range(group):
            at = (k * group + g) * size
            rows += [query[:, at : at + size] for query in queries]
        query = jnp.concatenate(rows, axis=0).astype(jnp.bfloat16)
        keys = keys_ref[:, k * size : (k + 1) * size]
        scores = lax.dot_general(query, keys, NT, preferred_element_type=jnp.float32)
        lines = [
            jnp.sum(jnp.where(here, scores[g * span : (g + 1) * span], 0.0), axis=0, keepdims=True)
            for g in range(group)
        ]
        lines = jnp.concatenate(lines, axis=0) * (1.0 / math.sqrt(size))
        scores_ref[k * group : (k + 1) * group, :] = lines.astype(scores_ref.dtype)


def partial_scores(heads, columns, keys, messages):
    tokens, width = keys.shape
    return pl.pallas_call(
        functools.partial(score_kernel, heads, columns),
        out_shape=[
            jax.ShapeDtypeStruct((columns * heads // width, tokens), jnp.bfloat16),
            jax.ShapeDtypeStruct((8, tokens), jnp.int32),
        ],
        compiler_params=params(),
        cost_estimate=pl.CostEstimate(flops=10**11, bytes_accessed=10**4, transcendentals=0),
        name="partial_scores",
    )(keys, *arranged(messages, QUERY_ORDER))


def mix_kernel(heads, requests, code_ref, values_ref, near_ref, cache_stats_ref, *refs):
    score_refs, (own_ref, far_ref, new_stats_ref, stats_ref) = refs[:4], refs[4:]
    own, before, across, after = [ref[...].astype(jnp.float32) for ref in score_refs]
    scores = (own + across) + (before + after)
    tokens, width = values_ref.shape
    size = width // heads
    group = scores.shape[0] // heads
    span = 2 * requests
    row = lax.broadcasted_iota(jnp.int32, (span, tokens), 0)
    here = jnp.where(row < requests, row, row + requests) == code_ref[0:1, :]
    lane = lax.broadcasted_iota(jnp.int32, (requests, stats_ref.shape[1]), 1)
    tops = jnp.full(lane.shape, 0.0, jnp.float32)
    totals = jnp.zeros(lane.shape, jnp.float32)
    for k in range(heads):
        weights = []
        for g in range(group):
            h = k * group + g
            line = jnp.where(here, jnp.broadcast_to(scores[h : h + 1, :], (span, tokens)), LOWEST)
            top = jnp.maximum(jnp.max(line, axis=1, keepdims=True), 0.1 * LOWEST)
            probs = jnp.exp(line - top)
            total = jnp.sum(probs, axis=1, keepdims=True)
            weights.append(probs)
            tops = jnp.where(lane == h, top[:requests], tops)
            totals = jnp.where(lane == h, total[:requests], totals)
        weights = jnp.concatenate(weights, axis=0).astype(jnp.bfloat16)
        columns = slice(k * size, (k + 1) * size)
        mixed = jnp.dot(weights, values_ref[:, columns], preferred_element_type=jnp.float32)
        mixed = mixed + jnp.dot(weights, near_ref[:, columns], preferred_element_type=jnp.float32)
        for g in range(group):
            at = slice((k * group + g) * size, (k * group + g + 1) * size)
            own_ref[:, at] = mixed[g * span : g * span + requests]
            far_ref[:, at] = mixed[g * span + requests : (g + 1) * span].astype(far_ref.dtype)
    new_stats_ref[...] = tops
    cache_tops = cache_stats_ref[:requests, :]
    both = jnp.maximum(cache_tops, tops)
    stats_ref[:requests, :] = both
    stats_ref[requests:, :] = cache_stats_ref[requests:, :] * jnp.exp(cache_tops - both) + totals * jnp.exp(
        tops - both
    )


def mix(heads, code, values, near_values, cache_stats, scores):
    requests, lanes = cache_stats.shape[0] // 2, cache_stats.shape[1]
    size = values.shape[1] // heads
    shape = (requests, scores[0].shape[0] * size)
    return pl.pallas_call(
        functools.partial(mix_kernel, heads, requests),
        out_shape=[
            jax.ShapeDtypeStruct(shape, jnp.float32),
            jax.ShapeDtypeStruct(shape, jnp.bfloat16),
            jax.ShapeDtypeStruct((requests, lanes), jnp.float32),
            jax.ShapeDtypeStruct(cache_stats.shape, jnp.float32),
        ],
        compiler_params=params(),
        name="mix",
    )(code, values, near_values, cache_stats, *arranged(scores, SCORE_ORDER))


def weigh_kernel(cache_ref, own_ref, cache_stats_ref, new_stats_ref, stats_ref, other_ref, base_ref, factor_ref):
    requests, columns = cache_ref.shape
    size = cache_stats_ref.shape[1]
    top, other_top = stats_ref[:requests, :], other_ref[:requests, :]
    both = jnp.maximum(top, other_top)
    total = stats_ref[requests:, :] * jnp.exp(top - both)
    total = total + other_ref[requests:, :] * jnp.exp(other_top - both)
    inverse = 1.0 / total
    cache_factor = jnp.exp(cache_stats_ref[:requests, :] - both) * inverse
    new_factor = jnp.exp(new_stats_ref[...] - both) * inverse
    for h in range(columns // size):
        at = slice(h * size, (h + 1) * size)
        factor = jnp.broadcast_to(new_factor[:, h : h + 1], (requests, size))
        factor_ref[:, at] = factor
        base_ref[:, at] = cache_ref[:, at] * cache_factor[:, h : h + 1] + own_ref[:, at] * factor


def weigh(cache_mixed, own, cache_stats, new_stats, stats, other):
    return pl.pallas_call(
        weigh_kernel,
        out_shape=[jax.ShapeDtypeStruct(own.shape, jnp.float32)] * 2,
        compiler_params=params(),
        name="weigh",
    )(cache_mixed, own, cache_stats, new_stats, stats, other)


def merge_kernel(base_ref, factor_ref, far_ref, out_ref):
    out = base_ref[...] + far_ref[...].astype(jnp.float32) * factor_ref[...]
    out_ref[...] = out.astype(out_ref.dtype)


def merge(base, factor, far):
    return pl.pallas_call(
        merge_kernel,
        out_shape=jax.ShapeDtypeStruct(far.shape, far.dtype),
        compiler_params=params(),
        name="merge",
    )(base, factor, far)


def finish_kernel(own_ref, other_ref, out_ref, out_buf, sems):
    copies = []
    for i, span in enumerate(eighths(own_ref.shape[1])):
        total = own_ref[:, span].astype(jnp.float32) + other_ref[:, span].astype(jnp.float32)
        out_buf[:, span] = total.astype(out_buf.dtype)
        copies.append(pltpu.make_async_copy(out_buf.at[:, span], out_ref.at[:, span], sems.at[i]))
        copies[-1].start()
    for copy in copies:
        copy.wait()


def finish(own, other):
    vmem = pl.BlockSpec(memory_space=pltpu.VMEM)
    return pl.pallas_call(
        finish_kernel,
        in_specs=[vmem] * 2,
        out_specs=pl.BlockSpec(memory_space=pl.ANY),
        out_shape=jax.ShapeDtypeStruct(own.shape, own.dtype),
        scratch_shapes=[pltpu.VMEM(own.shape, own.dtype), pltpu.SemaphoreType.DMA((8,))],
        compiler_params=params(),
        name="finish",
    )(own, other)


def from_partner(x, axis, distance):
    count = lax.axis_size(axis)
    return lax.ppermute(x, axis, [(i, i ^ distance) for i in range(count)])


def from_behind(x, axis, distance):
    count = lax.axis_size(axis)
    return lax.ppermute(x, axis, [(i, (i + distance) % count) for i in range(count)])


def on_device(tokens, kv_weight, owners, requests, signs, queries, kv_cache, lengths):
    seq_count = lax.axis_size("seq")
    heads = signs.shape[0] // 2
    query = queries[0, 0]
    request_count, columns = query.shape
    message = make_message(query, owners[:, :, 0], requests)
    messages = [message] + [from_partner(message, "seq", d) for d in range(1, seq_count)]
    keys, values = project(tokens, kv_weight)
    near_values = from_partner(values, "seq", 1)
    scores, code = partial_scores(heads, columns, keys, messages)
    scores = [scores] + [from_behind(scores, "seq", d) for d in range(1, seq_count)]
    cache_mixed, cache_stats = cache_part(lengths, query, kv_cache[0, 0], signs)
    own, far, new_stats, stats = mix(heads, code, values, near_values, cache_stats, scores)
    far = from_partner(far, "seq", 2)
    other = from_partner(stats, "tp", 1)
    base, factor = weigh(cache_mixed, own, cache_stats, new_stats, stats, other)
    share = merge(base, factor, far)
    return finish(share, from_partner(share, "tp", 1)).reshape(1, 1, request_count, columns)


def hadamard(order):
    rows = lax.broadcasted_iota(jnp.int32, (order, order), 0)
    cols = lax.broadcasted_iota(jnp.int32, (order, order), 1)
    parity = jnp.zeros((order, order), jnp.int32)
    for bit_number in range(order.bit_length() - 1):
        parity = parity + rows // 2**bit_number % 2 * (cols // 2**bit_number % 2)
    return (1 - 2 * (parity % 2)).astype(jnp.float32)


def rotate(blocks, sign_rows, matrix):
    product = jnp.einsum(
        "...h,hk->...k", blocks * sign_rows, matrix, precision=lax.Precision.HIGHEST
    )
    return product / math.sqrt(matrix.shape[0])


def encode(rotated):
    largest = jnp.max(jnp.abs(rotated), axis=-1) + 1e-06
    scales = largest.astype(jnp.bfloat16)
    encoded = (rotated / scales.astype(jnp.float32)[..., None]).astype(jnp.bfloat16)
    return (encoded, scales)


def decode(encoded, scales):
    return (encoded.astype(jnp.float32) * scales.astype(jnp.float32)[..., None]).astype(
        jnp.bfloat16
    )


def slot_numbers(targets, count, room):
    onehot = (targets[:, None] == lax.iota(jnp.int32, count)[None, :]).astype(jnp.int32)
    within = jnp.sum((jnp.cumsum(onehot, axis=0) - 1) * onehot, axis=1)
    return targets * room + within


def on_device_long(tokens, kv_weight, owners, requests, signs, queries, kv_cache, lengths):
    seq_count = lax.axis_size("seq")
    per_device = owners.shape[1]
    slots = max(2, (2 * per_device + seq_count - 1) // seq_count)
    head_blocks = signs.shape[0]
    kv_heads = head_blocks // 2
    head_size = signs.shape[1]
    matrix = hadamard(head_size)
    sign_rows = (2 * signs - 1).astype(jnp.float32)
    summed = lax.psum_scatter(
        jnp.dot(tokens, kv_weight, preferred_element_type=jnp.float32).astype(jnp.bfloat16),
        "seq",
        scatter_dimension=0,
        tiled=True,
    ).astype(jnp.float32)
    encoded, scales = encode(
        rotate(summed.reshape(per_device, head_blocks, head_size), sign_rows, matrix)
    )
    slot_index = slot_numbers(owners[0, :, 0], seq_count, slots)
    slot_total = seq_count * slots
    send_values = (
        jnp.zeros((slot_total, head_blocks, head_size), jnp.bfloat16).at[slot_index].set(encoded)
    )
    send_scales = jnp.zeros((slot_total, head_blocks), jnp.bfloat16).at[slot_index].set(scales)
    send_codes = jnp.zeros((slot_total,), jnp.int32).at[slot_index].set(requests[0] + 1)
    got_values, got_scales, arrived_codes = (
        lax.all_to_all(send_values, "seq", split_axis=0, concat_axis=0, tiled=True),
        lax.all_to_all(send_scales, "seq", split_axis=0, concat_axis=0, tiled=True),
        lax.all_to_all(send_codes, "seq", split_axis=0, concat_axis=0, tiled=True),
    )
    arrived = decode(got_values, got_scales)
    query = queries[0, 0]
    request_count = query.shape[0]
    group = query.shape[1] // (kv_heads * head_size)
    query_blocks = query.astype(jnp.float32).reshape(request_count, kv_heads, group, head_size)
    query_rot = rotate(query_blocks, sign_rows[:kv_heads][:, None, :], matrix).astype(jnp.bfloat16)
    local_cache = kv_cache[0, 0]
    cache_span = local_cache.shape[1]
    local_cache = local_cache.reshape(request_count, cache_span, head_blocks, head_size)
    score_scale = 1.0 / math.sqrt(head_size)
    lowest = -1e30
    highest = lax.Precision.HIGHEST
    score_cache = (
        jnp.einsum(
            "rkgd,rckd->rkgc",
            query_rot,
            local_cache[:, :, :kv_heads],
            preferred_element_type=jnp.float32,
        )
        * score_scale
    )
    score_new = (
        jnp.einsum(
            "rkgd,nkd->rkgn", query_rot, arrived[:, :kv_heads], preferred_element_type=jnp.float32
        )
        * score_scale
    )
    positions = lax.axis_index("tp") * cache_span + lax.iota(jnp.int32, cache_span)
    mask_cache = (positions[None, :] < lengths[0, 0][:, None])[:, None, None, :]
    match = arrived_codes[None, :] == (lax.iota(jnp.int32, request_count) + 1)[:, None]
    mask_new = match[:, None, None, :]
    top = jnp.maximum(
        jnp.max(jnp.where(mask_cache, score_cache, lowest), axis=-1),
        jnp.max(jnp.where(mask_new, score_new, lowest), axis=-1),
    )
    probs_cache = jnp.where(mask_cache, jnp.exp(score_cache - top[..., None]), 0.0)
    probs_new = jnp.where(mask_new, jnp.exp(score_new - top[..., None]), 0.0)
    total = jnp.sum(probs_cache, axis=-1) + jnp.sum(probs_new, axis=-1)
    mixed = jnp.einsum(
        "rkgc,rckd->rkgd",
        probs_cache,
        local_cache[:, :, kv_heads:].astype(jnp.float32),
        precision=highest,
    )
    mixed = mixed + jnp.einsum(
        "rkgn,nkd->rkgd", probs_new, arrived[:, kv_heads:].astype(jnp.float32), precision=highest
    )
    shared_top = lax.pmax(top, "tp")
    factor = jnp.exp(top - shared_top)
    total, mixed = (
        lax.psum((total * factor).astype(jnp.bfloat16), "tp").astype(jnp.float32),
        lax.psum((mixed * factor[..., None]).astype(jnp.bfloat16), "tp").astype(jnp.float32),
    )
    mixed = mixed / total[..., None]
    output = rotate(mixed, 1.0, matrix) * sign_rows[kv_heads:][None, :, None, :]
    return output.reshape(1, 1, request_count, group * kv_heads * head_size).astype(jnp.bfloat16)


def solution(mesh):
    placed = (
        P(("groups", "tp", "section"), "seq"),
        P("seq", None),
        P(("groups", "tp", "section"), "seq", None),
        P(("groups", "tp", "section"), "seq"),
        P(),
        P(("groups", "seq"), "section", None, None),
        P(("groups", "seq"), "section", None, "tp", None),
        P(("groups", "seq"), "section", None),
    )
    short = mesh.shape["seq"] == 4 and mesh.shape["tp"] == 2
    return jax.shard_map(
        on_device if short else on_device_long,
        mesh=mesh,
        in_specs=placed,
        out_specs=P(("groups", "seq"), "section", None, None),
        check_vma=False,
    )
```

```python
import functools
import math

import jax
import jax.numpy as jnp
from jax import lax
from jax.experimental import pallas as pl
from jax.experimental.pallas import tpu as pltpu
from jax.sharding import PartitionSpec as P

LOWEST = -1e30
MIB = 1024 * 1024
NT = (((1,), (1,)), ((), ()))


def params(mib=32):
    return pltpu.CompilerParams(vmem_limit_bytes=mib * MIB)


def in_hbm(x):
    return pltpu.with_memory_space_constraint(x, pltpu.HBM)


def in_vmem(x):
    return pltpu.with_memory_space_constraint(x, pltpu.VMEM)


def hadamard_tile(order):
    rows = lax.broadcasted_iota(jnp.int32, (order, order), 0)
    cols = lax.broadcasted_iota(jnp.int32, (order, order), 1)
    common = rows & cols
    parity = jnp.zeros((order, order), jnp.int32)
    for bit_number in range(order.bit_length() - 1):
        parity = parity ^ (common >> bit_number)
    return (1 - 2 * (parity & 1)).astype(jnp.float32).astype(jnp.bfloat16)


QUERY_ORDER = (3, 2, 1)
SCORE_ORDER = (1, 2, 3)
FINISH_PLACES = (2, 1, 0)


def arranged(blocks, order):
    return [blocks[0]] + [blocks[d] for d in order]


def by_distance(refs, order):
    return [refs[0]] + [refs[1 + order.index(d)] for d in range(1, len(refs))]


def project_kernel(tokens_ref, weight_ref, keys_ref, values_ref):
    width = keys_ref.shape[1]
    for out_ref, columns in ((keys_ref, slice(0, width)), (values_ref, slice(width, 2 * width))):
        out_ref[...] = jnp.dot(
            tokens_ref[...], weight_ref[:, columns], preferred_element_type=jnp.float32
        ).astype(out_ref.dtype)


def project(tokens, weight):
    rows, features = tokens.shape
    width = weight.shape[1] // 2
    vmem = pl.BlockSpec(memory_space=pltpu.VMEM)
    return pl.pallas_call(
        project_kernel,
        in_specs=[vmem] * 2,
        out_specs=[vmem] * 2,
        out_shape=[jax.ShapeDtypeStruct((rows, width), jnp.bfloat16)] * 2,
        compiler_params=params(32),
        cost_estimate=pl.CostEstimate(
            flops=4 * rows * features * width,
            bytes_accessed=2 * (rows * features + 2 * features * width),
            transcendentals=0,
        ),
        name="project",
    )(in_vmem(tokens), in_vmem(weight))


def message_kernel(query_ref, owners_ref, requests_ref, out_ref, owners_buf, requests_buf, sems):
    requests, columns = query_ref.shape
    per_device = owners_ref.shape[1]
    copies = [
        pltpu.make_async_copy(query_ref, out_ref.at[:, :columns], sems.at[0]),
        pltpu.make_async_copy(owners_ref, owners_buf, sems.at[1]),
        pltpu.make_async_copy(requests_ref, requests_buf, sems.at[2]),
    ]
    for copy in copies:
        copy.start()
    copies[1].wait()
    copies[2].wait()
    code = (owners_buf[...] * requests + requests_buf[...]).astype(jnp.float32)
    spare = jnp.zeros((1, out_ref.shape[1] - columns - per_device), jnp.float32)
    code = jnp.concatenate([code, spare], axis=1)
    out_ref[:, columns:] = jnp.broadcast_to(code, (requests, code.shape[1])).astype(out_ref.dtype)
    copies[0].wait()


def make_message(query, owners, requests):
    count, columns = query.shape
    lanes = -(-owners.shape[1] // 128) * 128
    return pl.pallas_call(
        message_kernel,
        in_specs=[pl.BlockSpec(memory_space=pl.ANY)] * 3,
        out_specs=pl.BlockSpec(memory_space=pltpu.VMEM),
        out_shape=jax.ShapeDtypeStruct((count, columns + lanes), query.dtype),
        scratch_shapes=[
            pltpu.VMEM(owners.shape, owners.dtype),
            pltpu.VMEM(requests.shape, requests.dtype),
            pltpu.SemaphoreType.DMA((3,)),
        ],
        compiler_params=params(16),
        cost_estimate=pl.CostEstimate(flops=10**11, bytes_accessed=10**4, transcendentals=0),
        name="make_message",
    )(in_hbm(query), in_hbm(owners), in_hbm(requests))


def cache_kernel(
    lengths_ref, query_ref, cache_ref, signs_ref, mixed_ref, stats_ref, query_buf, top_buf, total_buf, mixed_buf
):
    requests, span, _ = cache_ref.shape
    blocks, size = signs_ref.shape
    heads = blocks // 2
    width = heads * size
    count = query_ref.shape[1] // size
    group = count // heads
    norm = 1.0 / math.sqrt(size)
    matrix = hadamard_tile(size)
    signs = (2 * signs_ref[...] - 1).astype(jnp.float32)
    query = query_ref[...].astype(jnp.float32)
    query = jnp.concatenate(
        [query[:, h * size : (h + 1) * size] * signs[h // group : h // group + 1] for h in range(count)], axis=0
    )
    query_buf[...] = jnp.dot(query.astype(jnp.bfloat16), matrix, preferred_element_type=jnp.float32) * norm
    rows = 2 * count
    kv_head = lax.broadcasted_iota(jnp.int32, (rows, width), 0) // group & (heads - 1)
    own_head = kv_head == lax.broadcasted_iota(jnp.int32, (rows, width), 1) // size
    first = lax.broadcasted_iota(jnp.int32, (rows, span), 0) < count
    position = lax.axis_index("tp") * span + lax.broadcasted_iota(jnp.int32, (rows, span), 1)
    pairs = range(0, requests, 2)
    scores = []
    for r in pairs:
        both = [query_buf[pl.ds(r + i, count, stride=requests), :] for i in range(2)]
        wide = jnp.concatenate([jnp.concatenate(both, axis=0)] * heads, axis=1)
        wide = jnp.where(own_head, wide, 0.0).astype(jnp.bfloat16)
        keys = cache_ref[r : r + 2, :, :width].reshape(2 * span, width)
        scores.append(lax.dot_general(wide, keys, NT, preferred_element_type=jnp.float32))
    probs = []
    for r, score in zip(pairs, scores):
        score = jnp.where(first, score[:, :span], score[:, span:]) * norm
        live = position < jnp.where(first, lengths_ref[0, 0, r], lengths_ref[0, 0, r + 1])
        top = jnp.max(jnp.where(live, score, LOWEST), axis=1, keepdims=True)
        prob = jnp.where(live, jnp.exp(score - top), 0.0)
        total = jnp.sum(prob, axis=1, keepdims=True)
        at = slice(r * count, (r + 2) * count)
        top_buf[at, :] = jnp.broadcast_to(top, (rows, size))
        total_buf[at, :] = jnp.broadcast_to(total, (rows, size))
        probs.append(
            jnp.concatenate([jnp.where(first, prob, 0.0), jnp.where(first, 0.0, prob)], axis=1).astype(jnp.bfloat16)
        )
    mixed = []
    for r, prob in zip(pairs, probs):
        values = cache_ref[r : r + 2, :, width:].reshape(2 * span, width)
        wide = jnp.dot(prob, values, preferred_element_type=jnp.float32)
        wide = jnp.where(own_head, wide, 0.0)
        mixed.append(sum(wide[:, k * size : (k + 1) * size] for k in range(heads)))
    mixed = jnp.concatenate(mixed, axis=0)
    high = mixed.astype(jnp.bfloat16)
    low = (mixed - high.astype(jnp.float32)).astype(jnp.bfloat16)
    plain = jnp.dot(high, matrix, preferred_element_type=jnp.float32)
    mixed_buf[...] = plain + jnp.dot(low, matrix, preferred_element_type=jnp.float32)
    lane = lax.broadcasted_iota(jnp.int32, (requests, stats_ref.shape[1]), 1)
    tops = jnp.full(lane.shape, 0.0, jnp.float32)
    totals = jnp.ones(lane.shape, jnp.float32)
    for h in range(count):
        pick = pl.ds(h, requests, stride=count)
        column = slice(h * size, (h + 1) * size)
        k = heads + h // group
        mixed_ref[:, column] = mixed_buf[pick, :] * (signs[k : k + 1] * norm)
        tops = jnp.where(lane == h, top_buf[pick, :], tops)
        totals = jnp.where(lane == h, total_buf[pick, :], totals)
    stats_ref[:requests, :] = tops
    stats_ref[requests:, :] = totals


def cache_part(lengths, query, cache, signs):
    requests, span, width = cache.shape
    size = signs.shape[1]
    columns = query.shape[1]
    vmem = pl.BlockSpec(memory_space=pltpu.VMEM)
    return pl.pallas_call(
        cache_kernel,
        in_specs=[pl.BlockSpec(memory_space=pltpu.SMEM)] + [vmem] * 3,
        out_shape=[
            jax.ShapeDtypeStruct(query.shape, jnp.float32),
            jax.ShapeDtypeStruct((2 * requests, size), jnp.float32),
        ],
        scratch_shapes=[pltpu.VMEM((requests * columns // size, size), jnp.float32)] * 4,
        compiler_params=params(),
        cost_estimate=pl.CostEstimate(
            flops=4 * span * requests * columns,
            bytes_accessed=2 * requests * span * width,
            transcendentals=span * requests * columns // size,
        ),
        name="cache_part",
    )(lengths, query, cache, signs)


def code_row(message_refs, start, requests, tokens):
    count = len(message_refs)
    me = lax.axis_index("seq")
    pieces = [ref[0:1, start : start + tokens // count].astype(jnp.float32) for ref in message_refs]
    row = [sum(jnp.where(me ^ d == at, pieces[d], 0.0) for d in range(count)) for at in range(count)]
    code = jnp.concatenate(row, axis=1).astype(jnp.int32)
    return ((code // requests) ^ me) * requests + code % requests


def score_kernel(heads, start, keys_ref, *refs):
    message_refs, (scores_ref, code_ref) = by_distance(refs[:-2], QUERY_ORDER), refs[-2:]
    requests = message_refs[0].shape[0]
    tokens, width = keys_ref.shape
    size = width // heads
    group = start // width
    code = code_row(message_refs, start, requests, tokens)
    code_ref[...] = jnp.broadcast_to(code, code_ref.shape)
    span = len(message_refs) * requests
    here = lax.broadcasted_iota(jnp.int32, (span, tokens), 0) == code
    queries = [ref[:, :start].astype(jnp.float32) for ref in message_refs]
    for k in range(heads):
        rows = []
        for g in range(group):
            at = (k * group + g) * size
            rows += [query[:, at : at + size] for query in queries]
        query = jnp.concatenate(rows, axis=0).astype(jnp.bfloat16)
        keys = keys_ref[:, k * size : (k + 1) * size]
        scores = lax.dot_general(query, keys, NT, preferred_element_type=jnp.float32)
        lines = [
            jnp.sum(jnp.where(here, scores[g * span : (g + 1) * span], 0.0), axis=0, keepdims=True)
            for g in range(group)
        ]
        lines = jnp.concatenate(lines, axis=0) * (1.0 / math.sqrt(size))
        scores_ref[k * group : (k + 1) * group, :] = lines.astype(scores_ref.dtype)


def partial_scores(heads, columns, keys, messages):
    tokens, width = keys.shape
    return pl.pallas_call(
        functools.partial(score_kernel, heads, columns),
        out_shape=[
            jax.ShapeDtypeStruct((columns * heads // width, tokens), jnp.bfloat16),
            jax.ShapeDtypeStruct((8, tokens), jnp.int32),
        ],
        compiler_params=params(),
        cost_estimate=pl.CostEstimate(flops=10**11, bytes_accessed=10**4, transcendentals=0),
        name="partial_scores",
    )(keys, *arranged(messages, QUERY_ORDER))


def packed(value, count):
    lane = lax.broadcasted_iota(jnp.int32, value.shape, 1)
    high = value.astype(jnp.bfloat16).astype(jnp.float32)
    middle = (value - high).astype(jnp.bfloat16).astype(jnp.float32)
    low = value - high - middle
    middle, low = pltpu.roll(middle, count, 1), pltpu.roll(low, 2 * count, 1)
    return jnp.where(lane < count, high, jnp.where(lane < 2 * count, middle, low))


def unpacked(message, at, count):
    parts = [message[:, at + part * count : at + (part + 1) * count] for part in range(3)]
    return parts[0] + parts[1] + parts[2]


def mix_kernel(heads, requests, code_ref, values_ref, near_ref, cache_ref, cache_stats_ref, *refs):
    score_refs, (share_ref, far_ref) = refs[:4], refs[4:]
    own, before, across, after = [ref[...].astype(jnp.float32) for ref in score_refs]
    scores = (own + across) + (before + after)
    tokens, width = values_ref.shape
    size = width // heads
    count, columns = scores.shape[0], cache_ref.shape[1]
    group = count // heads
    span = 2 * requests
    row = lax.broadcasted_iota(jnp.int32, (span, tokens), 0)
    here = jnp.where(row < requests, row, row + requests) == code_ref[0:1, :]
    lane = lax.broadcasted_iota(jnp.int32, (requests, cache_stats_ref.shape[1]), 1)
    tops = jnp.full(lane.shape, 0.0, jnp.float32)
    totals = jnp.zeros(lane.shape, jnp.float32)
    parts = []
    for k in range(heads):
        weights = []
        for g in range(group):
            h = k * group + g
            line = jnp.where(here, jnp.broadcast_to(scores[h : h + 1, :], (span, tokens)), LOWEST)
            top = jnp.maximum(jnp.max(line, axis=1, keepdims=True), 0.1 * LOWEST)
            probs = jnp.exp(line - top)
            total = jnp.sum(probs, axis=1, keepdims=True)
            weights.append(probs)
            tops = jnp.where(lane == h, top[:requests], tops)
            totals = jnp.where(lane == h, total[:requests], totals)
        weights = jnp.concatenate(weights, axis=0).astype(jnp.bfloat16)
        part = slice(k * size, (k + 1) * size)
        mixed = jnp.dot(weights, values_ref[:, part], preferred_element_type=jnp.float32)
        mixed = mixed + jnp.dot(weights, near_ref[:, part], preferred_element_type=jnp.float32)
        for g in range(group):
            at = slice((k * group + g) * size, (k * group + g + 1) * size)
            parts.append(mixed[g * span : g * span + requests])
            far_ref[:, at] = mixed[g * span + requests : (g + 1) * span].astype(far_ref.dtype)
    cache_tops = cache_stats_ref[:requests, :]
    both = jnp.maximum(cache_tops, tops)
    cache_factor = jnp.exp(cache_tops - both)
    new_factor = jnp.exp(tops - both)
    total = cache_stats_ref[requests:, :] * cache_factor + totals * new_factor
    for h, part in enumerate(parts):
        at = slice(h * size, (h + 1) * size)
        share = cache_ref[:, at] * cache_factor[:, h : h + 1] + part * new_factor[:, h : h + 1]
        share_ref[:, at] = share.astype(share_ref.dtype)
    lanes = cache_stats_ref.shape[1]
    far_ref[:, columns:] = jnp.zeros((requests, 3 * lanes), far_ref.dtype)
    for i, value in enumerate((both, total, new_factor)):
        share_ref[:, columns + i * lanes : columns + (i + 1) * lanes] = packed(value, count).astype(share_ref.dtype)


def mix(heads, code, values, near_values, cache_mixed, cache_stats, scores):
    requests, lanes = cache_stats.shape[0] // 2, cache_stats.shape[1]
    columns = cache_mixed.shape[1]
    return pl.pallas_call(
        functools.partial(mix_kernel, heads, requests),
        out_shape=[
            jax.ShapeDtypeStruct((requests, columns + 3 * lanes), jnp.bfloat16),
        ]
        * 2,
        compiler_params=params(),
        name="mix",
    )(code, values, near_values, cache_mixed, cache_stats, *arranged(scores, SCORE_ORDER))


def finish_kernel(count, own_ref, *refs):
    out_ref = refs[-1]
    other_ref, own_far_ref, other_far_ref = [refs[i] for i in FINISH_PLACES]
    columns = out_ref.shape[1]
    size = columns // count
    lanes = (own_ref.shape[1] - columns) // 3
    first = lax.axis_index("tp") == 0

    def stats(ref):
        message = ref[:, columns:].astype(jnp.float32)
        return [unpacked(message, i * lanes, count) for i in range(3)]

    own_top, own_total, own_new = stats(own_ref)
    other_top, other_total, other_new = stats(other_ref)
    both = jnp.maximum(own_top, other_top)
    own_factor, other_factor = jnp.exp(own_top - both), jnp.exp(other_top - both)
    own_total, other_total = own_total * own_factor, other_total * other_factor
    total = jnp.where(first, own_total, other_total) + jnp.where(first, other_total, own_total)
    inverse = 1.0 / total
    sides = []
    for ref, far_ref, factor, new in (
        (own_ref, own_far_ref, own_factor, own_new),
        (other_ref, other_far_ref, other_factor, other_new),
    ):
        factor = factor * inverse
        sides.append((ref, far_ref, factor, factor * new))
    for h in range(count):
        at = slice(h * size, (h + 1) * size)
        terms = [
            ref[:, at].astype(jnp.float32) * factor[:, h : h + 1]
            + far_ref[:, at].astype(jnp.float32) * far_factor[:, h : h + 1]
            for ref, far_ref, factor, far_factor in sides
        ]
        out_ref[:, at] = (terms[0] + terms[1]).astype(out_ref.dtype)


def finish(count, columns, own, other, own_far, other_far):
    arrived = (other, own_far, other_far)
    return pl.pallas_call(
        functools.partial(finish_kernel, count),
        out_shape=jax.ShapeDtypeStruct((own.shape[0], columns), jnp.bfloat16),
        compiler_params=params(),
        name="finish",
    )(own, *[arrived[FINISH_PLACES.index(i)] for i in range(3)])


def from_partner(x, axis, distance):
    count = lax.axis_size(axis)
    return lax.ppermute(x, axis, [(i, i ^ distance) for i in range(count)])


def from_behind(x, axis, distance):
    count = lax.axis_size(axis)
    return lax.ppermute(x, axis, [(i, (i + distance) % count) for i in range(count)])


def on_device(tokens, kv_weight, owners, requests, signs, queries, kv_cache, lengths):
    seq_count = lax.axis_size("seq")
    heads = signs.shape[0] // 2
    query = queries[0, 0]
    request_count, columns = query.shape
    message = make_message(query, owners[:, :, 0], requests)
    messages = [message] + [from_partner(message, "seq", d) for d in range(1, seq_count)]
    keys, values = project(tokens, kv_weight)
    near_values = from_partner(values, "seq", 1)
    scores, code = partial_scores(heads, columns, keys, messages)
    scores = [scores] + [from_behind(scores, "seq", d) for d in range(1, seq_count)]
    cache_mixed, cache_stats = cache_part(lengths, query, kv_cache[0, 0], signs)
    share, far = mix(heads, code, values, near_values, cache_mixed, cache_stats, scores)
    far_pairs = [(i, i ^ 5) for i in range(2 * seq_count)]
    output = finish(
        columns // signs.shape[1],
        columns,
        share,
        from_partner(share, "tp", 1),
        from_partner(far, "seq", 2),
        lax.ppermute(far, ("seq", "tp"), far_pairs),
    )
    return output.reshape(1, 1, request_count, columns)


def hadamard(order):
    rows = lax.broadcasted_iota(jnp.int32, (order, order), 0)
    cols = lax.broadcasted_iota(jnp.int32, (order, order), 1)
    parity = jnp.zeros((order, order), jnp.int32)
    for bit_number in range(order.bit_length() - 1):
        parity = parity + rows // 2**bit_number % 2 * (cols // 2**bit_number % 2)
    return (1 - 2 * (parity % 2)).astype(jnp.float32)


def rotate(blocks, sign_rows, matrix):
    product = jnp.einsum(
        "...h,hk->...k", blocks * sign_rows, matrix, precision=lax.Precision.HIGHEST
    )
    return product / math.sqrt(matrix.shape[0])


def encode(rotated):
    largest = jnp.max(jnp.abs(rotated), axis=-1) + 1e-06
    scales = largest.astype(jnp.bfloat16)
    encoded = (rotated / scales.astype(jnp.float32)[..., None]).astype(jnp.bfloat16)
    return (encoded, scales)


def decode(encoded, scales):
    return (encoded.astype(jnp.float32) * scales.astype(jnp.float32)[..., None]).astype(
        jnp.bfloat16
    )


def slot_numbers(targets, count, room):
    onehot = (targets[:, None] == lax.iota(jnp.int32, count)[None, :]).astype(jnp.int32)
    within = jnp.sum((jnp.cumsum(onehot, axis=0) - 1) * onehot, axis=1)
    return targets * room + within


def on_device_long(tokens, kv_weight, owners, requests, signs, queries, kv_cache, lengths):
    seq_count = lax.axis_size("seq")
    per_device = owners.shape[1]
    slots = max(2, (2 * per_device + seq_count - 1) // seq_count)
    head_blocks = signs.shape[0]
    kv_heads = head_blocks // 2
    head_size = signs.shape[1]
    matrix = hadamard(head_size)
    sign_rows = (2 * signs - 1).astype(jnp.float32)
    summed = lax.psum_scatter(
        jnp.dot(tokens, kv_weight, preferred_element_type=jnp.float32).astype(jnp.bfloat16),
        "seq",
        scatter_dimension=0,
        tiled=True,
    ).astype(jnp.float32)
    encoded, scales = encode(
        rotate(summed.reshape(per_device, head_blocks, head_size), sign_rows, matrix)
    )
    slot_index = slot_numbers(owners[0, :, 0], seq_count, slots)
    slot_total = seq_count * slots
    send_values = (
        jnp.zeros((slot_total, head_blocks, head_size), jnp.bfloat16).at[slot_index].set(encoded)
    )
    send_scales = jnp.zeros((slot_total, head_blocks), jnp.bfloat16).at[slot_index].set(scales)
    send_codes = jnp.zeros((slot_total,), jnp.int32).at[slot_index].set(requests[0] + 1)
    got_values, got_scales, arrived_codes = (
        lax.all_to_all(send_values, "seq", split_axis=0, concat_axis=0, tiled=True),
        lax.all_to_all(send_scales, "seq", split_axis=0, concat_axis=0, tiled=True),
        lax.all_to_all(send_codes, "seq", split_axis=0, concat_axis=0, tiled=True),
    )
    arrived = decode(got_values, got_scales)
    query = queries[0, 0]
    request_count = query.shape[0]
    group = query.shape[1] // (kv_heads * head_size)
    query_blocks = query.astype(jnp.float32).reshape(request_count, kv_heads, group, head_size)
    query_rot = rotate(query_blocks, sign_rows[:kv_heads][:, None, :], matrix).astype(jnp.bfloat16)
    local_cache = kv_cache[0, 0]
    cache_span = local_cache.shape[1]
    local_cache = local_cache.reshape(request_count, cache_span, head_blocks, head_size)
    score_scale = 1.0 / math.sqrt(head_size)
    lowest = -1e30
    highest = lax.Precision.HIGHEST
    score_cache = (
        jnp.einsum(
            "rkgd,rckd->rkgc",
            query_rot,
            local_cache[:, :, :kv_heads],
            preferred_element_type=jnp.float32,
        )
        * score_scale
    )
    score_new = (
        jnp.einsum(
            "rkgd,nkd->rkgn", query_rot, arrived[:, :kv_heads], preferred_element_type=jnp.float32
        )
        * score_scale
    )
    positions = lax.axis_index("tp") * cache_span + lax.iota(jnp.int32, cache_span)
    mask_cache = (positions[None, :] < lengths[0, 0][:, None])[:, None, None, :]
    match = arrived_codes[None, :] == (lax.iota(jnp.int32, request_count) + 1)[:, None]
    mask_new = match[:, None, None, :]
    top = jnp.maximum(
        jnp.max(jnp.where(mask_cache, score_cache, lowest), axis=-1),
        jnp.max(jnp.where(mask_new, score_new, lowest), axis=-1),
    )
    probs_cache = jnp.where(mask_cache, jnp.exp(score_cache - top[..., None]), 0.0)
    probs_new = jnp.where(mask_new, jnp.exp(score_new - top[..., None]), 0.0)
    total = jnp.sum(probs_cache, axis=-1) + jnp.sum(probs_new, axis=-1)
    mixed = jnp.einsum(
        "rkgc,rckd->rkgd",
        probs_cache,
        local_cache[:, :, kv_heads:].astype(jnp.float32),
        precision=highest,
    )
    mixed = mixed + jnp.einsum(
        "rkgn,nkd->rkgd", probs_new, arrived[:, kv_heads:].astype(jnp.float32), precision=highest
    )
    shared_top = lax.pmax(top, "tp")
    factor = jnp.exp(top - shared_top)
    total, mixed = (
        lax.psum((total * factor).astype(jnp.bfloat16), "tp").astype(jnp.float32),
        lax.psum((mixed * factor[..., None]).astype(jnp.bfloat16), "tp").astype(jnp.float32),
    )
    mixed = mixed / total[..., None]
    output = rotate(mixed, 1.0, matrix) * sign_rows[kv_heads:][None, :, None, :]
    return output.reshape(1, 1, request_count, group * kv_heads * head_size).astype(jnp.bfloat16)


def solution(mesh):
    placed = (
        P(("groups", "tp", "section"), "seq"),
        P("seq", None),
        P(("groups", "tp", "section"), "seq", None),
        P(("groups", "tp", "section"), "seq"),
        P(),
        P(("groups", "seq"), "section", None, None),
        P(("groups", "seq"), "section", None, "tp", None),
        P(("groups", "seq"), "section", None),
    )
    short = mesh.shape["seq"] == 4 and mesh.shape["tp"] == 2
    return jax.shard_map(
        on_device if short else on_device_long,
        mesh=mesh,
        in_specs=placed,
        out_specs=P(("groups", "seq"), "section", None, None),
        check_vma=False,
    )
```

```python
import functools
import math

import jax
import jax.numpy as jnp
from jax import lax
from jax.experimental import pallas as pl
from jax.experimental.pallas import tpu as pltpu
from jax.sharding import PartitionSpec as P

LOWEST = -1e30
MIB = 1024 * 1024
NT = (((1,), (1,)), ((), ()))


def params(mib=32):
    return pltpu.CompilerParams(vmem_limit_bytes=mib * MIB)


def in_hbm(x):
    return pltpu.with_memory_space_constraint(x, pltpu.HBM)


def in_vmem(x):
    return pltpu.with_memory_space_constraint(x, pltpu.VMEM)


def hadamard_tile(order):
    rows = lax.broadcasted_iota(jnp.int32, (order, order), 0)
    cols = lax.broadcasted_iota(jnp.int32, (order, order), 1)
    common = rows & cols
    parity = jnp.zeros((order, order), jnp.int32)
    for bit_number in range(order.bit_length() - 1):
        parity = parity ^ (common >> bit_number)
    return (1 - 2 * (parity & 1)).astype(jnp.float32).astype(jnp.bfloat16)


QUERY_ORDER = (3, 2, 1)
SCORE_ORDER = (1, 2, 3)
FINISH_PLACES = (2, 0, 1)


def arranged(blocks, order):
    return [blocks[0]] + [blocks[d] for d in order]


def by_distance(refs, order):
    return [refs[0]] + [refs[1 + order.index(d)] for d in range(1, len(refs))]


def project_kernel(tokens_ref, weight_ref, keys_ref, values_ref):
    width = keys_ref.shape[1]
    for out_ref, columns in ((keys_ref, slice(0, width)), (values_ref, slice(width, 2 * width))):
        out_ref[...] = jnp.dot(
            tokens_ref[...], weight_ref[:, columns], preferred_element_type=jnp.float32
        ).astype(out_ref.dtype)


def project(tokens, weight):
    rows, features = tokens.shape
    width = weight.shape[1] // 2
    vmem = pl.BlockSpec(memory_space=pltpu.VMEM)
    return pl.pallas_call(
        project_kernel,
        in_specs=[vmem] * 2,
        out_specs=[vmem] * 2,
        out_shape=[jax.ShapeDtypeStruct((rows, width), jnp.bfloat16)] * 2,
        compiler_params=params(32),
        cost_estimate=pl.CostEstimate(
            flops=4 * rows * features * width,
            bytes_accessed=2 * (rows * features + 2 * features * width),
            transcendentals=0,
        ),
        name="project",
    )(in_vmem(tokens), in_vmem(weight))


def message_kernel(query_ref, owners_ref, requests_ref, out_ref, owners_buf, requests_buf, sems):
    requests, columns = query_ref.shape
    per_device = owners_ref.shape[1]
    copies = [
        pltpu.make_async_copy(query_ref, out_ref.at[:, :columns], sems.at[0]),
        pltpu.make_async_copy(owners_ref, owners_buf, sems.at[1]),
        pltpu.make_async_copy(requests_ref, requests_buf, sems.at[2]),
    ]
    for copy in copies:
        copy.start()
    copies[1].wait()
    copies[2].wait()
    code = (owners_buf[...] * requests + requests_buf[...]).astype(jnp.float32)
    spare = jnp.zeros((1, out_ref.shape[1] - columns - per_device), jnp.float32)
    code = jnp.concatenate([code, spare], axis=1)
    out_ref[:, columns:] = jnp.broadcast_to(code, (requests, code.shape[1])).astype(out_ref.dtype)
    copies[0].wait()


def make_message(query, owners, requests):
    count, columns = query.shape
    lanes = -(-owners.shape[1] // 128) * 128
    return pl.pallas_call(
        message_kernel,
        in_specs=[pl.BlockSpec(memory_space=pl.ANY)] * 3,
        out_specs=pl.BlockSpec(memory_space=pltpu.VMEM),
        out_shape=jax.ShapeDtypeStruct((count, columns + lanes), query.dtype),
        scratch_shapes=[
            pltpu.VMEM(owners.shape, owners.dtype),
            pltpu.VMEM(requests.shape, requests.dtype),
            pltpu.SemaphoreType.DMA((3,)),
        ],
        compiler_params=params(16),
        cost_estimate=pl.CostEstimate(flops=10**11, bytes_accessed=10**4, transcendentals=0),
        name="make_message",
    )(in_hbm(query), in_hbm(owners), in_hbm(requests))


def cache_kernel(
    lengths_ref, query_ref, cache_ref, signs_ref, mixed_ref, stats_ref, query_buf, top_buf, total_buf, mixed_buf
):
    requests, span, _ = cache_ref.shape
    blocks, size = signs_ref.shape
    heads = blocks // 2
    width = heads * size
    count = query_ref.shape[1] // size
    group = count // heads
    norm = 1.0 / math.sqrt(size)
    matrix = hadamard_tile(size)
    signs = (2 * signs_ref[...] - 1).astype(jnp.float32)
    query = query_ref[...].astype(jnp.float32)
    query = jnp.concatenate(
        [query[:, h * size : (h + 1) * size] * signs[h // group : h // group + 1] for h in range(count)], axis=0
    )
    query_buf[...] = jnp.dot(query.astype(jnp.bfloat16), matrix, preferred_element_type=jnp.float32) * norm
    rows = 2 * count
    kv_head = lax.broadcasted_iota(jnp.int32, (rows, width), 0) // group & (heads - 1)
    own_head = kv_head == lax.broadcasted_iota(jnp.int32, (rows, width), 1) // size
    first = lax.broadcasted_iota(jnp.int32, (rows, span), 0) < count
    position = lax.axis_index("tp") * span + lax.broadcasted_iota(jnp.int32, (rows, span), 1)
    pairs = range(0, requests, 2)
    scores = []
    for r in pairs:
        both = [query_buf[pl.ds(r + i, count, stride=requests), :] for i in range(2)]
        wide = jnp.concatenate([jnp.concatenate(both, axis=0)] * heads, axis=1)
        wide = jnp.where(own_head, wide, 0.0).astype(jnp.bfloat16)
        keys = cache_ref[r : r + 2, :, :width].reshape(2 * span, width)
        scores.append(lax.dot_general(wide, keys, NT, preferred_element_type=jnp.float32))
    probs = []
    for r, score in zip(pairs, scores):
        score = jnp.where(first, score[:, :span], score[:, span:]) * norm
        live = position < jnp.where(first, lengths_ref[0, 0, r], lengths_ref[0, 0, r + 1])
        top = jnp.max(jnp.where(live, score, LOWEST), axis=1, keepdims=True)
        prob = jnp.where(live, jnp.exp(score - top), 0.0)
        total = jnp.sum(prob, axis=1, keepdims=True)
        at = slice(r * count, (r + 2) * count)
        top_buf[at, :] = jnp.broadcast_to(top, (rows, size))
        total_buf[at, :] = jnp.broadcast_to(total, (rows, size))
        probs.append(
            jnp.concatenate([jnp.where(first, prob, 0.0), jnp.where(first, 0.0, prob)], axis=1).astype(jnp.bfloat16)
        )
    mixed = []
    for r, prob in zip(pairs, probs):
        values = cache_ref[r : r + 2, :, width:].reshape(2 * span, width)
        wide = jnp.dot(prob, values, preferred_element_type=jnp.float32)
        wide = jnp.where(own_head, wide, 0.0)
        mixed.append(sum(wide[:, k * size : (k + 1) * size] for k in range(heads)))
    mixed = jnp.concatenate(mixed, axis=0)
    high = mixed.astype(jnp.bfloat16)
    low = (mixed - high.astype(jnp.float32)).astype(jnp.bfloat16)
    plain = jnp.dot(high, matrix, preferred_element_type=jnp.float32)
    mixed_buf[...] = plain + jnp.dot(low, matrix, preferred_element_type=jnp.float32)
    lane = lax.broadcasted_iota(jnp.int32, (requests, stats_ref.shape[1]), 1)
    tops = jnp.full(lane.shape, 0.0, jnp.float32)
    totals = jnp.ones(lane.shape, jnp.float32)
    for h in range(count):
        pick = pl.ds(h, requests, stride=count)
        column = slice(h * size, (h + 1) * size)
        k = heads + h // group
        mixed_ref[:, column] = mixed_buf[pick, :] * (signs[k : k + 1] * norm)
        tops = jnp.where(lane == h, top_buf[pick, :], tops)
        totals = jnp.where(lane == h, total_buf[pick, :], totals)
    stats_ref[:requests, :] = tops
    stats_ref[requests:, :] = totals


def cache_part(lengths, query, cache, signs):
    requests, span, width = cache.shape
    size = signs.shape[1]
    columns = query.shape[1]
    vmem = pl.BlockSpec(memory_space=pltpu.VMEM)
    return pl.pallas_call(
        cache_kernel,
        in_specs=[pl.BlockSpec(memory_space=pltpu.SMEM)] + [vmem] * 3,
        out_shape=[
            jax.ShapeDtypeStruct(query.shape, jnp.float32),
            jax.ShapeDtypeStruct((2 * requests, size), jnp.float32),
        ],
        scratch_shapes=[pltpu.VMEM((requests * columns // size, size), jnp.float32)] * 4,
        compiler_params=params(),
        cost_estimate=pl.CostEstimate(
            flops=4 * span * requests * columns,
            bytes_accessed=2 * requests * span * width,
            transcendentals=span * requests * columns // size,
        ),
        name="cache_part",
    )(lengths, query, cache, signs)


def code_row(message_refs, start, requests, tokens):
    count = len(message_refs)
    me = lax.axis_index("seq")
    pieces = [ref[0:1, start : start + tokens // count].astype(jnp.float32) for ref in message_refs]
    row = [sum(jnp.where(me ^ d == at, pieces[d], 0.0) for d in range(count)) for at in range(count)]
    code = jnp.concatenate(row, axis=1).astype(jnp.int32)
    return ((code // requests) ^ me) * requests + code % requests


def score_kernel(heads, start, keys_ref, *refs):
    message_refs, (scores_ref, code_ref) = by_distance(refs[:-2], QUERY_ORDER), refs[-2:]
    requests = message_refs[0].shape[0]
    tokens, width = keys_ref.shape
    size = width // heads
    group = start // width
    code = code_row(message_refs, start, requests, tokens)
    code_ref[...] = jnp.broadcast_to(code, code_ref.shape)
    span = len(message_refs) * requests
    here = lax.broadcasted_iota(jnp.int32, (span, tokens), 0) == code
    queries = [ref[:, :start].astype(jnp.float32) for ref in message_refs]
    for k in range(heads):
        rows = []
        for g in range(group):
            at = (k * group + g) * size
            rows += [query[:, at : at + size] for query in queries]
        query = jnp.concatenate(rows, axis=0).astype(jnp.bfloat16)
        keys = keys_ref[:, k * size : (k + 1) * size]
        scores = lax.dot_general(query, keys, NT, preferred_element_type=jnp.float32)
        lines = [
            jnp.sum(jnp.where(here, scores[g * span : (g + 1) * span], 0.0), axis=0, keepdims=True)
            for g in range(group)
        ]
        lines = jnp.concatenate(lines, axis=0) * (1.0 / math.sqrt(size))
        scores_ref[k * group : (k + 1) * group, :] = lines.astype(scores_ref.dtype)


def partial_scores(heads, columns, keys, messages):
    tokens, width = keys.shape
    return pl.pallas_call(
        functools.partial(score_kernel, heads, columns),
        out_shape=[
            jax.ShapeDtypeStruct((columns * heads // width, tokens), jnp.bfloat16),
            jax.ShapeDtypeStruct((8, tokens), jnp.int32),
        ],
        compiler_params=params(),
        cost_estimate=pl.CostEstimate(flops=10**11, bytes_accessed=10**4, transcendentals=0),
        name="partial_scores",
    )(keys, *arranged(messages, QUERY_ORDER))


def packed(values, count):
    rows, lanes = values[0].shape
    lane = lax.broadcasted_iota(jnp.int32, (rows, lanes), 1)
    tiles = [jnp.zeros((rows, lanes), jnp.float32)] * (8 * count // lanes)
    slot = 0
    for value, parts in zip(values, (3, 3, 2)):
        for _ in range(parts):
            piece = value.astype(jnp.bfloat16).astype(jnp.float32)
            value = value - piece
            tile, at = divmod(slot * count, lanes)
            here = (lane >= at) & (lane < at + count)
            tiles[tile] = jnp.where(here, pltpu.roll(piece, at, 1) if at else piece, tiles[tile])
            slot += 1
    return jnp.concatenate(tiles, axis=1)


def unpacked(message, count):
    parts = [message[:, at * count : (at + 1) * count] for at in range(8)]
    return parts[0] + parts[1] + parts[2], parts[3] + parts[4] + parts[5], parts[6] + parts[7]


def mix_kernel(heads, requests, code_ref, values_ref, near_ref, cache_ref, cache_stats_ref, *refs):
    score_refs, (share_ref, far_ref) = refs[:4], refs[4:]
    own, before, across, after = [ref[...].astype(jnp.float32) for ref in score_refs]
    scores = (own + across) + (before + after)
    tokens, width = values_ref.shape
    size = width // heads
    count, columns = scores.shape[0], cache_ref.shape[1]
    group = count // heads
    span = 2 * requests
    row = lax.broadcasted_iota(jnp.int32, (span, tokens), 0)
    here = jnp.where(row < requests, row, row + requests) == code_ref[0:1, :]
    lane = lax.broadcasted_iota(jnp.int32, (requests, cache_stats_ref.shape[1]), 1)
    tops = jnp.full(lane.shape, 0.0, jnp.float32)
    totals = jnp.zeros(lane.shape, jnp.float32)
    parts = []
    for k in range(heads):
        weights = []
        for g in range(group):
            h = k * group + g
            line = jnp.where(here, jnp.broadcast_to(scores[h : h + 1, :], (span, tokens)), LOWEST)
            top = jnp.maximum(jnp.max(line, axis=1, keepdims=True), 0.1 * LOWEST)
            probs = jnp.exp(line - top)
            total = jnp.sum(probs, axis=1, keepdims=True)
            weights.append(probs)
            tops = jnp.where(lane == h, top[:requests], tops)
            totals = jnp.where(lane == h, total[:requests], totals)
        weights = jnp.concatenate(weights, axis=0).astype(jnp.bfloat16)
        part = slice(k * size, (k + 1) * size)
        mixed = jnp.dot(weights, values_ref[:, part], preferred_element_type=jnp.float32)
        mixed = mixed + jnp.dot(weights, near_ref[:, part], preferred_element_type=jnp.float32)
        for g in range(group):
            at = slice((k * group + g) * size, (k * group + g + 1) * size)
            parts.append(mixed[g * span : g * span + requests])
            far_ref[:, at] = mixed[g * span + requests : (g + 1) * span].astype(far_ref.dtype)
    cache_tops = cache_stats_ref[:requests, :]
    both = jnp.maximum(cache_tops, tops)
    cache_factor = jnp.exp(cache_tops - both)
    new_factor = jnp.exp(tops - both)
    total = cache_stats_ref[requests:, :] * cache_factor + totals * new_factor
    for h, part in enumerate(parts):
        at = slice(h * size, (h + 1) * size)
        share = cache_ref[:, at] * cache_factor[:, h : h + 1] + part * new_factor[:, h : h + 1]
        share_ref[:, at] = share.astype(share_ref.dtype)
    far_ref[:, columns:] = jnp.zeros((requests, 8 * count), far_ref.dtype)
    share_ref[:, columns:] = packed((both, total, new_factor), count).astype(share_ref.dtype)


def mix(heads, code, values, near_values, cache_mixed, cache_stats, scores):
    requests, columns = cache_mixed.shape
    count = columns // (values.shape[1] // heads)
    return pl.pallas_call(
        functools.partial(mix_kernel, heads, requests),
        out_shape=[
            jax.ShapeDtypeStruct((requests, columns + 8 * count), jnp.bfloat16),
        ]
        * 2,
        compiler_params=params(),
        name="mix",
    )(code, values, near_values, cache_mixed, cache_stats, *arranged(scores, SCORE_ORDER))


def finish_kernel(count, own_ref, *refs):
    out_ref = refs[-1]
    other_ref, own_far_ref, other_far_ref = [refs[i] for i in FINISH_PLACES]
    columns = out_ref.shape[1]
    size = columns // count
    first = lax.axis_index("tp") == 0
    own_top, own_total, own_new = unpacked(own_ref[:, columns:].astype(jnp.float32), count)
    other_top, other_total, other_new = unpacked(other_ref[:, columns:].astype(jnp.float32), count)
    both = jnp.maximum(own_top, other_top)
    own_factor, other_factor = jnp.exp(own_top - both), jnp.exp(other_top - both)
    own_total, other_total = own_total * own_factor, other_total * other_factor
    total = jnp.where(first, own_total, other_total) + jnp.where(first, other_total, own_total)
    inverse = 1.0 / total
    sides = []
    for ref, far_ref, factor, new in (
        (own_ref, own_far_ref, own_factor, own_new),
        (other_ref, other_far_ref, other_factor, other_new),
    ):
        factor = factor * inverse
        sides.append((ref, far_ref, factor, factor * new))
    for h in range(count):
        at = slice(h * size, (h + 1) * size)
        terms = [
            ref[:, at].astype(jnp.float32) * factor[:, h : h + 1]
            + far_ref[:, at].astype(jnp.float32) * far_factor[:, h : h + 1]
            for ref, far_ref, factor, far_factor in sides
        ]
        out_ref[:, at] = (terms[0] + terms[1]).astype(out_ref.dtype)


def finish(count, columns, own, other, own_far, other_far):
    arrived = (other, own_far, other_far)
    return pl.pallas_call(
        functools.partial(finish_kernel, count),
        out_shape=jax.ShapeDtypeStruct((own.shape[0], columns), jnp.bfloat16),
        compiler_params=params(),
        name="finish",
    )(own, *[arrived[FINISH_PLACES.index(i)] for i in range(3)])


def from_partner(x, axis, distance):
    count = lax.axis_size(axis)
    return lax.ppermute(x, axis, [(i, i ^ distance) for i in range(count)])


def from_behind(x, axis, distance):
    count = lax.axis_size(axis)
    return lax.ppermute(x, axis, [(i, (i + distance) % count) for i in range(count)])


def on_device(tokens, kv_weight, owners, requests, signs, queries, kv_cache, lengths):
    seq_count = lax.axis_size("seq")
    heads = signs.shape[0] // 2
    query = queries[0, 0]
    request_count, columns = query.shape
    message = make_message(query, owners[:, :, 0], requests)
    messages = [message] + [from_partner(message, "seq", d) for d in range(1, seq_count)]
    keys, values = project(tokens, kv_weight)
    near_values = from_partner(values, "seq", 1)
    scores, code = partial_scores(heads, columns, keys, messages)
    scores = [scores] + [from_behind(scores, "seq", d) for d in range(1, seq_count)]
    cache_mixed, cache_stats = cache_part(lengths, query, kv_cache[0, 0], signs)
    share, far = mix(heads, code, values, near_values, cache_mixed, cache_stats, scores)
    far_pairs = [(i, i ^ 5) for i in range(2 * seq_count)]
    output = finish(
        columns // signs.shape[1],
        columns,
        share,
        from_partner(share, "tp", 1),
        from_partner(far, "seq", 2),
        lax.ppermute(far, ("seq", "tp"), far_pairs),
    )
    return output.reshape(1, 1, request_count, columns)


def hadamard(order):
    rows = lax.broadcasted_iota(jnp.int32, (order, order), 0)
    cols = lax.broadcasted_iota(jnp.int32, (order, order), 1)
    parity = jnp.zeros((order, order), jnp.int32)
    for bit_number in range(order.bit_length() - 1):
        parity = parity + rows // 2**bit_number % 2 * (cols // 2**bit_number % 2)
    return (1 - 2 * (parity % 2)).astype(jnp.float32)


def rotate(blocks, sign_rows, matrix):
    product = jnp.einsum(
        "...h,hk->...k", blocks * sign_rows, matrix, precision=lax.Precision.HIGHEST
    )
    return product / math.sqrt(matrix.shape[0])


def encode(rotated):
    largest = jnp.max(jnp.abs(rotated), axis=-1) + 1e-06
    scales = largest.astype(jnp.bfloat16)
    encoded = (rotated / scales.astype(jnp.float32)[..., None]).astype(jnp.bfloat16)
    return (encoded, scales)


def decode(encoded, scales):
    return (encoded.astype(jnp.float32) * scales.astype(jnp.float32)[..., None]).astype(
        jnp.bfloat16
    )


def slot_numbers(targets, count, room):
    onehot = (targets[:, None] == lax.iota(jnp.int32, count)[None, :]).astype(jnp.int32)
    within = jnp.sum((jnp.cumsum(onehot, axis=0) - 1) * onehot, axis=1)
    return targets * room + within


def on_device_long(tokens, kv_weight, owners, requests, signs, queries, kv_cache, lengths):
    seq_count = lax.axis_size("seq")
    per_device = owners.shape[1]
    slots = max(2, (2 * per_device + seq_count - 1) // seq_count)
    head_blocks = signs.shape[0]
    kv_heads = head_blocks // 2
    head_size = signs.shape[1]
    matrix = hadamard(head_size)
    sign_rows = (2 * signs - 1).astype(jnp.float32)
    summed = lax.psum_scatter(
        jnp.dot(tokens, kv_weight, preferred_element_type=jnp.float32).astype(jnp.bfloat16),
        "seq",
        scatter_dimension=0,
        tiled=True,
    ).astype(jnp.float32)
    encoded, scales = encode(
        rotate(summed.reshape(per_device, head_blocks, head_size), sign_rows, matrix)
    )
    slot_index = slot_numbers(owners[0, :, 0], seq_count, slots)
    slot_total = seq_count * slots
    send_values = (
        jnp.zeros((slot_total, head_blocks, head_size), jnp.bfloat16).at[slot_index].set(encoded)
    )
    send_scales = jnp.zeros((slot_total, head_blocks), jnp.bfloat16).at[slot_index].set(scales)
    send_codes = jnp.zeros((slot_total,), jnp.int32).at[slot_index].set(requests[0] + 1)
    got_values, got_scales, arrived_codes = (
        lax.all_to_all(send_values, "seq", split_axis=0, concat_axis=0, tiled=True),
        lax.all_to_all(send_scales, "seq", split_axis=0, concat_axis=0, tiled=True),
        lax.all_to_all(send_codes, "seq", split_axis=0, concat_axis=0, tiled=True),
    )
    arrived = decode(got_values, got_scales)
    query = queries[0, 0]
    request_count = query.shape[0]
    group = query.shape[1] // (kv_heads * head_size)
    query_blocks = query.astype(jnp.float32).reshape(request_count, kv_heads, group, head_size)
    query_rot = rotate(query_blocks, sign_rows[:kv_heads][:, None, :], matrix).astype(jnp.bfloat16)
    local_cache = kv_cache[0, 0]
    cache_span = local_cache.shape[1]
    local_cache = local_cache.reshape(request_count, cache_span, head_blocks, head_size)
    score_scale = 1.0 / math.sqrt(head_size)
    lowest = -1e30
    highest = lax.Precision.HIGHEST
    score_cache = (
        jnp.einsum(
            "rkgd,rckd->rkgc",
            query_rot,
            local_cache[:, :, :kv_heads],
            preferred_element_type=jnp.float32,
        )
        * score_scale
    )
    score_new = (
        jnp.einsum(
            "rkgd,nkd->rkgn", query_rot, arrived[:, :kv_heads], preferred_element_type=jnp.float32
        )
        * score_scale
    )
    positions = lax.axis_index("tp") * cache_span + lax.iota(jnp.int32, cache_span)
    mask_cache = (positions[None, :] < lengths[0, 0][:, None])[:, None, None, :]
    match = arrived_codes[None, :] == (lax.iota(jnp.int32, request_count) + 1)[:, None]
    mask_new = match[:, None, None, :]
    top = jnp.maximum(
        jnp.max(jnp.where(mask_cache, score_cache, lowest), axis=-1),
        jnp.max(jnp.where(mask_new, score_new, lowest), axis=-1),
    )
    probs_cache = jnp.where(mask_cache, jnp.exp(score_cache - top[..., None]), 0.0)
    probs_new = jnp.where(mask_new, jnp.exp(score_new - top[..., None]), 0.0)
    total = jnp.sum(probs_cache, axis=-1) + jnp.sum(probs_new, axis=-1)
    mixed = jnp.einsum(
        "rkgc,rckd->rkgd",
        probs_cache,
        local_cache[:, :, kv_heads:].astype(jnp.float32),
        precision=highest,
    )
    mixed = mixed + jnp.einsum(
        "rkgn,nkd->rkgd", probs_new, arrived[:, kv_heads:].astype(jnp.float32), precision=highest
    )
    shared_top = lax.pmax(top, "tp")
    factor = jnp.exp(top - shared_top)
    total, mixed = (
        lax.psum((total * factor).astype(jnp.bfloat16), "tp").astype(jnp.float32),
        lax.psum((mixed * factor[..., None]).astype(jnp.bfloat16), "tp").astype(jnp.float32),
    )
    mixed = mixed / total[..., None]
    output = rotate(mixed, 1.0, matrix) * sign_rows[kv_heads:][None, :, None, :]
    return output.reshape(1, 1, request_count, group * kv_heads * head_size).astype(jnp.bfloat16)


def solution(mesh):
    placed = (
        P(("groups", "tp", "section"), "seq"),
        P("seq", None),
        P(("groups", "tp", "section"), "seq", None),
        P(("groups", "tp", "section"), "seq"),
        P(),
        P(("groups", "seq"), "section", None, None),
        P(("groups", "seq"), "section", None, "tp", None),
        P(("groups", "seq"), "section", None),
    )
    short = mesh.shape["seq"] == 4 and mesh.shape["tp"] == 2
    return jax.shard_map(
        on_device if short else on_device_long,
        mesh=mesh,
        in_specs=placed,
        out_specs=P(("groups", "seq"), "section", None, None),
        check_vma=False,
    )
```

```python
import functools
import math

import jax
import jax.numpy as jnp
from jax import lax
from jax.experimental import pallas as pl
from jax.experimental.pallas import tpu as pltpu
from jax.sharding import PartitionSpec as P

LOWEST = -1e30
MIB = 1024 * 1024
NT = (((1,), (1,)), ((), ()))


def params(mib=32):
    return pltpu.CompilerParams(vmem_limit_bytes=mib * MIB)


def in_hbm(x):
    return pltpu.with_memory_space_constraint(x, pltpu.HBM)


def in_vmem(x):
    return pltpu.with_memory_space_constraint(x, pltpu.VMEM)


def hadamard_tile(order):
    rows = lax.broadcasted_iota(jnp.int32, (order, order), 0)
    cols = lax.broadcasted_iota(jnp.int32, (order, order), 1)
    common = rows & cols
    parity = jnp.zeros((order, order), jnp.int32)
    for bit_number in range(order.bit_length() - 1):
        parity = parity ^ (common >> bit_number)
    return (1 - 2 * (parity & 1)).astype(jnp.float32).astype(jnp.bfloat16)


QUERY_ORDER = (3, 2, 1)
SCORE_ORDER = (1, 2, 3)
FINISH_PLACES = (2, 1, 0, 3)


def arranged(blocks, order):
    return [blocks[0]] + [blocks[d] for d in order]


def by_distance(refs, order):
    return [refs[0]] + [refs[1 + order.index(d)] for d in range(1, len(refs))]


def project_kernel(tokens_ref, weight_ref, keys_ref, values_ref):
    width = keys_ref.shape[1]
    for out_ref, columns in ((keys_ref, slice(0, width)), (values_ref, slice(width, 2 * width))):
        out_ref[...] = jnp.dot(
            tokens_ref[...], weight_ref[:, columns], preferred_element_type=jnp.float32
        ).astype(out_ref.dtype)


def project(tokens, weight):
    rows, features = tokens.shape
    width = weight.shape[1] // 2
    vmem = pl.BlockSpec(memory_space=pltpu.VMEM)
    return pl.pallas_call(
        project_kernel,
        in_specs=[vmem] * 2,
        out_specs=[vmem] * 2,
        out_shape=[jax.ShapeDtypeStruct((rows, width), jnp.bfloat16)] * 2,
        compiler_params=params(32),
        cost_estimate=pl.CostEstimate(
            flops=4 * rows * features * width,
            bytes_accessed=2 * (rows * features + 2 * features * width),
            transcendentals=0,
        ),
        name="project",
    )(in_vmem(tokens), in_vmem(weight))


def message_kernel(query_ref, owners_ref, requests_ref, out_ref, owners_buf, requests_buf, sems):
    requests, columns = query_ref.shape
    per_device = owners_ref.shape[1]
    copies = [
        pltpu.make_async_copy(query_ref, out_ref.at[:, :columns], sems.at[0]),
        pltpu.make_async_copy(owners_ref, owners_buf, sems.at[1]),
        pltpu.make_async_copy(requests_ref, requests_buf, sems.at[2]),
    ]
    for copy in copies:
        copy.start()
    copies[1].wait()
    copies[2].wait()
    code = (owners_buf[...] * requests + requests_buf[...]).astype(jnp.float32)
    spare = jnp.zeros((1, out_ref.shape[1] - columns - per_device), jnp.float32)
    code = jnp.concatenate([code, spare], axis=1)
    out_ref[:, columns:] = jnp.broadcast_to(code, (requests, code.shape[1])).astype(out_ref.dtype)
    copies[0].wait()


def make_message(query, owners, requests):
    count, columns = query.shape
    lanes = -(-owners.shape[1] // 128) * 128
    return pl.pallas_call(
        message_kernel,
        in_specs=[pl.BlockSpec(memory_space=pl.ANY)] * 3,
        out_specs=pl.BlockSpec(memory_space=pltpu.VMEM),
        out_shape=jax.ShapeDtypeStruct((count, columns + lanes), query.dtype),
        scratch_shapes=[
            pltpu.VMEM(owners.shape, owners.dtype),
            pltpu.VMEM(requests.shape, requests.dtype),
            pltpu.SemaphoreType.DMA((3,)),
        ],
        compiler_params=params(16),
        cost_estimate=pl.CostEstimate(flops=10**11, bytes_accessed=10**4, transcendentals=0),
        name="make_message",
    )(in_hbm(query), in_hbm(owners), in_hbm(requests))


def cache_kernel(
    lengths_ref, query_ref, cache_ref, signs_ref, mixed_ref, stats_ref, query_buf, top_buf, total_buf, mixed_buf
):
    requests, span, _ = cache_ref.shape
    blocks, size = signs_ref.shape
    heads = blocks // 2
    width = heads * size
    count = query_ref.shape[1] // size
    group = count // heads
    norm = 1.0 / math.sqrt(size)
    matrix = hadamard_tile(size)
    signs = (2 * signs_ref[...] - 1).astype(jnp.float32)
    query = query_ref[...].astype(jnp.float32)
    query = jnp.concatenate(
        [query[:, h * size : (h + 1) * size] * signs[h // group : h // group + 1] for h in range(count)], axis=0
    )
    query_buf[...] = jnp.dot(query.astype(jnp.bfloat16), matrix, preferred_element_type=jnp.float32) * norm
    rows = 2 * count
    kv_head = lax.broadcasted_iota(jnp.int32, (rows, width), 0) // group & (heads - 1)
    own_head = kv_head == lax.broadcasted_iota(jnp.int32, (rows, width), 1) // size
    first = lax.broadcasted_iota(jnp.int32, (rows, span), 0) < count
    position = lax.axis_index("tp") * span + lax.broadcasted_iota(jnp.int32, (rows, span), 1)
    pairs = range(0, requests, 2)
    scores = []
    for r in pairs:
        both = [query_buf[pl.ds(r + i, count, stride=requests), :] for i in range(2)]
        wide = jnp.concatenate([jnp.concatenate(both, axis=0)] * heads, axis=1)
        wide = jnp.where(own_head, wide, 0.0).astype(jnp.bfloat16)
        keys = cache_ref[r : r + 2, :, :width].reshape(2 * span, width)
        scores.append(lax.dot_general(wide, keys, NT, preferred_element_type=jnp.float32))
    probs = []
    for r, score in zip(pairs, scores):
        score = jnp.where(first, score[:, :span], score[:, span:]) * norm
        live = position < jnp.where(first, lengths_ref[0, 0, r], lengths_ref[0, 0, r + 1])
        top = jnp.max(jnp.where(live, score, LOWEST), axis=1, keepdims=True)
        prob = jnp.where(live, jnp.exp(score - top), 0.0)
        total = jnp.sum(prob, axis=1, keepdims=True)
        at = slice(r * count, (r + 2) * count)
        top_buf[at, :] = jnp.broadcast_to(top, (rows, size))
        total_buf[at, :] = jnp.broadcast_to(total, (rows, size))
        probs.append(
            jnp.concatenate([jnp.where(first, prob, 0.0), jnp.where(first, 0.0, prob)], axis=1).astype(jnp.bfloat16)
        )
    mixed = []
    for r, prob in zip(pairs, probs):
        values = cache_ref[r : r + 2, :, width:].reshape(2 * span, width)
        wide = jnp.dot(prob, values, preferred_element_type=jnp.float32)
        wide = jnp.where(own_head, wide, 0.0)
        mixed.append(sum(wide[:, k * size : (k + 1) * size] for k in range(heads)))
    mixed = jnp.concatenate(mixed, axis=0)
    high = mixed.astype(jnp.bfloat16)
    low = (mixed - high.astype(jnp.float32)).astype(jnp.bfloat16)
    plain = jnp.dot(high, matrix, preferred_element_type=jnp.float32)
    mixed_buf[...] = plain + jnp.dot(low, matrix, preferred_element_type=jnp.float32)
    lane = lax.broadcasted_iota(jnp.int32, (requests, stats_ref.shape[1]), 1)
    tops = jnp.full(lane.shape, 0.0, jnp.float32)
    totals = jnp.ones(lane.shape, jnp.float32)
    for h in range(count):
        pick = pl.ds(h, requests, stride=count)
        column = slice(h * size, (h + 1) * size)
        k = heads + h // group
        mixed_ref[:, column] = mixed_buf[pick, :] * (signs[k : k + 1] * norm)
        tops = jnp.where(lane == h, top_buf[pick, :], tops)
        totals = jnp.where(lane == h, total_buf[pick, :], totals)
    stats_ref[:requests, :] = tops
    stats_ref[requests:, :] = totals


def cache_part(lengths, query, cache, signs):
    requests, span, width = cache.shape
    size = signs.shape[1]
    columns = query.shape[1]
    vmem = pl.BlockSpec(memory_space=pltpu.VMEM)
    return pl.pallas_call(
        cache_kernel,
        in_specs=[pl.BlockSpec(memory_space=pltpu.SMEM)] + [vmem] * 3,
        out_shape=[
            jax.ShapeDtypeStruct(query.shape, jnp.float32),
            jax.ShapeDtypeStruct((2 * requests, size), jnp.float32),
        ],
        scratch_shapes=[pltpu.VMEM((requests * columns // size, size), jnp.float32)] * 4,
        compiler_params=params(),
        cost_estimate=pl.CostEstimate(
            flops=4 * span * requests * columns,
            bytes_accessed=2 * requests * span * width,
            transcendentals=span * requests * columns // size,
        ),
        name="cache_part",
    )(lengths, query, cache, signs)


def code_row(message_refs, start, requests, tokens):
    count = len(message_refs)
    me = lax.axis_index("seq")
    pieces = [ref[0:1, start : start + tokens // count].astype(jnp.float32) for ref in message_refs]
    row = [sum(jnp.where(me ^ d == at, pieces[d], 0.0) for d in range(count)) for at in range(count)]
    code = jnp.concatenate(row, axis=1).astype(jnp.int32)
    return ((code // requests) ^ me) * requests + code % requests


def score_kernel(heads, start, keys_ref, *refs):
    message_refs, (scores_ref, code_ref) = by_distance(refs[:-2], QUERY_ORDER), refs[-2:]
    requests = message_refs[0].shape[0]
    tokens, width = keys_ref.shape
    size = width // heads
    group = start // width
    code = code_row(message_refs, start, requests, tokens)
    code_ref[...] = jnp.broadcast_to(code, code_ref.shape)
    span = len(message_refs) * requests
    here = lax.broadcasted_iota(jnp.int32, (span, tokens), 0) == code
    queries = [ref[:, :start].astype(jnp.float32) for ref in message_refs]
    for k in range(heads):
        rows = []
        for g in range(group):
            at = (k * group + g) * size
            rows += [query[:, at : at + size] for query in queries]
        query = jnp.concatenate(rows, axis=0).astype(jnp.bfloat16)
        keys = keys_ref[:, k * size : (k + 1) * size]
        scores = lax.dot_general(query, keys, NT, preferred_element_type=jnp.float32)
        lines = [
            jnp.sum(jnp.where(here, scores[g * span : (g + 1) * span], 0.0), axis=0, keepdims=True)
            for g in range(group)
        ]
        lines = jnp.concatenate(lines, axis=0) * (1.0 / math.sqrt(size))
        scores_ref[k * group : (k + 1) * group, :] = lines.astype(scores_ref.dtype)


def partial_scores(heads, columns, keys, messages):
    tokens, width = keys.shape
    return pl.pallas_call(
        functools.partial(score_kernel, heads, columns),
        out_shape=[
            jax.ShapeDtypeStruct((columns * heads // width, tokens), jnp.bfloat16),
            jax.ShapeDtypeStruct((8, tokens), jnp.int32),
        ],
        compiler_params=params(),
        cost_estimate=pl.CostEstimate(flops=10**11, bytes_accessed=10**4, transcendentals=0),
        name="partial_scores",
    )(keys, *arranged(messages, QUERY_ORDER))


def mix_kernel(heads, requests, code_ref, values_ref, near_ref, cache_ref, cache_stats_ref, *refs):
    score_refs, (share_ref, far_ref, stats_ref) = refs[:4], refs[4:]
    own, before, across, after = [ref[...].astype(jnp.float32) for ref in score_refs]
    scores = (own + across) + (before + after)
    tokens, width = values_ref.shape
    size = width // heads
    count, columns = scores.shape[0], cache_ref.shape[1]
    group = count // heads
    span = 2 * requests
    row = lax.broadcasted_iota(jnp.int32, (span, tokens), 0)
    here = jnp.where(row < requests, row, row + requests) == code_ref[0:1, :]
    lane = lax.broadcasted_iota(jnp.int32, (requests, cache_stats_ref.shape[1]), 1)
    tops = jnp.full(lane.shape, 0.0, jnp.float32)
    totals = jnp.zeros(lane.shape, jnp.float32)
    parts = []
    for k in range(heads):
        weights = []
        for g in range(group):
            h = k * group + g
            line = jnp.where(here, jnp.broadcast_to(scores[h : h + 1, :], (span, tokens)), LOWEST)
            top = jnp.maximum(jnp.max(line, axis=1, keepdims=True), 0.1 * LOWEST)
            probs = jnp.exp(line - top)
            total = jnp.sum(probs, axis=1, keepdims=True)
            weights.append(probs)
            tops = jnp.where(lane == h, top[:requests], tops)
            totals = jnp.where(lane == h, total[:requests], totals)
        weights = jnp.concatenate(weights, axis=0).astype(jnp.bfloat16)
        part = slice(k * size, (k + 1) * size)
        mixed = jnp.dot(weights, values_ref[:, part], preferred_element_type=jnp.float32)
        mixed = mixed + jnp.dot(weights, near_ref[:, part], preferred_element_type=jnp.float32)
        for g in range(group):
            at = slice((k * group + g) * size, (k * group + g + 1) * size)
            parts.append(mixed[g * span : g * span + requests])
            far_ref[:, at] = mixed[g * span + requests : (g + 1) * span].astype(far_ref.dtype)
    cache_tops = cache_stats_ref[:requests, :]
    both = jnp.maximum(cache_tops, tops)
    cache_factor = jnp.exp(cache_tops - both)
    new_factor = jnp.exp(tops - both)
    total = cache_stats_ref[requests:, :] * cache_factor + totals * new_factor
    for h, part in enumerate(parts):
        at = slice(h * size, (h + 1) * size)
        share = cache_ref[:, at] * cache_factor[:, h : h + 1] + part * new_factor[:, h : h + 1]
        share_ref[:, at] = share.astype(share_ref.dtype)
    stats_ref[...] = jnp.concatenate([both, total, new_factor], axis=0)


def mix(heads, code, values, near_values, cache_mixed, cache_stats, scores):
    requests, lanes = cache_stats.shape[0] // 2, cache_stats.shape[1]
    columns = cache_mixed.shape[1]
    return pl.pallas_call(
        functools.partial(mix_kernel, heads, requests),
        out_shape=[
            jax.ShapeDtypeStruct((requests, columns), jnp.bfloat16),
            jax.ShapeDtypeStruct((requests, columns), jnp.bfloat16),
            jax.ShapeDtypeStruct((3 * requests, lanes), jnp.float32),
        ],
        compiler_params=params(),
        name="mix",
    )(code, values, near_values, cache_mixed, cache_stats, *arranged(scores, SCORE_ORDER))


def finish_kernel(own_ref, own_stats_ref, *refs):
    out_ref = refs[-1]
    other_ref, own_far_ref, other_far_ref, other_stats_ref = [refs[i] for i in FINISH_PLACES]
    requests, columns = out_ref.shape
    size = own_stats_ref.shape[1]
    first = lax.axis_index("tp") == 0
    own_top, own_total, own_new = [own_stats_ref[i * requests : (i + 1) * requests, :] for i in range(3)]
    other_top, other_total, other_new = [other_stats_ref[i * requests : (i + 1) * requests, :] for i in range(3)]
    both = jnp.maximum(own_top, other_top)
    own_factor, other_factor = jnp.exp(own_top - both), jnp.exp(other_top - both)
    own_total, other_total = own_total * own_factor, other_total * other_factor
    total = jnp.where(first, own_total, other_total) + jnp.where(first, other_total, own_total)
    inverse = 1.0 / total
    sides = []
    for ref, far_ref, factor, new in (
        (own_ref, own_far_ref, own_factor, own_new),
        (other_ref, other_far_ref, other_factor, other_new),
    ):
        factor = factor * inverse
        sides.append((ref, far_ref, factor, factor * new))
    for h in range(columns // size):
        at = slice(h * size, (h + 1) * size)
        terms = [
            ref[:, at].astype(jnp.float32) * factor[:, h : h + 1]
            + far_ref[:, at].astype(jnp.float32) * far_factor[:, h : h + 1]
            for ref, far_ref, factor, far_factor in sides
        ]
        out_ref[:, at] = (terms[0] + terms[1]).astype(out_ref.dtype)


def finish(own, own_stats, other, own_far, other_far, other_stats):
    arrived = (other, own_far, other_far, other_stats)
    return pl.pallas_call(
        finish_kernel,
        out_shape=jax.ShapeDtypeStruct(own.shape, own.dtype),
        compiler_params=params(),
        name="finish",
    )(own, own_stats, *[arrived[FINISH_PLACES.index(i)] for i in range(4)])


def from_partner(x, axis, distance):
    count = lax.axis_size(axis)
    return lax.ppermute(x, axis, [(i, i ^ distance) for i in range(count)])


def from_behind(x, axis, distance):
    count = lax.axis_size(axis)
    return lax.ppermute(x, axis, [(i, (i + distance) % count) for i in range(count)])


def on_device(tokens, kv_weight, owners, requests, signs, queries, kv_cache, lengths):
    seq_count = lax.axis_size("seq")
    heads = signs.shape[0] // 2
    query = queries[0, 0]
    request_count, columns = query.shape
    message = make_message(query, owners[:, :, 0], requests)
    messages = [message] + [from_partner(message, "seq", d) for d in range(1, seq_count)]
    keys, values = project(tokens, kv_weight)
    near_values = from_partner(values, "seq", 1)
    scores, code = partial_scores(heads, columns, keys, messages)
    scores = [scores] + [from_behind(scores, "seq", d) for d in range(1, seq_count)]
    cache_mixed, cache_stats = cache_part(lengths, query, kv_cache[0, 0], signs)
    share, far, stats = mix(heads, code, values, near_values, cache_mixed, cache_stats, scores)
    far_pairs = [(i, i ^ 5) for i in range(2 * seq_count)]
    output = finish(
        share,
        stats,
        from_partner(share, "tp", 1),
        from_partner(far, "seq", 2),
        lax.ppermute(far, ("seq", "tp"), far_pairs),
        from_partner(stats, "tp", 1),
    )
    return output.reshape(1, 1, request_count, columns)


def hadamard(order):
    rows = lax.broadcasted_iota(jnp.int32, (order, order), 0)
    cols = lax.broadcasted_iota(jnp.int32, (order, order), 1)
    parity = jnp.zeros((order, order), jnp.int32)
    for bit_number in range(order.bit_length() - 1):
        parity = parity + rows // 2**bit_number % 2 * (cols // 2**bit_number % 2)
    return (1 - 2 * (parity % 2)).astype(jnp.float32)


def rotate(blocks, sign_rows, matrix):
    product = jnp.einsum(
        "...h,hk->...k", blocks * sign_rows, matrix, precision=lax.Precision.HIGHEST
    )
    return product / math.sqrt(matrix.shape[0])


def encode(rotated):
    largest = jnp.max(jnp.abs(rotated), axis=-1) + 1e-06
    scales = largest.astype(jnp.bfloat16)
    encoded = (rotated / scales.astype(jnp.float32)[..., None]).astype(jnp.bfloat16)
    return (encoded, scales)


def decode(encoded, scales):
    return (encoded.astype(jnp.float32) * scales.astype(jnp.float32)[..., None]).astype(
        jnp.bfloat16
    )


def slot_numbers(targets, count, room):
    onehot = (targets[:, None] == lax.iota(jnp.int32, count)[None, :]).astype(jnp.int32)
    within = jnp.sum((jnp.cumsum(onehot, axis=0) - 1) * onehot, axis=1)
    return targets * room + within


def on_device_long(tokens, kv_weight, owners, requests, signs, queries, kv_cache, lengths):
    seq_count = lax.axis_size("seq")
    per_device = owners.shape[1]
    slots = max(2, (2 * per_device + seq_count - 1) // seq_count)
    head_blocks = signs.shape[0]
    kv_heads = head_blocks // 2
    head_size = signs.shape[1]
    matrix = hadamard(head_size)
    sign_rows = (2 * signs - 1).astype(jnp.float32)
    summed = lax.psum_scatter(
        jnp.dot(tokens, kv_weight, preferred_element_type=jnp.float32).astype(jnp.bfloat16),
        "seq",
        scatter_dimension=0,
        tiled=True,
    ).astype(jnp.float32)
    encoded, scales = encode(
        rotate(summed.reshape(per_device, head_blocks, head_size), sign_rows, matrix)
    )
    slot_index = slot_numbers(owners[0, :, 0], seq_count, slots)
    slot_total = seq_count * slots
    send_values = (
        jnp.zeros((slot_total, head_blocks, head_size), jnp.bfloat16).at[slot_index].set(encoded)
    )
    send_scales = jnp.zeros((slot_total, head_blocks), jnp.bfloat16).at[slot_index].set(scales)
    send_codes = jnp.zeros((slot_total,), jnp.int32).at[slot_index].set(requests[0] + 1)
    got_values, got_scales, arrived_codes = (
        lax.all_to_all(send_values, "seq", split_axis=0, concat_axis=0, tiled=True),
        lax.all_to_all(send_scales, "seq", split_axis=0, concat_axis=0, tiled=True),
        lax.all_to_all(send_codes, "seq", split_axis=0, concat_axis=0, tiled=True),
    )
    arrived = decode(got_values, got_scales)
    query = queries[0, 0]
    request_count = query.shape[0]
    group = query.shape[1] // (kv_heads * head_size)
    query_blocks = query.astype(jnp.float32).reshape(request_count, kv_heads, group, head_size)
    query_rot = rotate(query_blocks, sign_rows[:kv_heads][:, None, :], matrix).astype(jnp.bfloat16)
    local_cache = kv_cache[0, 0]
    cache_span = local_cache.shape[1]
    local_cache = local_cache.reshape(request_count, cache_span, head_blocks, head_size)
    score_scale = 1.0 / math.sqrt(head_size)
    lowest = -1e30
    highest = lax.Precision.HIGHEST
    score_cache = (
        jnp.einsum(
            "rkgd,rckd->rkgc",
            query_rot,
            local_cache[:, :, :kv_heads],
            preferred_element_type=jnp.float32,
        )
        * score_scale
    )
    score_new = (
        jnp.einsum(
            "rkgd,nkd->rkgn", query_rot, arrived[:, :kv_heads], preferred_element_type=jnp.float32
        )
        * score_scale
    )
    positions = lax.axis_index("tp") * cache_span + lax.iota(jnp.int32, cache_span)
    mask_cache = (positions[None, :] < lengths[0, 0][:, None])[:, None, None, :]
    match = arrived_codes[None, :] == (lax.iota(jnp.int32, request_count) + 1)[:, None]
    mask_new = match[:, None, None, :]
    top = jnp.maximum(
        jnp.max(jnp.where(mask_cache, score_cache, lowest), axis=-1),
        jnp.max(jnp.where(mask_new, score_new, lowest), axis=-1),
    )
    probs_cache = jnp.where(mask_cache, jnp.exp(score_cache - top[..., None]), 0.0)
    probs_new = jnp.where(mask_new, jnp.exp(score_new - top[..., None]), 0.0)
    total = jnp.sum(probs_cache, axis=-1) + jnp.sum(probs_new, axis=-1)
    mixed = jnp.einsum(
        "rkgc,rckd->rkgd",
        probs_cache,
        local_cache[:, :, kv_heads:].astype(jnp.float32),
        precision=highest,
    )
    mixed = mixed + jnp.einsum(
        "rkgn,nkd->rkgd", probs_new, arrived[:, kv_heads:].astype(jnp.float32), precision=highest
    )
    shared_top = lax.pmax(top, "tp")
    factor = jnp.exp(top - shared_top)
    total, mixed = (
        lax.psum((total * factor).astype(jnp.bfloat16), "tp").astype(jnp.float32),
        lax.psum((mixed * factor[..., None]).astype(jnp.bfloat16), "tp").astype(jnp.float32),
    )
    mixed = mixed / total[..., None]
    output = rotate(mixed, 1.0, matrix) * sign_rows[kv_heads:][None, :, None, :]
    return output.reshape(1, 1, request_count, group * kv_heads * head_size).astype(jnp.bfloat16)


def solution(mesh):
    placed = (
        P(("groups", "tp", "section"), "seq"),
        P("seq", None),
        P(("groups", "tp", "section"), "seq", None),
        P(("groups", "tp", "section"), "seq"),
        P(),
        P(("groups", "seq"), "section", None, None),
        P(("groups", "seq"), "section", None, "tp", None),
        P(("groups", "seq"), "section", None),
    )
    short = mesh.shape["seq"] == 4 and mesh.shape["tp"] == 2
    return jax.shard_map(
        on_device if short else on_device_long,
        mesh=mesh,
        in_specs=placed,
        out_specs=P(("groups", "seq"), "section", None, None),
        check_vma=False,
    )
```

```python
import functools
import math

import jax
import jax.numpy as jnp
from jax import lax
from jax.experimental import pallas as pl
from jax.experimental.pallas import tpu as pltpu
from jax.sharding import PartitionSpec as P

LOWEST = -1e30
MIB = 1024 * 1024
NT = (((1,), (1,)), ((), ()))


def params(mib=32):
    return pltpu.CompilerParams(vmem_limit_bytes=mib * MIB)


def in_hbm(x):
    return pltpu.with_memory_space_constraint(x, pltpu.HBM)


def in_vmem(x):
    return pltpu.with_memory_space_constraint(x, pltpu.VMEM)


def hadamard_tile(order):
    rows = lax.broadcasted_iota(jnp.int32, (order, order), 0)
    cols = lax.broadcasted_iota(jnp.int32, (order, order), 1)
    common = rows & cols
    parity = jnp.zeros((order, order), jnp.int32)
    for bit_number in range(order.bit_length() - 1):
        parity = parity ^ (common >> bit_number)
    return (1 - 2 * (parity & 1)).astype(jnp.float32).astype(jnp.bfloat16)


QUERY_ORDER = (3, 2, 1)
SCORE_ORDER = (1, 2, 3)
FINISH_PLACES = (0, 1, 2)


def arranged(blocks, order):
    return [blocks[0]] + [blocks[d] for d in order]


def by_distance(refs, order):
    return [refs[0]] + [refs[1 + order.index(d)] for d in range(1, len(refs))]


def project_kernel(tokens_ref, weight_ref, keys_ref, values_ref):
    width = keys_ref.shape[1]
    for out_ref, columns in ((keys_ref, slice(0, width)), (values_ref, slice(width, 2 * width))):
        out_ref[...] = jnp.dot(
            tokens_ref[...], weight_ref[:, columns], preferred_element_type=jnp.float32
        ).astype(out_ref.dtype)


def project(tokens, weight):
    rows, features = tokens.shape
    width = weight.shape[1] // 2
    vmem = pl.BlockSpec(memory_space=pltpu.VMEM)
    return pl.pallas_call(
        project_kernel,
        in_specs=[vmem] * 2,
        out_specs=[vmem] * 2,
        out_shape=[jax.ShapeDtypeStruct((rows, width), jnp.bfloat16)] * 2,
        compiler_params=params(32),
        cost_estimate=pl.CostEstimate(
            flops=4 * rows * features * width,
            bytes_accessed=2 * (rows * features + 2 * features * width),
            transcendentals=0,
        ),
        name="project",
    )(in_vmem(tokens), in_vmem(weight))


def message_kernel(query_ref, owners_ref, requests_ref, out_ref, owners_buf, requests_buf, sems):
    requests, columns = query_ref.shape
    per_device = owners_ref.shape[1]
    copies = [
        pltpu.make_async_copy(query_ref, out_ref.at[:, :columns], sems.at[0]),
        pltpu.make_async_copy(owners_ref, owners_buf, sems.at[1]),
        pltpu.make_async_copy(requests_ref, requests_buf, sems.at[2]),
    ]
    for copy in copies:
        copy.start()
    copies[1].wait()
    copies[2].wait()
    code = (owners_buf[...] * requests + requests_buf[...]).astype(jnp.float32)
    spare = jnp.zeros((1, out_ref.shape[1] - columns - per_device), jnp.float32)
    code = jnp.concatenate([code, spare], axis=1)
    out_ref[:, columns:] = jnp.broadcast_to(code, (requests, code.shape[1])).astype(out_ref.dtype)
    copies[0].wait()


def make_message(query, owners, requests):
    count, columns = query.shape
    lanes = -(-owners.shape[1] // 128) * 128
    return pl.pallas_call(
        message_kernel,
        in_specs=[pl.BlockSpec(memory_space=pl.ANY)] * 3,
        out_specs=pl.BlockSpec(memory_space=pltpu.VMEM),
        out_shape=jax.ShapeDtypeStruct((count, columns + lanes), query.dtype),
        scratch_shapes=[
            pltpu.VMEM(owners.shape, owners.dtype),
            pltpu.VMEM(requests.shape, requests.dtype),
            pltpu.SemaphoreType.DMA((3,)),
        ],
        compiler_params=params(16),
        cost_estimate=pl.CostEstimate(flops=10**11, bytes_accessed=10**4, transcendentals=0),
        name="make_message",
    )(in_hbm(query), in_hbm(owners), in_hbm(requests))


def cache_kernel(
    lengths_ref, query_ref, cache_ref, signs_ref, mixed_ref, stats_ref, query_buf, top_buf, total_buf, mixed_buf
):
    requests, span, _ = cache_ref.shape
    blocks, size = signs_ref.shape
    heads = blocks // 2
    width = heads * size
    count = query_ref.shape[1] // size
    group = count // heads
    norm = 1.0 / math.sqrt(size)
    matrix = hadamard_tile(size)
    signs = (2 * signs_ref[...] - 1).astype(jnp.float32)
    query = query_ref[...].astype(jnp.float32)
    query = jnp.concatenate(
        [query[:, h * size : (h + 1) * size] * signs[h // group : h // group + 1] for h in range(count)], axis=0
    )
    query_buf[...] = jnp.dot(query.astype(jnp.bfloat16), matrix, preferred_element_type=jnp.float32) * norm
    rows = 2 * count
    kv_head = lax.broadcasted_iota(jnp.int32, (rows, width), 0) // group & (heads - 1)
    own_head = kv_head == lax.broadcasted_iota(jnp.int32, (rows, width), 1) // size
    first = lax.broadcasted_iota(jnp.int32, (rows, span), 0) < count
    position = lax.axis_index("tp") * span + lax.broadcasted_iota(jnp.int32, (rows, span), 1)
    pairs = range(0, requests, 2)
    scores = []
    for r in pairs:
        both = [query_buf[pl.ds(r + i, count, stride=requests), :] for i in range(2)]
        wide = jnp.concatenate([jnp.concatenate(both, axis=0)] * heads, axis=1)
        wide = jnp.where(own_head, wide, 0.0).astype(jnp.bfloat16)
        keys = cache_ref[r : r + 2, :, :width].reshape(2 * span, width)
        scores.append(lax.dot_general(wide, keys, NT, preferred_element_type=jnp.float32))
    probs = []
    for r, score in zip(pairs, scores):
        score = jnp.where(first, score[:, :span], score[:, span:]) * norm
        live = position < jnp.where(first, lengths_ref[0, 0, r], lengths_ref[0, 0, r + 1])
        top = jnp.max(jnp.where(live, score, LOWEST), axis=1, keepdims=True)
        prob = jnp.where(live, jnp.exp(score - top), 0.0)
        total = jnp.sum(prob, axis=1, keepdims=True)
        at = slice(r * count, (r + 2) * count)
        top_buf[at, :] = jnp.broadcast_to(top, (rows, size))
        total_buf[at, :] = jnp.broadcast_to(total, (rows, size))
        probs.append(
            jnp.concatenate([jnp.where(first, prob, 0.0), jnp.where(first, 0.0, prob)], axis=1).astype(jnp.bfloat16)
        )
    mixed = []
    for r, prob in zip(pairs, probs):
        values = cache_ref[r : r + 2, :, width:].reshape(2 * span, width)
        wide = jnp.dot(prob, values, preferred_element_type=jnp.float32)
        wide = jnp.where(own_head, wide, 0.0)
        mixed.append(sum(wide[:, k * size : (k + 1) * size] for k in range(heads)))
    mixed = jnp.concatenate(mixed, axis=0)
    high = mixed.astype(jnp.bfloat16)
    low = (mixed - high.astype(jnp.float32)).astype(jnp.bfloat16)
    plain = jnp.dot(high, matrix, preferred_element_type=jnp.float32)
    mixed_buf[...] = plain + jnp.dot(low, matrix, preferred_element_type=jnp.float32)
    lane = lax.broadcasted_iota(jnp.int32, (requests, stats_ref.shape[1]), 1)
    tops = jnp.full(lane.shape, 0.0, jnp.float32)
    totals = jnp.ones(lane.shape, jnp.float32)
    for h in range(count):
        pick = pl.ds(h, requests, stride=count)
        column = slice(h * size, (h + 1) * size)
        k = heads + h // group
        mixed_ref[:, column] = mixed_buf[pick, :] * (signs[k : k + 1] * norm)
        tops = jnp.where(lane == h, top_buf[pick, :], tops)
        totals = jnp.where(lane == h, total_buf[pick, :], totals)
    stats_ref[:requests, :] = tops
    stats_ref[requests:, :] = totals


def cache_part(lengths, query, cache, signs):
    requests, span, width = cache.shape
    size = signs.shape[1]
    columns = query.shape[1]
    vmem = pl.BlockSpec(memory_space=pltpu.VMEM)
    return pl.pallas_call(
        cache_kernel,
        in_specs=[pl.BlockSpec(memory_space=pltpu.SMEM)] + [vmem] * 3,
        out_shape=[
            jax.ShapeDtypeStruct(query.shape, jnp.float32),
            jax.ShapeDtypeStruct((2 * requests, size), jnp.float32),
        ],
        scratch_shapes=[pltpu.VMEM((requests * columns // size, size), jnp.float32)] * 4,
        compiler_params=params(),
        cost_estimate=pl.CostEstimate(
            flops=4 * span * requests * columns,
            bytes_accessed=2 * requests * span * width,
            transcendentals=span * requests * columns // size,
        ),
        name="cache_part",
    )(lengths, query, cache, signs)


def code_row(message_refs, start, requests, tokens):
    count = len(message_refs)
    me = lax.axis_index("seq")
    pieces = [ref[0:1, start : start + tokens // count].astype(jnp.float32) for ref in message_refs]
    row = [sum(jnp.where(me ^ d == at, pieces[d], 0.0) for d in range(count)) for at in range(count)]
    code = jnp.concatenate(row, axis=1).astype(jnp.int32)
    return ((code // requests) ^ me) * requests + code % requests


def score_kernel(heads, start, keys_ref, *refs):
    message_refs, (scores_ref, code_ref) = by_distance(refs[:-2], QUERY_ORDER), refs[-2:]
    requests = message_refs[0].shape[0]
    tokens, width = keys_ref.shape
    size = width // heads
    group = start // width
    code = code_row(message_refs, start, requests, tokens)
    code_ref[...] = jnp.broadcast_to(code, code_ref.shape)
    span = len(message_refs) * requests
    here = lax.broadcasted_iota(jnp.int32, (span, tokens), 0) == code
    queries = [ref[:, :start].astype(jnp.float32) for ref in message_refs]
    for k in range(heads):
        rows = []
        for g in range(group):
            at = (k * group + g) * size
            rows += [query[:, at : at + size] for query in queries]
        query = jnp.concatenate(rows, axis=0).astype(jnp.bfloat16)
        keys = keys_ref[:, k * size : (k + 1) * size]
        scores = lax.dot_general(query, keys, NT, preferred_element_type=jnp.float32)
        lines = [
            jnp.sum(jnp.where(here, scores[g * span : (g + 1) * span], 0.0), axis=0, keepdims=True)
            for g in range(group)
        ]
        lines = jnp.concatenate(lines, axis=0) * (1.0 / math.sqrt(size))
        scores_ref[k * group : (k + 1) * group, :] = lines.astype(scores_ref.dtype)


def partial_scores(heads, columns, keys, messages):
    tokens, width = keys.shape
    return pl.pallas_call(
        functools.partial(score_kernel, heads, columns),
        out_shape=[
            jax.ShapeDtypeStruct((columns * heads // width, tokens), jnp.bfloat16),
            jax.ShapeDtypeStruct((8, tokens), jnp.int32),
        ],
        compiler_params=params(),
        cost_estimate=pl.CostEstimate(flops=10**11, bytes_accessed=10**4, transcendentals=0),
        name="partial_scores",
    )(keys, *arranged(messages, QUERY_ORDER))


def packed(value, count):
    lane = lax.broadcasted_iota(jnp.int32, value.shape, 1)
    high = value.astype(jnp.bfloat16).astype(jnp.float32)
    middle = (value - high).astype(jnp.bfloat16).astype(jnp.float32)
    low = value - high - middle
    middle, low = pltpu.roll(middle, count, 1), pltpu.roll(low, 2 * count, 1)
    return jnp.where(lane < count, high, jnp.where(lane < 2 * count, middle, low))


def unpacked(message, at, count):
    parts = [message[:, at + part * count : at + (part + 1) * count] for part in range(3)]
    return parts[0] + parts[1] + parts[2]


def even_rank():
    return lax.axis_index("seq") & 1 == 0


def mix_kernel(heads, requests, code_ref, values_ref, near_ref, cache_ref, cache_stats_ref, *refs):
    score_refs, (first_ref, far_ref, last_ref, share_ref) = refs[:4], refs[4:]
    own, before, across, after = [ref[...].astype(jnp.float32) for ref in score_refs]
    scores = (own + across) + (before + after)
    tokens, width = values_ref.shape
    size = width // heads
    count, columns = scores.shape[0], cache_ref.shape[1]
    group = count // heads
    span = 2 * requests
    row = lax.broadcasted_iota(jnp.int32, (span, tokens), 0)
    here = jnp.where(row < requests, row, row + requests) == code_ref[0:1, :]
    lane = lax.broadcasted_iota(jnp.int32, (requests, cache_stats_ref.shape[1]), 1)
    tops = jnp.full(lane.shape, 0.0, jnp.float32)
    totals = jnp.zeros(lane.shape, jnp.float32)
    parts = []
    for k in range(heads):
        weights = []
        for g in range(group):
            h = k * group + g
            line = jnp.where(here, jnp.broadcast_to(scores[h : h + 1, :], (span, tokens)), LOWEST)
            top = jnp.maximum(jnp.max(line, axis=1, keepdims=True), 0.1 * LOWEST)
            probs = jnp.exp(line - top)
            total = jnp.sum(probs, axis=1, keepdims=True)
            weights.append(probs)
            tops = jnp.where(lane == h, top[:requests], tops)
            totals = jnp.where(lane == h, total[:requests], totals)
        weights = jnp.concatenate(weights, axis=0).astype(jnp.bfloat16)
        part = slice(k * size, (k + 1) * size)
        mixed = jnp.dot(weights, values_ref[:, part], preferred_element_type=jnp.float32)
        mixed = mixed + jnp.dot(weights, near_ref[:, part], preferred_element_type=jnp.float32)
        for g in range(group):
            at = slice((k * group + g) * size, (k * group + g + 1) * size)
            parts.append(mixed[g * span : g * span + requests])
            far_ref[:, at] = mixed[g * span + requests : (g + 1) * span].astype(far_ref.dtype)
    cache_tops = cache_stats_ref[:requests, :]
    both = jnp.maximum(cache_tops, tops)
    cache_factor = jnp.exp(cache_tops - both)
    new_factor = jnp.exp(tops - both)
    total = cache_stats_ref[requests:, :] * cache_factor + totals * new_factor
    for h, part in enumerate(parts):
        at = slice(h * size, (h + 1) * size)
        share = cache_ref[:, at] * cache_factor[:, h : h + 1] + part * new_factor[:, h : h + 1]
        share_ref[:, at] = share
    lanes = cache_stats_ref.shape[1]
    far_ref[:, columns:] = jnp.zeros((requests, 3 * lanes), far_ref.dtype)
    for i, value in enumerate((both, total, new_factor)):
        share_ref[:, columns + i * lanes : columns + (i + 1) * lanes] = packed(value, count)
    share, far = share_ref[...], far_ref[...].astype(jnp.float32)
    even = even_rank()
    first_ref[...] = jnp.where(even, far, share).astype(first_ref.dtype)
    last_ref[...] = jnp.where(even, share, far).astype(last_ref.dtype)


def mix(heads, code, values, near_values, cache_mixed, cache_stats, scores):
    requests, lanes = cache_stats.shape[0] // 2, cache_stats.shape[1]
    columns = cache_mixed.shape[1]
    return pl.pallas_call(
        functools.partial(mix_kernel, heads, requests),
        out_shape=[
            jax.ShapeDtypeStruct((requests, columns + 3 * lanes), jnp.bfloat16),
        ]
        * 3,
        scratch_shapes=[pltpu.VMEM((requests, columns + 3 * lanes), jnp.float32)],
        compiler_params=params(),
        name="mix",
    )(code, values, near_values, cache_mixed, cache_stats, *arranged(scores, SCORE_ORDER))


def finish_kernel(count, own_first_ref, own_last_ref, *refs):
    out_ref = refs[-1]
    first_ref, own_far_ref, last_ref = [refs[i] for i in FINISH_PLACES]
    columns = out_ref.shape[1]
    size = columns // count
    lanes = (own_far_ref.shape[1] - columns) // 3
    even = even_rank()
    column_zero = lax.axis_index("tp") == 0

    def read(ref, other_ref, at):
        return jnp.where(even, ref[:, at].astype(jnp.float32), other_ref[:, at].astype(jnp.float32))

    def stats(ref, other_ref):
        message = read(ref, other_ref, slice(columns, columns + 3 * lanes))
        return [unpacked(message, i * lanes, count) for i in range(3)]

    own_top, own_total, own_new = stats(own_last_ref, own_first_ref)
    other_top, other_total, other_new = stats(last_ref, first_ref)
    both = jnp.maximum(own_top, other_top)
    own_factor, other_factor = jnp.exp(own_top - both), jnp.exp(other_top - both)
    own_total, other_total = own_total * own_factor, other_total * other_factor
    total = jnp.where(column_zero, own_total, other_total) + jnp.where(column_zero, other_total, own_total)
    inverse = 1.0 / total
    own_factor, other_factor = own_factor * inverse, other_factor * inverse
    own_new, other_new = own_factor * own_new, other_factor * other_new
    for h in range(count):
        at, lane = slice(h * size, (h + 1) * size), slice(h, h + 1)
        own = read(own_last_ref, own_first_ref, at) * own_factor[:, lane]
        own = own + own_far_ref[:, at].astype(jnp.float32) * own_new[:, lane]
        other = read(last_ref, first_ref, at) * other_factor[:, lane]
        other = other + read(first_ref, last_ref, at) * other_new[:, lane]
        out_ref[:, at] = (own + other).astype(out_ref.dtype)


def finish(count, columns, own_first, own_last, *arrived):
    return pl.pallas_call(
        functools.partial(finish_kernel, count),
        out_shape=jax.ShapeDtypeStruct((own_first.shape[0], columns), jnp.bfloat16),
        compiler_params=params(),
        name="finish",
    )(own_first, own_last, *[arrived[FINISH_PLACES.index(i)] for i in range(3)])


def from_partner(x, axis, distance):
    count = lax.axis_size(axis)
    return lax.ppermute(x, axis, [(i, i ^ distance) for i in range(count)])


def from_behind(x, axis, distance):
    count = lax.axis_size(axis)
    return lax.ppermute(x, axis, [(i, (i + distance) % count) for i in range(count)])


def on_device(tokens, kv_weight, owners, requests, signs, queries, kv_cache, lengths):
    seq_count = lax.axis_size("seq")
    heads = signs.shape[0] // 2
    query = queries[0, 0]
    request_count, columns = query.shape
    message = make_message(query, owners[:, :, 0], requests)
    messages = [message] + [from_partner(message, "seq", d) for d in range(1, seq_count)]
    keys, values = project(tokens, kv_weight)
    near_values = from_partner(values, "seq", 1)
    scores, code = partial_scores(heads, columns, keys, messages)
    scores = [scores] + [from_behind(scores, "seq", d) for d in range(1, seq_count)]
    cache_mixed, cache_stats = cache_part(lengths, query, kv_cache[0, 0], signs)
    first, far, last = mix(heads, code, values, near_values, cache_mixed, cache_stats, scores)
    devices = range(2 * seq_count)
    first_pairs = [(i, i ^ 1) if i & 2 else (i, i ^ 5) for i in devices]
    last_pairs = [(i, i ^ 5) if i & 2 else (i, i ^ 1) for i in devices]
    output = finish(
        columns // signs.shape[1],
        columns,
        first,
        last,
        lax.ppermute(first, ("seq", "tp"), first_pairs),
        from_partner(far, "seq", 2),
        lax.ppermute(last, ("seq", "tp"), last_pairs),
    )
    return output.reshape(1, 1, request_count, columns)


def hadamard(order):
    rows = lax.broadcasted_iota(jnp.int32, (order, order), 0)
    cols = lax.broadcasted_iota(jnp.int32, (order, order), 1)
    parity = jnp.zeros((order, order), jnp.int32)
    for bit_number in range(order.bit_length() - 1):
        parity = parity + rows // 2**bit_number % 2 * (cols // 2**bit_number % 2)
    return (1 - 2 * (parity % 2)).astype(jnp.float32)


def rotate(blocks, sign_rows, matrix):
    product = jnp.einsum(
        "...h,hk->...k", blocks * sign_rows, matrix, precision=lax.Precision.HIGHEST
    )
    return product / math.sqrt(matrix.shape[0])


def encode(rotated):
    largest = jnp.max(jnp.abs(rotated), axis=-1) + 1e-06
    scales = largest.astype(jnp.bfloat16)
    encoded = (rotated / scales.astype(jnp.float32)[..., None]).astype(jnp.bfloat16)
    return (encoded, scales)


def decode(encoded, scales):
    return (encoded.astype(jnp.float32) * scales.astype(jnp.float32)[..., None]).astype(
        jnp.bfloat16
    )


def slot_numbers(targets, count, room):
    onehot = (targets[:, None] == lax.iota(jnp.int32, count)[None, :]).astype(jnp.int32)
    within = jnp.sum((jnp.cumsum(onehot, axis=0) - 1) * onehot, axis=1)
    return targets * room + within


def on_device_long(tokens, kv_weight, owners, requests, signs, queries, kv_cache, lengths):
    seq_count = lax.axis_size("seq")
    per_device = owners.shape[1]
    slots = max(2, (2 * per_device + seq_count - 1) // seq_count)
    head_blocks = signs.shape[0]
    kv_heads = head_blocks // 2
    head_size = signs.shape[1]
    matrix = hadamard(head_size)
    sign_rows = (2 * signs - 1).astype(jnp.float32)
    summed = lax.psum_scatter(
        jnp.dot(tokens, kv_weight, preferred_element_type=jnp.float32).astype(jnp.bfloat16),
        "seq",
        scatter_dimension=0,
        tiled=True,
    ).astype(jnp.float32)
    encoded, scales = encode(
        rotate(summed.reshape(per_device, head_blocks, head_size), sign_rows, matrix)
    )
    slot_index = slot_numbers(owners[0, :, 0], seq_count, slots)
    slot_total = seq_count * slots
    send_values = (
        jnp.zeros((slot_total, head_blocks, head_size), jnp.bfloat16).at[slot_index].set(encoded)
    )
    send_scales = jnp.zeros((slot_total, head_blocks), jnp.bfloat16).at[slot_index].set(scales)
    send_codes = jnp.zeros((slot_total,), jnp.int32).at[slot_index].set(requests[0] + 1)
    got_values, got_scales, arrived_codes = (
        lax.all_to_all(send_values, "seq", split_axis=0, concat_axis=0, tiled=True),
        lax.all_to_all(send_scales, "seq", split_axis=0, concat_axis=0, tiled=True),
        lax.all_to_all(send_codes, "seq", split_axis=0, concat_axis=0, tiled=True),
    )
    arrived = decode(got_values, got_scales)
    query = queries[0, 0]
    request_count = query.shape[0]
    group = query.shape[1] // (kv_heads * head_size)
    query_blocks = query.astype(jnp.float32).reshape(request_count, kv_heads, group, head_size)
    query_rot = rotate(query_blocks, sign_rows[:kv_heads][:, None, :], matrix).astype(jnp.bfloat16)
    local_cache = kv_cache[0, 0]
    cache_span = local_cache.shape[1]
    local_cache = local_cache.reshape(request_count, cache_span, head_blocks, head_size)
    score_scale = 1.0 / math.sqrt(head_size)
    lowest = -1e30
    highest = lax.Precision.HIGHEST
    score_cache = (
        jnp.einsum(
            "rkgd,rckd->rkgc",
            query_rot,
            local_cache[:, :, :kv_heads],
            preferred_element_type=jnp.float32,
        )
        * score_scale
    )
    score_new = (
        jnp.einsum(
            "rkgd,nkd->rkgn", query_rot, arrived[:, :kv_heads], preferred_element_type=jnp.float32
        )
        * score_scale
    )
    positions = lax.axis_index("tp") * cache_span + lax.iota(jnp.int32, cache_span)
    mask_cache = (positions[None, :] < lengths[0, 0][:, None])[:, None, None, :]
    match = arrived_codes[None, :] == (lax.iota(jnp.int32, request_count) + 1)[:, None]
    mask_new = match[:, None, None, :]
    top = jnp.maximum(
        jnp.max(jnp.where(mask_cache, score_cache, lowest), axis=-1),
        jnp.max(jnp.where(mask_new, score_new, lowest), axis=-1),
    )
    probs_cache = jnp.where(mask_cache, jnp.exp(score_cache - top[..., None]), 0.0)
    probs_new = jnp.where(mask_new, jnp.exp(score_new - top[..., None]), 0.0)
    total = jnp.sum(probs_cache, axis=-1) + jnp.sum(probs_new, axis=-1)
    mixed = jnp.einsum(
        "rkgc,rckd->rkgd",
        probs_cache,
        local_cache[:, :, kv_heads:].astype(jnp.float32),
        precision=highest,
    )
    mixed = mixed + jnp.einsum(
        "rkgn,nkd->rkgd", probs_new, arrived[:, kv_heads:].astype(jnp.float32), precision=highest
    )
    shared_top = lax.pmax(top, "tp")
    factor = jnp.exp(top - shared_top)
    total, mixed = (
        lax.psum((total * factor).astype(jnp.bfloat16), "tp").astype(jnp.float32),
        lax.psum((mixed * factor[..., None]).astype(jnp.bfloat16), "tp").astype(jnp.float32),
    )
    mixed = mixed / total[..., None]
    output = rotate(mixed, 1.0, matrix) * sign_rows[kv_heads:][None, :, None, :]
    return output.reshape(1, 1, request_count, group * kv_heads * head_size).astype(jnp.bfloat16)


def solution(mesh):
    placed = (
        P(("groups", "tp", "section"), "seq"),
        P("seq", None),
        P(("groups", "tp", "section"), "seq", None),
        P(("groups", "tp", "section"), "seq"),
        P(),
        P(("groups", "seq"), "section", None, None),
        P(("groups", "seq"), "section", None, "tp", None),
        P(("groups", "seq"), "section", None),
    )
    short = mesh.shape["seq"] == 4 and mesh.shape["tp"] == 2
    return jax.shard_map(
        on_device if short else on_device_long,
        mesh=mesh,
        in_specs=placed,
        out_specs=P(("groups", "seq"), "section", None, None),
        check_vma=False,
    )
```

```python
import functools
import math

import jax
import jax.numpy as jnp
from jax import lax
from jax.experimental import pallas as pl
from jax.experimental.pallas import tpu as pltpu
from jax.sharding import PartitionSpec as P

LOWEST = -1e30
MIB = 1024 * 1024
NT = (((1,), (1,)), ((), ()))


def params(mib=32):
    return pltpu.CompilerParams(vmem_limit_bytes=mib * MIB)


def in_hbm(x):
    return pltpu.with_memory_space_constraint(x, pltpu.HBM)


def in_vmem(x):
    return pltpu.with_memory_space_constraint(x, pltpu.VMEM)


def hadamard_tile(order):
    rows = lax.broadcasted_iota(jnp.int32, (order, order), 0)
    cols = lax.broadcasted_iota(jnp.int32, (order, order), 1)
    common = rows & cols
    parity = jnp.zeros((order, order), jnp.int32)
    for bit_number in range(order.bit_length() - 1):
        parity = parity ^ (common >> bit_number)
    return (1 - 2 * (parity & 1)).astype(jnp.float32).astype(jnp.bfloat16)


QUERY_ORDER = (1, 2, 3)
SCORE_ORDER = (3, 2, 1)
FINISH_PLACES = (1, 0, 2)


def arranged(blocks, order):
    return [blocks[0]] + [blocks[d] for d in order]


def by_distance(refs, order):
    return [refs[0]] + [refs[1 + order.index(d)] for d in range(1, len(refs))]


def project_kernel(tokens_ref, weight_ref, keys_ref, values_ref):
    width = keys_ref.shape[1]
    for out_ref, columns in ((keys_ref, slice(0, width)), (values_ref, slice(width, 2 * width))):
        out_ref[...] = jnp.dot(
            tokens_ref[...], weight_ref[:, columns], preferred_element_type=jnp.float32
        ).astype(out_ref.dtype)


def project(tokens, weight):
    rows, features = tokens.shape
    width = weight.shape[1] // 2
    vmem = pl.BlockSpec(memory_space=pltpu.VMEM)
    return pl.pallas_call(
        project_kernel,
        in_specs=[vmem] * 2,
        out_specs=[vmem] * 2,
        out_shape=[jax.ShapeDtypeStruct((rows, width), jnp.bfloat16)] * 2,
        compiler_params=params(32),
        cost_estimate=pl.CostEstimate(
            flops=4 * rows * features * width,
            bytes_accessed=2 * (rows * features + 2 * features * width),
            transcendentals=0,
        ),
        name="project",
    )(in_vmem(tokens), in_vmem(weight))


def message_kernel(after_ref, query_ref, owners_ref, requests_ref, out_ref, owners_buf, requests_buf, sems):
    requests, columns = query_ref.shape
    per_device = owners_ref.shape[1]
    copies = [
        pltpu.make_async_copy(query_ref, out_ref.at[:, :columns], sems.at[0]),
        pltpu.make_async_copy(owners_ref, owners_buf, sems.at[1]),
        pltpu.make_async_copy(requests_ref, requests_buf, sems.at[2]),
    ]
    for copy in copies:
        copy.start()
    copies[1].wait()
    copies[2].wait()
    code = (owners_buf[...] * requests + requests_buf[...]).astype(jnp.float32)
    spare = jnp.zeros((1, out_ref.shape[1] - columns - per_device), jnp.float32)
    code = jnp.concatenate([code, spare], axis=1)
    out_ref[:, columns:] = jnp.broadcast_to(code, (requests, code.shape[1])).astype(out_ref.dtype)
    copies[0].wait()


def make_message(after, query, owners, requests):
    count, columns = query.shape
    lanes = -(-owners.shape[1] // 128) * 128
    return pl.pallas_call(
        message_kernel,
        in_specs=[pl.BlockSpec(memory_space=pl.ANY)] * 4,
        out_specs=pl.BlockSpec(memory_space=pltpu.VMEM),
        out_shape=jax.ShapeDtypeStruct((count, columns + lanes), query.dtype),
        scratch_shapes=[
            pltpu.VMEM(owners.shape, owners.dtype),
            pltpu.VMEM(requests.shape, requests.dtype),
            pltpu.SemaphoreType.DMA((3,)),
        ],
        compiler_params=params(16),
        cost_estimate=pl.CostEstimate(flops=10**11, bytes_accessed=10**4, transcendentals=0),
        name="make_message",
    )(after, in_hbm(query), in_hbm(owners), in_hbm(requests))


def cache_kernel(
    lengths_ref, query_ref, cache_ref, signs_ref, mixed_ref, stats_ref, query_buf, top_buf, total_buf, mixed_buf
):
    requests, span, _ = cache_ref.shape
    blocks, size = signs_ref.shape
    heads = blocks // 2
    width = heads * size
    count = query_ref.shape[1] // size
    group = count // heads
    norm = 1.0 / math.sqrt(size)
    matrix = hadamard_tile(size)
    signs = (2 * signs_ref[...] - 1).astype(jnp.float32)
    query = query_ref[...].astype(jnp.float32)
    query = jnp.concatenate(
        [query[:, h * size : (h + 1) * size] * signs[h // group : h // group + 1] for h in range(count)], axis=0
    )
    query_buf[...] = jnp.dot(query.astype(jnp.bfloat16), matrix, preferred_element_type=jnp.float32) * norm
    rows = 2 * count
    kv_head = lax.broadcasted_iota(jnp.int32, (rows, width), 0) // group & (heads - 1)
    own_head = kv_head == lax.broadcasted_iota(jnp.int32, (rows, width), 1) // size
    first = lax.broadcasted_iota(jnp.int32, (rows, span), 0) < count
    position = lax.axis_index("tp") * span + lax.broadcasted_iota(jnp.int32, (rows, span), 1)
    pairs = range(0, requests, 2)
    scores = []
    for r in pairs:
        both = [query_buf[pl.ds(r + i, count, stride=requests), :] for i in range(2)]
        wide = jnp.concatenate([jnp.concatenate(both, axis=0)] * heads, axis=1)
        wide = jnp.where(own_head, wide, 0.0).astype(jnp.bfloat16)
        keys = cache_ref[r : r + 2, :, :width].reshape(2 * span, width)
        scores.append(lax.dot_general(wide, keys, NT, preferred_element_type=jnp.float32))
    probs = []
    for r, score in zip(pairs, scores):
        score = jnp.where(first, score[:, :span], score[:, span:]) * norm
        live = position < jnp.where(first, lengths_ref[0, 0, r], lengths_ref[0, 0, r + 1])
        top = jnp.max(jnp.where(live, score, LOWEST), axis=1, keepdims=True)
        prob = jnp.where(live, jnp.exp(score - top), 0.0)
        total = jnp.sum(prob, axis=1, keepdims=True)
        at = slice(r * count, (r + 2) * count)
        top_buf[at, :] = jnp.broadcast_to(top, (rows, size))
        total_buf[at, :] = jnp.broadcast_to(total, (rows, size))
        probs.append(
            jnp.concatenate([jnp.where(first, prob, 0.0), jnp.where(first, 0.0, prob)], axis=1).astype(jnp.bfloat16)
        )
    mixed = []
    for r, prob in zip(pairs, probs):
        values = cache_ref[r : r + 2, :, width:].reshape(2 * span, width)
        wide = jnp.dot(prob, values, preferred_element_type=jnp.float32)
        wide = jnp.where(own_head, wide, 0.0)
        mixed.append(sum(wide[:, k * size : (k + 1) * size] for k in range(heads)))
    mixed = jnp.concatenate(mixed, axis=0)
    high = mixed.astype(jnp.bfloat16)
    low = (mixed - high.astype(jnp.float32)).astype(jnp.bfloat16)
    plain = jnp.dot(high, matrix, preferred_element_type=jnp.float32)
    mixed_buf[...] = plain + jnp.dot(low, matrix, preferred_element_type=jnp.float32)
    lane = lax.broadcasted_iota(jnp.int32, (requests, stats_ref.shape[1]), 1)
    tops = jnp.full(lane.shape, 0.0, jnp.float32)
    totals = jnp.ones(lane.shape, jnp.float32)
    for h in range(count):
        pick = pl.ds(h, requests, stride=count)
        column = slice(h * size, (h + 1) * size)
        k = heads + h // group
        mixed_ref[:, column] = mixed_buf[pick, :] * (signs[k : k + 1] * norm)
        tops = jnp.where(lane == h, top_buf[pick, :], tops)
        totals = jnp.where(lane == h, total_buf[pick, :], totals)
    stats_ref[:requests, :] = tops
    stats_ref[requests:, :] = totals


def early_kernel(
    lengths_ref, query_ref, cache_ref, signs_ref, mixed_ref, stats_ref, lengths_in, query_in, cache_in, signs_in, sems, *bufs
):
    @pl.when(lax.axis_index("section") == 1)
    def _():
        places = (lengths_in, query_in, cache_in, signs_in)
        copies = [
            pltpu.make_async_copy(source, place, sems.at[i])
            for i, (source, place) in enumerate(zip((lengths_ref, query_ref, cache_ref, signs_ref), places))
        ]
        for copy in copies:
            copy.start()
        for copy in copies:
            copy.wait()
        cache_kernel(lengths_in, query_in, cache_in, signs_in, mixed_ref, stats_ref, *bufs)


def late_kernel(lengths_ref, query_ref, cache_ref, signs_ref, early_mixed, early_stats, mixed_ref, stats_ref, *bufs):
    early = lax.axis_index("section") == 1

    @pl.when(early)
    def _():
        mixed_ref[...] = early_mixed[...]
        stats_ref[...] = early_stats[...]

    @pl.when(jnp.logical_not(early))
    def _():
        cache_kernel(lengths_ref, query_ref, cache_ref, signs_ref, mixed_ref, stats_ref, *bufs)


def cache_shapes(query, size):
    requests, columns = query.shape
    outputs = [
        jax.ShapeDtypeStruct(query.shape, jnp.float32),
        jax.ShapeDtypeStruct((2 * requests, size), jnp.float32),
    ]
    return outputs, [pltpu.VMEM((requests * columns // size, size), jnp.float32)] * 4


def early_cache_part(lengths, query, cache, signs):
    outputs, buffers = cache_shapes(query, signs.shape[1])
    return pl.pallas_call(
        early_kernel,
        in_specs=[pl.BlockSpec(memory_space=pl.ANY)] * 4,
        out_specs=[pl.BlockSpec(memory_space=pltpu.VMEM)] * 2,
        out_shape=outputs,
        scratch_shapes=[
            pltpu.SMEM(lengths.shape, lengths.dtype),
            pltpu.VMEM(query.shape, query.dtype),
            pltpu.VMEM(cache.shape, cache.dtype),
            pltpu.VMEM(signs.shape, signs.dtype),
            pltpu.SemaphoreType.DMA((4,)),
        ]
        + buffers,
        compiler_params=params(16),
        name="early_cache_part",
    )(in_hbm(lengths), in_hbm(query), in_hbm(cache), in_hbm(signs))


def cache_part(lengths, query, cache, signs, early):
    requests, span, width = cache.shape
    size = signs.shape[1]
    columns = query.shape[1]
    outputs, buffers = cache_shapes(query, size)
    vmem = pl.BlockSpec(memory_space=pltpu.VMEM)
    return pl.pallas_call(
        late_kernel,
        in_specs=[pl.BlockSpec(memory_space=pltpu.SMEM)] + [vmem] * 5,
        out_shape=outputs,
        scratch_shapes=buffers,
        compiler_params=params(),
        cost_estimate=pl.CostEstimate(
            flops=4 * span * requests * columns,
            bytes_accessed=2 * requests * span * width,
            transcendentals=span * requests * columns // size,
        ),
        name="cache_part",
    )(lengths, query, cache, signs, *early)


def code_row(message_refs, start, requests, tokens):
    count = len(message_refs)
    me = lax.axis_index("seq")
    pieces = [ref[0:1, start : start + tokens // count].astype(jnp.float32) for ref in message_refs]
    row = [sum(jnp.where(me ^ d == at, pieces[d], 0.0) for d in range(count)) for at in range(count)]
    code = jnp.concatenate(row, axis=1).astype(jnp.int32)
    return ((code // requests) ^ me) * requests + code % requests


def score_kernel(heads, start, keys_ref, *refs):
    message_refs, (scores_ref, code_ref) = by_distance(refs[:-2], QUERY_ORDER), refs[-2:]
    requests = message_refs[0].shape[0]
    tokens, width = keys_ref.shape
    size = width // heads
    group = start // width
    code = code_row(message_refs, start, requests, tokens)
    code_ref[...] = jnp.broadcast_to(code, code_ref.shape)
    span = len(message_refs) * requests
    here = lax.broadcasted_iota(jnp.int32, (span, tokens), 0) == code
    queries = [ref[:, :start].astype(jnp.float32) for ref in message_refs]
    for k in range(heads):
        rows = []
        for g in range(group):
            at = (k * group + g) * size
            rows += [query[:, at : at + size] for query in queries]
        query = jnp.concatenate(rows, axis=0).astype(jnp.bfloat16)
        keys = keys_ref[:, k * size : (k + 1) * size]
        scores = lax.dot_general(query, keys, NT, preferred_element_type=jnp.float32)
        lines = [
            jnp.sum(jnp.where(here, scores[g * span : (g + 1) * span], 0.0), axis=0, keepdims=True)
            for g in range(group)
        ]
        lines = jnp.concatenate(lines, axis=0) * (1.0 / math.sqrt(size))
        scores_ref[k * group : (k + 1) * group, :] = lines.astype(scores_ref.dtype)


def partial_scores(heads, columns, keys, messages):
    tokens, width = keys.shape
    return pl.pallas_call(
        functools.partial(score_kernel, heads, columns),
        out_shape=[
            jax.ShapeDtypeStruct((columns * heads // width, tokens), jnp.bfloat16),
            jax.ShapeDtypeStruct((8, tokens), jnp.int32),
        ],
        compiler_params=params(),
        cost_estimate=pl.CostEstimate(flops=10**11, bytes_accessed=10**4, transcendentals=0),
        name="partial_scores",
    )(keys, *arranged(messages, QUERY_ORDER))


def packed(value, count):
    lane = lax.broadcasted_iota(jnp.int32, value.shape, 1)
    high = value.astype(jnp.bfloat16).astype(jnp.float32)
    middle = (value - high).astype(jnp.bfloat16).astype(jnp.float32)
    low = value - high - middle
    middle, low = pltpu.roll(middle, count, 1), pltpu.roll(low, 2 * count, 1)
    return jnp.where(lane < count, high, jnp.where(lane < 2 * count, middle, low))


def unpacked(message, at, count):
    parts = [message[:, at + part * count : at + (part + 1) * count] for part in range(3)]
    return parts[0] + parts[1] + parts[2]


def mix_kernel(heads, requests, code_ref, values_ref, near_ref, cache_ref, cache_stats_ref, *refs):
    score_refs, (share_ref, far_ref) = refs[:4], refs[4:]
    own, after, across, before = [ref[...].astype(jnp.float32) for ref in score_refs]
    scores = (own + across) + (before + after)
    tokens, width = values_ref.shape
    size = width // heads
    count, columns = scores.shape[0], cache_ref.shape[1]
    group = count // heads
    span = 2 * requests
    row = lax.broadcasted_iota(jnp.int32, (span, tokens), 0)
    here = jnp.where(row < requests, row, row + requests) == code_ref[0:1, :]
    lane = lax.broadcasted_iota(jnp.int32, (requests, cache_stats_ref.shape[1]), 1)
    tops = jnp.full(lane.shape, 0.0, jnp.float32)
    totals = jnp.zeros(lane.shape, jnp.float32)
    parts = []
    for k in range(heads):
        weights = []
        for g in range(group):
            h = k * group + g
            line = jnp.where(here, jnp.broadcast_to(scores[h : h + 1, :], (span, tokens)), LOWEST)
            top = jnp.maximum(jnp.max(line, axis=1, keepdims=True), 0.1 * LOWEST)
            probs = jnp.exp(line - top)
            total = jnp.sum(probs, axis=1, keepdims=True)
            weights.append(probs)
            tops = jnp.where(lane == h, top[:requests], tops)
            totals = jnp.where(lane == h, total[:requests], totals)
        weights = jnp.concatenate(weights, axis=0).astype(jnp.bfloat16)
        part = slice(k * size, (k + 1) * size)
        mixed = jnp.dot(weights, values_ref[:, part], preferred_element_type=jnp.float32)
        mixed = mixed + jnp.dot(weights, near_ref[:, part], preferred_element_type=jnp.float32)
        for g in range(group):
            at = slice((k * group + g) * size, (k * group + g + 1) * size)
            parts.append(mixed[g * span : g * span + requests])
            far_ref[:, at] = mixed[g * span + requests : (g + 1) * span].astype(far_ref.dtype)
    cache_tops = cache_stats_ref[:requests, :]
    both = jnp.maximum(cache_tops, tops)
    cache_factor = jnp.exp(cache_tops - both)
    new_factor = jnp.exp(tops - both)
    total = cache_stats_ref[requests:, :] * cache_factor + totals * new_factor
    for h, part in enumerate(parts):
        at = slice(h * size, (h + 1) * size)
        share = cache_ref[:, at] * cache_factor[:, h : h + 1] + part * new_factor[:, h : h + 1]
        share_ref[:, at] = share.astype(share_ref.dtype)
    lanes = cache_stats_ref.shape[1]
    far_ref[:, columns:] = jnp.zeros((requests, 3 * lanes), far_ref.dtype)
    for i, value in enumerate((both, total, new_factor)):
        share_ref[:, columns + i * lanes : columns + (i + 1) * lanes] = packed(value, count).astype(share_ref.dtype)


def mix(heads, code, values, near_values, cache_mixed, cache_stats, scores):
    requests, lanes = cache_stats.shape[0] // 2, cache_stats.shape[1]
    columns = cache_mixed.shape[1]
    return pl.pallas_call(
        functools.partial(mix_kernel, heads, requests),
        out_shape=[
            jax.ShapeDtypeStruct((requests, columns + 3 * lanes), jnp.bfloat16),
        ]
        * 2,
        compiler_params=params(),
        name="mix",
    )(code, values, near_values, cache_mixed, cache_stats, *arranged(scores, SCORE_ORDER))


def finish_kernel(count, *refs):
    own_ref, out_ref = refs[-2:]
    other_ref, own_far_ref, other_far_ref = [refs[i] for i in FINISH_PLACES]
    columns = out_ref.shape[1]
    size = columns // count
    lanes = (own_ref.shape[1] - columns) // 3
    first = lax.axis_index("tp") == 0

    def stats(ref):
        message = ref[:, columns:].astype(jnp.float32)
        return [unpacked(message, i * lanes, count) for i in range(3)]

    own_top, own_total, own_new = stats(own_ref)
    other_top, other_total, other_new = stats(other_ref)
    both = jnp.maximum(own_top, other_top)
    own_factor, other_factor = jnp.exp(own_top - both), jnp.exp(other_top - both)
    own_total, other_total = own_total * own_factor, other_total * other_factor
    total = jnp.where(first, own_total, other_total) + jnp.where(first, other_total, own_total)
    inverse = 1.0 / total
    sides = []
    for ref, far_ref, factor, new in (
        (own_ref, own_far_ref, own_factor, own_new),
        (other_ref, other_far_ref, other_factor, other_new),
    ):
        factor = factor * inverse
        sides.append((ref, far_ref, factor, factor * new))
    for h in range(count):
        at = slice(h * size, (h + 1) * size)
        terms = [
            ref[:, at].astype(jnp.float32) * factor[:, h : h + 1]
            + far_ref[:, at].astype(jnp.float32) * far_factor[:, h : h + 1]
            for ref, far_ref, factor, far_factor in sides
        ]
        out_ref[:, at] = (terms[0] + terms[1]).astype(out_ref.dtype)


def finish(count, columns, own, other, own_far, other_far):
    arrived = (other, own_far, other_far)
    return pl.pallas_call(
        functools.partial(finish_kernel, count),
        out_shape=jax.ShapeDtypeStruct((own.shape[0], columns), jnp.bfloat16),
        compiler_params=params(),
        name="finish",
    )(*[arrived[FINISH_PLACES.index(i)] for i in range(3)], own)


def from_partner(x, axis, distance):
    count = lax.axis_size(axis)
    return lax.ppermute(x, axis, [(i, i ^ distance) for i in range(count)])


def from_behind(x, axis, distance):
    count = lax.axis_size(axis)
    return lax.ppermute(x, axis, [(i, (i + distance) % count) for i in range(count)])


def on_device(tokens, kv_weight, owners, requests, signs, queries, kv_cache, lengths):
    seq_count = lax.axis_size("seq")
    heads = signs.shape[0] // 2
    query = queries[0, 0]
    request_count, columns = query.shape
    early = early_cache_part(lengths, query, kv_cache[0, 0], signs)
    message = make_message(early[1], query, owners[:, :, 0], requests)
    messages = [message] + [from_partner(message, "seq", d) for d in range(1, seq_count)]
    keys, values = project(tokens, kv_weight)
    near_values = from_partner(values, "seq", 1)
    scores, code = partial_scores(heads, columns, keys, messages)
    scores = [scores] + [from_behind(scores, "seq", d) for d in range(1, seq_count)]
    cache_mixed, cache_stats = cache_part(lengths, query, kv_cache[0, 0], signs, early)
    share, far = mix(heads, code, values, near_values, cache_mixed, cache_stats, scores)
    far_pairs = [(i, i ^ 5) for i in range(2 * seq_count)]
    output = finish(
        columns // signs.shape[1],
        columns,
        share,
        from_partner(share, "tp", 1),
        from_partner(far, "seq", 2),
        lax.ppermute(far, ("seq", "tp"), far_pairs),
    )
    return output.reshape(1, 1, request_count, columns)


def hadamard(order):
    rows = lax.broadcasted_iota(jnp.int32, (order, order), 0)
    cols = lax.broadcasted_iota(jnp.int32, (order, order), 1)
    parity = jnp.zeros((order, order), jnp.int32)
    for bit_number in range(order.bit_length() - 1):
        parity = parity + rows // 2**bit_number % 2 * (cols // 2**bit_number % 2)
    return (1 - 2 * (parity % 2)).astype(jnp.float32)


def rotate(blocks, sign_rows, matrix):
    product = jnp.einsum(
        "...h,hk->...k", blocks * sign_rows, matrix, precision=lax.Precision.HIGHEST
    )
    return product / math.sqrt(matrix.shape[0])


def encode(rotated):
    largest = jnp.max(jnp.abs(rotated), axis=-1) + 1e-06
    scales = largest.astype(jnp.bfloat16)
    encoded = (rotated / scales.astype(jnp.float32)[..., None]).astype(jnp.bfloat16)
    return (encoded, scales)


def decode(encoded, scales):
    return (encoded.astype(jnp.float32) * scales.astype(jnp.float32)[..., None]).astype(
        jnp.bfloat16
    )


def slot_numbers(targets, count, room):
    onehot = (targets[:, None] == lax.iota(jnp.int32, count)[None, :]).astype(jnp.int32)
    within = jnp.sum((jnp.cumsum(onehot, axis=0) - 1) * onehot, axis=1)
    return targets * room + within


def on_device_long(tokens, kv_weight, owners, requests, signs, queries, kv_cache, lengths):
    seq_count = lax.axis_size("seq")
    per_device = owners.shape[1]
    slots = max(2, (2 * per_device + seq_count - 1) // seq_count)
    head_blocks = signs.shape[0]
    kv_heads = head_blocks // 2
    head_size = signs.shape[1]
    matrix = hadamard(head_size)
    sign_rows = (2 * signs - 1).astype(jnp.float32)
    summed = lax.psum_scatter(
        jnp.dot(tokens, kv_weight, preferred_element_type=jnp.float32).astype(jnp.bfloat16),
        "seq",
        scatter_dimension=0,
        tiled=True,
    ).astype(jnp.float32)
    encoded, scales = encode(
        rotate(summed.reshape(per_device, head_blocks, head_size), sign_rows, matrix)
    )
    slot_index = slot_numbers(owners[0, :, 0], seq_count, slots)
    slot_total = seq_count * slots
    send_values = (
        jnp.zeros((slot_total, head_blocks, head_size), jnp.bfloat16).at[slot_index].set(encoded)
    )
    send_scales = jnp.zeros((slot_total, head_blocks), jnp.bfloat16).at[slot_index].set(scales)
    send_codes = jnp.zeros((slot_total,), jnp.int32).at[slot_index].set(requests[0] + 1)
    got_values, got_scales, arrived_codes = (
        lax.all_to_all(send_values, "seq", split_axis=0, concat_axis=0, tiled=True),
        lax.all_to_all(send_scales, "seq", split_axis=0, concat_axis=0, tiled=True),
        lax.all_to_all(send_codes, "seq", split_axis=0, concat_axis=0, tiled=True),
    )
    arrived = decode(got_values, got_scales)
    query = queries[0, 0]
    request_count = query.shape[0]
    group = query.shape[1] // (kv_heads * head_size)
    query_blocks = query.astype(jnp.float32).reshape(request_count, kv_heads, group, head_size)
    query_rot = rotate(query_blocks, sign_rows[:kv_heads][:, None, :], matrix).astype(jnp.bfloat16)
    local_cache = kv_cache[0, 0]
    cache_span = local_cache.shape[1]
    local_cache = local_cache.reshape(request_count, cache_span, head_blocks, head_size)
    score_scale = 1.0 / math.sqrt(head_size)
    lowest = -1e30
    highest = lax.Precision.HIGHEST
    score_cache = (
        jnp.einsum(
            "rkgd,rckd->rkgc",
            query_rot,
            local_cache[:, :, :kv_heads],
            preferred_element_type=jnp.float32,
        )
        * score_scale
    )
    score_new = (
        jnp.einsum(
            "rkgd,nkd->rkgn", query_rot, arrived[:, :kv_heads], preferred_element_type=jnp.float32
        )
        * score_scale
    )
    positions = lax.axis_index("tp") * cache_span + lax.iota(jnp.int32, cache_span)
    mask_cache = (positions[None, :] < lengths[0, 0][:, None])[:, None, None, :]
    match = arrived_codes[None, :] == (lax.iota(jnp.int32, request_count) + 1)[:, None]
    mask_new = match[:, None, None, :]
    top = jnp.maximum(
        jnp.max(jnp.where(mask_cache, score_cache, lowest), axis=-1),
        jnp.max(jnp.where(mask_new, score_new, lowest), axis=-1),
    )
    probs_cache = jnp.where(mask_cache, jnp.exp(score_cache - top[..., None]), 0.0)
    probs_new = jnp.where(mask_new, jnp.exp(score_new - top[..., None]), 0.0)
    total = jnp.sum(probs_cache, axis=-1) + jnp.sum(probs_new, axis=-1)
    mixed = jnp.einsum(
        "rkgc,rckd->rkgd",
        probs_cache,
        local_cache[:, :, kv_heads:].astype(jnp.float32),
        precision=highest,
    )
    mixed = mixed + jnp.einsum(
        "rkgn,nkd->rkgd", probs_new, arrived[:, kv_heads:].astype(jnp.float32), precision=highest
    )
    shared_top = lax.pmax(top, "tp")
    factor = jnp.exp(top - shared_top)
    total, mixed = (
        lax.psum((total * factor).astype(jnp.bfloat16), "tp").astype(jnp.float32),
        lax.psum((mixed * factor[..., None]).astype(jnp.bfloat16), "tp").astype(jnp.float32),
    )
    mixed = mixed / total[..., None]
    output = rotate(mixed, 1.0, matrix) * sign_rows[kv_heads:][None, :, None, :]
    return output.reshape(1, 1, request_count, group * kv_heads * head_size).astype(jnp.bfloat16)


def solution(mesh):
    placed = (
        P(("groups", "tp", "section"), "seq"),
        P("seq", None),
        P(("groups", "tp", "section"), "seq", None),
        P(("groups", "tp", "section"), "seq"),
        P(),
        P(("groups", "seq"), "section", None, None),
        P(("groups", "seq"), "section", None, "tp", None),
        P(("groups", "seq"), "section", None),
    )
    short = mesh.shape["seq"] == 4 and mesh.shape["tp"] == 2
    return jax.shard_map(
        on_device if short else on_device_long,
        mesh=mesh,
        in_specs=placed,
        out_specs=P(("groups", "seq"), "section", None, None),
        check_vma=False,
    )
```

```python
import functools
import math

import jax
import jax.numpy as jnp
from jax import lax
from jax.experimental import pallas as pl
from jax.experimental.pallas import tpu as pltpu
from jax.sharding import PartitionSpec as P

LOWEST = -1e30
MIB = 1024 * 1024
NT = (((1,), (1,)), ((), ()))


def params(mib=32):
    return pltpu.CompilerParams(vmem_limit_bytes=mib * MIB)


def in_hbm(x):
    return pltpu.with_memory_space_constraint(x, pltpu.HBM)


def in_vmem(x):
    return pltpu.with_memory_space_constraint(x, pltpu.VMEM)


def hadamard_tile(order):
    rows = lax.broadcasted_iota(jnp.int32, (order, order), 0)
    cols = lax.broadcasted_iota(jnp.int32, (order, order), 1)
    common = rows & cols
    parity = jnp.zeros((order, order), jnp.int32)
    for bit_number in range(order.bit_length() - 1):
        parity = parity ^ (common >> bit_number)
    return (1 - 2 * (parity & 1)).astype(jnp.float32).astype(jnp.bfloat16)


QUERY_ORDER = (3, 2, 1)
SCORE_ORDER = (1, 2, 3)
FINISH_PLACES = (2, 1, 0)


def arranged(blocks, order):
    return [blocks[0]] + [blocks[d] for d in order]


def by_distance(refs, order):
    return [refs[0]] + [refs[1 + order.index(d)] for d in range(1, len(refs))]


def project_kernel(tokens_ref, weight_ref, keys_ref, values_ref):
    width = keys_ref.shape[1]
    for out_ref, columns in ((keys_ref, slice(0, width)), (values_ref, slice(width, 2 * width))):
        out_ref[...] = jnp.dot(
            tokens_ref[...], weight_ref[:, columns], preferred_element_type=jnp.float32
        ).astype(out_ref.dtype)


def project(tokens, weight):
    rows, features = tokens.shape
    width = weight.shape[1] // 2
    vmem = pl.BlockSpec(memory_space=pltpu.VMEM)
    return pl.pallas_call(
        project_kernel,
        in_specs=[vmem] * 2,
        out_specs=[vmem] * 2,
        out_shape=[jax.ShapeDtypeStruct((rows, width), jnp.bfloat16)] * 2,
        compiler_params=params(32),
        cost_estimate=pl.CostEstimate(
            flops=4 * rows * features * width,
            bytes_accessed=2 * (rows * features + 2 * features * width),
            transcendentals=0,
        ),
        name="project",
    )(in_vmem(tokens), in_vmem(weight))


def message_kernel(query_ref, owners_ref, requests_ref, out_ref, owners_buf, requests_buf, sems):
    requests, columns = query_ref.shape
    per_device = owners_ref.shape[1]
    copies = [
        pltpu.make_async_copy(query_ref, out_ref.at[:, :columns], sems.at[0]),
        pltpu.make_async_copy(owners_ref, owners_buf, sems.at[1]),
        pltpu.make_async_copy(requests_ref, requests_buf, sems.at[2]),
    ]
    for copy in copies:
        copy.start()
    copies[1].wait()
    copies[2].wait()
    code = (owners_buf[...] * requests + requests_buf[...]).astype(jnp.float32)
    spare = jnp.zeros((1, out_ref.shape[1] - columns - per_device), jnp.float32)
    code = jnp.concatenate([code, spare], axis=1)
    out_ref[:, columns:] = jnp.broadcast_to(code, (requests, code.shape[1])).astype(out_ref.dtype)
    copies[0].wait()


def make_message(query, owners, requests):
    count, columns = query.shape
    lanes = -(-owners.shape[1] // 128) * 128
    return pl.pallas_call(
        message_kernel,
        in_specs=[pl.BlockSpec(memory_space=pl.ANY)] * 3,
        out_specs=pl.BlockSpec(memory_space=pltpu.VMEM),
        out_shape=jax.ShapeDtypeStruct((count, columns + lanes), query.dtype),
        scratch_shapes=[
            pltpu.VMEM(owners.shape, owners.dtype),
            pltpu.VMEM(requests.shape, requests.dtype),
            pltpu.SemaphoreType.DMA((3,)),
        ],
        compiler_params=params(16),
        cost_estimate=pl.CostEstimate(flops=10**11, bytes_accessed=10**4, transcendentals=0),
        name="make_message",
    )(in_hbm(query), in_hbm(owners), in_hbm(requests))


def cache_kernel(
    lengths_ref, query_ref, cache_ref, signs_ref, mixed_ref, stats_ref, query_buf, top_buf, total_buf, mixed_buf
):
    requests, span, _ = cache_ref.shape
    blocks, size = signs_ref.shape
    heads = blocks // 2
    width = heads * size
    count = query_ref.shape[1] // size
    group = count // heads
    norm = 1.0 / math.sqrt(size)
    matrix = hadamard_tile(size)
    signs = (2 * signs_ref[...] - 1).astype(jnp.float32)
    query = query_ref[...].astype(jnp.float32)
    query = jnp.concatenate(
        [query[:, h * size : (h + 1) * size] * signs[h // group : h // group + 1] for h in range(count)], axis=0
    )
    query_buf[...] = jnp.dot(query.astype(jnp.bfloat16), matrix, preferred_element_type=jnp.float32) * norm
    rows = 2 * count
    kv_head = lax.broadcasted_iota(jnp.int32, (rows, width), 0) // group & (heads - 1)
    own_head = kv_head == lax.broadcasted_iota(jnp.int32, (rows, width), 1) // size
    first = lax.broadcasted_iota(jnp.int32, (rows, span), 0) < count
    position = lax.axis_index("tp") * span + lax.broadcasted_iota(jnp.int32, (rows, span), 1)
    pairs = range(0, requests, 2)
    scores = []
    for r in pairs:
        both = [query_buf[pl.ds(r + i, count, stride=requests), :] for i in range(2)]
        wide = jnp.concatenate([jnp.concatenate(both, axis=0)] * heads, axis=1)
        wide = jnp.where(own_head, wide, 0.0).astype(jnp.bfloat16)
        keys = cache_ref[r : r + 2, :, :width].reshape(2 * span, width)
        scores.append(lax.dot_general(wide, keys, NT, preferred_element_type=jnp.float32))
    probs = []
    for r, score in zip(pairs, scores):
        score = jnp.where(first, score[:, :span], score[:, span:]) * norm
        live = position < jnp.where(first, lengths_ref[0, 0, r], lengths_ref[0, 0, r + 1])
        top = jnp.max(jnp.where(live, score, LOWEST), axis=1, keepdims=True)
        prob = jnp.where(live, jnp.exp(score - top), 0.0)
        total = jnp.sum(prob, axis=1, keepdims=True)
        at = slice(r * count, (r + 2) * count)
        top_buf[at, :] = jnp.broadcast_to(top, (rows, size))
        total_buf[at, :] = jnp.broadcast_to(total, (rows, size))
        probs.append(
            jnp.concatenate([jnp.where(first, prob, 0.0), jnp.where(first, 0.0, prob)], axis=1).astype(jnp.bfloat16)
        )
    mixed = []
    for r, prob in zip(pairs, probs):
        values = cache_ref[r : r + 2, :, width:].reshape(2 * span, width)
        wide = jnp.dot(prob, values, preferred_element_type=jnp.float32)
        wide = jnp.where(own_head, wide, 0.0)
        mixed.append(sum(wide[:, k * size : (k + 1) * size] for k in range(heads)))
    mixed = jnp.concatenate(mixed, axis=0)
    high = mixed.astype(jnp.bfloat16)
    low = (mixed - high.astype(jnp.float32)).astype(jnp.bfloat16)
    plain = jnp.dot(high, matrix, preferred_element_type=jnp.float32)
    mixed_buf[...] = plain + jnp.dot(low, matrix, preferred_element_type=jnp.float32)
    lane = lax.broadcasted_iota(jnp.int32, (requests, stats_ref.shape[1]), 1)
    tops = jnp.full(lane.shape, 0.0, jnp.float32)
    totals = jnp.ones(lane.shape, jnp.float32)
    for h in range(count):
        pick = pl.ds(h, requests, stride=count)
        column = slice(h * size, (h + 1) * size)
        k = heads + h // group
        mixed_ref[:, column] = mixed_buf[pick, :] * (signs[k : k + 1] * norm)
        tops = jnp.where(lane == h, top_buf[pick, :], tops)
        totals = jnp.where(lane == h, total_buf[pick, :], totals)
    stats_ref[:requests, :] = tops
    stats_ref[requests:, :] = totals


def cache_part(lengths, query, cache, signs):
    requests, span, width = cache.shape
    size = signs.shape[1]
    columns = query.shape[1]
    vmem = pl.BlockSpec(memory_space=pltpu.VMEM)
    return pl.pallas_call(
        cache_kernel,
        in_specs=[pl.BlockSpec(memory_space=pltpu.SMEM)] + [vmem] * 3,
        out_shape=[
            jax.ShapeDtypeStruct(query.shape, jnp.float32),
            jax.ShapeDtypeStruct((2 * requests, size), jnp.float32),
        ],
        scratch_shapes=[pltpu.VMEM((requests * columns // size, size), jnp.float32)] * 4,
        compiler_params=params(),
        cost_estimate=pl.CostEstimate(
            flops=4 * span * requests * columns,
            bytes_accessed=2 * requests * span * width,
            transcendentals=span * requests * columns // size,
        ),
        name="cache_part",
    )(lengths, query, cache, signs)


def code_row(message_refs, start, requests, tokens):
    count = len(message_refs)
    me = lax.axis_index("seq")
    pieces = [ref[0:1, start : start + tokens // count].astype(jnp.float32) for ref in message_refs]
    row = [sum(jnp.where(me ^ d == at, pieces[d], 0.0) for d in range(count)) for at in range(count)]
    code = jnp.concatenate(row, axis=1).astype(jnp.int32)
    return ((code // requests) ^ me) * requests + code % requests


def score_kernel(heads, start, keys_ref, *refs):
    message_refs, (scores_ref, code_ref) = by_distance(refs[:-2], QUERY_ORDER), refs[-2:]
    requests = message_refs[0].shape[0]
    tokens, width = keys_ref.shape
    size = width // heads
    group = start // width
    code = code_row(message_refs, start, requests, tokens)
    code_ref[...] = jnp.broadcast_to(code, code_ref.shape)
    span = len(message_refs) * requests
    here = lax.broadcasted_iota(jnp.int32, (span, tokens), 0) == code
    queries = [ref[:, :start].astype(jnp.float32) for ref in message_refs]
    for k in range(heads):
        rows = []
        for g in range(group):
            at = (k * group + g) * size
            rows += [query[:, at : at + size] for query in queries]
        query = jnp.concatenate(rows, axis=0).astype(jnp.bfloat16)
        keys = keys_ref[:, k * size : (k + 1) * size]
        scores = lax.dot_general(query, keys, NT, preferred_element_type=jnp.float32)
        lines = [
            jnp.sum(jnp.where(here, scores[g * span : (g + 1) * span], 0.0), axis=0, keepdims=True)
            for g in range(group)
        ]
        lines = jnp.concatenate(lines, axis=0) * (1.0 / math.sqrt(size))
        scores_ref[k * group : (k + 1) * group, :] = lines.astype(scores_ref.dtype)


def partial_scores(heads, columns, keys, messages):
    tokens, width = keys.shape
    return pl.pallas_call(
        functools.partial(score_kernel, heads, columns),
        out_shape=[
            jax.ShapeDtypeStruct((columns * heads // width, tokens), jnp.bfloat16),
            jax.ShapeDtypeStruct((8, tokens), jnp.int32),
        ],
        compiler_params=params(),
        cost_estimate=pl.CostEstimate(flops=10**11, bytes_accessed=10**4, transcendentals=0),
        name="partial_scores",
    )(keys, *arranged(messages, QUERY_ORDER))


def packed(values, count):
    lane = lax.broadcasted_iota(jnp.int32, values[0].shape, 1)
    out = values[0]
    for i, value in enumerate(values[1:], 1):
        out = jnp.where(lane < i * count, out, pltpu.roll(value, i * count, 1))
    return out


def unpacked(message, count):
    parts = [message[:, i * count : (i + 1) * count] for i in range(4)]
    return parts[0] + parts[1], parts[2], parts[3]


def mix_kernel(heads, requests, code_ref, values_ref, near_ref, cache_ref, cache_stats_ref, *refs):
    score_refs, (share_ref, far_ref) = refs[:4], refs[4:]
    own, before, across, after = [ref[...].astype(jnp.float32) for ref in score_refs]
    scores = (own + across) + (before + after)
    tokens, width = values_ref.shape
    size = width // heads
    count, columns = scores.shape[0], cache_ref.shape[1]
    group = count // heads
    span = 2 * requests
    row = lax.broadcasted_iota(jnp.int32, (span, tokens), 0)
    here = jnp.where(row < requests, row, row + requests) == code_ref[0:1, :]
    lane = lax.broadcasted_iota(jnp.int32, (requests, cache_stats_ref.shape[1]), 1)
    tops = jnp.full(lane.shape, 0.0, jnp.float32)
    totals = jnp.zeros(lane.shape, jnp.float32)
    parts = []
    for k in range(heads):
        weights = []
        for g in range(group):
            h = k * group + g
            line = jnp.where(here, jnp.broadcast_to(scores[h : h + 1, :], (span, tokens)), LOWEST)
            top = jnp.maximum(jnp.max(line, axis=1, keepdims=True), 0.1 * LOWEST)
            probs = jnp.exp(line - top)
            total = jnp.sum(probs, axis=1, keepdims=True)
            weights.append(probs)
            tops = jnp.where(lane == h, top[:requests], tops)
            totals = jnp.where(lane == h, total[:requests], totals)
        weights = jnp.concatenate(weights, axis=0).astype(jnp.bfloat16)
        part = slice(k * size, (k + 1) * size)
        mixed = jnp.dot(weights, values_ref[:, part], preferred_element_type=jnp.float32)
        mixed = mixed + jnp.dot(weights, near_ref[:, part], preferred_element_type=jnp.float32)
        for g in range(group):
            at = slice((k * group + g) * size, (k * group + g + 1) * size)
            parts.append(mixed[g * span : g * span + requests])
            far_ref[:, at] = mixed[g * span + requests : (g + 1) * span].astype(far_ref.dtype)
    cache_tops = cache_stats_ref[:requests, :]
    both = jnp.maximum(cache_tops, tops)
    high = both.astype(jnp.bfloat16).astype(jnp.float32)
    low = (both - high).astype(jnp.bfloat16).astype(jnp.float32)
    cache_factor = jnp.exp(jnp.minimum(cache_tops - (high + low), 60.0))
    new_factor = jnp.exp(jnp.minimum(tops - (high + low), 60.0))
    total = cache_stats_ref[requests:, :] * cache_factor + totals * new_factor
    for h, part in enumerate(parts):
        at = slice(h * size, (h + 1) * size)
        share = cache_ref[:, at] * cache_factor[:, h : h + 1] + part * new_factor[:, h : h + 1]
        share_ref[:, at] = share.astype(share_ref.dtype)
    far_ref[:, columns:] = jnp.zeros((requests, 4 * count), far_ref.dtype)
    share_ref[:, columns:] = packed((high, low, total, new_factor), count).astype(share_ref.dtype)


def mix(heads, code, values, near_values, cache_mixed, cache_stats, scores):
    requests, lanes = cache_stats.shape[0] // 2, cache_stats.shape[1]
    columns = cache_mixed.shape[1]
    return pl.pallas_call(
        functools.partial(mix_kernel, heads, requests),
        out_shape=[
            jax.ShapeDtypeStruct((requests, columns + lanes), jnp.bfloat16),
        ]
        * 2,
        compiler_params=params(),
        name="mix",
    )(code, values, near_values, cache_mixed, cache_stats, *arranged(scores, SCORE_ORDER))


def finish_kernel(count, own_ref, *refs):
    out_ref = refs[-1]
    other_ref, own_far_ref, other_far_ref = [refs[i] for i in FINISH_PLACES]
    columns = out_ref.shape[1]
    size = columns // count
    first = lax.axis_index("tp") == 0
    own_top, own_total, own_new = unpacked(own_ref[:, columns:].astype(jnp.float32), count)
    other_top, other_total, other_new = unpacked(other_ref[:, columns:].astype(jnp.float32), count)
    both = jnp.maximum(own_top, other_top)
    own_factor, other_factor = jnp.exp(own_top - both), jnp.exp(other_top - both)
    own_total, other_total = own_total * own_factor, other_total * other_factor
    total = jnp.where(first, own_total, other_total) + jnp.where(first, other_total, own_total)
    inverse = 1.0 / total
    sides = []
    for ref, far_ref, factor, new in (
        (own_ref, own_far_ref, own_factor, own_new),
        (other_ref, other_far_ref, other_factor, other_new),
    ):
        factor = factor * inverse
        sides.append((ref, far_ref, factor, factor * new))
    for h in range(count):
        at = slice(h * size, (h + 1) * size)
        terms = [
            ref[:, at].astype(jnp.float32) * factor[:, h : h + 1]
            + far_ref[:, at].astype(jnp.float32) * far_factor[:, h : h + 1]
            for ref, far_ref, factor, far_factor in sides
        ]
        out_ref[:, at] = (terms[0] + terms[1]).astype(out_ref.dtype)


def finish(count, columns, own, other, own_far, other_far):
    arrived = (other, own_far, other_far)
    return pl.pallas_call(
        functools.partial(finish_kernel, count),
        out_shape=jax.ShapeDtypeStruct((own.shape[0], columns), jnp.bfloat16),
        compiler_params=params(),
        name="finish",
    )(own, *[arrived[FINISH_PLACES.index(i)] for i in range(3)])


def from_partner(x, axis, distance):
    count = lax.axis_size(axis)
    return lax.ppermute(x, axis, [(i, i ^ distance) for i in range(count)])


def from_behind(x, axis, distance):
    count = lax.axis_size(axis)
    return lax.ppermute(x, axis, [(i, (i + distance) % count) for i in range(count)])


def on_device(tokens, kv_weight, owners, requests, signs, queries, kv_cache, lengths):
    seq_count = lax.axis_size("seq")
    heads = signs.shape[0] // 2
    query = queries[0, 0]
    request_count, columns = query.shape
    message = make_message(query, owners[:, :, 0], requests)
    messages = [message] + [from_partner(message, "seq", d) for d in range(1, seq_count)]
    keys, values = project(tokens, kv_weight)
    near_values = from_partner(values, "seq", 1)
    scores, code = partial_scores(heads, columns, keys, messages)
    scores = [scores] + [from_behind(scores, "seq", d) for d in range(1, seq_count)]
    cache_mixed, cache_stats = cache_part(lengths, query, kv_cache[0, 0], signs)
    share, far = mix(heads, code, values, near_values, cache_mixed, cache_stats, scores)
    far_pairs = [(i, i ^ 5) for i in range(2 * seq_count)]
    output = finish(
        columns // signs.shape[1],
        columns,
        share,
        from_partner(share, "tp", 1),
        from_partner(far, "seq", 2),
        lax.ppermute(far, ("seq", "tp"), far_pairs),
    )
    return output.reshape(1, 1, request_count, columns)


def hadamard(order):
    rows = lax.broadcasted_iota(jnp.int32, (order, order), 0)
    cols = lax.broadcasted_iota(jnp.int32, (order, order), 1)
    parity = jnp.zeros((order, order), jnp.int32)
    for bit_number in range(order.bit_length() - 1):
        parity = parity + rows // 2**bit_number % 2 * (cols // 2**bit_number % 2)
    return (1 - 2 * (parity % 2)).astype(jnp.float32)


def rotate(blocks, sign_rows, matrix):
    product = jnp.einsum(
        "...h,hk->...k", blocks * sign_rows, matrix, precision=lax.Precision.HIGHEST
    )
    return product / math.sqrt(matrix.shape[0])


def encode(rotated):
    largest = jnp.max(jnp.abs(rotated), axis=-1) + 1e-06
    scales = largest.astype(jnp.bfloat16)
    encoded = (rotated / scales.astype(jnp.float32)[..., None]).astype(jnp.bfloat16)
    return (encoded, scales)


def decode(encoded, scales):
    return (encoded.astype(jnp.float32) * scales.astype(jnp.float32)[..., None]).astype(
        jnp.bfloat16
    )


def slot_numbers(targets, count, room):
    onehot = (targets[:, None] == lax.iota(jnp.int32, count)[None, :]).astype(jnp.int32)
    within = jnp.sum((jnp.cumsum(onehot, axis=0) - 1) * onehot, axis=1)
    return targets * room + within


def on_device_long(tokens, kv_weight, owners, requests, signs, queries, kv_cache, lengths):
    seq_count = lax.axis_size("seq")
    per_device = owners.shape[1]
    slots = max(2, (2 * per_device + seq_count - 1) // seq_count)
    head_blocks = signs.shape[0]
    kv_heads = head_blocks // 2
    head_size = signs.shape[1]
    matrix = hadamard(head_size)
    sign_rows = (2 * signs - 1).astype(jnp.float32)
    summed = lax.psum_scatter(
        jnp.dot(tokens, kv_weight, preferred_element_type=jnp.float32).astype(jnp.bfloat16),
        "seq",
        scatter_dimension=0,
        tiled=True,
    ).astype(jnp.float32)
    encoded, scales = encode(
        rotate(summed.reshape(per_device, head_blocks, head_size), sign_rows, matrix)
    )
    slot_index = slot_numbers(owners[0, :, 0], seq_count, slots)
    slot_total = seq_count * slots
    send_values = (
        jnp.zeros((slot_total, head_blocks, head_size), jnp.bfloat16).at[slot_index].set(encoded)
    )
    send_scales = jnp.zeros((slot_total, head_blocks), jnp.bfloat16).at[slot_index].set(scales)
    send_codes = jnp.zeros((slot_total,), jnp.int32).at[slot_index].set(requests[0] + 1)
    got_values, got_scales, arrived_codes = (
        lax.all_to_all(send_values, "seq", split_axis=0, concat_axis=0, tiled=True),
        lax.all_to_all(send_scales, "seq", split_axis=0, concat_axis=0, tiled=True),
        lax.all_to_all(send_codes, "seq", split_axis=0, concat_axis=0, tiled=True),
    )
    arrived = decode(got_values, got_scales)
    query = queries[0, 0]
    request_count = query.shape[0]
    group = query.shape[1] // (kv_heads * head_size)
    query_blocks = query.astype(jnp.float32).reshape(request_count, kv_heads, group, head_size)
    query_rot = rotate(query_blocks, sign_rows[:kv_heads][:, None, :], matrix).astype(jnp.bfloat16)
    local_cache = kv_cache[0, 0]
    cache_span = local_cache.shape[1]
    local_cache = local_cache.reshape(request_count, cache_span, head_blocks, head_size)
    score_scale = 1.0 / math.sqrt(head_size)
    lowest = -1e30
    highest = lax.Precision.HIGHEST
    score_cache = (
        jnp.einsum(
            "rkgd,rckd->rkgc",
            query_rot,
            local_cache[:, :, :kv_heads],
            preferred_element_type=jnp.float32,
        )
        * score_scale
    )
    score_new = (
        jnp.einsum(
            "rkgd,nkd->rkgn", query_rot, arrived[:, :kv_heads], preferred_element_type=jnp.float32
        )
        * score_scale
    )
    positions = lax.axis_index("tp") * cache_span + lax.iota(jnp.int32, cache_span)
    mask_cache = (positions[None, :] < lengths[0, 0][:, None])[:, None, None, :]
    match = arrived_codes[None, :] == (lax.iota(jnp.int32, request_count) + 1)[:, None]
    mask_new = match[:, None, None, :]
    top = jnp.maximum(
        jnp.max(jnp.where(mask_cache, score_cache, lowest), axis=-1),
        jnp.max(jnp.where(mask_new, score_new, lowest), axis=-1),
    )
    probs_cache = jnp.where(mask_cache, jnp.exp(score_cache - top[..., None]), 0.0)
    probs_new = jnp.where(mask_new, jnp.exp(score_new - top[..., None]), 0.0)
    total = jnp.sum(probs_cache, axis=-1) + jnp.sum(probs_new, axis=-1)
    mixed = jnp.einsum(
        "rkgc,rckd->rkgd",
        probs_cache,
        local_cache[:, :, kv_heads:].astype(jnp.float32),
        precision=highest,
    )
    mixed = mixed + jnp.einsum(
        "rkgn,nkd->rkgd", probs_new, arrived[:, kv_heads:].astype(jnp.float32), precision=highest
    )
    shared_top = lax.pmax(top, "tp")
    factor = jnp.exp(top - shared_top)
    total, mixed = (
        lax.psum((total * factor).astype(jnp.bfloat16), "tp").astype(jnp.float32),
        lax.psum((mixed * factor[..., None]).astype(jnp.bfloat16), "tp").astype(jnp.float32),
    )
    mixed = mixed / total[..., None]
    output = rotate(mixed, 1.0, matrix) * sign_rows[kv_heads:][None, :, None, :]
    return output.reshape(1, 1, request_count, group * kv_heads * head_size).astype(jnp.bfloat16)


def solution(mesh):
    placed = (
        P(("groups", "tp", "section"), "seq"),
        P("seq", None),
        P(("groups", "tp", "section"), "seq", None),
        P(("groups", "tp", "section"), "seq"),
        P(),
        P(("groups", "seq"), "section", None, None),
        P(("groups", "seq"), "section", None, "tp", None),
        P(("groups", "seq"), "section", None),
    )
    short = mesh.shape["seq"] == 4 and mesh.shape["tp"] == 2
    return jax.shard_map(
        on_device if short else on_device_long,
        mesh=mesh,
        in_specs=placed,
        out_specs=P(("groups", "seq"), "section", None, None),
        check_vma=False,
    )
```

```python
import functools
import math

import jax
import jax.numpy as jnp
from jax import lax
from jax.experimental import pallas as pl
from jax.experimental.pallas import tpu as pltpu
from jax.sharding import PartitionSpec as P

LOWEST = -1e30
MIB = 1024 * 1024
NT = (((1,), (1,)), ((), ()))


def params(mib=32):
    return pltpu.CompilerParams(vmem_limit_bytes=mib * MIB)


def in_hbm(x):
    return pltpu.with_memory_space_constraint(x, pltpu.HBM)


def in_vmem(x):
    return pltpu.with_memory_space_constraint(x, pltpu.VMEM)


def hadamard_tile(order):
    rows = lax.broadcasted_iota(jnp.int32, (order, order), 0)
    cols = lax.broadcasted_iota(jnp.int32, (order, order), 1)
    common = rows & cols
    parity = jnp.zeros((order, order), jnp.int32)
    for bit_number in range(order.bit_length() - 1):
        parity = parity ^ (common >> bit_number)
    return (1 - 2 * (parity & 1)).astype(jnp.float32).astype(jnp.bfloat16)


QUERY_ORDER = (3, 2, 1)
SCORE_ORDER = (1, 2, 3)
FINISH_PLACES = (1, 0)


def arranged(blocks, order):
    return [blocks[0]] + [blocks[d] for d in order]


def by_distance(refs, order):
    return [refs[0]] + [refs[1 + order.index(d)] for d in range(1, len(refs))]


def project_kernel(tokens_ref, weight_ref, keys_ref, values_ref):
    width = keys_ref.shape[1]
    for out_ref, columns in ((keys_ref, slice(0, width)), (values_ref, slice(width, 2 * width))):
        out_ref[...] = jnp.dot(
            tokens_ref[...], weight_ref[:, columns], preferred_element_type=jnp.float32
        ).astype(out_ref.dtype)


def project(tokens, weight):
    rows, features = tokens.shape
    width = weight.shape[1] // 2
    vmem = pl.BlockSpec(memory_space=pltpu.VMEM)
    return pl.pallas_call(
        project_kernel,
        in_specs=[vmem] * 2,
        out_specs=[vmem] * 2,
        out_shape=[jax.ShapeDtypeStruct((rows, width), jnp.bfloat16)] * 2,
        compiler_params=params(32),
        cost_estimate=pl.CostEstimate(
            flops=4 * rows * features * width,
            bytes_accessed=2 * (rows * features + 2 * features * width),
            transcendentals=0,
        ),
        name="project",
    )(in_vmem(tokens), in_vmem(weight))


def message_kernel(query_ref, owners_ref, requests_ref, out_ref, owners_buf, requests_buf, sems):
    requests, columns = query_ref.shape
    per_device = owners_ref.shape[1]
    copies = [
        pltpu.make_async_copy(query_ref, out_ref.at[:, :columns], sems.at[0]),
        pltpu.make_async_copy(owners_ref, owners_buf, sems.at[1]),
        pltpu.make_async_copy(requests_ref, requests_buf, sems.at[2]),
    ]
    for copy in copies:
        copy.start()
    copies[1].wait()
    copies[2].wait()
    code = (owners_buf[...] * requests + requests_buf[...]).astype(jnp.float32)
    spare = jnp.zeros((1, out_ref.shape[1] - columns - per_device), jnp.float32)
    code = jnp.concatenate([code, spare], axis=1)
    out_ref[:, columns:] = jnp.broadcast_to(code, (requests, code.shape[1])).astype(out_ref.dtype)
    copies[0].wait()


def make_message(query, owners, requests):
    count, columns = query.shape
    lanes = -(-owners.shape[1] // 128) * 128
    return pl.pallas_call(
        message_kernel,
        in_specs=[pl.BlockSpec(memory_space=pl.ANY)] * 3,
        out_specs=pl.BlockSpec(memory_space=pltpu.VMEM),
        out_shape=jax.ShapeDtypeStruct((count, columns + lanes), query.dtype),
        scratch_shapes=[
            pltpu.VMEM(owners.shape, owners.dtype),
            pltpu.VMEM(requests.shape, requests.dtype),
            pltpu.SemaphoreType.DMA((3,)),
        ],
        compiler_params=params(16),
        cost_estimate=pl.CostEstimate(flops=10**11, bytes_accessed=10**4, transcendentals=0),
        name="make_message",
    )(in_hbm(query), in_hbm(owners), in_hbm(requests))


def cache_kernel(
    lengths_ref, query_ref, cache_ref, signs_ref, mixed_ref, stats_ref, query_buf, top_buf, total_buf, mixed_buf
):
    requests, span, _ = cache_ref.shape
    blocks, size = signs_ref.shape
    heads = blocks // 2
    width = heads * size
    count = query_ref.shape[1] // size
    group = count // heads
    norm = 1.0 / math.sqrt(size)
    matrix = hadamard_tile(size)
    signs = (2 * signs_ref[...] - 1).astype(jnp.float32)
    query = query_ref[...].astype(jnp.float32)
    query = jnp.concatenate(
        [query[:, h * size : (h + 1) * size] * signs[h // group : h // group + 1] for h in range(count)], axis=0
    )
    query_buf[...] = jnp.dot(query.astype(jnp.bfloat16), matrix, preferred_element_type=jnp.float32) * norm
    rows = 2 * count
    kv_head = lax.broadcasted_iota(jnp.int32, (rows, width), 0) // group & (heads - 1)
    own_head = kv_head == lax.broadcasted_iota(jnp.int32, (rows, width), 1) // size
    first = lax.broadcasted_iota(jnp.int32, (rows, span), 0) < count
    position = lax.axis_index("tp") * span + lax.broadcasted_iota(jnp.int32, (rows, span), 1)
    pairs = range(0, requests, 2)
    scores = []
    for r in pairs:
        both = [query_buf[pl.ds(r + i, count, stride=requests), :] for i in range(2)]
        wide = jnp.concatenate([jnp.concatenate(both, axis=0)] * heads, axis=1)
        wide = jnp.where(own_head, wide, 0.0).astype(jnp.bfloat16)
        keys = cache_ref[r : r + 2, :, :width].reshape(2 * span, width)
        scores.append(lax.dot_general(wide, keys, NT, preferred_element_type=jnp.float32))
    probs = []
    for r, score in zip(pairs, scores):
        score = jnp.where(first, score[:, :span], score[:, span:]) * norm
        live = position < jnp.where(first, lengths_ref[0, 0, r], lengths_ref[0, 0, r + 1])
        top = jnp.max(jnp.where(live, score, LOWEST), axis=1, keepdims=True)
        prob = jnp.where(live, jnp.exp(score - top), 0.0)
        total = jnp.sum(prob, axis=1, keepdims=True)
        at = slice(r * count, (r + 2) * count)
        top_buf[at, :] = jnp.broadcast_to(top, (rows, size))
        total_buf[at, :] = jnp.broadcast_to(total, (rows, size))
        probs.append(
            jnp.concatenate([jnp.where(first, prob, 0.0), jnp.where(first, 0.0, prob)], axis=1).astype(jnp.bfloat16)
        )
    mixed = []
    for r, prob in zip(pairs, probs):
        values = cache_ref[r : r + 2, :, width:].reshape(2 * span, width)
        wide = jnp.dot(prob, values, preferred_element_type=jnp.float32)
        wide = jnp.where(own_head, wide, 0.0)
        mixed.append(sum(wide[:, k * size : (k + 1) * size] for k in range(heads)))
    mixed = jnp.concatenate(mixed, axis=0)
    high = mixed.astype(jnp.bfloat16)
    low = (mixed - high.astype(jnp.float32)).astype(jnp.bfloat16)
    plain = jnp.dot(high, matrix, preferred_element_type=jnp.float32)
    mixed_buf[...] = plain + jnp.dot(low, matrix, preferred_element_type=jnp.float32)
    lane = lax.broadcasted_iota(jnp.int32, (requests, stats_ref.shape[1]), 1)
    tops = jnp.full(lane.shape, 0.0, jnp.float32)
    totals = jnp.ones(lane.shape, jnp.float32)
    for h in range(count):
        pick = pl.ds(h, requests, stride=count)
        column = slice(h * size, (h + 1) * size)
        k = heads + h // group
        mixed_ref[:, column] = mixed_buf[pick, :] * (signs[k : k + 1] * norm)
        tops = jnp.where(lane == h, top_buf[pick, :], tops)
        totals = jnp.where(lane == h, total_buf[pick, :], totals)
    stats_ref[:requests, :] = tops
    stats_ref[requests:, :] = totals


def cache_part(lengths, query, cache, signs):
    requests, span, width = cache.shape
    size = signs.shape[1]
    columns = query.shape[1]
    vmem = pl.BlockSpec(memory_space=pltpu.VMEM)
    return pl.pallas_call(
        cache_kernel,
        in_specs=[pl.BlockSpec(memory_space=pltpu.SMEM)] + [vmem] * 3,
        out_shape=[
            jax.ShapeDtypeStruct(query.shape, jnp.float32),
            jax.ShapeDtypeStruct((2 * requests, size), jnp.float32),
        ],
        scratch_shapes=[pltpu.VMEM((requests * columns // size, size), jnp.float32)] * 4,
        compiler_params=params(),
        cost_estimate=pl.CostEstimate(
            flops=4 * span * requests * columns,
            bytes_accessed=2 * requests * span * width,
            transcendentals=span * requests * columns // size,
        ),
        name="cache_part",
    )(lengths, query, cache, signs)


def code_row(message_refs, start, requests, tokens):
    count = len(message_refs)
    me = lax.axis_index("seq")
    pieces = [ref[0:1, start : start + tokens // count].astype(jnp.float32) for ref in message_refs]
    row = [sum(jnp.where(me ^ d == at, pieces[d], 0.0) for d in range(count)) for at in range(count)]
    code = jnp.concatenate(row, axis=1).astype(jnp.int32)
    return ((code // requests) ^ me) * requests + code % requests


def score_kernel(heads, start, keys_ref, *refs):
    message_refs, (scores_ref, code_ref) = by_distance(refs[:-2], QUERY_ORDER), refs[-2:]
    requests = message_refs[0].shape[0]
    tokens, width = keys_ref.shape
    size = width // heads
    group = start // width
    code = code_row(message_refs, start, requests, tokens)
    code_ref[...] = jnp.broadcast_to(code, code_ref.shape)
    span = len(message_refs) * requests
    here = lax.broadcasted_iota(jnp.int32, (span, tokens), 0) == code
    queries = [ref[:, :start].astype(jnp.float32) for ref in message_refs]
    for k in range(heads):
        rows = []
        for g in range(group):
            at = (k * group + g) * size
            rows += [query[:, at : at + size] for query in queries]
        query = jnp.concatenate(rows, axis=0).astype(jnp.bfloat16)
        keys = keys_ref[:, k * size : (k + 1) * size]
        scores = lax.dot_general(query, keys, NT, preferred_element_type=jnp.float32)
        lines = [
            jnp.sum(jnp.where(here, scores[g * span : (g + 1) * span], 0.0), axis=0, keepdims=True)
            for g in range(group)
        ]
        lines = jnp.concatenate(lines, axis=0) * (1.0 / math.sqrt(size))
        scores_ref[k * group : (k + 1) * group, :] = lines.astype(scores_ref.dtype)


def partial_scores(heads, columns, keys, messages):
    tokens, width = keys.shape
    return pl.pallas_call(
        functools.partial(score_kernel, heads, columns),
        out_shape=[
            jax.ShapeDtypeStruct((columns * heads // width, tokens), jnp.bfloat16),
            jax.ShapeDtypeStruct((8, tokens), jnp.int32),
        ],
        compiler_params=params(),
        cost_estimate=pl.CostEstimate(flops=10**11, bytes_accessed=10**4, transcendentals=0),
        name="partial_scores",
    )(keys, *arranged(messages, QUERY_ORDER))


def packed(value, count):
    lane = lax.broadcasted_iota(jnp.int32, value.shape, 1)
    high = value.astype(jnp.bfloat16).astype(jnp.float32)
    middle = (value - high).astype(jnp.bfloat16).astype(jnp.float32)
    low = value - high - middle
    middle, low = pltpu.roll(middle, count, 1), pltpu.roll(low, 2 * count, 1)
    return jnp.where(lane < count, high, jnp.where(lane < 2 * count, middle, low))


def unpacked(message, at, count):
    parts = [message[:, at + part * count : at + (part + 1) * count] for part in range(3)]
    return parts[0] + parts[1] + parts[2]


def mix_kernel(heads, requests, code_ref, values_ref, near_ref, cache_ref, cache_stats_ref, *refs):
    score_refs, (share_ref, far_ref) = refs[:4], refs[4:]
    own, before, across, after = [ref[...].astype(jnp.float32) for ref in score_refs]
    scores = (own + across) + (before + after)
    tokens, width = values_ref.shape
    size = width // heads
    count, columns = scores.shape[0], cache_ref.shape[1]
    group = count // heads
    span = 2 * requests
    row = lax.broadcasted_iota(jnp.int32, (span, tokens), 0)
    here = jnp.where(row < requests, row, row + requests) == code_ref[0:1, :]
    lane = lax.broadcasted_iota(jnp.int32, (requests, cache_stats_ref.shape[1]), 1)
    tops = jnp.full(lane.shape, 0.0, jnp.float32)
    totals = jnp.zeros(lane.shape, jnp.float32)
    parts = []
    for k in range(heads):
        weights = []
        for g in range(group):
            h = k * group + g
            line = jnp.where(here, jnp.broadcast_to(scores[h : h + 1, :], (span, tokens)), LOWEST)
            top = jnp.maximum(jnp.max(line, axis=1, keepdims=True), 0.1 * LOWEST)
            probs = jnp.exp(line - top)
            total = jnp.sum(probs, axis=1, keepdims=True)
            weights.append(probs)
            tops = jnp.where(lane == h, top[:requests], tops)
            totals = jnp.where(lane == h, total[:requests], totals)
        weights = jnp.concatenate(weights, axis=0).astype(jnp.bfloat16)
        part = slice(k * size, (k + 1) * size)
        mixed = jnp.dot(weights, values_ref[:, part], preferred_element_type=jnp.float32)
        mixed = mixed + jnp.dot(weights, near_ref[:, part], preferred_element_type=jnp.float32)
        for g in range(group):
            at = slice((k * group + g) * size, (k * group + g + 1) * size)
            parts.append(mixed[g * span : g * span + requests])
            far_ref[:, at] = mixed[g * span + requests : (g + 1) * span].astype(far_ref.dtype)
    cache_tops = cache_stats_ref[:requests, :]
    both = jnp.maximum(cache_tops, tops)
    cache_factor = jnp.exp(cache_tops - both)
    new_factor = jnp.exp(tops - both)
    total = cache_stats_ref[requests:, :] * cache_factor + totals * new_factor
    for h, part in enumerate(parts):
        at = slice(h * size, (h + 1) * size)
        share = cache_ref[:, at] * cache_factor[:, h : h + 1] + part * new_factor[:, h : h + 1]
        share_ref[:, at] = share.astype(share_ref.dtype)
    lanes = cache_stats_ref.shape[1]
    for i, value in enumerate((both, total, new_factor)):
        share_ref[:, columns + i * lanes : columns + (i + 1) * lanes] = packed(value, count).astype(share_ref.dtype)


def mix(heads, code, values, near_values, cache_mixed, cache_stats, scores):
    requests, lanes = cache_stats.shape[0] // 2, cache_stats.shape[1]
    columns = cache_mixed.shape[1]
    return pl.pallas_call(
        functools.partial(mix_kernel, heads, requests),
        out_shape=[
            jax.ShapeDtypeStruct((requests, columns + 3 * lanes), jnp.bfloat16),
            jax.ShapeDtypeStruct((requests, columns), jnp.bfloat16),
        ],
        compiler_params=params(),
        name="mix",
    )(code, values, near_values, cache_mixed, cache_stats, *arranged(scores, SCORE_ORDER))


def weigh_kernel(count, own_ref, other_ref, *out_refs):
    columns = out_refs[0].shape[1]
    size = columns // count
    lanes = (own_ref.shape[1] - columns) // 3
    first = lax.axis_index("tp") == 0

    def stats(ref):
        message = ref[:, columns:].astype(jnp.float32)
        return [unpacked(message, i * lanes, count) for i in range(3)]

    own_top, own_total, own_new = stats(own_ref)
    other_top, other_total, other_new = stats(other_ref)
    both = jnp.maximum(own_top, other_top)
    own_factor, other_factor = jnp.exp(own_top - both), jnp.exp(other_top - both)
    own_total, other_total = own_total * own_factor, other_total * other_factor
    total = jnp.where(first, own_total, other_total) + jnp.where(first, other_total, own_total)
    inverse = 1.0 / total
    for i, (ref, factor, new) in enumerate(((own_ref, own_factor, own_new), (other_ref, other_factor, other_new))):
        factor = factor * inverse
        far_factor = factor * new
        base_ref, weight_ref = out_refs[2 * i], out_refs[2 * i + 1]
        for h in range(count):
            at = slice(h * size, (h + 1) * size)
            base_ref[:, at] = ref[:, at].astype(jnp.float32) * factor[:, h : h + 1]
            weight_ref[:, at] = jnp.broadcast_to(far_factor[:, h : h + 1], (ref.shape[0], size))


def weigh(count, columns, own, other):
    return pl.pallas_call(
        functools.partial(weigh_kernel, count),
        out_shape=[jax.ShapeDtypeStruct((own.shape[0], columns), jnp.float32)] * 4,
        compiler_params=params(),
        name="weigh",
    )(own, other)


def finish_kernel(own_base, own_weight, other_base, other_weight, *refs):
    out_ref = refs[-1]
    own_far, other_far = [refs[i] for i in FINISH_PLACES]
    columns = out_ref.shape[1]
    terms = [
        base[...] + far[:, :columns].astype(jnp.float32) * weight[...]
        for base, far, weight in ((own_base, own_far, own_weight), (other_base, other_far, other_weight))
    ]
    out_ref[...] = (terms[0] + terms[1]).astype(out_ref.dtype)


def finish(weighed, own_far, other_far):
    arrived = (own_far, other_far)
    return pl.pallas_call(
        finish_kernel,
        out_shape=jax.ShapeDtypeStruct(weighed[0].shape, own_far.dtype),
        compiler_params=params(),
        name="finish",
    )(*weighed, *[arrived[FINISH_PLACES.index(i)] for i in range(2)])


def from_partner(x, axis, distance):
    count = lax.axis_size(axis)
    return lax.ppermute(x, axis, [(i, i ^ distance) for i in range(count)])


def from_behind(x, axis, distance):
    count = lax.axis_size(axis)
    return lax.ppermute(x, axis, [(i, (i + distance) % count) for i in range(count)])


def on_device(tokens, kv_weight, owners, requests, signs, queries, kv_cache, lengths):
    seq_count = lax.axis_size("seq")
    heads = signs.shape[0] // 2
    query = queries[0, 0]
    request_count, columns = query.shape
    message = make_message(query, owners[:, :, 0], requests)
    messages = [message] + [from_partner(message, "seq", d) for d in range(1, seq_count)]
    keys, values = project(tokens, kv_weight)
    near_values = from_partner(values, "seq", 1)
    scores, code = partial_scores(heads, columns, keys, messages)
    scores = [scores] + [from_behind(scores, "seq", d) for d in range(1, seq_count)]
    cache_mixed, cache_stats = cache_part(lengths, query, kv_cache[0, 0], signs)
    share, far = mix(heads, code, values, near_values, cache_mixed, cache_stats, scores)
    far_pairs = [(i, i ^ 5) for i in range(2 * seq_count)]
    weighed = weigh(columns // signs.shape[1], columns, share, from_partner(share, "tp", 1))
    diagonal = lax.ppermute(far, ("seq", "tp"), far_pairs)
    output = finish(weighed, from_partner(far, "seq", 2), diagonal)
    return output.reshape(1, 1, request_count, columns)


def hadamard(order):
    rows = lax.broadcasted_iota(jnp.int32, (order, order), 0)
    cols = lax.broadcasted_iota(jnp.int32, (order, order), 1)
    parity = jnp.zeros((order, order), jnp.int32)
    for bit_number in range(order.bit_length() - 1):
        parity = parity + rows // 2**bit_number % 2 * (cols // 2**bit_number % 2)
    return (1 - 2 * (parity % 2)).astype(jnp.float32)


def rotate(blocks, sign_rows, matrix):
    product = jnp.einsum(
        "...h,hk->...k", blocks * sign_rows, matrix, precision=lax.Precision.HIGHEST
    )
    return product / math.sqrt(matrix.shape[0])


def encode(rotated):
    largest = jnp.max(jnp.abs(rotated), axis=-1) + 1e-06
    scales = largest.astype(jnp.bfloat16)
    encoded = (rotated / scales.astype(jnp.float32)[..., None]).astype(jnp.bfloat16)
    return (encoded, scales)


def decode(encoded, scales):
    return (encoded.astype(jnp.float32) * scales.astype(jnp.float32)[..., None]).astype(
        jnp.bfloat16
    )


def slot_numbers(targets, count, room):
    onehot = (targets[:, None] == lax.iota(jnp.int32, count)[None, :]).astype(jnp.int32)
    within = jnp.sum((jnp.cumsum(onehot, axis=0) - 1) * onehot, axis=1)
    return targets * room + within


def on_device_long(tokens, kv_weight, owners, requests, signs, queries, kv_cache, lengths):
    seq_count = lax.axis_size("seq")
    per_device = owners.shape[1]
    slots = max(2, (2 * per_device + seq_count - 1) // seq_count)
    head_blocks = signs.shape[0]
    kv_heads = head_blocks // 2
    head_size = signs.shape[1]
    matrix = hadamard(head_size)
    sign_rows = (2 * signs - 1).astype(jnp.float32)
    summed = lax.psum_scatter(
        jnp.dot(tokens, kv_weight, preferred_element_type=jnp.float32).astype(jnp.bfloat16),
        "seq",
        scatter_dimension=0,
        tiled=True,
    ).astype(jnp.float32)
    encoded, scales = encode(
        rotate(summed.reshape(per_device, head_blocks, head_size), sign_rows, matrix)
    )
    slot_index = slot_numbers(owners[0, :, 0], seq_count, slots)
    slot_total = seq_count * slots
    send_values = (
        jnp.zeros((slot_total, head_blocks, head_size), jnp.bfloat16).at[slot_index].set(encoded)
    )
    send_scales = jnp.zeros((slot_total, head_blocks), jnp.bfloat16).at[slot_index].set(scales)
    send_codes = jnp.zeros((slot_total,), jnp.int32).at[slot_index].set(requests[0] + 1)
    got_values, got_scales, arrived_codes = (
        lax.all_to_all(send_values, "seq", split_axis=0, concat_axis=0, tiled=True),
        lax.all_to_all(send_scales, "seq", split_axis=0, concat_axis=0, tiled=True),
        lax.all_to_all(send_codes, "seq", split_axis=0, concat_axis=0, tiled=True),
    )
    arrived = decode(got_values, got_scales)
    query = queries[0, 0]
    request_count = query.shape[0]
    group = query.shape[1] // (kv_heads * head_size)
    query_blocks = query.astype(jnp.float32).reshape(request_count, kv_heads, group, head_size)
    query_rot = rotate(query_blocks, sign_rows[:kv_heads][:, None, :], matrix).astype(jnp.bfloat16)
    local_cache = kv_cache[0, 0]
    cache_span = local_cache.shape[1]
    local_cache = local_cache.reshape(request_count, cache_span, head_blocks, head_size)
    score_scale = 1.0 / math.sqrt(head_size)
    lowest = -1e30
    highest = lax.Precision.HIGHEST
    score_cache = (
        jnp.einsum(
            "rkgd,rckd->rkgc",
            query_rot,
            local_cache[:, :, :kv_heads],
            preferred_element_type=jnp.float32,
        )
        * score_scale
    )
    score_new = (
        jnp.einsum(
            "rkgd,nkd->rkgn", query_rot, arrived[:, :kv_heads], preferred_element_type=jnp.float32
        )
        * score_scale
    )
    positions = lax.axis_index("tp") * cache_span + lax.iota(jnp.int32, cache_span)
    mask_cache = (positions[None, :] < lengths[0, 0][:, None])[:, None, None, :]
    match = arrived_codes[None, :] == (lax.iota(jnp.int32, request_count) + 1)[:, None]
    mask_new = match[:, None, None, :]
    top = jnp.maximum(
        jnp.max(jnp.where(mask_cache, score_cache, lowest), axis=-1),
        jnp.max(jnp.where(mask_new, score_new, lowest), axis=-1),
    )
    probs_cache = jnp.where(mask_cache, jnp.exp(score_cache - top[..., None]), 0.0)
    probs_new = jnp.where(mask_new, jnp.exp(score_new - top[..., None]), 0.0)
    total = jnp.sum(probs_cache, axis=-1) + jnp.sum(probs_new, axis=-1)
    mixed = jnp.einsum(
        "rkgc,rckd->rkgd",
        probs_cache,
        local_cache[:, :, kv_heads:].astype(jnp.float32),
        precision=highest,
    )
    mixed = mixed + jnp.einsum(
        "rkgn,nkd->rkgd", probs_new, arrived[:, kv_heads:].astype(jnp.float32), precision=highest
    )
    shared_top = lax.pmax(top, "tp")
    factor = jnp.exp(top - shared_top)
    total, mixed = (
        lax.psum((total * factor).astype(jnp.bfloat16), "tp").astype(jnp.float32),
        lax.psum((mixed * factor[..., None]).astype(jnp.bfloat16), "tp").astype(jnp.float32),
    )
    mixed = mixed / total[..., None]
    output = rotate(mixed, 1.0, matrix) * sign_rows[kv_heads:][None, :, None, :]
    return output.reshape(1, 1, request_count, group * kv_heads * head_size).astype(jnp.bfloat16)


def solution(mesh):
    placed = (
        P(("groups", "tp", "section"), "seq"),
        P("seq", None),
        P(("groups", "tp", "section"), "seq", None),
        P(("groups", "tp", "section"), "seq"),
        P(),
        P(("groups", "seq"), "section", None, None),
        P(("groups", "seq"), "section", None, "tp", None),
        P(("groups", "seq"), "section", None),
    )
    short = mesh.shape["seq"] == 4 and mesh.shape["tp"] == 2
    return jax.shard_map(
        on_device if short else on_device_long,
        mesh=mesh,
        in_specs=placed,
        out_specs=P(("groups", "seq"), "section", None, None),
        check_vma=False,
    )
```

```python
import functools
import math

import jax
import jax.numpy as jnp
from jax import lax
from jax.experimental import pallas as pl
from jax.experimental.pallas import tpu as pltpu
from jax.sharding import PartitionSpec as P

LOWEST = -1e30
MIB = 1024 * 1024
NT = (((1,), (1,)), ((), ()))


def params(mib=32):
    return pltpu.CompilerParams(vmem_limit_bytes=mib * MIB)


def in_hbm(x):
    return pltpu.with_memory_space_constraint(x, pltpu.HBM)


def in_vmem(x):
    return pltpu.with_memory_space_constraint(x, pltpu.VMEM)


def hadamard_tile(order):
    rows = lax.broadcasted_iota(jnp.int32, (order, order), 0)
    cols = lax.broadcasted_iota(jnp.int32, (order, order), 1)
    common = rows & cols
    parity = jnp.zeros((order, order), jnp.int32)
    for bit_number in range(order.bit_length() - 1):
        parity = parity ^ (common >> bit_number)
    return (1 - 2 * (parity & 1)).astype(jnp.float32).astype(jnp.bfloat16)


QUERY_ORDER = (3, 2, 1)
SCORE_ORDER = (1, 2, 3)
FINISH_PLACES = (2, 1, 0)


def arranged(blocks, order):
    return [blocks[0]] + [blocks[d] for d in order]


def by_distance(refs, order):
    return [refs[0]] + [refs[1 + order.index(d)] for d in range(1, len(refs))]


def project_kernel(tokens_ref, weight_ref, keys_ref, values_ref):
    width = keys_ref.shape[1]
    for out_ref, columns in ((keys_ref, slice(0, width)), (values_ref, slice(width, 2 * width))):
        out_ref[...] = jnp.dot(
            tokens_ref[...], weight_ref[:, columns], preferred_element_type=jnp.float32
        ).astype(out_ref.dtype)


def project(tokens, weight):
    rows, features = tokens.shape
    width = weight.shape[1] // 2
    vmem = pl.BlockSpec(memory_space=pltpu.VMEM)
    return pl.pallas_call(
        project_kernel,
        in_specs=[vmem] * 2,
        out_specs=[vmem] * 2,
        out_shape=[jax.ShapeDtypeStruct((rows, width), jnp.bfloat16)] * 2,
        compiler_params=params(32),
        cost_estimate=pl.CostEstimate(
            flops=4 * rows * features * width,
            bytes_accessed=2 * (rows * features + 2 * features * width),
            transcendentals=0,
        ),
        name="project",
    )(in_vmem(tokens), in_vmem(weight))


def message_kernel(query_ref, owners_ref, requests_ref, out_ref, owners_buf, requests_buf, sems):
    requests, columns = query_ref.shape
    per_device = owners_ref.shape[1]
    copies = [
        pltpu.make_async_copy(query_ref, out_ref.at[:, :columns], sems.at[0]),
        pltpu.make_async_copy(owners_ref, owners_buf, sems.at[1]),
        pltpu.make_async_copy(requests_ref, requests_buf, sems.at[2]),
    ]
    for copy in copies:
        copy.start()
    copies[1].wait()
    copies[2].wait()
    code = (owners_buf[...] * requests + requests_buf[...]).astype(jnp.float32)
    spare = jnp.zeros((1, out_ref.shape[1] - columns - per_device), jnp.float32)
    code = jnp.concatenate([code, spare], axis=1)
    out_ref[:, columns:] = jnp.broadcast_to(code, (requests, code.shape[1])).astype(out_ref.dtype)
    copies[0].wait()


def make_message(query, owners, requests):
    count, columns = query.shape
    lanes = -(-owners.shape[1] // 128) * 128
    return pl.pallas_call(
        message_kernel,
        in_specs=[pl.BlockSpec(memory_space=pl.ANY)] * 3,
        out_specs=pl.BlockSpec(memory_space=pltpu.VMEM),
        out_shape=jax.ShapeDtypeStruct((count, columns + lanes), query.dtype),
        scratch_shapes=[
            pltpu.VMEM(owners.shape, owners.dtype),
            pltpu.VMEM(requests.shape, requests.dtype),
            pltpu.SemaphoreType.DMA((3,)),
        ],
        compiler_params=params(16),
        cost_estimate=pl.CostEstimate(flops=10**11, bytes_accessed=10**4, transcendentals=0),
        name="make_message",
    )(in_hbm(query), in_hbm(owners), in_hbm(requests))


def cache_kernel(
    lengths_ref, query_ref, cache_ref, signs_ref, mixed_ref, stats_ref, query_buf, top_buf, total_buf, mixed_buf
):
    requests, span, _ = cache_ref.shape
    blocks, size = signs_ref.shape
    heads = blocks // 2
    width = heads * size
    count = query_ref.shape[1] // size
    group = count // heads
    norm = 1.0 / math.sqrt(size)
    matrix = hadamard_tile(size)
    signs = (2 * signs_ref[...] - 1).astype(jnp.float32)
    query = query_ref[...].astype(jnp.float32)
    query = jnp.concatenate(
        [query[:, h * size : (h + 1) * size] * signs[h // group : h // group + 1] for h in range(count)], axis=0
    )
    query_buf[...] = jnp.dot(query.astype(jnp.bfloat16), matrix, preferred_element_type=jnp.float32) * norm
    rows = 2 * count
    kv_head = lax.broadcasted_iota(jnp.int32, (rows, width), 0) // group & (heads - 1)
    own_head = kv_head == lax.broadcasted_iota(jnp.int32, (rows, width), 1) // size
    first = lax.broadcasted_iota(jnp.int32, (rows, span), 0) < count
    position = lax.axis_index("tp") * span + lax.broadcasted_iota(jnp.int32, (rows, span), 1)
    pairs = range(0, requests, 2)
    scores = []
    for r in pairs:
        both = [query_buf[pl.ds(r + i, count, stride=requests), :] for i in range(2)]
        wide = jnp.concatenate([jnp.concatenate(both, axis=0)] * heads, axis=1)
        wide = jnp.where(own_head, wide, 0.0).astype(jnp.bfloat16)
        keys = cache_ref[r : r + 2, :, :width].reshape(2 * span, width)
        scores.append(lax.dot_general(wide, keys, NT, preferred_element_type=jnp.float32))
    probs = []
    for r, score in zip(pairs, scores):
        score = jnp.where(first, score[:, :span], score[:, span:]) * norm
        live = position < jnp.where(first, lengths_ref[0, 0, r], lengths_ref[0, 0, r + 1])
        top = jnp.max(jnp.where(live, score, LOWEST), axis=1, keepdims=True)
        prob = jnp.where(live, jnp.exp(score - top), 0.0)
        total = jnp.sum(prob, axis=1, keepdims=True)
        at = slice(r * count, (r + 2) * count)
        top_buf[at, :] = jnp.broadcast_to(top, (rows, size))
        total_buf[at, :] = jnp.broadcast_to(total, (rows, size))
        probs.append(
            jnp.concatenate([jnp.where(first, prob, 0.0), jnp.where(first, 0.0, prob)], axis=1).astype(jnp.bfloat16)
        )
    mixed = []
    for r, prob in zip(pairs, probs):
        values = cache_ref[r : r + 2, :, width:].reshape(2 * span, width)
        wide = jnp.dot(prob, values, preferred_element_type=jnp.float32)
        wide = jnp.where(own_head, wide, 0.0)
        mixed.append(sum(wide[:, k * size : (k + 1) * size] for k in range(heads)))
    mixed = jnp.concatenate(mixed, axis=0)
    high = mixed.astype(jnp.bfloat16)
    low = (mixed - high.astype(jnp.float32)).astype(jnp.bfloat16)
    plain = jnp.dot(high, matrix, preferred_element_type=jnp.float32)
    mixed_buf[...] = plain + jnp.dot(low, matrix, preferred_element_type=jnp.float32)
    lane = lax.broadcasted_iota(jnp.int32, (requests, stats_ref.shape[1]), 1)
    tops = jnp.full(lane.shape, 0.0, jnp.float32)
    totals = jnp.ones(lane.shape, jnp.float32)
    for h in range(count):
        pick = pl.ds(h, requests, stride=count)
        column = slice(h * size, (h + 1) * size)
        k = heads + h // group
        mixed_ref[:, column] = mixed_buf[pick, :] * (signs[k : k + 1] * norm)
        tops = jnp.where(lane == h, top_buf[pick, :], tops)
        totals = jnp.where(lane == h, total_buf[pick, :], totals)
    stats_ref[:requests, :] = tops
    stats_ref[requests:, :] = totals


def cache_part(lengths, query, cache, signs):
    requests, span, width = cache.shape
    size = signs.shape[1]
    columns = query.shape[1]
    vmem = pl.BlockSpec(memory_space=pltpu.VMEM)
    return pl.pallas_call(
        cache_kernel,
        in_specs=[pl.BlockSpec(memory_space=pltpu.SMEM)] + [vmem] * 3,
        out_shape=[
            jax.ShapeDtypeStruct(query.shape, jnp.float32),
            jax.ShapeDtypeStruct((2 * requests, size), jnp.float32),
        ],
        scratch_shapes=[pltpu.VMEM((requests * columns // size, size), jnp.float32)] * 4,
        compiler_params=params(),
        cost_estimate=pl.CostEstimate(
            flops=4 * span * requests * columns,
            bytes_accessed=2 * requests * span * width,
            transcendentals=span * requests * columns // size,
        ),
        name="cache_part",
    )(lengths, query, cache, signs)


def code_row(message_refs, start, requests, tokens):
    count = len(message_refs)
    me = lax.axis_index("seq")
    pieces = [ref[0:1, start : start + tokens // count].astype(jnp.float32) for ref in message_refs]
    row = [sum(jnp.where(me ^ d == at, pieces[d], 0.0) for d in range(count)) for at in range(count)]
    code = jnp.concatenate(row, axis=1).astype(jnp.int32)
    return ((code // requests) ^ me) * requests + code % requests


def score_kernel(heads, start, keys_ref, *refs):
    message_refs, (scores_ref, code_ref) = by_distance(refs[:-2], QUERY_ORDER), refs[-2:]
    requests = message_refs[0].shape[0]
    tokens, width = keys_ref.shape
    size = width // heads
    group = start // width
    code = code_row(message_refs, start, requests, tokens)
    code_ref[...] = jnp.broadcast_to(code, code_ref.shape)
    span = len(message_refs) * requests
    here = lax.broadcasted_iota(jnp.int32, (span, tokens), 0) == code
    queries = [ref[:, :start].astype(jnp.float32) for ref in message_refs]
    for k in range(heads):
        rows = []
        for g in range(group):
            at = (k * group + g) * size
            rows += [query[:, at : at + size] for query in queries]
        query = jnp.concatenate(rows, axis=0).astype(jnp.bfloat16)
        keys = keys_ref[:, k * size : (k + 1) * size]
        scores = lax.dot_general(query, keys, NT, preferred_element_type=jnp.float32)
        lines = [
            jnp.sum(jnp.where(here, scores[g * span : (g + 1) * span], 0.0), axis=0, keepdims=True)
            for g in range(group)
        ]
        lines = jnp.concatenate(lines, axis=0) * (1.0 / math.sqrt(size))
        scores_ref[k * group : (k + 1) * group, :] = lines.astype(scores_ref.dtype)


def partial_scores(heads, columns, keys, messages):
    tokens, width = keys.shape
    return pl.pallas_call(
        functools.partial(score_kernel, heads, columns),
        out_shape=[
            jax.ShapeDtypeStruct((columns * heads // width, tokens), jnp.bfloat16),
            jax.ShapeDtypeStruct((8, tokens), jnp.int32),
        ],
        compiler_params=params(),
        cost_estimate=pl.CostEstimate(flops=10**11, bytes_accessed=10**4, transcendentals=0),
        name="partial_scores",
    )(keys, *arranged(messages, QUERY_ORDER))


def packed(value, count):
    lane = lax.broadcasted_iota(jnp.int32, value.shape, 1)
    high = value.astype(jnp.bfloat16).astype(jnp.float32)
    middle = (value - high).astype(jnp.bfloat16).astype(jnp.float32)
    low = value - high - middle
    middle, low = pltpu.roll(middle, count, 1), pltpu.roll(low, 2 * count, 1)
    return jnp.where(lane < count, high, jnp.where(lane < 2 * count, middle, low))


def unpacked(message, at, count):
    parts = [message[:, at + part * count : at + (part + 1) * count] for part in range(3)]
    return parts[0] + parts[1] + parts[2]


def mix_kernel(heads, requests, code_ref, values_ref, near_ref, cache_ref, cache_stats_ref, *refs):
    score_refs, (share_ref, far_ref) = refs[:4], refs[4:]
    own, before, across, after = [ref[...].astype(jnp.float32) for ref in score_refs]
    scores = (own + across) + (before + after)
    tokens, width = values_ref.shape
    size = width // heads
    count, columns = scores.shape[0], cache_ref.shape[1]
    group = count // heads
    span = 2 * requests
    row = lax.broadcasted_iota(jnp.int32, (span, tokens), 0)
    here = jnp.where(row < requests, row, row + requests) == code_ref[0:1, :]
    lane = lax.broadcasted_iota(jnp.int32, (requests, cache_stats_ref.shape[1]), 1)
    tops = jnp.full(lane.shape, 0.0, jnp.float32)
    totals = jnp.zeros(lane.shape, jnp.float32)
    parts = []
    for k in range(heads):
        weights = []
        for g in range(group):
            h = k * group + g
            line = jnp.where(here, jnp.broadcast_to(scores[h : h + 1, :], (span, tokens)), LOWEST)
            top = jnp.maximum(jnp.max(line, axis=1, keepdims=True), 0.1 * LOWEST)
            probs = jnp.exp(line - top)
            total = jnp.sum(probs, axis=1, keepdims=True)
            weights.append(probs)
            tops = jnp.where(lane == h, top[:requests], tops)
            totals = jnp.where(lane == h, total[:requests], totals)
        weights = jnp.concatenate(weights, axis=0).astype(jnp.bfloat16)
        part = slice(k * size, (k + 1) * size)
        mixed = jnp.dot(weights, values_ref[:, part], preferred_element_type=jnp.float32)
        mixed = mixed + jnp.dot(weights, near_ref[:, part], preferred_element_type=jnp.float32)
        for g in range(group):
            at = slice((k * group + g) * size, (k * group + g + 1) * size)
            parts.append(mixed[g * span : g * span + requests])
            far_ref[:, at] = mixed[g * span + requests : (g + 1) * span].astype(far_ref.dtype)
    cache_tops = cache_stats_ref[:requests, :]
    both = jnp.maximum(cache_tops, tops)
    cache_factor = jnp.exp(cache_tops - both)
    new_factor = jnp.exp(tops - both)
    total = cache_stats_ref[requests:, :] * cache_factor + totals * new_factor
    for h, part in enumerate(parts):
        at = slice(h * size, (h + 1) * size)
        share = cache_ref[:, at] * cache_factor[:, h : h + 1] + part * new_factor[:, h : h + 1]
        share_ref[:, at] = share.astype(share_ref.dtype)
    lanes = cache_stats_ref.shape[1]
    far_ref[:, columns:] = jnp.zeros((requests, 3 * lanes), far_ref.dtype)
    for i, value in enumerate((both, total, new_factor)):
        share_ref[:, columns + i * lanes : columns + (i + 1) * lanes] = packed(value, count).astype(share_ref.dtype)


def mix(heads, code, values, near_values, cache_mixed, cache_stats, scores):
    requests, lanes = cache_stats.shape[0] // 2, cache_stats.shape[1]
    columns = cache_mixed.shape[1]
    return pl.pallas_call(
        functools.partial(mix_kernel, heads, requests),
        out_shape=[
            jax.ShapeDtypeStruct((requests, columns + 3 * lanes), jnp.bfloat16),
        ]
        * 2,
        compiler_params=params(),
        name="mix",
    )(code, values, near_values, cache_mixed, cache_stats, *arranged(scores, SCORE_ORDER))


def finish_kernel(count, own_ref, *refs):
    out_ref = refs[-1]
    other_ref, own_far_ref, other_far_ref = [refs[i] for i in FINISH_PLACES]
    columns = out_ref.shape[1]
    size = columns // count
    lanes = (own_ref.shape[1] - columns) // 3
    first = lax.axis_index("tp") == 0

    def stats(ref):
        message = ref[:, columns:].astype(jnp.float32)
        return [unpacked(message, i * lanes, count) for i in range(3)]

    own_top, own_total, own_new = stats(own_ref)
    other_top, other_total, other_new = stats(other_ref)
    both = jnp.maximum(own_top, other_top)
    own_factor, other_factor = jnp.exp(own_top - both), jnp.exp(other_top - both)
    own_total, other_total = own_total * own_factor, other_total * other_factor
    total = jnp.where(first, own_total, other_total) + jnp.where(first, other_total, own_total)
    inverse = 1.0 / total
    sides = []
    for ref, far_ref, factor, new in (
        (own_ref, own_far_ref, own_factor, own_new),
        (other_ref, other_far_ref, other_factor, other_new),
    ):
        factor = factor * inverse
        sides.append((ref, far_ref, factor, factor * new))
    for h in range(count):
        at = slice(h * size, (h + 1) * size)
        terms = [
            ref[:, at].astype(jnp.float32) * factor[:, h : h + 1]
            + far_ref[:, at].astype(jnp.float32) * far_factor[:, h : h + 1]
            for ref, far_ref, factor, far_factor in sides
        ]
        out_ref[:, at] = (terms[0] + terms[1]).astype(out_ref.dtype)


def finish(count, columns, own, other, own_far, other_far):
    arrived = (other, own_far, other_far)
    return pl.pallas_call(
        functools.partial(finish_kernel, count),
        out_shape=jax.ShapeDtypeStruct((own.shape[0], columns), jnp.bfloat16),
        compiler_params=params(),
        name="finish",
    )(own, *[arrived[FINISH_PLACES.index(i)] for i in range(3)])


def from_partner(x, axis, distance):
    count = lax.axis_size(axis)
    return lax.ppermute(x, axis, [(i, i ^ distance) for i in range(count)])


def from_behind(x, axis, distance):
    count = lax.axis_size(axis)
    return lax.ppermute(x, axis, [(i, (i + distance) % count) for i in range(count)])


def on_device(tokens, kv_weight, owners, requests, signs, queries, kv_cache, lengths):
    seq_count = lax.axis_size("seq")
    heads = signs.shape[0] // 2
    query = queries[0, 0]
    request_count, columns = query.shape
    message = make_message(query, owners[:, :, 0], requests)
    messages = [message] + [from_partner(message, "seq", d) for d in range(1, seq_count)]
    keys, values = project(tokens, kv_weight)
    near_values = from_partner(values, "seq", 1)
    scores, code = partial_scores(heads, columns, keys, messages)
    scores = [scores] + [from_partner(scores, "seq", seq_count - d) for d in range(1, seq_count)]
    cache_mixed, cache_stats = cache_part(lengths, query, kv_cache[0, 0], signs)
    share, far = mix(heads, code, values, near_values, cache_mixed, cache_stats, scores)
    far_pairs = [(i, i ^ 5) for i in range(2 * seq_count)]
    output = finish(
        columns // signs.shape[1],
        columns,
        share,
        from_partner(share, "tp", 1),
        from_partner(far, "seq", 2),
        lax.ppermute(far, ("seq", "tp"), far_pairs),
    )
    return output.reshape(1, 1, request_count, columns)


def hadamard(order):
    rows = lax.broadcasted_iota(jnp.int32, (order, order), 0)
    cols = lax.broadcasted_iota(jnp.int32, (order, order), 1)
    parity = jnp.zeros((order, order), jnp.int32)
    for bit_number in range(order.bit_length() - 1):
        parity = parity + rows // 2**bit_number % 2 * (cols // 2**bit_number % 2)
    return (1 - 2 * (parity % 2)).astype(jnp.float32)


def rotate(blocks, sign_rows, matrix):
    product = jnp.einsum(
        "...h,hk->...k", blocks * sign_rows, matrix, precision=lax.Precision.HIGHEST
    )
    return product / math.sqrt(matrix.shape[0])


def encode(rotated):
    largest = jnp.max(jnp.abs(rotated), axis=-1) + 1e-06
    scales = largest.astype(jnp.bfloat16)
    encoded = (rotated / scales.astype(jnp.float32)[..., None]).astype(jnp.bfloat16)
    return (encoded, scales)


def decode(encoded, scales):
    return (encoded.astype(jnp.float32) * scales.astype(jnp.float32)[..., None]).astype(
        jnp.bfloat16
    )


def slot_numbers(targets, count, room):
    onehot = (targets[:, None] == lax.iota(jnp.int32, count)[None, :]).astype(jnp.int32)
    within = jnp.sum((jnp.cumsum(onehot, axis=0) - 1) * onehot, axis=1)
    return targets * room + within


def on_device_long(tokens, kv_weight, owners, requests, signs, queries, kv_cache, lengths):
    seq_count = lax.axis_size("seq")
    per_device = owners.shape[1]
    slots = max(2, (2 * per_device + seq_count - 1) // seq_count)
    head_blocks = signs.shape[0]
    kv_heads = head_blocks // 2
    head_size = signs.shape[1]
    matrix = hadamard(head_size)
    sign_rows = (2 * signs - 1).astype(jnp.float32)
    summed = lax.psum_scatter(
        jnp.dot(tokens, kv_weight, preferred_element_type=jnp.float32).astype(jnp.bfloat16),
        "seq",
        scatter_dimension=0,
        tiled=True,
    ).astype(jnp.float32)
    encoded, scales = encode(
        rotate(summed.reshape(per_device, head_blocks, head_size), sign_rows, matrix)
    )
    slot_index = slot_numbers(owners[0, :, 0], seq_count, slots)
    slot_total = seq_count * slots
    send_values = (
        jnp.zeros((slot_total, head_blocks, head_size), jnp.bfloat16).at[slot_index].set(encoded)
    )
    send_scales = jnp.zeros((slot_total, head_blocks), jnp.bfloat16).at[slot_index].set(scales)
    send_codes = jnp.zeros((slot_total,), jnp.int32).at[slot_index].set(requests[0] + 1)
    got_values, got_scales, arrived_codes = (
        lax.all_to_all(send_values, "seq", split_axis=0, concat_axis=0, tiled=True),
        lax.all_to_all(send_scales, "seq", split_axis=0, concat_axis=0, tiled=True),
        lax.all_to_all(send_codes, "seq", split_axis=0, concat_axis=0, tiled=True),
    )
    arrived = decode(got_values, got_scales)
    query = queries[0, 0]
    request_count = query.shape[0]
    group = query.shape[1] // (kv_heads * head_size)
    query_blocks = query.astype(jnp.float32).reshape(request_count, kv_heads, group, head_size)
    query_rot = rotate(query_blocks, sign_rows[:kv_heads][:, None, :], matrix).astype(jnp.bfloat16)
    local_cache = kv_cache[0, 0]
    cache_span = local_cache.shape[1]
    local_cache = local_cache.reshape(request_count, cache_span, head_blocks, head_size)
    score_scale = 1.0 / math.sqrt(head_size)
    lowest = -1e30
    highest = lax.Precision.HIGHEST
    score_cache = (
        jnp.einsum(
            "rkgd,rckd->rkgc",
            query_rot,
            local_cache[:, :, :kv_heads],
            preferred_element_type=jnp.float32,
        )
        * score_scale
    )
    score_new = (
        jnp.einsum(
            "rkgd,nkd->rkgn", query_rot, arrived[:, :kv_heads], preferred_element_type=jnp.float32
        )
        * score_scale
    )
    positions = lax.axis_index("tp") * cache_span + lax.iota(jnp.int32, cache_span)
    mask_cache = (positions[None, :] < lengths[0, 0][:, None])[:, None, None, :]
    match = arrived_codes[None, :] == (lax.iota(jnp.int32, request_count) + 1)[:, None]
    mask_new = match[:, None, None, :]
    top = jnp.maximum(
        jnp.max(jnp.where(mask_cache, score_cache, lowest), axis=-1),
        jnp.max(jnp.where(mask_new, score_new, lowest), axis=-1),
    )
    probs_cache = jnp.where(mask_cache, jnp.exp(score_cache - top[..., None]), 0.0)
    probs_new = jnp.where(mask_new, jnp.exp(score_new - top[..., None]), 0.0)
    total = jnp.sum(probs_cache, axis=-1) + jnp.sum(probs_new, axis=-1)
    mixed = jnp.einsum(
        "rkgc,rckd->rkgd",
        probs_cache,
        local_cache[:, :, kv_heads:].astype(jnp.float32),
        precision=highest,
    )
    mixed = mixed + jnp.einsum(
        "rkgn,nkd->rkgd", probs_new, arrived[:, kv_heads:].astype(jnp.float32), precision=highest
    )
    shared_top = lax.pmax(top, "tp")
    factor = jnp.exp(top - shared_top)
    total, mixed = (
        lax.psum((total * factor).astype(jnp.bfloat16), "tp").astype(jnp.float32),
        lax.psum((mixed * factor[..., None]).astype(jnp.bfloat16), "tp").astype(jnp.float32),
    )
    mixed = mixed / total[..., None]
    output = rotate(mixed, 1.0, matrix) * sign_rows[kv_heads:][None, :, None, :]
    return output.reshape(1, 1, request_count, group * kv_heads * head_size).astype(jnp.bfloat16)


def solution(mesh):
    placed = (
        P(("groups", "tp", "section"), "seq"),
        P("seq", None),
        P(("groups", "tp", "section"), "seq", None),
        P(("groups", "tp", "section"), "seq"),
        P(),
        P(("groups", "seq"), "section", None, None),
        P(("groups", "seq"), "section", None, "tp", None),
        P(("groups", "seq"), "section", None),
    )
    short = mesh.shape["seq"] == 4 and mesh.shape["tp"] == 2
    return jax.shard_map(
        on_device if short else on_device_long,
        mesh=mesh,
        in_specs=placed,
        out_specs=P(("groups", "seq"), "section", None, None),
        check_vma=False,
    )
```
